32 devices in a mesh: gx: 8 (over y, x, core), gy: 4 (over z).
Axes of the slice: x: 2, y: 2, z: 4, core: 2. Of those that a mesh axis runs over, the one named last changes fastest.
Arguments:
- concentration: float32 [32, 256, 128], P('gx', 'gy'), may hold values from -4 to 4
- potential: float32 [32, 256, 128], P('gx', 'gy'), may hold values from -4 to 4
- mass_source: float32 [32, 256, 128], P('gx', 'gy'), may hold values from -7 to 7
- potential_source: float32 [32, 256, 128], P('gx', 'gy'), may hold values from -7 to 7
- pore_mask: int32 [32, 256, 128], P('gx', 'gy'), may hold values 0 or 1
- mobility_class: int32 [32, 256, 128], P('gx', 'gy'), may hold values from 0 to 7
- mobility_table: float32 [8], replicated, may hold values from 0.05 to 1
- owner_map: int32 [8, 256], P(None, 'gy'), may hold values from 0 to 7, as said below
Outputs:
- conc_out: float32 [32, 256, 128], P('gx', 'gy')
- pot_out: float32 [32, 256, 128], P('gx', 'gy')
The draws below stay inside these ranges and needn't reach their ends.
Inputs may be any that keep to these rules, and one draw needn't show every extreme that they name: `owner_map`: no owner is named by more than 16 entries of one device; in every draw, for each gy index, one owner is named by exactly 16 entries of every device of that gy index.
All inputs are finite; a program needn't handle non-finite values. No bound on the sum of `pore_mask` on one device may be relied on, other than what follows from the above.
Results may differ from the reference program's by a relative error of at most 0.000058.
Values sent between devices are 32-bit elements; how exact they have to be, the bound alone decides.
No kernel may reach another device: no remote copies, remote signals or barrier semaphores. Data moves between devices by JAX's collectives and lax.ppermute only.
A program may use at most 64 MiB of HBM per device.

```python
import math
import jax
import jax.numpy as jnp

X_DEV = 4
NB = 64
Y_DEV = 64
P_SIZE = 128
CAP = 16
NCLASS = 8
PRE = 1
POST = 1
CSWEEP = 3
NX = 32
NY = 256
N_GX = 8
N_GY = 4


def source_field(key):
    keys = jax.random.split(key, 5)
    freq_x = jax.random.randint(keys[0], (), 1, 4).astype(jnp.float32)
    freq_y = jax.random.randint(keys[1], (), 1, 4).astype(jnp.float32)
    freq_p = jax.random.randint(keys[2], (), 1, 3).astype(jnp.float32)
    phase = jax.random.uniform(keys[3], (), jnp.float32, 0.0, 2.0 * math.pi)
    coord_x = jnp.arange(NX, dtype=jnp.float32) / NX
    coord_y = jnp.arange(NY, dtype=jnp.float32) / NY
    coord_p = jnp.arange(P_SIZE, dtype=jnp.float32) / P_SIZE
    wave = jnp.sin(2.0 * math.pi * (freq_x * coord_x[:, None, None] + freq_y * coord_y[None, :, None] + freq_p * coord_p[None, None, :]) + phase)
    rough = jnp.clip(jax.random.normal(keys[4], (NX, NY, P_SIZE), jnp.float32), -4.0, 4.0)
    smooth = 1.5 * wave
    return (rough + smooth).astype(jnp.float32)


def draw_mass_source(key, part):
    return source_field(jax.random.fold_in(key, 101))


def draw_potential_source(key, part):
    return source_field(jax.random.fold_in(key, 202))


def draw_owner_map(key, part):
    device_count = N_GX * N_GY
    slot_count = N_GX * CAP
    device_keys = jax.random.split(jax.random.fold_in(key, 11), device_count)
    reward_extra = jax.random.randint(jax.random.fold_in(key, 23), (N_GY, N_GX), 0, 3 * (1 << 20))
    forced = jax.random.randint(jax.random.fold_in(key, 37), (N_GY,), 0, N_GX)
    slot_holder = jnp.arange(slot_count, dtype=jnp.int32) // CAP
    slot_index = jnp.arange(slot_count, dtype=jnp.int32)

    def one_device(device_key, cluster_index):
        noise_key, order_key = jax.random.split(device_key)
        random_jitter = jax.random.randint(noise_key, (slot_count,), 0, 1 << 20)
        ranking_value = random_jitter + reward_extra[cluster_index][slot_holder]
        ranking_value = jnp.where(slot_holder == forced[cluster_index], 1 << 22, ranking_value)
        ranking_value = ranking_value * 256 + slot_index
        order = jnp.argsort(-ranking_value, stable=True)
        chosen = slot_holder[order[:NB]]
        shuffle = jax.random.permutation(order_key, NB)
        return chosen[shuffle]
    group_ids = (jnp.arange(device_count, dtype=jnp.int32) % N_GY).astype(jnp.int32)
    rows_all = jax.vmap(one_device)(device_keys, group_ids)
    return rows_all.reshape(N_GX, N_GY * NB).astype(jnp.int32)


def with_ends(array, rng, low, largest):
    longest = array.shape.index(max(array.shape))
    spots = []
    for shift in (0, 1):
        where = [jax.random.randint(jax.random.fold_in(rng, axis), (), 0, length) for axis, length in enumerate(array.shape)]
        where[longest] = (where[longest] + shift) % array.shape[longest]
        spots.append(tuple(where))
    return array.at[spots[0]].set(low).at[spots[1]].set(largest)


def steps_of(rng, extent, cuts, least, largest):
    level, own = 1.0, jax.random.fold_in(rng, 6)
    for axis_at, shards_of in cuts:
        draws = jnp.exp(jax.random.uniform(jax.random.fold_in(own, axis_at), (shards_of,), jnp.float32, least / len(cuts), largest / len(cuts)))
        level = level * jnp.repeat(draws, extent[axis_at] // shards_of).reshape([-1 if axis == axis_at else 1 for axis in range(len(extent))])
    return level


def gaussian(key, dims, scale, bound, shards=(), kind=jnp.bfloat16):
    loudness = steps_of(key, dims, shards, -0.22, 0.18) if shards else 1.0
    drawn = jax.random.normal(key, dims, jnp.float32) * scale * loudness
    return jnp.minimum(jnp.maximum(drawn, -bound), bound).astype(kind)


def setup_inputs(seed: int = 0) -> dict:
    arg_keys = jax.random.split(jax.random.key(seed), 9)
    return {
        "concentration": gaussian(arg_keys[0], (NX, NY, P_SIZE), 0.5, 4.0, ((0, 8), (1, 4)), jnp.float32),
        "potential": gaussian(arg_keys[1], (NX, NY, P_SIZE), 0.5, 4.0, ((0, 8), (1, 4)), jnp.float32),
        "mass_source": draw_mass_source(jax.random.fold_in(arg_keys[8], 71), 0),
        "potential_source": draw_potential_source(jax.random.fold_in(arg_keys[8], 71), 0),
        "pore_mask": with_ends((jax.random.randint(arg_keys[4], (NX, NY, P_SIZE), 0, 4) < 3).astype(jnp.int32), jax.random.fold_in(arg_keys[4], 1), 0, 1),
        "mobility_class": with_ends(jax.random.randint(arg_keys[5], (NX, NY, P_SIZE), 0, NCLASS), jax.random.fold_in(arg_keys[5], 1), 0, NCLASS - 1).astype(jnp.int32),
        "mobility_table": jnp.clip(jnp.exp(jax.random.uniform(arg_keys[6], (NCLASS,), jnp.float32, math.log(0.05), math.log(1.0))), 0.05, 1.0),
        "owner_map": draw_owner_map(jax.random.fold_in(arg_keys[8], 71), 0),
    }


time_step = 0.25
split_slope = 1.0
interface = 0.5
relax_fine = 0.6
relax_coarse = 0.6
coarse_flux = 0.0625
coarse_bend = 0.125
coarse_det = 1.0 + 2.0 * coarse_flux * (split_slope + 2.0 * coarse_bend)


def lookup_mobility(pore_mask, mobility_class, mobility_table):
    values = jnp.zeros(mobility_class.shape, jnp.float32)
    for class_marker in range(NCLASS):
        values = jnp.where(mobility_class == class_marker, mobility_table[class_marker], values)
    return pore_mask.astype(jnp.float32) * values


def neighbours(padded):
    center = padded[1:-1, 1:-1, :]
    along_planes = jnp.pad(center, ((0, 0), (0, 0), (1, 1)))
    return (padded[2:, 1:-1, :], padded[:-2, 1:-1, :], padded[1:-1, 2:, :], padded[1:-1, :-2, :], along_planes[:, :, 2:], along_planes[:, :, :-2])


def face_terms(padded_mobility):
    center = padded_mobility[1:-1, 1:-1, :]
    return tuple(0.5 * (center + other) for other in neighbours(padded_mobility))


def residuals(padded_conc, padded_pot, faces, mass_source, potential_source):
    conc_now = padded_conc[1:-1, 1:-1, :]
    pot_now = padded_pot[1:-1, 1:-1, :]
    flux = jnp.zeros_like(pot_now)
    for face, other in zip(faces, neighbours(padded_pot)):
        flux = flux + face * (other - pot_now)
    laplace = -6.0 * conc_now
    for other in neighbours(padded_conc):
        laplace = laplace + other
    excess_mass = mass_source - (conc_now - time_step * flux)
    excess_pot = potential_source - (pot_now - split_slope * conc_now + interface * laplace)
    return excess_mass, excess_pot


def relax_pair(conc_now, pot_now, excess_mass, excess_pot, diagonal):
    other_diagonal = -(split_slope + 6.0 * interface)
    determinant = 1.0 - diagonal * other_diagonal
    new_conc = conc_now + relax_fine * (excess_mass - diagonal * excess_pot) / determinant
    new_pot = pot_now + relax_fine * (excess_pot - other_diagonal * excess_mass) / determinant
    return new_conc, new_pot


def restrict(field):
    size_x, size_y, size_p = field.shape
    return field.reshape(size_x // 2, 2, size_y // 2, 2, size_p // 2, 2).sum(axis=(1, 3, 5)) / 8.0


def prolong(coarse):
    size_x, size_y, size_p = coarse.shape
    wide = jnp.broadcast_to(coarse[:, None, :, None, :, None], (size_x, 2, size_y, 2, size_p, 2))
    return wide.reshape(2 * size_x, 2 * size_y, 2 * size_p)


def neighbour_sum(values):
    padded = jnp.pad(values, [(0, 0)] * (values.ndim - 1) + [(1, 1)])
    return padded[..., 2:] + padded[..., :-2]


def coarse_solve(mean):
    half_planes = mean.shape[-1] // 2
    mass_mean = mean[..., :half_planes]
    pot_mean = mean[..., half_planes:]
    coarse_conc = jnp.zeros_like(mass_mean)
    coarse_pot = jnp.zeros_like(pot_mean)
    for pass_index in range(CSWEEP):
        mass_gap = mass_mean - (coarse_conc + coarse_flux * (2.0 * coarse_pot - neighbour_sum(coarse_pot)))
        pot_gap = pot_mean - (coarse_pot - split_slope * coarse_conc + coarse_bend * (neighbour_sum(coarse_conc) - 2.0 * coarse_conc))
        coarse_conc = coarse_conc + relax_coarse * (mass_gap - 2.0 * coarse_flux * pot_gap) / coarse_det
        coarse_pot = coarse_pot + relax_coarse * (pot_gap + (split_slope + 2.0 * coarse_bend) * mass_gap) / coarse_det
    return jnp.concatenate([coarse_conc, coarse_pot], axis=-1)


def reference(concentration, potential, mass_source, potential_source, pore_mask, mobility_class, mobility_table, owner_map):
    spread = ((1, 1), (1, 1), (0, 0))
    mobility = lookup_mobility(pore_mask, mobility_class, mobility_table)
    faces = face_terms(jnp.pad(mobility, spread))
    diagonal = jnp.zeros_like(mobility)
    for face in faces:
        diagonal = diagonal + face
    diagonal = time_step * diagonal

    def excess_of(conc_now, pot_now):
        return residuals(jnp.pad(conc_now, spread), jnp.pad(pot_now, spread), faces, mass_source, potential_source)

    conc_now, pot_now = concentration, potential
    for pass_index in range(PRE):
        excess_mass, excess_pot = excess_of(conc_now, pot_now)
        conc_now, pot_now = relax_pair(conc_now, pot_now, excess_mass, excess_pot, diagonal)
    excess_mass, excess_pot = excess_of(conc_now, pot_now)
    blocks = jnp.concatenate([restrict(excess_mass), restrict(excess_pot)], axis=-1)
    coarse_x, coarse_y, planes = blocks.shape
    half_x = X_DEV // 2
    half_y = Y_DEV // 2
    owner_grid = owner_map.reshape(N_GX, N_GY, half_x, half_y).transpose(0, 2, 1, 3).reshape(coarse_x, coarse_y)
    group = (jnp.arange(coarse_y) // half_y).astype(jnp.int32)
    segment = (group[None, :] * N_GX + owner_grid).reshape(-1).astype(jnp.int32)
    flat_blocks = blocks.reshape(coarse_x * coarse_y, planes)
    totals = jax.ops.segment_sum(flat_blocks, segment, num_segments=N_GY * N_GX)
    counts = jax.ops.segment_sum(jnp.ones((coarse_x * coarse_y,), jnp.float32), segment, num_segments=N_GY * N_GX)
    means = totals / jnp.maximum(counts, 1.0)[:, None]
    solved = coarse_solve(means)
    correction = solved[segment].reshape(coarse_x, coarse_y, planes)
    half_planes = planes // 2
    conc_now = conc_now + prolong(correction[..., :half_planes])
    pot_now = pot_now + prolong(correction[..., half_planes:])
    for pass_index in range(POST):
        excess_mass, excess_pot = excess_of(conc_now, pot_now)
        conc_now, pot_now = relax_pair(conc_now, pot_now, excess_mass, excess_pot, diagonal)
    return conc_now, pot_now
```

```python
import functools

import jax
import jax.numpy as jnp
from jax import lax
from jax.experimental import pallas as pl
from jax.experimental.pallas import tpu as pltpu
from jax.sharding import PartitionSpec as P

CSWEEP = 3

time_step = 0.25
split_slope = 1.0
interface = 0.5
relax_fine = 0.6
relax_coarse = 0.6
coarse_flux = 0.0625
coarse_bend = 0.125
coarse_det = 1.0 + 2.0 * coarse_flux * (split_slope + 2.0 * coarse_bend)

F32 = jnp.float32
BF16 = jnp.bfloat16
VMEM_LIMIT = 48 * 1024 * 1024


def iota(shape, dim):
    return lax.broadcasted_iota(jnp.int32, shape, dim)


def x_pair(field, low, high):
    return (
        jnp.concatenate([low, field[:-1]], axis=0),
        jnp.concatenate([field[1:], high], axis=0),
    )


def y_pair(field, low, high):
    size = field.shape[1]
    where = iota(field.shape, 1)
    return (
        jnp.where(where == 0, low, pltpu.roll(field, 1, 1)),
        jnp.where(where == size - 1, high, pltpu.roll(field, size - 1, 1)),
    )


def plane_pair(field):
    size = field.shape[2]
    where = iota(field.shape, 2)
    return (
        jnp.where(where == 0, 0.0, pltpu.roll(field, 1, 2)),
        jnp.where(where == size - 1, 0.0, pltpu.roll(field, size - 1, 2)),
    )


def neighbours(field, halo):
    xm, xp, ym, yp = halo
    return (*x_pair(field, xm, xp), *y_pair(field, ym, yp), *plane_pair(field))


def excess_of(conc, pot, conc_halo, pot_halo, faces, mass_source, pot_source):
    flux = jnp.zeros_like(pot)
    for face, other in zip(faces, neighbours(pot, pot_halo)):
        flux = flux + face * (other - pot)
    laplace = -6.0 * conc
    for other in neighbours(conc, conc_halo):
        laplace = laplace + other
    excess_mass = mass_source - (conc - time_step * flux)
    excess_pot = pot_source - (pot - split_slope * conc + interface * laplace)
    return excess_mass, excess_pot


def relax_pair(conc, pot, excess_mass, excess_pot, diagonal):
    other_diagonal = -(split_slope + 6.0 * interface)
    scale = relax_fine / (1.0 - diagonal * other_diagonal)
    new_conc = conc + (excess_mass - diagonal * excess_pot) * scale
    new_pot = pot + (excess_pot - other_diagonal * excess_mass) * scale
    return new_conc, new_pot


def faces_of(mobility, halo):
    faces = tuple(0.5 * (mobility + other) for other in neighbours(mobility, halo))
    diagonal = faces[0]
    for face in faces[1:]:
        diagonal = diagonal + face
    return faces, time_step * diagonal


def split_dot(ones, values, contract):
    dims = (contract, ((), ()))
    total = None
    rest = values
    for _ in range(3):
        term = rest.astype(BF16)
        rest = rest - term.astype(F32)
        part = lax.dot_general(ones, term, dims, preferred_element_type=F32)
        total = part if total is None else total + part
    return total


def round_up(value, unit):
    return -(-value // unit) * unit


class Plan:
    def __init__(self, shape, owners, groups):
        self.x, self.y, self.p = shape
        self.owners, self.groups = owners, groups
        self.half_x, self.half_y = self.x // 2, self.y // 2
        self.id_row = 3 * self.x
        self.count_row = round_up(self.id_row + self.half_x, 8)
        self.y_rows = self.count_row + owners
        self.cells = self.x * self.y
        self.rows = self.cells + 2 * self.y


def side_rows(plan, rows, which):
    return rows[which * plan.y : (which + 1) * plan.y][None]


def side_columns(plan, rows, which):
    return rows[which * plan.x : (which + 1) * plan.x][:, None]


def column_of(plan):
    shape = (plan.rows, plan.half_x * plan.half_y)
    row = iota(shape, 0)
    x = row // plan.y
    y = row % plan.y
    own = (x // 2) * plan.half_y + y // 2
    low = (plan.half_x - 1) * plan.half_y + y // 2
    high = y // 2
    column = jnp.where(x < plan.x, own, jnp.where(x == plan.x, low, high))
    return row, column == iota(shape, 1)


def owner_hits(plan, owner_ref):
    g = lax.axis_index("gx")
    last = plan.owners - 1
    owner = iota((plan.owners, plan.half_x * plan.half_y), 0)
    own = owner_ref[pl.ds(g, 1), :] == owner
    low = (owner_ref[pl.ds(jnp.maximum(g - 1, 0), 1), :] == owner) & (g > 0)
    high = (owner_ref[pl.ds(jnp.minimum(g + 1, last), 1), :] == owner) & (g < last)
    return own, low, high


def membership(plan, owner_ref):
    row, column = column_of(plan)
    spans = ((0, plan.cells), (plan.cells, plan.cells + plan.y), (plan.cells + plan.y, plan.rows))
    gather, spread = None, None
    for (begin, end), hits in zip(spans, owner_hits(plan, owner_ref)):
        place = (column & (row >= begin) & (row < end)).astype(F32).astype(BF16)
        hits = hits.astype(F32).astype(BF16)
        nt = (((1,), (1,)), ((), ()))
        part = lax.dot_general(hits, place, nt, preferred_element_type=F32)
        gather = part if gather is None else gather + part
        part = lax.dot_general(place, hits, nt, preferred_element_type=F32)
        spread = part if spread is None else spread + part
    return gather.astype(BF16), spread


def prepare_kernel(
    plan, conc_ref, pot_ref, mask_ref, class_ref, table_ref, owner_ref,
    mob_ref, x_low_ref, x_high_ref, y_low_ref, y_high_ref,
):
    kind = class_ref[...]
    values = jnp.zeros(kind.shape, F32)
    for marker in range(table_ref.shape[0]):
        values = jnp.where(kind == marker, table_ref[marker], values)
    mobility = mask_ref[...].astype(F32) * values
    mob_ref[...] = mobility
    fields = (conc_ref[...], pot_ref[...], mobility)
    for which, field in enumerate(fields):
        x_low_ref[pl.ds(which * plan.y, plan.y), :] = field[0]
        x_high_ref[pl.ds(which * plan.y, plan.y), :] = field[plan.x - 1]
        for x in range(plan.x):
            y_low_ref[pl.ds(which * plan.x + x, 1), :] = field[x, 0:1]
            y_high_ref[pl.ds(which * plan.x + x, 1), :] = field[x, plan.y - 1 : plan.y]
    columns = plan.half_x * plan.half_y
    owner = iota((plan.owners, columns), 0)
    hits = jnp.zeros((plan.owners, columns), F32)
    for g in range(plan.owners):
        hits = hits + (owner_ref[g : g + 1, :] == owner).astype(F32)
    count = jnp.broadcast_to(jnp.sum(hits, axis=1, keepdims=True), (plan.owners, plan.p))
    own = owner_ref[pl.ds(lax.axis_index("gx"), 1), :].astype(F32)
    for ref, at in ((y_low_ref, 0), (y_high_ref, plan.half_y - 1)):
        ref[pl.ds(plan.count_row, plan.owners), :] = count
        ref[pl.ds(plan.id_row, plan.count_row - plan.id_row), :] = jnp.zeros(
            (plan.count_row - plan.id_row, plan.p), F32
        )
        for i in range(plan.half_x):
            b = i * plan.half_y + at
            ref[pl.ds(plan.id_row + i, 1), :] = jnp.broadcast_to(own[:, b : b + 1], (1, plan.p))


def first_kernel(
    plan, conc_ref, pot_ref, mob_ref, mass_ref, pots_ref, x_low_ref, x_high_ref,
    y_low_ref, y_high_ref, owner_ref,
    conc_out, pot_out, total_out, spread_out, x_low_out, x_high_out, y_low_out, y_high_out,
):
    sides = (x_low_ref[...], x_high_ref[...])
    ends = (y_low_ref[...], y_high_ref[...])

    def halo(which):
        return tuple(side_rows(plan, rows, which) for rows in sides) + tuple(
            side_columns(plan, rows, which) for rows in ends
        )

    mobility, mob_halo = mob_ref[...], halo(2)
    faces, diagonal = faces_of(mobility, mob_halo)
    mass_source, pot_source = mass_ref[...], pots_ref[...]
    conc, pot = conc_ref[...], pot_ref[...]
    excess = excess_of(conc, pot, halo(0), halo(1), faces, mass_source, pot_source)
    conc, pot = relax_pair(conc, pot, *excess, diagonal)
    conc_out[...] = conc
    pot_out[...] = pot
    x_low_out[...] = jnp.concatenate([conc[0], pot[0]], axis=0)
    x_high_out[...] = jnp.concatenate([conc[plan.x - 1], pot[plan.x - 1]], axis=0)
    for which, field in enumerate((conc, pot)):
        for x in range(plan.x):
            y_low_out[pl.ds(which * plan.x + x, 1), :] = field[x, 0:1]
            y_high_out[pl.ds(which * plan.x + x, 1), :] = field[x, plan.y - 1 : plan.y]

    nothing = tuple(jnp.zeros_like(part) for part in mob_halo)
    own_mass, own_pot = excess_of(conc, pot, nothing, nothing, faces, mass_source, pot_source)
    give_mass = [own_mass.reshape(plan.cells, plan.p)]
    give_pot = [own_pot.reshape(plan.cells, plan.p)]
    for x, side in ((0, 0), (plan.x - 1, 1)):
        face = 0.5 * (mobility[x] + mob_halo[side][0])
        give_mass.append(time_step * face * pot[x])
        give_pot.append(-interface * conc[x])
    gather, spread = membership(plan, owner_ref)
    spread_out[...] = spread
    give = jnp.concatenate(
        [jnp.concatenate(give_mass, axis=0), jnp.concatenate(give_pot, axis=0)], axis=1
    )
    total = split_dot(gather, give, ((1,), (0,)))

    def packed(both):
        mass, other = both[:, : plan.p], both[:, plan.p :]
        even = iota(mass.shape, 1) % 2 == 0
        return jnp.where(
            even, mass + pltpu.roll(mass, plan.p - 1, 1), other + pltpu.roll(other, 1, 1)
        )

    owner = iota((plan.owners, 1), 0)
    count = jnp.sum(gather.astype(F32)[:, : plan.cells], axis=1, keepdims=True)
    h = lax.axis_index("gy")
    total_out[...] = jnp.zeros_like(total_out)

    def scale_of(count):
        return 0.125 / jnp.maximum(count, 1.0)

    def put(place, values):
        total_out[pl.ds(pl.multiple_of((h + place) * plan.owners, 8), plan.owners), :] = values

    del count
    own_hits = jnp.zeros((plan.owners, plan.half_x * plan.half_y), F32)
    owner_grid = iota(own_hits.shape, 0)
    for g in range(plan.owners):
        own_hits = own_hits + (owner_ref[g : g + 1, :] == owner_grid).astype(F32)
    own_count = jnp.sum(own_hits, axis=1, keepdims=True)
    put(1, packed(total) * scale_of(own_count))
    for place, y, side in ((0, 0, 2), (2, plan.y - 1, 3)):
        rows = ends[side - 2]
        inside = (h > 0) if place == 0 else (h < plan.groups - 1)
        edge_mob = jnp.concatenate([mobility[x, y : y + 1] for x in range(plan.x)], axis=0)
        edge_pot = jnp.concatenate([pot[x, y : y + 1] for x in range(plan.x)], axis=0)
        edge_conc = jnp.concatenate([conc[x, y : y + 1] for x in range(plan.x)], axis=0)
        face = 0.5 * (edge_mob + mob_halo[side][:, 0])
        both = jnp.concatenate([time_step * face * edge_pot, -interface * edge_conc], axis=1)
        part = jnp.zeros((plan.owners, 2 * plan.p), F32)
        for i in range(plan.half_x):
            ident = rows[plan.id_row + i : plan.id_row + i + 1, 0:1].astype(jnp.int32)
            pair = both[2 * i : 2 * i + 1] + both[2 * i + 1 : 2 * i + 2]
            part = part + jnp.where((owner == ident) & inside, pair, 0.0)
        put(place, packed(part) * scale_of(rows[plan.count_row : plan.count_row + plan.owners]))


def coarse_solve(packed, planes):
    lane = iota(packed.shape, 1)
    even = lane % 2 == 0
    mass_mean = jnp.where(even, packed, pltpu.roll(packed, 1, 1))
    pot_mean = jnp.where(even, pltpu.roll(packed, planes - 1, 1), packed)

    def neighbour_sum(values):
        return jnp.where(lane >= 2, pltpu.roll(values, 2, 1), 0.0) + jnp.where(
            lane < planes - 2, pltpu.roll(values, planes - 2, 1), 0.0
        )

    coarse_conc = jnp.zeros_like(mass_mean)
    coarse_pot = jnp.zeros_like(pot_mean)
    for _ in range(CSWEEP):
        mass_gap = mass_mean - (
            coarse_conc + coarse_flux * (2.0 * coarse_pot - neighbour_sum(coarse_pot))
        )
        pot_gap = pot_mean - (
            coarse_pot
            - split_slope * coarse_conc
            + coarse_bend * (neighbour_sum(coarse_conc) - 2.0 * coarse_conc)
        )
        coarse_conc = coarse_conc + (relax_coarse / coarse_det) * (
            mass_gap - 2.0 * coarse_flux * pot_gap
        )
        coarse_pot = coarse_pot + (relax_coarse / coarse_det) * (
            pot_gap + (split_slope + 2.0 * coarse_bend) * mass_gap
        )
    return coarse_conc, coarse_pot


def last_kernel(
    plan, conc_ref, pot_ref, mob_ref, mass_ref, pots_ref, x_low_mob, x_high_mob,
    y_low_msg, y_high_msg, x_low_ref, x_high_ref, y_low_ref, y_high_ref, total_ref, spread_ref,
    conc_out, pot_out,
):
    h = lax.axis_index("gy")
    base = pl.multiple_of(h * plan.owners, 8)
    means = total_ref[pl.ds(base, 3 * plan.owners), :]
    solved = jnp.concatenate(coarse_solve(means, plan.p), axis=1)
    own = split_dot(
        spread_ref[...].astype(BF16), solved[plan.owners : 2 * plan.owners], ((1,), (0,))
    )
    owner = iota((plan.owners, 1), 0)

    def edge_correction(place, rows, inside):
        part = solved[place * plan.owners : (place + 1) * plan.owners]
        out = []
        for i in range(plan.half_x):
            ident = rows[plan.id_row + i : plan.id_row + i + 1, 0:1].astype(jnp.int32)
            row = jnp.sum(jnp.where((owner == ident) & inside, part, 0.0), axis=0, keepdims=True)
            out += [row, row]
        return jnp.concatenate(out, axis=0)

    y_corr = (
        edge_correction(0, y_low_msg[...], h > 0),
        edge_correction(2, y_high_msg[...], h < plan.groups - 1),
    )

    def updated(which, ref):
        lanes = slice(which * plan.p, (which + 1) * plan.p)
        corr = own[:, lanes]
        field = ref[...] + corr[: plan.cells].reshape(plan.x, plan.y, plan.p)
        halo = []
        for side, rows in enumerate((x_low_ref[...], x_high_ref[...])):
            begin = plan.cells + side * plan.y
            halo.append(side_rows(plan, rows, which) + corr[begin : begin + plan.y][None])
        for rows, edge in zip((y_low_ref[...], y_high_ref[...]), y_corr):
            halo.append((rows[which * plan.x : (which + 1) * plan.x] + edge[:, lanes])[:, None])
        return field, halo

    conc, conc_halo = updated(0, conc_ref)
    pot, pot_halo = updated(1, pot_ref)
    mob_halo = (
        x_low_mob[pl.ds(2 * plan.y, plan.y), :][None],
        x_high_mob[pl.ds(2 * plan.y, plan.y), :][None],
        side_columns(plan, y_low_msg[...], 2),
        side_columns(plan, y_high_msg[...], 2),
    )
    faces, diagonal = faces_of(mob_ref[...], mob_halo)
    excess = excess_of(conc, pot, conc_halo, pot_halo, faces, mass_ref[...], pots_ref[...])
    conc_out[...], pot_out[...] = relax_pair(conc, pot, *excess, diagonal)


def call(kernel, plan, outs, args, smem=()):
    return pl.pallas_call(
        functools.partial(kernel, plan),
        out_shape=[jax.ShapeDtypeStruct(shape, F32) for shape in outs],
        in_specs=[
            pl.BlockSpec(memory_space=pltpu.SMEM if i in smem else pltpu.VMEM)
            for i in range(len(args))
        ],
        out_specs=[pl.BlockSpec(memory_space=pltpu.VMEM)] * len(outs),
        compiler_params=pltpu.CompilerParams(vmem_limit_bytes=VMEM_LIMIT),
    )(*args)


def swap_sides(low, high, axis):
    count = lax.axis_size(axis)
    from_below = lax.ppermute(high, axis, [(i, i + 1) for i in range(count - 1)])
    from_above = lax.ppermute(low, axis, [(i + 1, i) for i in range(count - 1)])
    return from_below, from_above


def on_device(conc, pot, mass_source, pot_source, mask, kind, table, owner_map):
    plan = Plan(conc.shape, lax.axis_size("gx"), lax.axis_size("gy"))
    block = conc.shape
    mob, x_low, x_high, y_low, y_high = call(
        prepare_kernel,
        plan,
        [block, *[(3 * plan.y, plan.p)] * 2, *[(plan.y_rows, plan.p)] * 2],
        [conc, pot, mask, kind, table, owner_map],
        smem=(4,),
    )
    x_low, x_high = swap_sides(x_low, x_high, "gx")
    y_low, y_high = swap_sides(y_low, y_high, "gy")
    conc, pot, total, spread, x_low1, x_high1, y_low1, y_high1 = call(
        first_kernel,
        plan,
        [
            block,
            block,
            ((plan.groups + 2) * plan.owners, plan.p),
            (plan.rows, plan.owners),
            *[(2 * plan.y, plan.p)] * 2,
            *[(2 * plan.x, plan.p)] * 2,
        ],
        [conc, pot, mob, mass_source, pot_source, x_low, x_high, y_low, y_high, owner_map],
    )
    total = lax.psum(total, ("gx", "gy"))
    x_low1, x_high1 = swap_sides(x_low1, x_high1, "gx")
    y_low1, y_high1 = swap_sides(y_low1, y_high1, "gy")
    return tuple(
        call(
            last_kernel,
            plan,
            [block, block],
            [
                conc, pot, mob, mass_source, pot_source, x_low, x_high, y_low, y_high,
                x_low1, x_high1, y_low1, y_high1, total, spread,
            ],
        )
    )


def solution(mesh):
    grid = P("gx", "gy", None)
    return jax.shard_map(
        on_device,
        mesh=mesh,
        in_specs=(grid,) * 6 + (P(), P(None, "gy")),
        out_specs=(grid, grid),
        check_vma=False,
    )
```

```python
import functools

import jax
import jax.numpy as jnp
from jax import lax
from jax.experimental import pallas as pl
from jax.experimental.pallas import tpu as pltpu
from jax.sharding import PartitionSpec as P

CSWEEP = 3

time_step = 0.25
split_slope = 1.0
interface = 0.5
relax_fine = 0.6
relax_coarse = 0.6
coarse_flux = 0.0625
coarse_bend = 0.125
coarse_det = 1.0 + 2.0 * coarse_flux * (split_slope + 2.0 * coarse_bend)

F32 = jnp.float32
BF16 = jnp.bfloat16
VMEM_LIMIT = 48 * 1024 * 1024
LARGE_LIMIT = 60 * 1024 * 1024


def iota(shape, dim):
    return lax.broadcasted_iota(jnp.int32, shape, dim)


def x_pair(field, low, high):
    return (
        jnp.concatenate([low, field[:-1]], axis=0),
        jnp.concatenate([field[1:], high], axis=0),
    )


def y_pair(field, low, high):
    size = field.shape[1]
    where = iota(field.shape, 1)
    return (
        jnp.where(where == 0, low, pltpu.roll(field, 1, 1)),
        jnp.where(where == size - 1, high, pltpu.roll(field, size - 1, 1)),
    )


def plane_pair(field):
    size = field.shape[2]
    where = iota(field.shape, 2)
    return (
        jnp.where(where == 0, 0.0, pltpu.roll(field, 1, 2)),
        jnp.where(where == size - 1, 0.0, pltpu.roll(field, size - 1, 2)),
    )


def neighbours(field, halo):
    xm, xp, ym, yp = halo
    return (*x_pair(field, xm, xp), *y_pair(field, ym, yp), *plane_pair(field))


def excess_of(conc, pot, conc_halo, pot_halo, faces, mass_source, pot_source):
    flux = jnp.zeros_like(pot)
    for face, other in zip(faces, neighbours(pot, pot_halo)):
        flux = flux + face * (other - pot)
    laplace = -6.0 * conc
    for other in neighbours(conc, conc_halo):
        laplace = laplace + other
    excess_mass = mass_source - (conc - time_step * flux)
    excess_pot = pot_source - (pot - split_slope * conc + interface * laplace)
    return excess_mass, excess_pot


def relax_pair(conc, pot, excess_mass, excess_pot, diagonal):
    other_diagonal = -(split_slope + 6.0 * interface)
    scale = relax_fine / (1.0 - diagonal * other_diagonal)
    new_conc = conc + (excess_mass - diagonal * excess_pot) * scale
    new_pot = pot + (excess_pot - other_diagonal * excess_mass) * scale
    return new_conc, new_pot


def faces_of(mobility, halo):
    faces = tuple(0.5 * (mobility + other) for other in neighbours(mobility, halo))
    diagonal = faces[0]
    for face in faces[1:]:
        diagonal = diagonal + face
    return faces, time_step * diagonal


def split_dot(ones, values, contract):
    dims = (contract, ((), ()))
    total = None
    rest = values
    for _ in range(3):
        term = rest.astype(BF16)
        rest = rest - term.astype(F32)
        part = lax.dot_general(ones, term, dims, preferred_element_type=F32)
        total = part if total is None else total + part
    return total


def round_up(value, unit):
    return -(-value // unit) * unit


class Plan:
    def __init__(self, shape, owners, groups):
        self.x, self.y, self.p = shape
        self.owners, self.groups = owners, groups
        self.half_x, self.half_y = self.x // 2, self.y // 2
        self.id_row = 3 * self.x
        self.count_row = round_up(self.id_row + self.half_x, 8)
        self.y_rows = self.count_row + owners
        self.cells = self.x * self.y
        self.rows = self.cells + 2 * self.y


def side_rows(plan, rows, which):
    return rows[which * plan.y : (which + 1) * plan.y][None]


def side_columns(plan, rows, which):
    return rows[which * plan.x : (which + 1) * plan.x][:, None]


def column_of(plan):
    shape = (plan.rows, plan.half_x * plan.half_y)
    row = iota(shape, 0)
    x = row // plan.y
    y = row % plan.y
    own = (x // 2) * plan.half_y + y // 2
    low = (plan.half_x - 1) * plan.half_y + y // 2
    high = y // 2
    column = jnp.where(x < plan.x, own, jnp.where(x == plan.x, low, high))
    return row, column == iota(shape, 1)


def owner_hits(plan, owner_ref):
    g = lax.axis_index("gx")
    last = plan.owners - 1
    owner = iota((plan.owners, plan.half_x * plan.half_y), 0)
    own = owner_ref[pl.ds(g, 1), :] == owner
    low = (owner_ref[pl.ds(jnp.maximum(g - 1, 0), 1), :] == owner) & (g > 0)
    high = (owner_ref[pl.ds(jnp.minimum(g + 1, last), 1), :] == owner) & (g < last)
    return own, low, high


def membership(plan, owner_ref):
    row, column = column_of(plan)
    spans = ((0, plan.cells), (plan.cells, plan.cells + plan.y), (plan.cells + plan.y, plan.rows))
    gather, spread = None, None
    for (begin, end), hits in zip(spans, owner_hits(plan, owner_ref)):
        place = (column & (row >= begin) & (row < end)).astype(F32).astype(BF16)
        hits = hits.astype(F32).astype(BF16)
        nt = (((1,), (1,)), ((), ()))
        part = lax.dot_general(hits, place, nt, preferred_element_type=F32)
        gather = part if gather is None else gather + part
        part = lax.dot_general(place, hits, nt, preferred_element_type=F32)
        spread = part if spread is None else spread + part
    return gather.astype(BF16), spread


def prepare_kernel(
    plan, conc_hbm, pot_hbm, mask_hbm, class_hbm, owner_hbm, table_hbm,
    mob_ref, x_low_ref, x_high_ref, y_low_ref, y_high_ref,
    conc_ref, pot_ref, owner_ref, mask_ref, class_ref, table_ref, sems,
):
    pairs = (
        (table_hbm, table_ref), (class_hbm, class_ref), (mask_hbm, mask_ref),
        (conc_hbm, conc_ref), (pot_hbm, pot_ref), (owner_hbm, owner_ref),
    )
    copies = [
        pltpu.make_async_copy(source, target, sems.at[i])
        for i, (source, target) in enumerate(pairs)
    ]
    for copy in copies:
        copy.start()
    for copy in copies:
        copy.wait()
    kind = class_ref[...]
    values = jnp.zeros(kind.shape, F32)
    for marker in range(table_ref.shape[0]):
        values = jnp.where(kind == marker, table_ref[marker], values)
    mobility = mask_ref[...].astype(F32) * values
    mob_ref[...] = mobility
    fields = (conc_ref[...], pot_ref[...], mobility)
    for which, field in enumerate(fields):
        x_low_ref[pl.ds(which * plan.y, plan.y), :] = field[0]
        x_high_ref[pl.ds(which * plan.y, plan.y), :] = field[plan.x - 1]
        for x in range(plan.x):
            y_low_ref[pl.ds(which * plan.x + x, 1), :] = field[x, 0:1]
            y_high_ref[pl.ds(which * plan.x + x, 1), :] = field[x, plan.y - 1 : plan.y]
    columns = plan.half_x * plan.half_y
    owner = iota((plan.owners, columns), 0)
    hits = jnp.zeros((plan.owners, columns), F32)
    for g in range(plan.owners):
        hits = hits + (owner_ref[g : g + 1, :] == owner).astype(F32)
    count = jnp.broadcast_to(jnp.sum(hits, axis=1, keepdims=True), (plan.owners, plan.p))
    own = owner_ref[pl.ds(lax.axis_index("gx"), 1), :].astype(F32)
    for ref, at in ((y_low_ref, 0), (y_high_ref, plan.half_y - 1)):
        ref[pl.ds(plan.count_row, plan.owners), :] = count
        ref[pl.ds(plan.id_row, plan.count_row - plan.id_row), :] = jnp.zeros(
            (plan.count_row - plan.id_row, plan.p), F32
        )
        for i in range(plan.half_x):
            b = i * plan.half_y + at
            ref[pl.ds(plan.id_row + i, 1), :] = jnp.broadcast_to(own[:, b : b + 1], (1, plan.p))


def first_kernel(
    plan, conc_ref, pot_ref, mob_ref, mass_ref, pots_ref, x_low_ref, x_high_ref,
    y_low_ref, y_high_ref, owner_ref,
    conc_out, pot_out, total_out, spread_out, x_low_out, x_high_out, y_low_out, y_high_out,
):
    sides = (x_low_ref[...], x_high_ref[...])
    ends = (y_low_ref[...], y_high_ref[...])

    def halo(which):
        return tuple(side_rows(plan, rows, which) for rows in sides) + tuple(
            side_columns(plan, rows, which) for rows in ends
        )

    mobility, mob_halo = mob_ref[...], halo(2)
    faces, diagonal = faces_of(mobility, mob_halo)
    mass_source, pot_source = mass_ref[...], pots_ref[...]
    conc, pot = conc_ref[...], pot_ref[...]
    excess = excess_of(conc, pot, halo(0), halo(1), faces, mass_source, pot_source)
    conc, pot = relax_pair(conc, pot, *excess, diagonal)
    conc_out[...] = conc
    pot_out[...] = pot
    x_low_out[...] = jnp.concatenate([conc[0], pot[0]], axis=0)
    x_high_out[...] = jnp.concatenate([conc[plan.x - 1], pot[plan.x - 1]], axis=0)
    for which, field in enumerate((conc, pot)):
        for x in range(plan.x):
            y_low_out[pl.ds(which * plan.x + x, 1), :] = field[x, 0:1]
            y_high_out[pl.ds(which * plan.x + x, 1), :] = field[x, plan.y - 1 : plan.y]

    nothing = tuple(jnp.zeros_like(part) for part in mob_halo)
    own_mass, own_pot = excess_of(conc, pot, nothing, nothing, faces, mass_source, pot_source)
    give_mass = [own_mass.reshape(plan.cells, plan.p)]
    give_pot = [own_pot.reshape(plan.cells, plan.p)]
    for x, side in ((0, 0), (plan.x - 1, 1)):
        face = 0.5 * (mobility[x] + mob_halo[side][0])
        give_mass.append(time_step * face * pot[x])
        give_pot.append(-interface * conc[x])
    gather, spread = membership(plan, owner_ref)
    spread_out[...] = spread
    give = jnp.concatenate(
        [jnp.concatenate(give_mass, axis=0), jnp.concatenate(give_pot, axis=0)], axis=1
    )
    total = split_dot(gather, give, ((1,), (0,)))

    def packed(both):
        mass, other = both[:, : plan.p], both[:, plan.p :]
        even = iota(mass.shape, 1) % 2 == 0
        return jnp.where(
            even, mass + pltpu.roll(mass, plan.p - 1, 1), other + pltpu.roll(other, 1, 1)
        )

    owner = iota((plan.owners, 1), 0)
    h = lax.axis_index("gy")

    def scale_of(count):
        return 0.125 / jnp.maximum(count, 1.0)

    def put(place, values):
        total_out[pl.ds(place * plan.owners, plan.owners), :] = values

    own_hits = jnp.zeros((plan.owners, plan.half_x * plan.half_y), F32)
    owner_grid = iota(own_hits.shape, 0)
    for g in range(plan.owners):
        own_hits = own_hits + (owner_ref[g : g + 1, :] == owner_grid).astype(F32)
    own_count = jnp.sum(own_hits, axis=1, keepdims=True)
    put(1, packed(total) * scale_of(own_count))
    for place, y, side in ((0, 0, 2), (2, plan.y - 1, 3)):
        rows = ends[side - 2]
        inside = (h > 0) if place == 0 else (h < plan.groups - 1)
        edge_mob = jnp.concatenate([mobility[x, y : y + 1] for x in range(plan.x)], axis=0)
        edge_pot = jnp.concatenate([pot[x, y : y + 1] for x in range(plan.x)], axis=0)
        edge_conc = jnp.concatenate([conc[x, y : y + 1] for x in range(plan.x)], axis=0)
        face = 0.5 * (edge_mob + mob_halo[side][:, 0])
        both = jnp.concatenate([time_step * face * edge_pot, -interface * edge_conc], axis=1)
        part = jnp.zeros((plan.owners, 2 * plan.p), F32)
        for i in range(plan.half_x):
            ident = rows[plan.id_row + i : plan.id_row + i + 1, 0:1].astype(jnp.int32)
            pair = both[2 * i : 2 * i + 1] + both[2 * i + 1 : 2 * i + 2]
            part = part + jnp.where((owner == ident) & inside, pair, 0.0)
        put(place, packed(part) * scale_of(rows[plan.count_row : plan.count_row + plan.owners]))


def coarse_solve(packed, planes):
    lane = iota(packed.shape, 1)
    even = lane % 2 == 0
    mass_mean = jnp.where(even, packed, pltpu.roll(packed, 1, 1))
    pot_mean = jnp.where(even, pltpu.roll(packed, planes - 1, 1), packed)

    def neighbour_sum(values):
        return jnp.where(lane >= 2, pltpu.roll(values, 2, 1), 0.0) + jnp.where(
            lane < planes - 2, pltpu.roll(values, planes - 2, 1), 0.0
        )

    coarse_conc = jnp.zeros_like(mass_mean)
    coarse_pot = jnp.zeros_like(pot_mean)
    for _ in range(CSWEEP):
        mass_gap = mass_mean - (
            coarse_conc + coarse_flux * (2.0 * coarse_pot - neighbour_sum(coarse_pot))
        )
        pot_gap = pot_mean - (
            coarse_pot
            - split_slope * coarse_conc
            + coarse_bend * (neighbour_sum(coarse_conc) - 2.0 * coarse_conc)
        )
        coarse_conc = coarse_conc + (relax_coarse / coarse_det) * (
            mass_gap - 2.0 * coarse_flux * pot_gap
        )
        coarse_pot = coarse_pot + (relax_coarse / coarse_det) * (
            pot_gap + (split_slope + 2.0 * coarse_bend) * mass_gap
        )
    return coarse_conc, coarse_pot


def last_kernel(
    plan, conc_ref, pot_ref, mob_ref, mass_ref, pots_ref, x_low_mob, x_high_mob,
    y_low_msg, y_high_msg, x_low_ref, x_high_ref, y_low_ref, y_high_ref, total_ref, spread_ref,
    conc_out, pot_out, frame,
):
    h = lax.axis_index("gy")
    frame[...] = jnp.zeros_like(frame)
    for group in range(plan.groups):
        part = total_ref[0, group]
        for i in range(1, total_ref.shape[0]):
            part = part + total_ref[i, group]
        frame[pl.ds(group * plan.owners, 3 * plan.owners), :] += part
    base = pl.multiple_of(h * plan.owners, 8)
    means = frame[pl.ds(base, 3 * plan.owners), :]
    solved = jnp.concatenate(coarse_solve(means, plan.p), axis=1)
    own = split_dot(
        spread_ref[...].astype(BF16), solved[plan.owners : 2 * plan.owners], ((1,), (0,))
    )
    owner = iota((plan.owners, 1), 0)

    def edge_correction(place, rows, inside):
        part = solved[place * plan.owners : (place + 1) * plan.owners]
        out = []
        for i in range(plan.half_x):
            ident = rows[plan.id_row + i : plan.id_row + i + 1, 0:1].astype(jnp.int32)
            row = jnp.sum(jnp.where((owner == ident) & inside, part, 0.0), axis=0, keepdims=True)
            out += [row, row]
        return jnp.concatenate(out, axis=0)

    y_corr = (
        edge_correction(0, y_low_msg[...], h > 0),
        edge_correction(2, y_high_msg[...], h < plan.groups - 1),
    )

    def updated(which, ref):
        lanes = slice(which * plan.p, (which + 1) * plan.p)
        corr = own[:, lanes]
        field = ref[...] + corr[: plan.cells].reshape(plan.x, plan.y, plan.p)
        halo = []
        for side, rows in enumerate((x_low_ref[...], x_high_ref[...])):
            begin = plan.cells + side * plan.y
            halo.append(side_rows(plan, rows, which) + corr[begin : begin + plan.y][None])
        for rows, edge in zip((y_low_ref[...], y_high_ref[...]), y_corr):
            halo.append((rows[which * plan.x : (which + 1) * plan.x] + edge[:, lanes])[:, None])
        return field, halo

    conc, conc_halo = updated(0, conc_ref)
    pot, pot_halo = updated(1, pot_ref)
    mob_halo = (
        x_low_mob[pl.ds(2 * plan.y, plan.y), :][None],
        x_high_mob[pl.ds(2 * plan.y, plan.y), :][None],
        side_columns(plan, y_low_msg[...], 2),
        side_columns(plan, y_high_msg[...], 2),
    )
    faces, diagonal = faces_of(mob_ref[...], mob_halo)
    excess = excess_of(conc, pot, conc_halo, pot_halo, faces, mass_ref[...], pots_ref[...])
    conc_out[...], pot_out[...] = relax_pair(conc, pot, *excess, diagonal)


def call(kernel, plan, outs, args, far=(), scratch=(), limit=VMEM_LIMIT):
    return pl.pallas_call(
        functools.partial(kernel, plan),
        out_shape=[jax.ShapeDtypeStruct(shape, F32) for shape in outs],
        in_specs=[
            pl.BlockSpec(memory_space=pl.ANY if i in far else pltpu.VMEM)
            for i in range(len(args))
        ],
        out_specs=[pl.BlockSpec(memory_space=pltpu.VMEM)] * len(outs),
        scratch_shapes=list(scratch),
        compiler_params=pltpu.CompilerParams(vmem_limit_bytes=limit),
    )(*args)


def swap_sides(low, high, axis):
    count = lax.axis_size(axis)
    from_below = lax.ppermute(high, axis, [(i, i + 1) for i in range(count - 1)])
    from_above = lax.ppermute(low, axis, [(i + 1, i) for i in range(count - 1)])
    return from_below, from_above


def gather_totals(plan, total):
    if plan.owners * plan.groups <= 64:
        parts = lax.all_gather(total, ("gx", "gy"))
        return parts.reshape(plan.owners, plan.groups, *total.shape)
    parts = lax.all_gather(lax.psum(total, "gx"), "gy")
    return parts[None]


def on_device(conc, pot, mass_source, pot_source, mask, kind, table, owner_map):
    plan = Plan(conc.shape, lax.axis_size("gx"), lax.axis_size("gy"))
    block = conc.shape
    mob, x_low, x_high, y_low, y_high = call(
        prepare_kernel,
        plan,
        [block, *[(3 * plan.y, plan.p)] * 2, *[(plan.y_rows, plan.p)] * 2],
        [conc, pot, mask, kind, owner_map, table],
        far=range(6),
        limit=LARGE_LIMIT,
        scratch=(
            pltpu.VMEM(block, F32),
            pltpu.VMEM(block, F32),
            pltpu.VMEM(owner_map.shape, owner_map.dtype),
            pltpu.VMEM(block, mask.dtype),
            pltpu.VMEM(block, kind.dtype),
            pltpu.SMEM(table.shape, table.dtype),
            pltpu.SemaphoreType.DMA((6,)),
        ),
    )
    x_low, x_high = swap_sides(x_low, x_high, "gx")
    y_low, y_high = swap_sides(y_low, y_high, "gy")
    conc, pot, total, spread, x_low1, x_high1, y_low1, y_high1 = call(
        first_kernel,
        plan,
        [
            block,
            block,
            (3 * plan.owners, plan.p),
            (plan.rows, plan.owners),
            *[(2 * plan.y, plan.p)] * 2,
            *[(2 * plan.x, plan.p)] * 2,
        ],
        [conc, pot, mob, mass_source, pot_source, x_low, x_high, y_low, y_high, owner_map],
    )
    total = gather_totals(plan, total)
    x_low1, x_high1 = swap_sides(x_low1, x_high1, "gx")
    y_low1, y_high1 = swap_sides(y_low1, y_high1, "gy")
    return tuple(
        call(
            last_kernel,
            plan,
            [block, block],
            [
                conc, pot, mob, mass_source, pot_source, x_low, x_high, y_low, y_high,
                x_low1, x_high1, y_low1, y_high1, total, spread,
            ],
            scratch=[pltpu.VMEM(((plan.groups + 2) * plan.owners, plan.p), F32)],
        )
    )


def solution(mesh):
    grid = P("gx", "gy", None)
    return jax.shard_map(
        on_device,
        mesh=mesh,
        in_specs=(grid,) * 6 + (P(), P(None, "gy")),
        out_specs=(grid, grid),
        check_vma=False,
    )
```

```python
import functools

import jax
import jax.numpy as jnp
from jax import lax
from jax.experimental import pallas as pl
from jax.experimental.pallas import tpu as pltpu
from jax.sharding import PartitionSpec as P

CSWEEP = 3

time_step = 0.25
split_slope = 1.0
interface = 0.5
relax_fine = 0.6
relax_coarse = 0.6
coarse_flux = 0.0625
coarse_bend = 0.125
coarse_det = 1.0 + 2.0 * coarse_flux * (split_slope + 2.0 * coarse_bend)

F32 = jnp.float32
BF16 = jnp.bfloat16
VMEM_LIMIT = 48 * 1024 * 1024
LARGE_LIMIT = 60 * 1024 * 1024


def iota(shape, dim):
    return lax.broadcasted_iota(jnp.int32, shape, dim)


def x_pair(field, low, high):
    return (
        jnp.concatenate([low, field[:-1]], axis=0),
        jnp.concatenate([field[1:], high], axis=0),
    )


def y_pair(field, low, high):
    size = field.shape[1]
    where = iota(field.shape, 1)
    return (
        jnp.where(where == 0, low, pltpu.roll(field, 1, 1)),
        jnp.where(where == size - 1, high, pltpu.roll(field, size - 1, 1)),
    )


def plane_pair(field):
    size = field.shape[2]
    where = iota(field.shape, 2)
    return (
        jnp.where(where == 0, 0.0, pltpu.roll(field, 1, 2)),
        jnp.where(where == size - 1, 0.0, pltpu.roll(field, size - 1, 2)),
    )


def neighbours(field, halo):
    xm, xp, ym, yp = halo
    return (*x_pair(field, xm, xp), *y_pair(field, ym, yp), *plane_pair(field))


def excess_of(conc, pot, conc_halo, pot_halo, faces, mass_source, pot_source):
    flux = jnp.zeros_like(pot)
    for face, other in zip(faces, neighbours(pot, pot_halo)):
        flux = flux + face * (other - pot)
    laplace = -6.0 * conc
    for other in neighbours(conc, conc_halo):
        laplace = laplace + other
    excess_mass = mass_source - (conc - time_step * flux)
    excess_pot = pot_source - (pot - split_slope * conc + interface * laplace)
    return excess_mass, excess_pot


def relax_pair(conc, pot, excess_mass, excess_pot, diagonal):
    other_diagonal = -(split_slope + 6.0 * interface)
    scale = relax_fine / (1.0 - diagonal * other_diagonal)
    new_conc = conc + (excess_mass - diagonal * excess_pot) * scale
    new_pot = pot + (excess_pot - other_diagonal * excess_mass) * scale
    return new_conc, new_pot


def faces_of(mobility, halo):
    faces = tuple(0.5 * (mobility + other) for other in neighbours(mobility, halo))
    diagonal = faces[0]
    for face in faces[1:]:
        diagonal = diagonal + face
    return faces, time_step * diagonal


def split_dot(ones, values, contract):
    dims = (contract, ((), ()))
    total = None
    rest = values
    for _ in range(3):
        term = rest.astype(BF16)
        rest = rest - term.astype(F32)
        part = lax.dot_general(ones, term, dims, preferred_element_type=F32)
        total = part if total is None else total + part
    return total


def round_up(value, unit):
    return -(-value // unit) * unit


class Plan:
    def __init__(self, shape, owners, groups):
        self.x, self.y, self.p = shape
        self.owners, self.groups = owners, groups
        self.half_x, self.half_y = self.x // 2, self.y // 2
        self.id_row = 3 * self.x
        self.count_row = round_up(self.id_row + self.half_x, 8)
        self.y_rows = self.count_row + owners
        self.cells = self.x * self.y
        self.rows = self.cells + 2 * self.y


def side_rows(plan, rows, which):
    return rows[which * plan.y : (which + 1) * plan.y][None]


def side_columns(plan, rows, which):
    return rows[which * plan.x : (which + 1) * plan.x][:, None]


def column_of(plan):
    shape = (plan.rows, plan.half_x * plan.half_y)
    row = iota(shape, 0)
    x = row // plan.y
    y = row % plan.y
    own = (x // 2) * plan.half_y + y // 2
    low = (plan.half_x - 1) * plan.half_y + y // 2
    high = y // 2
    column = jnp.where(x < plan.x, own, jnp.where(x == plan.x, low, high))
    return row, column == iota(shape, 1)


def owner_hits(plan, owner_ref):
    g = lax.axis_index("gx")
    last = plan.owners - 1
    owner = iota((plan.owners, plan.half_x * plan.half_y), 0)
    own = owner_ref[pl.ds(g, 1), :] == owner
    low = (owner_ref[pl.ds(jnp.maximum(g - 1, 0), 1), :] == owner) & (g > 0)
    high = (owner_ref[pl.ds(jnp.minimum(g + 1, last), 1), :] == owner) & (g < last)
    return own, low, high


def membership(plan, owner_ref):
    row, column = column_of(plan)
    spans = ((0, plan.cells), (plan.cells, plan.cells + plan.y), (plan.cells + plan.y, plan.rows))
    gather, spread = None, None
    for (begin, end), hits in zip(spans, owner_hits(plan, owner_ref)):
        place = (column & (row >= begin) & (row < end)).astype(F32).astype(BF16)
        hits = hits.astype(F32).astype(BF16)
        nt = (((1,), (1,)), ((), ()))
        part = lax.dot_general(hits, place, nt, preferred_element_type=F32)
        gather = part if gather is None else gather + part
        part = lax.dot_general(place, hits, nt, preferred_element_type=F32)
        spread = part if spread is None else spread + part
    return gather.astype(BF16), spread


def mobility_of(mask_ref, class_ref, table_ref):
    kind = class_ref[...]
    values = jnp.zeros(kind.shape, F32)
    for marker in range(table_ref.shape[0]):
        values = jnp.where(kind == marker, table_ref[marker], values)
    return mask_ref[...].astype(F32) * values


def x_even():
    return lax.rem(lax.axis_index("gx"), 2) == 0


def put_x(plan, fields, near_ref, far_ref):
    even = x_even()
    for which, field in enumerate(fields):
        low, high = field[0], field[plan.x - 1]
        near_ref[pl.ds(which * plan.y, plan.y), :] = jnp.where(even, high, low)
        far_ref[pl.ds(which * plan.y, plan.y), :] = jnp.where(even, low, high)


def get_x(near_ref, far_ref):
    even = x_even()
    near, far = near_ref[...], far_ref[...]
    return jnp.where(even, far, near), jnp.where(even, near, far)


def put_y(plan, fields, slots_ref):
    h = lax.axis_index("gy")
    for which, field in enumerate(fields):
        for x in range(plan.x):
            low, high = field[x, 0:1], field[x, plan.y - 1 : plan.y]
            for slot in range(plan.groups):
                slots_ref[slot, pl.ds(which * plan.x + x, 1), :] = jnp.where(h < slot, high, low)


def get_y(plan, slots_ref):
    h = lax.axis_index("gy")
    last = plan.groups - 1
    low = slots_ref[pl.ds(jnp.maximum(h - 1, 0), 1)][0]
    high = slots_ref[pl.ds(jnp.minimum(h + 1, last), 1)][0]
    return jnp.where(h > 0, low, 0.0), jnp.where(h < last, high, 0.0)


def prepare_kernel(
    plan, conc_hbm, pot_hbm, mask_hbm, class_hbm, owner_hbm, table_hbm,
    x_near_ref, x_far_ref, y_ref,
    conc_ref, pot_ref, owner_ref, mask_ref, class_ref, table_ref, sems,
):
    pairs = (
        (table_hbm, table_ref), (class_hbm, class_ref), (mask_hbm, mask_ref),
        (conc_hbm, conc_ref), (pot_hbm, pot_ref), (owner_hbm, owner_ref),
    )
    copies = [
        pltpu.make_async_copy(source, target, sems.at[i])
        for i, (source, target) in enumerate(pairs)
    ]
    for copy in copies:
        copy.start()
    for copy in copies:
        copy.wait()
    mobility = mobility_of(mask_ref, class_ref, table_ref)
    fields = (conc_ref[...], pot_ref[...], mobility)
    put_x(plan, fields, x_near_ref, x_far_ref)
    put_y(plan, fields, y_ref)
    columns = plan.half_x * plan.half_y
    owner = iota((plan.owners, columns), 0)
    hits = jnp.zeros((plan.owners, columns), F32)
    for g in range(plan.owners):
        hits = hits + (owner_ref[g : g + 1, :] == owner).astype(F32)
    count = jnp.broadcast_to(jnp.sum(hits, axis=1, keepdims=True), (plan.owners, plan.p))
    own = owner_ref[pl.ds(lax.axis_index("gx"), 1), :].astype(F32)
    blank = plan.count_row - plan.id_row - plan.half_x
    for slot in range(plan.groups):
        y_ref[slot, pl.ds(plan.count_row, plan.owners), :] = count
        if blank:
            y_ref[slot, pl.ds(plan.id_row + plan.half_x, blank), :] = jnp.zeros((blank, plan.p), F32)
        for i in range(plan.half_x):
            b = i * plan.half_y
            low, high = own[:, b : b + 1], own[:, b + plan.half_y - 1 : b + plan.half_y]
            ident = jnp.where(lax.axis_index("gy") < slot, high, low)
            y_ref[slot, pl.ds(plan.id_row + i, 1), :] = jnp.broadcast_to(ident, (1, plan.p))


def first_kernel(
    plan, conc_ref, pot_ref, mask_ref, class_ref, table_ref, mass_ref, pots_ref,
    x_near_ref, x_far_ref, y_ref, owner_ref,
    conc_out, pot_out, mob_out, total_out, spread_out, x_near_out, x_far_out, y_out,
):
    sides = get_x(x_near_ref, x_far_ref)
    ends = get_y(plan, y_ref)

    def halo(which):
        return tuple(side_rows(plan, rows, which) for rows in sides) + tuple(
            side_columns(plan, rows, which) for rows in ends
        )

    mobility, mob_halo = mobility_of(mask_ref, class_ref, table_ref), halo(2)
    mob_out[...] = mobility
    faces, diagonal = faces_of(mobility, mob_halo)
    mass_source, pot_source = mass_ref[...], pots_ref[...]
    conc, pot = conc_ref[...], pot_ref[...]
    excess = excess_of(conc, pot, halo(0), halo(1), faces, mass_source, pot_source)
    conc, pot = relax_pair(conc, pot, *excess, diagonal)
    conc_out[...] = conc
    pot_out[...] = pot
    put_x(plan, (conc, pot), x_near_out, x_far_out)
    put_y(plan, (conc, pot), y_out)

    nothing = tuple(jnp.zeros_like(part) for part in mob_halo)
    own_mass, own_pot = excess_of(conc, pot, nothing, nothing, faces, mass_source, pot_source)
    give_mass = [own_mass.reshape(plan.cells, plan.p)]
    give_pot = [own_pot.reshape(plan.cells, plan.p)]
    for x, side in ((0, 0), (plan.x - 1, 1)):
        face = 0.5 * (mobility[x] + mob_halo[side][0])
        give_mass.append(time_step * face * pot[x])
        give_pot.append(-interface * conc[x])
    gather, spread = membership(plan, owner_ref)
    spread_out[...] = spread
    give = jnp.concatenate(
        [jnp.concatenate(give_mass, axis=0), jnp.concatenate(give_pot, axis=0)], axis=1
    )
    total = split_dot(gather, give, ((1,), (0,)))

    def packed(both):
        mass, other = both[:, : plan.p], both[:, plan.p :]
        even = iota(mass.shape, 1) % 2 == 0
        return jnp.where(
            even, mass + pltpu.roll(mass, plan.p - 1, 1), other + pltpu.roll(other, 1, 1)
        )

    owner = iota((plan.owners, 1), 0)
    h = lax.axis_index("gy")

    def scale_of(count):
        return 0.125 / jnp.maximum(count, 1.0)

    def put(place, values):
        for slot in range(total_out.shape[0]):
            total_out[slot, pl.ds(place * plan.owners, plan.owners), :] = values

    own_hits = jnp.zeros((plan.owners, plan.half_x * plan.half_y), F32)
    owner_grid = iota(own_hits.shape, 0)
    for g in range(plan.owners):
        own_hits = own_hits + (owner_ref[g : g + 1, :] == owner_grid).astype(F32)
    own_count = jnp.sum(own_hits, axis=1, keepdims=True)
    put(1, packed(total) * scale_of(own_count))
    for place, y, side in ((0, 0, 2), (2, plan.y - 1, 3)):
        rows = ends[side - 2]
        inside = (h > 0) if place == 0 else (h < plan.groups - 1)
        edge_mob = jnp.concatenate([mobility[x, y : y + 1] for x in range(plan.x)], axis=0)
        edge_pot = jnp.concatenate([pot[x, y : y + 1] for x in range(plan.x)], axis=0)
        edge_conc = jnp.concatenate([conc[x, y : y + 1] for x in range(plan.x)], axis=0)
        face = 0.5 * (edge_mob + mob_halo[side][:, 0])
        both = jnp.concatenate([time_step * face * edge_pot, -interface * edge_conc], axis=1)
        part = jnp.zeros((plan.owners, 2 * plan.p), F32)
        for i in range(plan.half_x):
            ident = rows[plan.id_row + i : plan.id_row + i + 1, 0:1].astype(jnp.int32)
            pair = both[2 * i : 2 * i + 1] + both[2 * i + 1 : 2 * i + 2]
            part = part + jnp.where((owner == ident) & inside, pair, 0.0)
        put(place, packed(part) * scale_of(rows[plan.count_row : plan.count_row + plan.owners]))


def coarse_solve(packed, planes):
    lane = iota(packed.shape, 1)
    even = lane % 2 == 0
    mass_mean = jnp.where(even, packed, pltpu.roll(packed, 1, 1))
    pot_mean = jnp.where(even, pltpu.roll(packed, planes - 1, 1), packed)

    def neighbour_sum(values):
        return jnp.where(lane >= 2, pltpu.roll(values, 2, 1), 0.0) + jnp.where(
            lane < planes - 2, pltpu.roll(values, planes - 2, 1), 0.0
        )

    coarse_conc = jnp.zeros_like(mass_mean)
    coarse_pot = jnp.zeros_like(pot_mean)
    for _ in range(CSWEEP):
        mass_gap = mass_mean - (
            coarse_conc + coarse_flux * (2.0 * coarse_pot - neighbour_sum(coarse_pot))
        )
        pot_gap = pot_mean - (
            coarse_pot
            - split_slope * coarse_conc
            + coarse_bend * (neighbour_sum(coarse_conc) - 2.0 * coarse_conc)
        )
        coarse_conc = coarse_conc + (relax_coarse / coarse_det) * (
            mass_gap - 2.0 * coarse_flux * pot_gap
        )
        coarse_pot = coarse_pot + (relax_coarse / coarse_det) * (
            pot_gap + (split_slope + 2.0 * coarse_bend) * mass_gap
        )
    return coarse_conc, coarse_pot


def last_kernel(
    plan, conc_ref, pot_ref, mob_ref, mass_ref, pots_ref, x_near_msg, x_far_msg, y_msg,
    x_near_ref, x_far_ref, y_ref, total_ref, spread_ref,
    conc_out, pot_out, frame,
):
    h = lax.axis_index("gy")
    frame[...] = jnp.zeros_like(frame)
    for group in range(plan.groups):
        part = total_ref[0, group]
        for i in range(1, total_ref.shape[0]):
            part = part + total_ref[i, group]
        frame[pl.ds(group * plan.owners, 3 * plan.owners), :] += part
    base = pl.multiple_of(h * plan.owners, 8)
    means = frame[pl.ds(base, 3 * plan.owners), :]
    solved = jnp.concatenate(coarse_solve(means, plan.p), axis=1)
    own = split_dot(
        spread_ref[...].astype(BF16), solved[plan.owners : 2 * plan.owners], ((1,), (0,))
    )
    owner = iota((plan.owners, 1), 0)

    def edge_correction(place, rows, inside):
        part = solved[place * plan.owners : (place + 1) * plan.owners]
        out = []
        for i in range(plan.half_x):
            ident = rows[plan.id_row + i : plan.id_row + i + 1, 0:1].astype(jnp.int32)
            row = jnp.sum(jnp.where((owner == ident) & inside, part, 0.0), axis=0, keepdims=True)
            out += [row, row]
        return jnp.concatenate(out, axis=0)

    ends = get_y(plan, y_msg)
    sides = get_x(x_near_msg, x_far_msg)
    y_corr = (
        edge_correction(0, ends[0], h > 0),
        edge_correction(2, ends[1], h < plan.groups - 1),
    )
    new_ends = get_y(plan, y_ref)
    new_sides = get_x(x_near_ref, x_far_ref)

    def updated(which, ref):
        lanes = slice(which * plan.p, (which + 1) * plan.p)
        corr = own[:, lanes]
        field = ref[...] + corr[: plan.cells].reshape(plan.x, plan.y, plan.p)
        halo = []
        for side, rows in enumerate(new_sides):
            begin = plan.cells + side * plan.y
            halo.append(side_rows(plan, rows, which) + corr[begin : begin + plan.y][None])
        for rows, edge in zip(new_ends, y_corr):
            halo.append((rows[which * plan.x : (which + 1) * plan.x] + edge[:, lanes])[:, None])
        return field, halo

    conc, conc_halo = updated(0, conc_ref)
    pot, pot_halo = updated(1, pot_ref)
    mob_halo = (
        side_rows(plan, sides[0], 2),
        side_rows(plan, sides[1], 2),
        side_columns(plan, ends[0], 2),
        side_columns(plan, ends[1], 2),
    )
    faces, diagonal = faces_of(mob_ref[...], mob_halo)
    excess = excess_of(conc, pot, conc_halo, pot_halo, faces, mass_ref[...], pots_ref[...])
    conc_out[...], pot_out[...] = relax_pair(conc, pot, *excess, diagonal)


def call(kernel, plan, outs, args, far=(), smem=(), scratch=(), limit=VMEM_LIMIT):
    def space(i):
        return pl.ANY if i in far else pltpu.SMEM if i in smem else pltpu.VMEM

    return pl.pallas_call(
        functools.partial(kernel, plan),
        out_shape=[jax.ShapeDtypeStruct(shape, F32) for shape in outs],
        in_specs=[pl.BlockSpec(memory_space=space(i)) for i in range(len(args))],
        out_specs=[pl.BlockSpec(memory_space=pltpu.VMEM)] * len(outs),
        scratch_shapes=list(scratch),
        compiler_params=pltpu.CompilerParams(vmem_limit_bytes=limit),
    )(*args)


def swap_x(near, far):
    count = lax.axis_size("gx")
    out = []
    for rows, begin in ((near, 0), (far, 1)):
        pairs = [(i, i + 1) for i in range(begin, count - 1, 2)]
        out.append(lax.ppermute(rows, "gx", pairs + [(j, i) for i, j in pairs]))
    return out


def swap_y(slots):
    return lax.all_to_all(slots, "gy", split_axis=0, concat_axis=0, tiled=True)


def gather_totals(plan, total):
    if total.shape[0] > 1:
        parts = lax.all_to_all(total, ("gx", "gy"), split_axis=0, concat_axis=0, tiled=True)
        return parts.reshape(plan.owners, plan.groups, *total.shape[1:])
    return lax.all_gather(lax.psum(total, "gx"), "gy", axis=1)


def on_device(conc, pot, mass_source, pot_source, mask, kind, table, owner_map):
    plan = Plan(conc.shape, lax.axis_size("gx"), lax.axis_size("gy"))
    block = conc.shape
    slots = plan.owners * plan.groups
    slots = slots if slots <= 64 else 1
    messages = call(
        prepare_kernel,
        plan,
        [*[(3 * plan.y, plan.p)] * 2, (plan.groups, plan.y_rows, plan.p)],
        [conc, pot, mask, kind, owner_map, table],
        far=range(6),
        limit=LARGE_LIMIT,
        scratch=(
            pltpu.VMEM(block, F32),
            pltpu.VMEM(block, F32),
            pltpu.VMEM(owner_map.shape, owner_map.dtype),
            pltpu.VMEM(block, mask.dtype),
            pltpu.VMEM(block, kind.dtype),
            pltpu.SMEM(table.shape, table.dtype),
            pltpu.SemaphoreType.DMA((6,)),
        ),
    )
    y_msg = swap_y(messages[2])
    x_msg = swap_x(*messages[:2])
    conc, pot, mob, total, spread, *messages = call(
        first_kernel,
        plan,
        [
            block,
            block,
            block,
            (slots, 3 * plan.owners, plan.p),
            (plan.rows, plan.owners),
            *[(2 * plan.y, plan.p)] * 2,
            (plan.groups, 2 * plan.x, plan.p),
        ],
        [conc, pot, mask, kind, table, mass_source, pot_source, *x_msg, y_msg, owner_map],
        smem=(4,),
    )
    total = gather_totals(plan, total)
    y_new = swap_y(messages[2])
    x_new = swap_x(*messages[:2])
    return tuple(
        call(
            last_kernel,
            plan,
            [block, block],
            [conc, pot, mob, mass_source, pot_source, *x_msg, y_msg, *x_new, y_new, total, spread],
            scratch=[pltpu.VMEM(((plan.groups + 2) * plan.owners, plan.p), F32)],
        )
    )


def solution(mesh):
    grid = P("gx", "gy", None)
    return jax.shard_map(
        on_device,
        mesh=mesh,
        in_specs=(grid,) * 6 + (P(), P(None, "gy")),
        out_specs=(grid, grid),
        check_vma=False,
    )
```

```python
import functools

import jax
import jax.numpy as jnp
from jax import lax
from jax.experimental import pallas as pl
from jax.experimental.pallas import tpu as pltpu
from jax.sharding import PartitionSpec as P

CSWEEP = 3

time_step = 0.25
split_slope = 1.0
interface = 0.5
relax_fine = 0.6
relax_coarse = 0.6
coarse_flux = 0.0625
coarse_bend = 0.125
coarse_det = 1.0 + 2.0 * coarse_flux * (split_slope + 2.0 * coarse_bend)

F32 = jnp.float32
BF16 = jnp.bfloat16
VMEM_LIMIT = 48 * 1024 * 1024
LARGE_LIMIT = 60 * 1024 * 1024


def iota(shape, dim):
    return lax.broadcasted_iota(jnp.int32, shape, dim)


def x_pair(field, low, high):
    return (
        jnp.concatenate([low, field[:-1]], axis=0),
        jnp.concatenate([field[1:], high], axis=0),
    )


def y_pair(field, low, high):
    size = field.shape[1]
    where = iota(field.shape, 1)
    return (
        jnp.where(where == 0, low, pltpu.roll(field, 1, 1)),
        jnp.where(where == size - 1, high, pltpu.roll(field, size - 1, 1)),
    )


def plane_pair(field):
    size = field.shape[2]
    where = iota(field.shape, 2)
    return (
        jnp.where(where == 0, 0.0, pltpu.roll(field, 1, 2)),
        jnp.where(where == size - 1, 0.0, pltpu.roll(field, size - 1, 2)),
    )


def neighbours(field, halo):
    xm, xp, ym, yp = halo
    return (*x_pair(field, xm, xp), *y_pair(field, ym, yp), *plane_pair(field))


def excess_of(conc, pot, conc_halo, pot_halo, faces, mass_source, pot_source):
    flux = jnp.zeros_like(pot)
    for face, other in zip(faces, neighbours(pot, pot_halo)):
        flux = flux + face * (other - pot)
    laplace = -6.0 * conc
    for other in neighbours(conc, conc_halo):
        laplace = laplace + other
    excess_mass = mass_source - (conc - time_step * flux)
    excess_pot = pot_source - (pot - split_slope * conc + interface * laplace)
    return excess_mass, excess_pot


def relax_pair(conc, pot, excess_mass, excess_pot, diagonal):
    other_diagonal = -(split_slope + 6.0 * interface)
    scale = relax_fine / (1.0 - diagonal * other_diagonal)
    new_conc = conc + (excess_mass - diagonal * excess_pot) * scale
    new_pot = pot + (excess_pot - other_diagonal * excess_mass) * scale
    return new_conc, new_pot


def faces_of(mobility, halo):
    faces = tuple(0.5 * (mobility + other) for other in neighbours(mobility, halo))
    diagonal = faces[0]
    for face in faces[1:]:
        diagonal = diagonal + face
    return faces, time_step * diagonal


def split_dot(ones, values, contract):
    dims = (contract, ((), ()))
    total = None
    rest = values
    for _ in range(3):
        term = rest.astype(BF16)
        rest = rest - term.astype(F32)
        part = lax.dot_general(ones, term, dims, preferred_element_type=F32)
        total = part if total is None else total + part
    return total


def round_up(value, unit):
    return -(-value // unit) * unit


class Plan:
    def __init__(self, shape, owners, groups):
        self.x, self.y, self.p = shape
        self.owners, self.groups = owners, groups
        self.half_x, self.half_y = self.x // 2, self.y // 2
        self.id_row = 3 * self.x
        self.count_row = round_up(self.id_row + self.half_x, 8)
        self.y_rows = self.count_row + owners
        self.cells = self.x * self.y
        self.rows = self.cells + 2 * self.y


def side_rows(plan, rows, which):
    return rows[which * plan.y : (which + 1) * plan.y][None]


def side_columns(plan, rows, which):
    return rows[which * plan.x : (which + 1) * plan.x][:, None]


def column_of(plan):
    shape = (plan.rows, plan.half_x * plan.half_y)
    row = iota(shape, 0)
    x = row // plan.y
    y = row % plan.y
    own = (x // 2) * plan.half_y + y // 2
    low = (plan.half_x - 1) * plan.half_y + y // 2
    high = y // 2
    column = jnp.where(x < plan.x, own, jnp.where(x == plan.x, low, high))
    return row, column == iota(shape, 1)


def owner_hits(plan, owner_ref):
    g = lax.axis_index("gx")
    last = plan.owners - 1
    owner = iota((plan.owners, plan.half_x * plan.half_y), 0)
    own = owner_ref[pl.ds(g, 1), :] == owner
    low = (owner_ref[pl.ds(jnp.maximum(g - 1, 0), 1), :] == owner) & (g > 0)
    high = (owner_ref[pl.ds(jnp.minimum(g + 1, last), 1), :] == owner) & (g < last)
    return own, low, high


def membership(plan, owner_ref):
    row, column = column_of(plan)
    spans = ((0, plan.cells), (plan.cells, plan.cells + plan.y), (plan.cells + plan.y, plan.rows))
    gather, spread = None, None
    for (begin, end), hits in zip(spans, owner_hits(plan, owner_ref)):
        place = (column & (row >= begin) & (row < end)).astype(F32).astype(BF16)
        hits = hits.astype(F32).astype(BF16)
        nt = (((1,), (1,)), ((), ()))
        part = lax.dot_general(hits, place, nt, preferred_element_type=F32)
        gather = part if gather is None else gather + part
        part = lax.dot_general(place, hits, nt, preferred_element_type=F32)
        spread = part if spread is None else spread + part
    return gather.astype(BF16), spread


def mobility_of(mask_ref, class_ref, table_ref):
    kind = class_ref[...]
    values = jnp.zeros(kind.shape, F32)
    for marker in range(table_ref.shape[0]):
        values = jnp.where(kind == marker, table_ref[marker], values)
    return mask_ref[...].astype(F32) * values


def even(axis):
    return lax.rem(lax.axis_index(axis), 2) == 0


def put_x(plan, fields, near_ref, far_ref):
    up = even("gx")
    for which, field in enumerate(fields):
        low, high = field[0], field[plan.x - 1]
        near_ref[pl.ds(which * plan.y, plan.y), :] = jnp.where(up, high, low)
        far_ref[pl.ds(which * plan.y, plan.y), :] = jnp.where(up, low, high)


def put_y(plan, fields, near_ref, far_ref):
    up = even("gy")
    for which, field in enumerate(fields):
        for x in range(plan.x):
            low, high = field[x, 0:1], field[x, plan.y - 1 : plan.y]
            near_ref[pl.ds(which * plan.x + x, 1), :] = jnp.where(up, high, low)
            far_ref[pl.ds(which * plan.x + x, 1), :] = jnp.where(up, low, high)


def received(axis, near_ref, far_ref):
    up = even(axis)
    near, far = near_ref[...], far_ref[...]
    return jnp.where(up, far, near), jnp.where(up, near, far)


def prepare_kernel(
    plan, conc_hbm, pot_hbm, mask_hbm, class_hbm, owner_hbm, table_hbm,
    x_near_ref, x_far_ref, y_near_ref, y_far_ref,
    conc_ref, pot_ref, owner_ref, mask_ref, class_ref, table_ref, sems,
):
    pairs = (
        (table_hbm, table_ref), (class_hbm, class_ref), (mask_hbm, mask_ref),
        (conc_hbm, conc_ref), (pot_hbm, pot_ref), (owner_hbm, owner_ref),
    )
    copies = [
        pltpu.make_async_copy(source, target, sems.at[i])
        for i, (source, target) in enumerate(pairs)
    ]
    for copy in copies:
        copy.start()
    for copy in copies:
        copy.wait()
    mobility = mobility_of(mask_ref, class_ref, table_ref)
    fields = (conc_ref[...], pot_ref[...], mobility)
    put_x(plan, fields, x_near_ref, x_far_ref)
    put_y(plan, fields, y_near_ref, y_far_ref)
    columns = plan.half_x * plan.half_y
    owner = iota((plan.owners, columns), 0)
    hits = jnp.zeros((plan.owners, columns), F32)
    for g in range(plan.owners):
        hits = hits + (owner_ref[g : g + 1, :] == owner).astype(F32)
    count = jnp.broadcast_to(jnp.sum(hits, axis=1, keepdims=True), (plan.owners, plan.p))
    own = owner_ref[pl.ds(lax.axis_index("gx"), 1), :].astype(F32)
    blank = plan.count_row - plan.id_row - plan.half_x
    up = even("gy")
    for ref, top in ((y_near_ref, up), (y_far_ref, jnp.logical_not(up))):
        ref[pl.ds(plan.count_row, plan.owners), :] = count
        if blank:
            ref[pl.ds(plan.id_row + plan.half_x, blank), :] = jnp.zeros((blank, plan.p), F32)
        for i in range(plan.half_x):
            b = i * plan.half_y
            low, high = own[:, b : b + 1], own[:, b + plan.half_y - 1 : b + plan.half_y]
            ident = jnp.where(top, high, low)
            ref[pl.ds(plan.id_row + i, 1), :] = jnp.broadcast_to(ident, (1, plan.p))


def first_kernel(
    plan, conc_ref, pot_ref, mask_ref, class_ref, table_ref, mass_ref, pots_ref,
    x_near_ref, x_far_ref, y_near_ref, y_far_ref, owner_ref,
    conc_out, pot_out, mob_out, total_out, spread_out,
    x_near_out, x_far_out, y_near_out, y_far_out,
):
    sides = received("gx", x_near_ref, x_far_ref)
    ends = received("gy", y_near_ref, y_far_ref)

    def halo(which):
        return tuple(side_rows(plan, rows, which) for rows in sides) + tuple(
            side_columns(plan, rows, which) for rows in ends
        )

    mobility, mob_halo = mobility_of(mask_ref, class_ref, table_ref), halo(2)
    mob_out[...] = mobility
    faces, diagonal = faces_of(mobility, mob_halo)
    mass_source, pot_source = mass_ref[...], pots_ref[...]
    conc, pot = conc_ref[...], pot_ref[...]
    excess = excess_of(conc, pot, halo(0), halo(1), faces, mass_source, pot_source)
    conc, pot = relax_pair(conc, pot, *excess, diagonal)
    conc_out[...] = conc
    pot_out[...] = pot
    put_x(plan, (conc, pot), x_near_out, x_far_out)
    put_y(plan, (conc, pot), y_near_out, y_far_out)

    nothing = tuple(jnp.zeros_like(part) for part in mob_halo)
    own_mass, own_pot = excess_of(conc, pot, nothing, nothing, faces, mass_source, pot_source)
    give_mass = [own_mass.reshape(plan.cells, plan.p)]
    give_pot = [own_pot.reshape(plan.cells, plan.p)]
    for x, side in ((0, 0), (plan.x - 1, 1)):
        face = 0.5 * (mobility[x] + mob_halo[side][0])
        give_mass.append(time_step * face * pot[x])
        give_pot.append(-interface * conc[x])
    gather, spread = membership(plan, owner_ref)
    spread_out[...] = spread
    give = jnp.concatenate(
        [jnp.concatenate(give_mass, axis=0), jnp.concatenate(give_pot, axis=0)], axis=1
    )
    total = split_dot(gather, give, ((1,), (0,)))

    def packed(both):
        mass, other = both[:, : plan.p], both[:, plan.p :]
        even = iota(mass.shape, 1) % 2 == 0
        return jnp.where(
            even, mass + pltpu.roll(mass, plan.p - 1, 1), other + pltpu.roll(other, 1, 1)
        )

    owner = iota((plan.owners, 1), 0)
    h = lax.axis_index("gy")

    def scale_of(count):
        return 0.125 / jnp.maximum(count, 1.0)

    def put(place, values):
        for slot in range(total_out.shape[0]):
            total_out[slot, pl.ds(place * plan.owners, plan.owners), :] = values

    own_hits = jnp.zeros((plan.owners, plan.half_x * plan.half_y), F32)
    owner_grid = iota(own_hits.shape, 0)
    for g in range(plan.owners):
        own_hits = own_hits + (owner_ref[g : g + 1, :] == owner_grid).astype(F32)
    own_count = jnp.sum(own_hits, axis=1, keepdims=True)
    put(1, packed(total) * scale_of(own_count))
    for place, y, side in ((0, 0, 2), (2, plan.y - 1, 3)):
        rows = ends[side - 2]
        inside = (h > 0) if place == 0 else (h < plan.groups - 1)
        edge_mob = jnp.concatenate([mobility[x, y : y + 1] for x in range(plan.x)], axis=0)
        edge_pot = jnp.concatenate([pot[x, y : y + 1] for x in range(plan.x)], axis=0)
        edge_conc = jnp.concatenate([conc[x, y : y + 1] for x in range(plan.x)], axis=0)
        face = 0.5 * (edge_mob + mob_halo[side][:, 0])
        both = jnp.concatenate([time_step * face * edge_pot, -interface * edge_conc], axis=1)
        part = jnp.zeros((plan.owners, 2 * plan.p), F32)
        for i in range(plan.half_x):
            ident = rows[plan.id_row + i : plan.id_row + i + 1, 0:1].astype(jnp.int32)
            pair = both[2 * i : 2 * i + 1] + both[2 * i + 1 : 2 * i + 2]
            part = part + jnp.where((owner == ident) & inside, pair, 0.0)
        put(place, packed(part) * scale_of(rows[plan.count_row : plan.count_row + plan.owners]))


def coarse_solve(packed, planes):
    lane = iota(packed.shape, 1)
    even = lane % 2 == 0
    mass_mean = jnp.where(even, packed, pltpu.roll(packed, 1, 1))
    pot_mean = jnp.where(even, pltpu.roll(packed, planes - 1, 1), packed)

    def neighbour_sum(values):
        return jnp.where(lane >= 2, pltpu.roll(values, 2, 1), 0.0) + jnp.where(
            lane < planes - 2, pltpu.roll(values, planes - 2, 1), 0.0
        )

    coarse_conc = jnp.zeros_like(mass_mean)
    coarse_pot = jnp.zeros_like(pot_mean)
    for _ in range(CSWEEP):
        mass_gap = mass_mean - (
            coarse_conc + coarse_flux * (2.0 * coarse_pot - neighbour_sum(coarse_pot))
        )
        pot_gap = pot_mean - (
            coarse_pot
            - split_slope * coarse_conc
            + coarse_bend * (neighbour_sum(coarse_conc) - 2.0 * coarse_conc)
        )
        coarse_conc = coarse_conc + (relax_coarse / coarse_det) * (
            mass_gap - 2.0 * coarse_flux * pot_gap
        )
        coarse_pot = coarse_pot + (relax_coarse / coarse_det) * (
            pot_gap + (split_slope + 2.0 * coarse_bend) * mass_gap
        )
    return coarse_conc, coarse_pot


def last_kernel(
    plan, conc_ref, pot_ref, mob_ref, mass_ref, pots_ref, x_near_msg, x_far_msg,
    y_near_msg, y_far_msg, x_near_ref, x_far_ref, y_near_ref, y_far_ref, total_ref, spread_ref,
    conc_out, pot_out, frame,
):
    h = lax.axis_index("gy")
    frame[...] = jnp.zeros_like(frame)
    for group in range(plan.groups):
        part = total_ref[0, group]
        for i in range(1, total_ref.shape[0]):
            part = part + total_ref[i, group]
        frame[pl.ds(group * plan.owners, 3 * plan.owners), :] += part
    base = pl.multiple_of(h * plan.owners, 8)
    means = frame[pl.ds(base, 3 * plan.owners), :]
    solved = jnp.concatenate(coarse_solve(means, plan.p), axis=1)
    own = split_dot(
        spread_ref[...].astype(BF16), solved[plan.owners : 2 * plan.owners], ((1,), (0,))
    )
    owner = iota((plan.owners, 1), 0)

    def edge_correction(place, rows, inside):
        part = solved[place * plan.owners : (place + 1) * plan.owners]
        out = []
        for i in range(plan.half_x):
            ident = rows[plan.id_row + i : plan.id_row + i + 1, 0:1].astype(jnp.int32)
            row = jnp.sum(jnp.where((owner == ident) & inside, part, 0.0), axis=0, keepdims=True)
            out += [row, row]
        return jnp.concatenate(out, axis=0)

    ends = received("gy", y_near_msg, y_far_msg)
    sides = received("gx", x_near_msg, x_far_msg)
    y_corr = (
        edge_correction(0, ends[0], h > 0),
        edge_correction(2, ends[1], h < plan.groups - 1),
    )
    new_ends = received("gy", y_near_ref, y_far_ref)
    new_sides = received("gx", x_near_ref, x_far_ref)

    def updated(which, ref):
        lanes = slice(which * plan.p, (which + 1) * plan.p)
        corr = own[:, lanes]
        field = ref[...] + corr[: plan.cells].reshape(plan.x, plan.y, plan.p)
        halo = []
        for side, rows in enumerate(new_sides):
            begin = plan.cells + side * plan.y
            halo.append(side_rows(plan, rows, which) + corr[begin : begin + plan.y][None])
        for rows, edge in zip(new_ends, y_corr):
            halo.append((rows[which * plan.x : (which + 1) * plan.x] + edge[:, lanes])[:, None])
        return field, halo

    conc, conc_halo = updated(0, conc_ref)
    pot, pot_halo = updated(1, pot_ref)
    mob_halo = (
        side_rows(plan, sides[0], 2),
        side_rows(plan, sides[1], 2),
        side_columns(plan, ends[0], 2),
        side_columns(plan, ends[1], 2),
    )
    faces, diagonal = faces_of(mob_ref[...], mob_halo)
    excess = excess_of(conc, pot, conc_halo, pot_halo, faces, mass_ref[...], pots_ref[...])
    conc_out[...], pot_out[...] = relax_pair(conc, pot, *excess, diagonal)


def call(kernel, plan, outs, args, far=(), smem=(), scratch=(), limit=VMEM_LIMIT):
    def space(i):
        return pl.ANY if i in far else pltpu.SMEM if i in smem else pltpu.VMEM

    return pl.pallas_call(
        functools.partial(kernel, plan),
        out_shape=[jax.ShapeDtypeStruct(shape, F32) for shape in outs],
        in_specs=[pl.BlockSpec(memory_space=space(i)) for i in range(len(args))],
        out_specs=[pl.BlockSpec(memory_space=pltpu.VMEM)] * len(outs),
        scratch_shapes=list(scratch),
        compiler_params=pltpu.CompilerParams(vmem_limit_bytes=limit),
    )(*args)


def swap(axis, near, far):
    count = lax.axis_size(axis)
    out = []
    for rows, begin in ((near, 0), (far, 1)):
        pairs = [(i, i + 1) for i in range(begin, count - 1, 2)]
        out.append(lax.ppermute(rows, axis, pairs + [(j, i) for i, j in pairs]))
    return out


def swap_all(x_near, x_far, y_near, y_far):
    return *swap("gx", x_near, x_far), *swap("gy", y_near, y_far)


def gather_totals(plan, total):
    if total.shape[0] > 1:
        parts = lax.all_to_all(total, ("gx", "gy"), split_axis=0, concat_axis=0, tiled=True)
        return parts.reshape(plan.owners, plan.groups, *total.shape[1:])
    return lax.all_gather(lax.psum(total, "gx"), "gy", axis=1)


def on_device(conc, pot, mass_source, pot_source, mask, kind, table, owner_map):
    plan = Plan(conc.shape, lax.axis_size("gx"), lax.axis_size("gy"))
    block = conc.shape
    slots = plan.owners * plan.groups
    slots = slots if slots <= 64 else 1
    messages = call(
        prepare_kernel,
        plan,
        [*[(3 * plan.y, plan.p)] * 2, *[(plan.y_rows, plan.p)] * 2],
        [conc, pot, mask, kind, owner_map, table],
        far=range(6),
        limit=LARGE_LIMIT,
        scratch=(
            pltpu.VMEM(block, F32),
            pltpu.VMEM(block, F32),
            pltpu.VMEM(owner_map.shape, owner_map.dtype),
            pltpu.VMEM(block, mask.dtype),
            pltpu.VMEM(block, kind.dtype),
            pltpu.SMEM(table.shape, table.dtype),
            pltpu.SemaphoreType.DMA((6,)),
        ),
    )
    old = swap_all(*messages)
    conc, pot, mob, total, spread, *messages = call(
        first_kernel,
        plan,
        [
            block,
            block,
            block,
            (slots, 3 * plan.owners, plan.p),
            (plan.rows, plan.owners),
            *[(2 * plan.y, plan.p)] * 2,
            *[(2 * plan.x, plan.p)] * 2,
        ],
        [conc, pot, mask, kind, table, mass_source, pot_source, *old, owner_map],
        smem=(4,),
    )
    total = gather_totals(plan, total)
    new = swap_all(*messages)
    return tuple(
        call(
            last_kernel,
            plan,
            [block, block],
            [conc, pot, mob, mass_source, pot_source, *old, *new, total, spread],
            scratch=[pltpu.VMEM(((plan.groups + 2) * plan.owners, plan.p), F32)],
        )
    )


def solution(mesh):
    grid = P("gx", "gy", None)
    return jax.shard_map(
        on_device,
        mesh=mesh,
        in_specs=(grid,) * 6 + (P(), P(None, "gy")),
        out_specs=(grid, grid),
        check_vma=False,
    )
```

```python
import functools

import jax
import jax.numpy as jnp
from jax import lax
from jax.experimental import pallas as pl
from jax.experimental.pallas import tpu as pltpu
from jax.sharding import PartitionSpec as P

CSWEEP = 3

time_step = 0.25
split_slope = 1.0
interface = 0.5
relax_fine = 0.6
relax_coarse = 0.6
coarse_flux = 0.0625
coarse_bend = 0.125
coarse_det = 1.0 + 2.0 * coarse_flux * (split_slope + 2.0 * coarse_bend)

F32 = jnp.float32
BF16 = jnp.bfloat16
VMEM_LIMIT = 48 * 1024 * 1024
LARGE_LIMIT = 60 * 1024 * 1024


def iota(shape, dim):
    return lax.broadcasted_iota(jnp.int32, shape, dim)


def x_pair(field, low, high):
    return (
        jnp.concatenate([low, field[:-1]], axis=0),
        jnp.concatenate([field[1:], high], axis=0),
    )


def y_pair(field, low, high):
    size = field.shape[1]
    where = iota(field.shape, 1)
    return (
        jnp.where(where == 0, low, pltpu.roll(field, 1, 1)),
        jnp.where(where == size - 1, high, pltpu.roll(field, size - 1, 1)),
    )


def plane_pair(field):
    size = field.shape[2]
    where = iota(field.shape, 2)
    return (
        jnp.where(where == 0, 0.0, pltpu.roll(field, 1, 2)),
        jnp.where(where == size - 1, 0.0, pltpu.roll(field, size - 1, 2)),
    )


def neighbours(field, halo):
    xm, xp, ym, yp = halo
    return (*x_pair(field, xm, xp), *y_pair(field, ym, yp), *plane_pair(field))


def excess_of(conc, pot, conc_halo, pot_halo, faces, mass_source, pot_source):
    flux = jnp.zeros_like(pot)
    for face, other in zip(faces, neighbours(pot, pot_halo)):
        flux = flux + face * (other - pot)
    laplace = -6.0 * conc
    for other in neighbours(conc, conc_halo):
        laplace = laplace + other
    excess_mass = mass_source - (conc - time_step * flux)
    excess_pot = pot_source - (pot - split_slope * conc + interface * laplace)
    return excess_mass, excess_pot


def relax_pair(conc, pot, excess_mass, excess_pot, diagonal):
    other_diagonal = -(split_slope + 6.0 * interface)
    scale = relax_fine / (1.0 - diagonal * other_diagonal)
    new_conc = conc + (excess_mass - diagonal * excess_pot) * scale
    new_pot = pot + (excess_pot - other_diagonal * excess_mass) * scale
    return new_conc, new_pot


def faces_of(mobility, halo):
    faces = tuple(0.5 * (mobility + other) for other in neighbours(mobility, halo))
    diagonal = faces[0]
    for face in faces[1:]:
        diagonal = diagonal + face
    return faces, time_step * diagonal


def split_dot(ones, values, contract):
    dims = (contract, ((), ()))
    total = None
    rest = values
    for _ in range(3):
        term = rest.astype(BF16)
        rest = rest - term.astype(F32)
        part = lax.dot_general(ones, term, dims, preferred_element_type=F32)
        total = part if total is None else total + part
    return total


def round_up(value, unit):
    return -(-value // unit) * unit


class Plan:
    def __init__(self, shape, owners, groups):
        self.x, self.y, self.p = shape
        self.owners, self.groups = owners, groups
        self.half_x, self.half_y = self.x // 2, self.y // 2
        self.columns = self.half_x * self.half_y
        self.map_row = round_up(3 * self.x, 8)
        self.y_rows = self.map_row + owners
        self.cells = self.x * self.y
        self.rows = self.cells + 2 * self.y
        self.low_row = owners
        self.high_row = owners + self.half_x
        self.slot_rows = round_up(owners + 2 * self.half_x, 8)
        slots = owners * groups
        self.slots = slots if slots <= 64 else 0


def side_rows(plan, rows, which):
    return rows[which * plan.y : (which + 1) * plan.y][None]


def side_columns(plan, rows, which):
    return rows[which * plan.x : (which + 1) * plan.x][:, None]


def membership(plan, owner_ref):
    g = lax.axis_index("gx")
    last = plan.owners - 1
    owner = iota((plan.owners, plan.columns), 0)
    shape = (plan.x + 2, plan.y, plan.columns)
    x, y, column = iota(shape, 0), iota(shape, 1), iota(shape, 2)
    half = jnp.where(x < plan.x, x >> 1, jnp.where(x == plan.x, plan.half_x - 1, 0))
    place = column == half * plan.half_y + (y >> 1)
    sides = (
        (x < plan.x, g, True),
        (x == plan.x, jnp.maximum(g - 1, 0), g > 0),
        (x == plan.x + 1, jnp.minimum(g + 1, last), g < last),
    )
    gather, spread = None, None
    for part, row, inside in sides:
        hits = ((owner_ref[pl.ds(row, 1), :] == owner) & inside).astype(F32).astype(BF16)
        where = (place & part).astype(F32).reshape(plan.rows, plan.columns).astype(BF16)
        nt = (((1,), (1,)), ((), ()))
        some = lax.dot_general(hits, where, nt, preferred_element_type=F32)
        gather = some if gather is None else gather + some
        some = lax.dot_general(where, hits, nt, preferred_element_type=F32)
        spread = some if spread is None else spread + some
    return gather, spread


def scale_of(plan, owners):
    owner = iota((plan.owners, plan.columns), 0).astype(owners.dtype)
    hits = jnp.zeros((plan.owners, plan.columns), F32)
    for g in range(plan.owners):
        hits = hits + (owners[g : g + 1] == owner).astype(F32)
    count = jnp.sum(hits, axis=1, keepdims=True)
    return jnp.broadcast_to(0.125 / jnp.maximum(count, 1.0), (plan.owners, plan.p))


def mobility_of(mask, kind, table):
    values = jnp.zeros(kind.shape, F32)
    for marker, value in enumerate(table):
        values = jnp.where(kind == marker, value, values)
    return mask.astype(F32) * values


def even(axis):
    return lax.rem(lax.axis_index(axis), 2) == 0


def put_edges(plan, fields, x_near, x_far, y_near, y_far):
    up_x, up_y = even("gx"), even("gy")
    whole = slice(0, plan.y)
    for which, field in enumerate(fields):
        low, high = field(0, whole), field(plan.x - 1, whole)
        x_near[pl.ds(which * plan.y, plan.y), :] = jnp.where(up_x, high, low)
        x_far[pl.ds(which * plan.y, plan.y), :] = jnp.where(up_x, low, high)
        for x in range(plan.x):
            low, high = field(x, slice(0, 1)), field(x, slice(plan.y - 1, plan.y))
            y_near[pl.ds(which * plan.x + x, 1), :] = jnp.where(up_y, high, low)
            y_far[pl.ds(which * plan.x + x, 1), :] = jnp.where(up_y, low, high)


def received(axis, near_ref, far_ref):
    up = even(axis)
    near, far = near_ref[...], far_ref[...]
    return jnp.where(up, far, near), jnp.where(up, near, far)


def prepare_kernel(
    plan, conc_hbm, pot_hbm, mask_hbm, class_hbm, owner_hbm, table_hbm,
    x_near_ref, x_far_ref, y_near_ref, y_far_ref,
    conc_ref, pot_ref, owner_ref, mask_ref, class_ref, table_ref, sems,
):
    pairs = (
        (table_hbm, table_ref), (class_hbm, class_ref), (mask_hbm, mask_ref),
        (conc_hbm, conc_ref), (pot_hbm, pot_ref), (owner_hbm, owner_ref),
    )
    copies = [
        pltpu.make_async_copy(source, target, sems.at[i])
        for i, (source, target) in enumerate(pairs)
    ]
    for copy in copies:
        copy.start()
    for copy in copies:
        copy.wait()
    table = [table_ref[marker] for marker in range(table_ref.shape[0])]
    send = (x_near_ref, x_far_ref, y_near_ref, y_far_ref)
    edges = [lambda x, y: conc_ref[x, y], lambda x, y: pot_ref[x, y]]
    edges.append(lambda x, y: mobility_of(mask_ref[x, y], class_ref[x, y], table))
    put_edges(plan, edges, *send)
    used = 3 * plan.x
    for ref in (y_near_ref, y_far_ref):
        ref[pl.ds(used, plan.y_rows - used), :] = jnp.zeros((plan.y_rows - used, plan.p), F32)
        ref[pl.ds(plan.map_row, plan.owners), pl.ds(0, plan.columns)] = owner_ref[...].astype(F32)


def local_kernel(
    plan, mask_ref, class_ref, table_ref, owner_ref, mob_ref, gather_ref, spread_ref, scale_ref
):
    table = [table_ref[marker] for marker in range(table_ref.shape[0])]
    mob_ref[...] = mobility_of(mask_ref[...], class_ref[...], table)
    gather_ref[...], spread_ref[...] = membership(plan, owner_ref)
    scale_ref[...] = scale_of(plan, owner_ref[...])


def first_kernel(
    plan, conc_ref, pot_ref, mob_ref, mass_ref, pots_ref, gather_ref, scale_ref, owner_ref,
    x_near_ref, x_far_ref, y_near_ref, y_far_ref,
    conc_out, pot_out, total_out, *send,
):
    sides = received("gx", x_near_ref, x_far_ref)
    ends = received("gy", y_near_ref, y_far_ref)

    def halo(which):
        return tuple(side_rows(plan, rows, which) for rows in sides) + tuple(
            side_columns(plan, rows, which) for rows in ends
        )

    mobility, mob_halo = mob_ref[...], halo(2)
    faces, diagonal = faces_of(mobility, mob_halo)
    mass_source, pot_source = mass_ref[...], pots_ref[...]
    conc, pot = conc_ref[...], pot_ref[...]
    excess = excess_of(conc, pot, halo(0), halo(1), faces, mass_source, pot_source)
    conc, pot = relax_pair(conc, pot, *excess, diagonal)
    conc_out[...] = conc
    pot_out[...] = pot
    put_edges(plan, (lambda x, y: conc[x, y], lambda x, y: pot[x, y]), *send)

    nothing = tuple(jnp.zeros_like(part) for part in mob_halo)
    own_mass, own_pot = excess_of(conc, pot, nothing, nothing, faces, mass_source, pot_source)
    give_mass = [own_mass.reshape(plan.cells, plan.p)]
    give_pot = [own_pot.reshape(plan.cells, plan.p)]
    for x, side in ((0, 0), (plan.x - 1, 1)):
        face = 0.5 * (mobility[x] + mob_halo[side][0])
        give_mass.append(time_step * face * pot[x])
        give_pot.append(-interface * conc[x])
    give = jnp.concatenate(
        [jnp.concatenate(give_mass, axis=0), jnp.concatenate(give_pot, axis=0)], axis=1
    )

    def packed(both):
        mass, other = both[:, : plan.p], both[:, plan.p :]
        first = iota(mass.shape, 1) & 1 == 0
        return jnp.where(
            first, mass + pltpu.roll(mass, plan.p - 1, 1), other + pltpu.roll(other, 1, 1)
        )

    h = lax.axis_index("gy")
    inside = (h > 0, None, h < plan.groups - 1)
    maps = [rows[plan.map_row : plan.map_row + plan.owners, : plan.columns] for rows in ends]
    maps.insert(1, owner_ref[...].astype(F32))
    owner = iota((plan.owners, 1), 0)
    is_mine = owner == lax.axis_index("gx")

    def column(place, i, at):
        b = i * plan.half_y + at
        return maps[place][:, b : b + 1]

    sums = [None, packed(split_dot(gather_ref[...].astype(BF16), give, ((1,), (0,)))), None]
    sums[1] = sums[1] * scale_ref[...]
    for place, y, at, side in ((0, 0, plan.half_y - 1, 2), (2, plan.y - 1, 0, 3)):
        edge_mob, edge_pot, edge_conc = (
            jnp.concatenate([field[x, y : y + 1] for x in range(plan.x)], axis=0)
            for field in (mobility, pot, conc)
        )
        face = 0.5 * (edge_mob + mob_halo[side][:, 0])
        both = jnp.concatenate([time_step * face * edge_pot, -interface * edge_conc], axis=1)
        part = jnp.zeros((plan.owners, 2 * plan.p), F32)
        for i in range(plan.half_x):
            ident = jnp.sum(jnp.where(is_mine, column(place, i, at), 0.0), axis=0, keepdims=True)
            pair = both[2 * i : 2 * i + 1] + both[2 * i + 1 : 2 * i + 2]
            part = part + jnp.where((owner.astype(F32) == ident) & inside[place], pair, 0.0)
        sums[place] = packed(part) * scale_of(plan, maps[place])

    if not plan.slots:
        total_out[...] = jnp.concatenate(sums, axis=0)
        return

    def picked(place, i, at):
        ident = jnp.broadcast_to(column(place, i, at), (plan.owners, plan.p))
        out = jnp.zeros((plan.owners, plan.p), F32)
        for o in range(plan.owners):
            out = jnp.where(ident == float(o), sums[place][o : o + 1], out)
        return out

    below = [[picked(k, i, plan.half_y - 1) for i in range(plan.half_x)] for k in range(3)]
    above = [[picked(k, i, 0) for i in range(plan.half_x)] for k in range(3)]

    def of_plane(plane, choices):
        out = jnp.zeros_like(choices[0])
        for k in range(3):
            out = jnp.where(plane == h + (k - 1), choices[k], out)
        return out

    blank = plan.slot_rows - plan.high_row - plan.half_x
    for plane in range(plan.groups):
        main = of_plane(plane, sums)
        beside = []
        for i in range(plan.half_x):
            beside.append((plan.low_row + i, of_plane(plane - 1, [k[i] for k in below])))
            beside.append((plan.high_row + i, of_plane(plane + 1, [k[i] for k in above])))
        for g in range(plan.owners):
            slot = g * plan.groups + plane
            total_out[slot, pl.ds(0, plan.owners), :] = main
            for row, values in beside:
                total_out[slot, pl.ds(row, 1), :] = values[g : g + 1]
            if blank:
                total_out[slot, pl.ds(plan.slot_rows - blank, blank), :] = jnp.zeros(
                    (blank, plan.p), F32
                )


def coarse_solve(packed, planes):
    lane = iota(packed.shape, 1)
    even = lane & 1 == 0
    mass_mean = jnp.where(even, packed, pltpu.roll(packed, 1, 1))
    pot_mean = jnp.where(even, pltpu.roll(packed, planes - 1, 1), packed)

    def neighbour_sum(values):
        return jnp.where(lane >= 2, pltpu.roll(values, 2, 1), 0.0) + jnp.where(
            lane < planes - 2, pltpu.roll(values, planes - 2, 1), 0.0
        )

    coarse_conc = jnp.zeros_like(mass_mean)
    coarse_pot = jnp.zeros_like(pot_mean)
    for _ in range(CSWEEP):
        mass_gap = mass_mean - (
            coarse_conc + coarse_flux * (2.0 * coarse_pot - neighbour_sum(coarse_pot))
        )
        pot_gap = pot_mean - (
            coarse_pot
            - split_slope * coarse_conc
            + coarse_bend * (neighbour_sum(coarse_conc) - 2.0 * coarse_conc)
        )
        coarse_conc = coarse_conc + (relax_coarse / coarse_det) * (
            mass_gap - 2.0 * coarse_flux * pot_gap
        )
        coarse_pot = coarse_pot + (relax_coarse / coarse_det) * (
            pot_gap + (split_slope + 2.0 * coarse_bend) * mass_gap
        )
    return coarse_conc, coarse_pot


def last_kernel(
    plan, conc_ref, pot_ref, mob_ref, mass_ref, pots_ref, x_near_msg, x_far_msg,
    y_near_msg, y_far_msg, x_near_ref, x_far_ref, y_near_ref, y_far_ref, total_ref, spread_ref,
    conc_out, pot_out,
):
    means = total_ref[0]
    for slot in range(1, total_ref.shape[0]):
        means = means + total_ref[slot]
    solved = jnp.concatenate(coarse_solve(means, plan.p), axis=1)
    own = split_dot(spread_ref[...].astype(BF16), solved[: plan.owners], ((1,), (0,)))
    ends = received("gy", y_near_msg, y_far_msg)
    sides = received("gx", x_near_msg, x_far_msg)
    y_corr = []
    for begin in (plan.low_row, plan.high_row):
        rows = [solved[begin + (x >> 1) : begin + (x >> 1) + 1] for x in range(plan.x)]
        y_corr.append(jnp.concatenate(rows, axis=0))
    new_ends = received("gy", y_near_ref, y_far_ref)
    new_sides = received("gx", x_near_ref, x_far_ref)

    def updated(which, ref):
        lanes = slice(which * plan.p, (which + 1) * plan.p)
        corr = own[:, lanes]
        field = ref[...] + corr[: plan.cells].reshape(plan.x, plan.y, plan.p)
        halo = []
        for side, rows in enumerate(new_sides):
            begin = plan.cells + side * plan.y
            halo.append(side_rows(plan, rows, which) + corr[begin : begin + plan.y][None])
        for rows, edge in zip(new_ends, y_corr):
            halo.append((rows[which * plan.x : (which + 1) * plan.x] + edge[:, lanes])[:, None])
        return field, halo

    conc, conc_halo = updated(0, conc_ref)
    pot, pot_halo = updated(1, pot_ref)
    mob_halo = (
        side_rows(plan, sides[0], 2),
        side_rows(plan, sides[1], 2),
        side_columns(plan, ends[0], 2),
        side_columns(plan, ends[1], 2),
    )
    faces, diagonal = faces_of(mob_ref[...], mob_halo)
    excess = excess_of(conc, pot, conc_halo, pot_halo, faces, mass_ref[...], pots_ref[...])
    conc_out[...], pot_out[...] = relax_pair(conc, pot, *excess, diagonal)


def call(kernel, plan, outs, args, far=(), smem=(), scratch=(), limit=VMEM_LIMIT):
    def space(i):
        return pl.ANY if i in far else pltpu.SMEM if i in smem else pltpu.VMEM

    return pl.pallas_call(
        functools.partial(kernel, plan),
        out_shape=[jax.ShapeDtypeStruct(shape, F32) for shape in outs],
        in_specs=[pl.BlockSpec(memory_space=space(i)) for i in range(len(args))],
        out_specs=[pl.BlockSpec(memory_space=pltpu.VMEM)] * len(outs),
        scratch_shapes=list(scratch),
        compiler_params=pltpu.CompilerParams(vmem_limit_bytes=limit),
    )(*args)


def swap(axis, near, far):
    count = lax.axis_size(axis)
    out = []
    for rows, begin in ((near, 0), (far, 1)):
        pairs = [(i, i + 1) for i in range(begin, count - 1, 2)]
        out.append(lax.ppermute(rows, axis, pairs + [(j, i) for i, j in pairs]))
    return out


def swap_all(x_near, x_far, y_near, y_far):
    return *swap("gx", x_near, x_far), *swap("gy", y_near, y_far)


def gather_totals(plan, total, y_near, y_far):
    if plan.slots:
        return lax.all_to_all(total, ("gx", "gy"), split_axis=0, concat_axis=0, tiled=True)
    shape = (plan.groups, 3, plan.owners, plan.p)
    parts = lax.all_gather(lax.psum(total, "gx"), "gy").reshape(shape)
    blank = jnp.zeros((1, plan.owners, plan.p), F32)
    to_below, own, to_above = (parts[:, k] for k in range(3))
    own = own + jnp.concatenate([blank, to_above[:-1]]) + jnp.concatenate([to_below[1:], blank])
    own = jnp.concatenate([blank, own, blank])
    g, h = lax.axis_index("gx"), lax.axis_index("gy")
    rows = [lax.dynamic_index_in_dim(own, h + 1, 0, False)]
    up = lax.rem(h, 2) == 0
    for place, at, msg in (
        (h, plan.half_y - 1, jnp.where(up, y_far, y_near)),
        (h + 2, 0, jnp.where(up, y_near, y_far)),
    ):
        ident = lax.dynamic_index_in_dim(msg, plan.map_row + g, 0, False).astype(jnp.int32)
        ident = jnp.stack([ident[i * plan.half_y + at] for i in range(plan.half_x)])
        rows.append(lax.dynamic_index_in_dim(own, place, 0, False)[ident])
    rows = jnp.concatenate(rows)
    return jnp.pad(rows, ((0, plan.slot_rows - rows.shape[0]), (0, 0)))[None]


def on_device(conc, pot, mass_source, pot_source, mask, kind, table, owner_map):
    plan = Plan(conc.shape, lax.axis_size("gx"), lax.axis_size("gy"))
    block = conc.shape
    messages = call(
        prepare_kernel,
        plan,
        [*[(3 * plan.y, plan.p)] * 2, *[(plan.y_rows, plan.p)] * 2],
        [conc, pot, mask, kind, owner_map, table],
        far=range(6),
        limit=LARGE_LIMIT,
        scratch=(
            pltpu.VMEM(block, F32),
            pltpu.VMEM(block, F32),
            pltpu.VMEM(owner_map.shape, owner_map.dtype),
            pltpu.VMEM(block, mask.dtype),
            pltpu.VMEM(block, kind.dtype),
            pltpu.SMEM(table.shape, table.dtype),
            pltpu.SemaphoreType.DMA((6,)),
        ),
    )
    old = swap_all(*messages)
    near, mask, kind = lax.optimization_barrier((old[0], mask, kind))
    old = (near, *old[1:])
    mob, gather, spread, scale = call(
        local_kernel,
        plan,
        [block, (plan.owners, plan.rows), (plan.rows, plan.owners), (plan.owners, plan.p)],
        [mask, kind, table, owner_map],
        smem=(2,),
    )
    conc, pot, total, *messages = call(
        first_kernel,
        plan,
        [
            block,
            block,
            (plan.slots, plan.slot_rows, plan.p) if plan.slots else (3 * plan.owners, plan.p),
            *[(2 * plan.y, plan.p)] * 2,
            *[(2 * plan.x, plan.p)] * 2,
        ],
        [conc, pot, mob, mass_source, pot_source, gather, scale, owner_map, *old],
    )
    total = gather_totals(plan, total, *old[2:])
    new = swap_all(*messages)
    return tuple(
        call(
            last_kernel,
            plan,
            [block, block],
            [conc, pot, mob, mass_source, pot_source, *old, *new, total, spread],
        )
    )


def solution(mesh):
    grid = P("gx", "gy", None)
    return jax.shard_map(
        on_device,
        mesh=mesh,
        in_specs=(grid,) * 6 + (P(), P(None, "gy")),
        out_specs=(grid, grid),
        check_vma=False,
    )
```

```python
import functools

import jax
import jax.numpy as jnp
from jax import lax
from jax.experimental import pallas as pl
from jax.experimental.pallas import tpu as pltpu
from jax.sharding import PartitionSpec as P

CSWEEP = 3

time_step = 0.25
split_slope = 1.0
interface = 0.5
relax_fine = 0.6
relax_coarse = 0.6
coarse_flux = 0.0625
coarse_bend = 0.125
coarse_det = 1.0 + 2.0 * coarse_flux * (split_slope + 2.0 * coarse_bend)

F32 = jnp.float32
BF16 = jnp.bfloat16
VMEM_LIMIT = 48 * 1024 * 1024
LARGE_LIMIT = 60 * 1024 * 1024


def iota(shape, dim):
    return lax.broadcasted_iota(jnp.int32, shape, dim)


def x_pair(field, low, high):
    return (
        jnp.concatenate([low, field[:-1]], axis=0),
        jnp.concatenate([field[1:], high], axis=0),
    )


def y_pair(field, low, high):
    size = field.shape[1]
    where = iota(field.shape, 1)
    return (
        jnp.where(where == 0, low, pltpu.roll(field, 1, 1)),
        jnp.where(where == size - 1, high, pltpu.roll(field, size - 1, 1)),
    )


def plane_pair(field):
    size = field.shape[2]
    where = iota(field.shape, 2)
    return (
        jnp.where(where == 0, 0.0, pltpu.roll(field, 1, 2)),
        jnp.where(where == size - 1, 0.0, pltpu.roll(field, size - 1, 2)),
    )


def neighbours(field, halo):
    xm, xp, ym, yp = halo
    return (*x_pair(field, xm, xp), *y_pair(field, ym, yp), *plane_pair(field))


def excess_of(conc, pot, conc_beside, pot_beside, faces, diagonal, mass_source, pot_source):
    excess_mass = (mass_source - conc) - diagonal * pot
    for face, other in zip(faces, pot_beside):
        excess_mass = excess_mass + face * other
    beside = conc_beside[0]
    for other in conc_beside[1:]:
        beside = beside + other
    excess_pot = (pot_source - pot) + (split_slope + 6.0 * interface) * conc - interface * beside
    return excess_mass, excess_pot


def scale_from(diagonal):
    return relax_fine / (1.0 + (split_slope + 6.0 * interface) * diagonal)


def relax_pair(conc, pot, excess_mass, excess_pot, diagonal, scale):
    new_conc = conc + (excess_mass - diagonal * excess_pot) * scale
    new_pot = pot + (excess_pot + (split_slope + 6.0 * interface) * excess_mass) * scale
    return new_conc, new_pot


def faces_of(mobility, beside):
    faces = tuple((0.5 * time_step) * (mobility + other) for other in beside)
    diagonal = faces[0]
    for face in faces[1:]:
        diagonal = diagonal + face
    return faces, diagonal


def split_dot(ones, values, contract):
    dims = (contract, ((), ()))
    total = None
    rest = values
    for _ in range(3):
        term = rest.astype(BF16)
        rest = rest - term.astype(F32)
        part = lax.dot_general(ones, term, dims, preferred_element_type=F32)
        total = part if total is None else total + part
    return total


def three_terms(values):
    out = []
    for _ in range(3):
        out.append(values.astype(BF16).astype(F32))
        values = values - out[-1]
    return jnp.concatenate(out, axis=0)


def round_up(value, unit):
    return -(-value // unit) * unit


class Plan:
    def __init__(self, shape, owners, groups):
        self.x, self.y, self.p = shape
        self.owners, self.groups = owners, groups
        self.half_x, self.half_y = self.x // 2, self.y // 2
        self.columns = self.half_x * self.half_y
        self.map_row = round_up(8 * self.x, 8)
        self.y_rows = self.map_row + owners
        self.cells = self.x * self.y
        self.rows = self.cells + 2 * self.y
        self.low_row = owners
        self.high_row = owners + self.half_x
        self.slot_parts = -(-(owners + 2 * self.half_x) // 4)
        slots = owners * groups
        self.slots = slots if slots <= 64 else 0


def side_rows(plan, rows, which):
    return rows[which * plan.y : (which + 1) * plan.y][None]


def side_columns(plan, rows, which):
    return rows[which * plan.x : (which + 1) * plan.x][:, None]


def membership(plan, owner_ref):
    g = lax.axis_index("gx")
    last = plan.owners - 1
    owner = iota((plan.owners, plan.columns), 0)
    shape = (plan.x + 2, plan.y, plan.columns)
    x, y, column = iota(shape, 0), iota(shape, 1), iota(shape, 2)
    half = jnp.where(x < plan.x, x >> 1, jnp.where(x == plan.x, plan.half_x - 1, 0))
    place = column == half * plan.half_y + (y >> 1)
    sides = (
        (x < plan.x, g, True),
        (x == plan.x, jnp.maximum(g - 1, 0), g > 0),
        (x == plan.x + 1, jnp.minimum(g + 1, last), g < last),
    )
    gather, spread = None, None
    for part, row, inside in sides:
        hits = ((owner_ref[pl.ds(row, 1), :] == owner) & inside).astype(F32).astype(BF16)
        where = (place & part).astype(F32).reshape(plan.rows, plan.columns).astype(BF16)
        nt = (((1,), (1,)), ((), ()))
        some = lax.dot_general(hits, where, nt, preferred_element_type=F32)
        gather = some if gather is None else gather + some
        some = lax.dot_general(where, hits, nt, preferred_element_type=F32)
        spread = some if spread is None else spread + some
    return gather, jnp.concatenate([spread] * 3, axis=1)


def scale_of(plan, owners):
    owner = iota((plan.owners, plan.columns), 0).astype(owners.dtype)
    hits = jnp.zeros((plan.owners, plan.columns), F32)
    for g in range(plan.owners):
        hits = hits + (owners[g : g + 1] == owner).astype(F32)
    count = jnp.sum(hits, axis=1, keepdims=True)
    return jnp.broadcast_to(0.125 / jnp.maximum(count, 1.0), (plan.owners, plan.p))


def mobility_of(mask, kind, table):
    values = jnp.zeros(kind.shape, F32)
    for marker, value in enumerate(table):
        values = jnp.where(kind == marker, value, values)
    return mask.astype(F32) * values


def even(axis):
    return lax.rem(lax.axis_index(axis), 2) == 0


def put_x(plan, lows, highs, near, far):
    up = even("gx")
    for which, (low, high) in enumerate(zip(lows, highs)):
        near[pl.ds(which * plan.y, plan.y), :] = jnp.where(up, high, low)
        far[pl.ds(which * plan.y, plan.y), :] = jnp.where(up, low, high)


def received(axis, near_ref, far_ref):
    up = even(axis)
    near, far = near_ref[...], far_ref[...]
    return jnp.where(up, far, near), jnp.where(up, near, far)


def prepare_kernel(plan, *refs):
    hbm, refs = refs[:8], refs[8:]
    x_near_ref, x_far_ref, y_near_ref, y_far_ref = refs[:4]
    x_refs, y_refs, (owner_ref, table_ref, sems) = refs[4:8], refs[8:14], refs[14:]
    copies = []

    def start(source, target):
        copies.append(pltpu.make_async_copy(source, target, sems.at[len(copies)]))
        copies[-1].start()

    start(hbm[7], table_ref)
    start(hbm[6], owner_ref)
    for source, target in zip(hbm[:4], x_refs):
        start(source.at[0], target.at[0])
        start(source.at[plan.x - 1], target.at[1])
    for source, target in zip(hbm[:6], y_refs):
        start(source.at[:, pl.ds(0, 8)], target.at[0])
        start(source.at[:, pl.ds(plan.y - 8, 8)], target.at[1])
    for copy in copies:
        copy.wait()
    table = [table_ref[marker] for marker in range(table_ref.shape[0])]
    conc, pot, mask, kind = (ref[...] for ref in x_refs)
    fields = (conc, pot, mobility_of(mask, kind, table))
    put_x(plan, [f[0] for f in fields], [f[1] for f in fields], x_near_ref, x_far_ref)
    conc, pot, mask, kind, mass, pots = (ref[...] for ref in y_refs)
    fields = (conc, pot, mobility_of(mask, kind, table))
    up = even("gy")
    rows = [(field, at) for at in range(2) for field in fields] + [(mass, 0), (pots, 0)]
    for which, (field, at) in enumerate(rows):
        for x in range(plan.x):
            low, high = field[0, x, at : at + 1], field[1, x, 7 - at : 8 - at]
            y_near_ref[pl.ds(which * plan.x + x, 1), :] = jnp.where(up, high, low)
            y_far_ref[pl.ds(which * plan.x + x, 1), :] = jnp.where(up, low, high)
    used = 8 * plan.x
    for ref in (y_near_ref, y_far_ref):
        ref[pl.ds(used, plan.y_rows - used), :] = jnp.zeros((plan.y_rows - used, plan.p), F32)
        ref[pl.ds(plan.map_row, plan.owners), pl.ds(0, plan.columns)] = owner_ref[...].astype(F32)


def local_kernel(
    plan, mask_ref, class_ref, table_ref, owner_ref, mob_ref, gather_ref, spread_ref, scale_ref
):
    table = [table_ref[marker] for marker in range(table_ref.shape[0])]
    mob_ref[...] = mobility_of(mask_ref[...], class_ref[...], table)
    gather_ref[...], spread_ref[...] = membership(plan, owner_ref)
    scale_ref[...] = scale_of(plan, owner_ref[...])


def first_kernel(
    plan, conc_ref, pot_ref, mob_ref, mass_ref, pots_ref, gather_ref, scale_ref, owner_ref,
    x_near_ref, x_far_ref, y_near_ref, y_far_ref,
    conc_out, pot_out, total_out, raw_out, x_near_out, x_far_out,
):
    sides = received("gx", x_near_ref, x_far_ref)
    ends = received("gy", y_near_ref, y_far_ref)

    def halo(which):
        return tuple(side_rows(plan, rows, which) for rows in sides) + tuple(
            side_columns(plan, rows, which) for rows in ends
        )

    mobility, mob_halo = mob_ref[...], halo(2)
    faces, diagonal = faces_of(mobility, neighbours(mobility, mob_halo))
    mass_source, pot_source = mass_ref[...], pots_ref[...]
    conc, pot = conc_ref[...], pot_ref[...]
    for at, field in enumerate((conc, pot)):
        for x in range(plan.x):
            raw_out[pl.ds(2 * at * plan.x + x, 1), :] = field[x, 0:1]
            raw_out[pl.ds((2 * at + 1) * plan.x + x, 1), :] = field[x, plan.y - 1 : plan.y]
    excess = excess_of(
        conc, pot, neighbours(conc, halo(0)), neighbours(pot, halo(1)), faces, diagonal,
        mass_source, pot_source,
    )
    conc, pot = relax_pair(conc, pot, *excess, diagonal, scale_from(diagonal))
    conc_out[...] = conc
    pot_out[...] = pot
    put_x(plan, (conc[0], pot[0]), (conc[plan.x - 1], pot[plan.x - 1]), x_near_out, x_far_out)
    up = even("gx")
    base = 2 * plan.y
    for which in range(3):
        for end, rows in enumerate(ends):
            low = rows[which * plan.x : which * plan.x + 1]
            high = rows[(which + 1) * plan.x - 1 : (which + 1) * plan.x]
            x_near_out[pl.ds(base + 2 * which + end, 1), :] = jnp.where(up, high, low)
            x_far_out[pl.ds(base + 2 * which + end, 1), :] = jnp.where(up, low, high)
    for ref in (x_near_out, x_far_out):
        ref[pl.ds(base + 6, 2), :] = jnp.zeros((2, plan.p), F32)

    nothing = tuple(jnp.zeros_like(part) for part in mob_halo)
    own_mass, own_pot = excess_of(
        conc, pot, neighbours(conc, nothing), neighbours(pot, nothing), faces, diagonal,
        mass_source, pot_source,
    )
    give_mass = [own_mass.reshape(plan.cells, plan.p)]
    give_pot = [own_pot.reshape(plan.cells, plan.p)]
    for x, side in ((0, 0), (plan.x - 1, 1)):
        face = 0.5 * (mobility[x] + mob_halo[side][0])
        give_mass.append(time_step * face * pot[x])
        give_pot.append(-interface * conc[x])
    give = jnp.concatenate(
        [jnp.concatenate(give_mass, axis=0), jnp.concatenate(give_pot, axis=0)], axis=1
    )

    def packed(both):
        mass, other = both[:, : plan.p], both[:, plan.p :]
        first = iota(mass.shape, 1) & 1 == 0
        return jnp.where(
            first, mass + pltpu.roll(mass, plan.p - 1, 1), other + pltpu.roll(other, 1, 1)
        )

    h = lax.axis_index("gy")
    inside = (h > 0, None, h < plan.groups - 1)
    maps = [rows[plan.map_row : plan.map_row + plan.owners, : plan.columns] for rows in ends]
    maps.insert(1, owner_ref[...].astype(F32))
    owner = iota((plan.owners, 1), 0)
    is_mine = owner == lax.axis_index("gx")

    def column(place, i, at):
        b = i * plan.half_y + at
        return maps[place][:, b : b + 1]

    sums = [None, packed(split_dot(gather_ref[...].astype(BF16), give, ((1,), (0,)))), None]
    sums[1] = sums[1] * scale_ref[...]
    for place, y, at, side in ((0, 0, plan.half_y - 1, 2), (2, plan.y - 1, 0, 3)):
        edge_mob, edge_pot, edge_conc = (
            jnp.concatenate([field[x, y : y + 1] for x in range(plan.x)], axis=0)
            for field in (mobility, pot, conc)
        )
        face = 0.5 * (edge_mob + mob_halo[side][:, 0])
        both = jnp.concatenate([time_step * face * edge_pot, -interface * edge_conc], axis=1)
        part = jnp.zeros((plan.owners, 2 * plan.p), F32)
        for i in range(plan.half_x):
            ident = jnp.sum(jnp.where(is_mine, column(place, i, at), 0.0), axis=0, keepdims=True)
            pair = both[2 * i : 2 * i + 1] + both[2 * i + 1 : 2 * i + 2]
            part = part + jnp.where((owner.astype(F32) == ident) & inside[place], pair, 0.0)
        sums[place] = packed(part) * scale_of(plan, maps[place])

    if not plan.slots:
        total_out[...] = jnp.concatenate(sums, axis=0)
        return

    def picked(place, i, at):
        ident = jnp.broadcast_to(column(place, i, at), (plan.owners, plan.p))
        out = jnp.zeros((plan.owners, plan.p), F32)
        for o in range(plan.owners):
            out = jnp.where(ident == float(o), sums[place][o : o + 1], out)
        return out

    below = [[picked(k, i, plan.half_y - 1) for i in range(plan.half_x)] for k in range(3)]
    above = [[picked(k, i, 0) for i in range(plan.half_x)] for k in range(3)]

    def of_plane(plane, choices):
        out = jnp.zeros_like(choices[0])
        for k in range(3):
            out = jnp.where(plane == h + (k - 1), choices[k], out)
        return out

    for plane in range(plan.groups):
        main = of_plane(plane, sums)
        beside = []
        for i in range(plan.half_x):
            beside.append((plan.low_row + i, of_plane(plane - 1, [k[i] for k in below])))
            beside.append((plan.high_row + i, of_plane(plane + 1, [k[i] for k in above])))
        beside += [(row, jnp.zeros_like(main)) for row in range(plan.high_row + plan.half_x, 4 * plan.slot_parts)]
        for g in range(plan.owners):
            slot = g * plan.groups + plane
            for part in range(plan.owners // 4):
                total_out[slot, part] = main[4 * part : 4 * part + 4]
            for row, values in beside:
                total_out[slot, row // 4, pl.ds(row % 4, 1), :] = values[g : g + 1]


def coarse_solve(packed, planes):
    lane = iota(packed.shape, 1)
    even = lane & 1 == 0
    mass_mean = jnp.where(even, packed, pltpu.roll(packed, 1, 1))
    pot_mean = jnp.where(even, pltpu.roll(packed, planes - 1, 1), packed)

    def neighbour_sum(values):
        return jnp.where(lane >= 2, pltpu.roll(values, 2, 1), 0.0) + jnp.where(
            lane < planes - 2, pltpu.roll(values, planes - 2, 1), 0.0
        )

    coarse_conc = jnp.zeros_like(mass_mean)
    coarse_pot = jnp.zeros_like(pot_mean)
    for _ in range(CSWEEP):
        mass_gap = mass_mean - (
            coarse_conc + coarse_flux * (2.0 * coarse_pot - neighbour_sum(coarse_pot))
        )
        pot_gap = pot_mean - (
            coarse_pot
            - split_slope * coarse_conc
            + coarse_bend * (neighbour_sum(coarse_conc) - 2.0 * coarse_conc)
        )
        coarse_conc = coarse_conc + (relax_coarse / coarse_det) * (
            mass_gap - 2.0 * coarse_flux * pot_gap
        )
        coarse_pot = coarse_pot + (relax_coarse / coarse_det) * (
            pot_gap + (split_slope + 2.0 * coarse_bend) * mass_gap
        )
    return coarse_conc, coarse_pot


def beside_kernel(
    plan, mob_ref, raw_ref, x_near_msg, x_far_msg, y_near_msg, y_far_msg, x_near_ref, x_far_ref,
    faces_out, diagonal_out, scale_out, ends_out,
):
    mobility = mob_ref[...]
    sides = received("gx", x_near_msg, x_far_msg)
    ends = received("gy", y_near_msg, y_far_msg)
    halo = tuple(side_rows(plan, rows, 2) for rows in sides) + tuple(
        side_columns(plan, rows, 2) for rows in ends
    )
    faces, diagonal = faces_of(mobility, neighbours(mobility, halo))
    for i, face in enumerate(faces):
        faces_out[i] = face
    diagonal_out[...] = diagonal
    scale_out[...] = scale_from(diagonal)

    corners = received("gx", x_near_ref, x_far_ref)
    h = lax.axis_index("gy")
    inside = (h > 0, h < plan.groups - 1)
    own_mob = [
        jnp.concatenate([mobility[x, y : y + 1] for x in range(plan.x)], axis=0)
        for y in (0, plan.y - 1)
    ]
    for end, rows in enumerate(ends):

        def row(which):
            return rows[which * plan.x : (which + 1) * plan.x]

        def beside(which, own):
            here = row(which)
            at = 2 * plan.y + 2 * which + end
            wide = jnp.concatenate([corners[0][at : at + 1], here, corners[1][at : at + 1]], axis=0)
            return (
                wide[: plan.x], wide[2:], own, row(which + 3),
                *(part[0] for part in plane_pair(here[None])),
            )

        raw = [
            raw_ref[pl.ds((2 * which + end) * plan.x, plan.x), :] for which in range(2)
        ]
        faces, diagonal = faces_of(row(2), beside(2, own_mob[end]))
        excess = excess_of(
            row(0), row(1), beside(0, raw[0]), beside(1, raw[1]), faces, diagonal, row(6), row(7)
        )
        new = relax_pair(row(0), row(1), *excess, diagonal, scale_from(diagonal))
        for which, values in enumerate(new):
            ends_out[pl.ds((2 * which + end) * plan.x, plan.x), :] = jnp.where(
                inside[end], values, 0.0
            )


def last_kernel(
    plan, conc_ref, pot_ref, mass_ref, pots_ref, faces_ref, diagonal_ref, scale_ref,
    x_near_ref, x_far_ref, ends_ref, spread_ref, total_ref,
    conc_hbm, pot_hbm, conc_out, pot_out, sems,
):
    parts = []
    for part in range(plan.slot_parts):
        mean = total_ref[0, part]
        for slot in range(1, total_ref.shape[0]):
            mean = mean + total_ref[slot, part]
        parts.append(mean)
    solved = jnp.concatenate(
        coarse_solve(jnp.concatenate(parts, axis=0), plan.p), axis=1
    )
    own = lax.dot_general(
        spread_ref[...].astype(BF16),
        three_terms(solved[: plan.owners]).astype(BF16),
        (((1,), (0,)), ((), ())),
        preferred_element_type=F32,
    )
    sides = received("gx", x_near_ref, x_far_ref)

    def updated(which, ref):
        lanes = slice(which * plan.p, (which + 1) * plan.p)
        corr = own[:, lanes]
        slabs = [side_rows(plan, sides[0], which)]
        slabs += [ref[pl.ds(x, 1)] for x in range(plan.x)]
        slabs.append(side_rows(plan, sides[1], which))
        order = [plan.x, *range(plan.x), plan.x + 1]
        slabs = [
            slab + corr[x * plan.y : (x + 1) * plan.y][None] for slab, x in zip(slabs, order)
        ]
        ends = []
        for end, begin in enumerate((plan.low_row, plan.high_row)):
            rows = ends_ref[pl.ds((2 * which + end) * plan.x, plan.x), :]
            ends.append([
                (rows[x : x + 1] + solved[begin + (x >> 1) : begin + (x >> 1) + 1, lanes])[None]
                for x in range(plan.x)
            ])
        return slabs, ends

    conc, conc_ends = updated(0, conc_ref)
    pot, pot_ends = updated(1, pot_ref)

    def beside(slabs, ends, x):
        here = slabs[x + 1]
        return (
            slabs[x], slabs[x + 2], *y_pair(here, ends[0][x], ends[1][x]), *plane_pair(here)
        )

    copies = []
    for x in range(plan.x):
        one = pl.ds(x, 1)
        diagonal = diagonal_ref[one]
        excess = excess_of(
            conc[x + 1], pot[x + 1], beside(conc, conc_ends, x), beside(pot, pot_ends, x),
            [faces_ref[i, one] for i in range(6)], diagonal, mass_ref[one], pots_ref[one],
        )
        conc_out[one], pot_out[one] = relax_pair(
            conc[x + 1], pot[x + 1], *excess, diagonal, scale_ref[one]
        )
        for source, target in ((conc_out, conc_hbm), (pot_out, pot_hbm)):
            copies.append(
                pltpu.make_async_copy(source.at[one], target.at[one], sems.at[len(copies)])
            )
            copies[-1].start()
    for copy in copies:
        copy.wait()


def call(kernel, plan, outs, args, far=(), smem=(), scratch=(), limit=VMEM_LIMIT, out_far=False):
    def space(i):
        return pl.ANY if i in far else pltpu.SMEM if i in smem else pltpu.VMEM

    return pl.pallas_call(
        functools.partial(kernel, plan),
        out_shape=[jax.ShapeDtypeStruct(shape, F32) for shape in outs],
        in_specs=[pl.BlockSpec(memory_space=space(i)) for i in range(len(args))],
        out_specs=[pl.BlockSpec(memory_space=pl.ANY if out_far else pltpu.VMEM)] * len(outs),
        scratch_shapes=list(scratch),
        compiler_params=pltpu.CompilerParams(vmem_limit_bytes=limit),
    )(*args)


def swap(axis, near, far):
    count = lax.axis_size(axis)
    out = []
    for rows, begin in ((near, 0), (far, 1)):
        pairs = [(i, i + 1) for i in range(begin, count - 1, 2)]
        out.append(lax.ppermute(rows, axis, pairs + [(j, i) for i, j in pairs]))
    return out


def gather_totals(plan, total, y_near, y_far):
    if plan.slots:
        return lax.all_to_all(total, ("gx", "gy"), split_axis=0, concat_axis=0, tiled=True)
    shape = (plan.groups, 3, plan.owners, plan.p)
    parts = lax.all_gather(lax.psum(total, "gx"), "gy").reshape(shape)
    blank = jnp.zeros((1, plan.owners, plan.p), F32)
    to_below, own, to_above = (parts[:, k] for k in range(3))
    own = own + jnp.concatenate([blank, to_above[:-1]]) + jnp.concatenate([to_below[1:], blank])
    own = jnp.concatenate([blank, own, blank])
    g, h = lax.axis_index("gx"), lax.axis_index("gy")
    rows = [lax.dynamic_index_in_dim(own, h + 1, 0, False)]
    up = lax.rem(h, 2) == 0
    for place, at, msg in (
        (h, plan.half_y - 1, jnp.where(up, y_far, y_near)),
        (h + 2, 0, jnp.where(up, y_near, y_far)),
    ):
        ident = lax.dynamic_index_in_dim(msg, plan.map_row + g, 0, False).astype(jnp.int32)
        ident = jnp.stack([ident[i * plan.half_y + at] for i in range(plan.half_x)])
        rows.append(lax.dynamic_index_in_dim(own, place, 0, False)[ident])
    rows = jnp.concatenate(rows)
    rows = jnp.pad(rows, ((0, 4 * plan.slot_parts - rows.shape[0]), (0, 0)))
    return rows.reshape(1, plan.slot_parts, 4, plan.p)


def on_device(conc, pot, mass_source, pot_source, mask, kind, table, owner_map):
    plan = Plan(conc.shape, lax.axis_size("gx"), lax.axis_size("gy"))
    block = conc.shape
    fields = [conc, pot, mask, kind, mass_source, pot_source]
    messages = call(
        prepare_kernel,
        plan,
        [*[(3 * plan.y, plan.p)] * 2, *[(plan.y_rows, plan.p)] * 2],
        [*fields, owner_map, table],
        far=range(8),
        limit=LARGE_LIMIT,
        scratch=(
            *[pltpu.VMEM((2, plan.y, plan.p), field.dtype) for field in fields[:4]],
            *[pltpu.VMEM((2, plan.x, 8, plan.p), field.dtype) for field in fields],
            pltpu.VMEM(owner_map.shape, owner_map.dtype),
            pltpu.SMEM(table.shape, table.dtype),
            pltpu.SemaphoreType.DMA((22,)),
        ),
    )
    old = [*swap("gx", *messages[:2]), *swap("gy", *messages[2:])]
    old[0], mask, kind = lax.optimization_barrier((old[0], mask, kind))
    mob, gather, spread, scale = call(
        local_kernel,
        plan,
        [block, (plan.owners, plan.rows), (plan.rows, 3 * plan.owners), (plan.owners, plan.p)],
        [mask, kind, table, owner_map],
        smem=(2,),
    )
    slots = (plan.slots, plan.slot_parts, 4, plan.p)
    conc, pot, total, raw, *messages = call(
        first_kernel,
        plan,
        [
            block,
            block,
            slots if plan.slots else (3 * plan.owners, plan.p),
            (4 * plan.x, plan.p),
            *[(2 * plan.y + 8, plan.p)] * 2,
        ],
        [conc, pot, mob, mass_source, pot_source, gather, scale, owner_map, *old],
    )
    total = gather_totals(plan, total, *old[2:])
    new = swap("gx", *messages)
    faces, diagonal, scale, ends = call(
        beside_kernel,
        plan,
        [(6, *block), block, block, (4 * plan.x, plan.p)],
        [mob, raw, *old, *new],
    )
    return tuple(
        call(
            last_kernel,
            plan,
            [block, block],
            [conc, pot, mass_source, pot_source, faces, diagonal, scale, *new, ends, spread, total],
            out_far=True,
            scratch=(
                pltpu.VMEM(block, F32),
                pltpu.VMEM(block, F32),
                pltpu.SemaphoreType.DMA((2 * plan.x,)),
            ),
        )
    )


def solution(mesh):
    grid = P("gx", "gy", None)
    return jax.shard_map(
        on_device,
        mesh=mesh,
        in_specs=(grid,) * 6 + (P(), P(None, "gy")),
        out_specs=(grid, grid),
        check_vma=False,
    )
```

```python
import functools

import jax
import jax.numpy as jnp
from jax import lax
from jax.experimental import pallas as pl
from jax.experimental.pallas import tpu as pltpu
from jax.sharding import PartitionSpec as P

CSWEEP = 3

time_step = 0.25
split_slope = 1.0
interface = 0.5
relax_fine = 0.6
relax_coarse = 0.6
coarse_flux = 0.0625
coarse_bend = 0.125
coarse_det = 1.0 + 2.0 * coarse_flux * (split_slope + 2.0 * coarse_bend)

F32 = jnp.float32
BF16 = jnp.bfloat16
VMEM_LIMIT = 48 * 1024 * 1024
LARGE_LIMIT = 60 * 1024 * 1024


def iota(shape, dim):
    return lax.broadcasted_iota(jnp.int32, shape, dim)


def x_pair(field, low, high):
    return (
        jnp.concatenate([low, field[:-1]], axis=0),
        jnp.concatenate([field[1:], high], axis=0),
    )


def y_pair(field, low, high):
    size = field.shape[1]
    where = iota(field.shape, 1)
    return (
        jnp.where(where == 0, low, pltpu.roll(field, 1, 1)),
        jnp.where(where == size - 1, high, pltpu.roll(field, size - 1, 1)),
    )


def plane_pair(field):
    size = field.shape[2]
    where = iota(field.shape, 2)
    return (
        jnp.where(where == 0, 0.0, pltpu.roll(field, 1, 2)),
        jnp.where(where == size - 1, 0.0, pltpu.roll(field, size - 1, 2)),
    )


def neighbours(field, halo):
    xm, xp, ym, yp = halo
    return (*x_pair(field, xm, xp), *y_pair(field, ym, yp), *plane_pair(field))


def excess_of(conc, pot, conc_beside, pot_beside, faces, diagonal, mass_source, pot_source):
    excess_mass = (mass_source - conc) - diagonal * pot
    for face, other in zip(faces, pot_beside):
        excess_mass = excess_mass + face * other
    beside = conc_beside[0]
    for other in conc_beside[1:]:
        beside = beside + other
    excess_pot = (pot_source - pot) + (split_slope + 6.0 * interface) * conc - interface * beside
    return excess_mass, excess_pot


def scale_from(diagonal):
    return relax_fine / (1.0 + (split_slope + 6.0 * interface) * diagonal)


def relax_pair(conc, pot, excess_mass, excess_pot, diagonal, scale):
    new_conc = conc + (excess_mass - diagonal * excess_pot) * scale
    new_pot = pot + (excess_pot + (split_slope + 6.0 * interface) * excess_mass) * scale
    return new_conc, new_pot


def faces_of(mobility, beside):
    faces = tuple((0.5 * time_step) * (mobility + other) for other in beside)
    diagonal = faces[0]
    for face in faces[1:]:
        diagonal = diagonal + face
    return faces, diagonal


def split_dot(ones, values, contract):
    dims = (contract, ((), ()))
    total = None
    rest = values
    for _ in range(3):
        term = rest.astype(BF16)
        rest = rest - term.astype(F32)
        part = lax.dot_general(ones, term, dims, preferred_element_type=F32)
        total = part if total is None else total + part
    return total


def three_terms(values):
    out = []
    for _ in range(3):
        out.append(values.astype(BF16).astype(F32))
        values = values - out[-1]
    return jnp.concatenate(out, axis=0)


def round_up(value, unit):
    return -(-value // unit) * unit


class Plan:
    def __init__(self, shape, owners, groups):
        self.x, self.y, self.p = shape
        self.owners, self.groups = owners, groups
        self.half_x, self.half_y = self.x // 2, self.y // 2
        self.columns = self.half_x * self.half_y
        self.map_row = round_up(8 * self.x, 8)
        self.y_rows = self.map_row + owners
        self.cells = self.x * self.y
        self.rows = (self.half_x + 2) * self.y
        self.sums_row = 2 * self.y + 8
        self.low_row = owners
        self.high_row = owners + self.half_x
        self.slot_parts = -(-(owners + 2 * self.half_x) // 4)
        slots = owners * groups // 2
        self.slots = slots if slots <= 32 and 9 * owners <= self.p and owners % 2 == 0 else 0


def side_rows(plan, rows, which):
    return rows[which * plan.y : (which + 1) * plan.y][None]


def side_columns(plan, rows, which):
    return rows[which * plan.x : (which + 1) * plan.x][:, None]


def membership(plan, owner_ref):
    g = lax.axis_index("gx")
    last = plan.owners - 1
    owner = iota((plan.owners, plan.columns), 0)
    low, high = plan.half_x, plan.half_x + 1
    shape = (plan.half_x + 2, plan.y, plan.columns)
    x, y, column = iota(shape, 0), iota(shape, 1), iota(shape, 2)
    half = jnp.where(x < low, x, jnp.where(x == low, plan.half_x - 1, 0))
    place = column == half * plan.half_y + (y >> 1)
    sides = (
        (x < low, g, True),
        (x == low, jnp.maximum(g - 1, 0), g > 0),
        (x == high, jnp.minimum(g + 1, last), g < last),
    )
    gather, spread = None, None
    for part, row, inside in sides:
        hits = ((owner_ref[pl.ds(row, 1), :] == owner) & inside).astype(F32).astype(BF16)
        where = (place & part).astype(F32).reshape(plan.rows, plan.columns).astype(BF16)
        nt = (((1,), (1,)), ((), ()))
        some = lax.dot_general(hits, where, nt, preferred_element_type=F32)
        gather = some if gather is None else gather + some
        some = lax.dot_general(where, hits, nt, preferred_element_type=F32)
        spread = some if spread is None else spread + some
    return gather, jnp.concatenate([spread] * 3, axis=1)


def scale_of(plan, owners):
    owner = iota((plan.owners, plan.columns), 0).astype(owners.dtype)
    hits = jnp.zeros((plan.owners, plan.columns), F32)
    for g in range(plan.owners):
        hits = hits + (owners[g : g + 1] == owner).astype(F32)
    count = jnp.sum(hits, axis=1, keepdims=True)
    return jnp.broadcast_to(0.125 / jnp.maximum(count, 1.0), (plan.owners, plan.p))


def mobility_of(mask, kind, table):
    values = jnp.zeros(kind.shape, F32)
    for marker, value in enumerate(table):
        values = jnp.where(kind == marker, value, values)
    return mask.astype(F32) * values


def even(axis):
    return lax.rem(lax.axis_index(axis), 2) == 0


def put_x(plan, lows, highs, near, far):
    up = even("gx")
    for which, (low, high) in enumerate(zip(lows, highs)):
        near[pl.ds(which * plan.y, plan.y), :] = jnp.where(up, high, low)
        far[pl.ds(which * plan.y, plan.y), :] = jnp.where(up, low, high)


def received(axis, near_ref, far_ref):
    up = even(axis)
    rows = pl.ds(0, min(near_ref.shape[0], far_ref.shape[0]))
    near, far = near_ref[rows, :], far_ref[rows, :]
    return jnp.where(up, far, near), jnp.where(up, near, far)


def prepare_kernel(plan, *refs):
    hbm, refs = refs[:8], refs[8:]
    x_near_ref, x_far_ref, y_near_ref, y_far_ref = refs[:4]
    x_refs, y_refs, (owner_ref, table_ref, sems) = refs[4:8], refs[8:14], refs[14:]
    copies = []

    def start(source, target):
        copies.append(pltpu.make_async_copy(source, target, sems.at[len(copies)]))
        copies[-1].start()

    start(hbm[7], table_ref)
    start(hbm[6], owner_ref)
    for source, target in zip(hbm[:4], x_refs):
        start(source.at[0], target.at[0])
        start(source.at[plan.x - 1], target.at[1])
    for source, target in zip(hbm[:6], y_refs):
        start(source.at[:, pl.ds(0, 8)], target.at[0])
        start(source.at[:, pl.ds(plan.y - 8, 8)], target.at[1])
    for copy in copies:
        copy.wait()
    table = [table_ref[marker] for marker in range(table_ref.shape[0])]
    conc, pot, mask, kind = (ref[...] for ref in x_refs)
    fields = (conc, pot, mobility_of(mask, kind, table))
    put_x(plan, [f[0] for f in fields], [f[1] for f in fields], x_near_ref, x_far_ref)
    conc, pot, mask, kind, mass, pots = (ref[...] for ref in y_refs)
    fields = (conc, pot, mobility_of(mask, kind, table))
    up = even("gy")
    rows = [(field, at) for at in range(2) for field in fields] + [(mass, 0), (pots, 0)]
    for which, (field, at) in enumerate(rows):
        for x in range(plan.x):
            low, high = field[0, x, at : at + 1], field[1, x, 7 - at : 8 - at]
            y_near_ref[pl.ds(which * plan.x + x, 1), :] = jnp.where(up, high, low)
            y_far_ref[pl.ds(which * plan.x + x, 1), :] = jnp.where(up, low, high)
    used = 8 * plan.x
    for ref in (y_near_ref, y_far_ref):
        ref[pl.ds(used, plan.y_rows - used), :] = jnp.zeros((plan.y_rows - used, plan.p), F32)
        ref[pl.ds(plan.map_row, plan.owners), pl.ds(0, plan.columns)] = owner_ref[...].astype(F32)


def local_kernel(
    plan, mask_ref, class_ref, table_ref, owner_ref, mob_ref, gather_ref, spread_ref, scale_ref
):
    table = [table_ref[marker] for marker in range(table_ref.shape[0])]
    mob_ref[...] = mobility_of(mask_ref[...], class_ref[...], table)
    gather_ref[...], spread_ref[...] = membership(plan, owner_ref)
    scale_ref[...] = scale_of(plan, owner_ref[...])


def first_kernel(
    plan, conc_ref, pot_ref, mob_ref, mass_ref, pots_ref, gather_ref, scale_ref, owner_ref,
    x_near_ref, x_far_ref, y_near_ref, y_far_ref,
    conc_out, pot_out, raw_out, x_near_out, x_far_out,
):
    sides = received("gx", x_near_ref, x_far_ref)
    ends = received("gy", y_near_ref, y_far_ref)

    def halo(which):
        return tuple(side_rows(plan, rows, which) for rows in sides) + tuple(
            side_columns(plan, rows, which) for rows in ends
        )

    mobility, mob_halo = mob_ref[...], halo(2)
    faces, diagonal = faces_of(mobility, neighbours(mobility, mob_halo))
    mass_source, pot_source = mass_ref[...], pots_ref[...]
    conc, pot = conc_ref[...], pot_ref[...]
    for at, field in enumerate((conc, pot)):
        for x in range(plan.x):
            raw_out[pl.ds(2 * at * plan.x + x, 1), :] = field[x, 0:1]
            raw_out[pl.ds((2 * at + 1) * plan.x + x, 1), :] = field[x, plan.y - 1 : plan.y]
    excess = excess_of(
        conc, pot, neighbours(conc, halo(0)), neighbours(pot, halo(1)), faces, diagonal,
        mass_source, pot_source,
    )
    conc, pot = relax_pair(conc, pot, *excess, diagonal, scale_from(diagonal))
    conc_out[...] = conc
    pot_out[...] = pot
    put_x(plan, (conc[0], pot[0]), (conc[plan.x - 1], pot[plan.x - 1]), x_near_out, x_far_out)
    up = even("gx")
    base = 2 * plan.y
    for which in range(3):
        for end, rows in enumerate(ends):
            low = rows[which * plan.x : which * plan.x + 1]
            high = rows[(which + 1) * plan.x - 1 : (which + 1) * plan.x]
            x_near_out[pl.ds(base + 2 * which + end, 1), :] = jnp.where(up, high, low)
            x_far_out[pl.ds(base + 2 * which + end, 1), :] = jnp.where(up, low, high)
    for ref in (x_near_out, x_far_out):
        ref[pl.ds(base + 6, 2), :] = jnp.zeros((2, plan.p), F32)

    nothing = tuple(jnp.zeros_like(part) for part in mob_halo)
    own_mass, own_pot = excess_of(
        conc, pot, neighbours(conc, nothing), neighbours(pot, nothing), faces, diagonal,
        mass_source, pot_source,
    )
    give_mass, give_pot = (
        [field[x] + field[x + 1] for x in range(0, plan.x, 2)] for field in (own_mass, own_pot)
    )
    for x, side in ((0, 0), (plan.x - 1, 1)):
        face = 0.5 * (mobility[x] + mob_halo[side][0])
        give_mass.append(time_step * face * pot[x])
        give_pot.append(-interface * conc[x])

    def packed(mass, other):
        first = iota(mass.shape, 1) & 1 == 0
        return jnp.where(
            first, mass + pltpu.roll(mass, plan.p - 1, 1), other + pltpu.roll(other, 1, 1)
        )

    give = packed(jnp.concatenate(give_mass, axis=0), jnp.concatenate(give_pot, axis=0))
    h = lax.axis_index("gy")
    inside = (h > 0, None, h < plan.groups - 1)
    maps = [rows[plan.map_row : plan.map_row + plan.owners, : plan.columns] for rows in ends]
    maps.insert(1, owner_ref[...].astype(F32))
    owner = iota((plan.owners, 1), 0)
    is_mine = owner == lax.axis_index("gx")

    sums = [None, split_dot(gather_ref[...].astype(BF16), give, ((1,), (0,))), None]
    sums[1] = sums[1] * scale_ref[...]
    for place, y, at, side in ((0, 0, plan.half_y - 1, 2), (2, plan.y - 1, 0, 3)):
        edge_mob, edge_pot, edge_conc = (
            jnp.concatenate([field[x, y : y + 1] for x in range(plan.x)], axis=0)
            for field in (mobility, pot, conc)
        )
        face = 0.5 * (edge_mob + mob_halo[side][:, 0])
        both = packed(time_step * face * edge_pot, -interface * edge_conc)
        part = jnp.zeros((plan.owners, plan.p), F32)
        for i in range(plan.half_x):
            column = owner_column(plan, maps[place], i, at)
            ident = jnp.sum(jnp.where(is_mine, column, 0.0), axis=0, keepdims=True)
            pair = both[2 * i : 2 * i + 1] + both[2 * i + 1 : 2 * i + 2]
            part = part + jnp.where((owner.astype(F32) == ident) & inside[place], pair, 0.0)
        sums[place] = part * scale_of(plan, maps[place])
    x_near_out[pl.ds(plan.sums_row, 3 * plan.owners), :] = jnp.concatenate(sums, axis=0)


def owner_column(plan, owners, i, at):
    b = i * plan.half_y + at
    return owners[:, b : b + 1]


def pick_kernel(plan, owner_ref, y_near_ref, y_far_ref, pick_out):
    h = lax.axis_index("gy")
    maps = [
        rows[plan.map_row : plan.map_row + plan.owners, : plan.columns]
        for rows in received("gy", y_near_ref, y_far_ref)
    ]
    maps.insert(1, owner_ref[...].astype(F32))
    inside = (h > 0, True, h < plan.groups - 1)
    shape = (plan.owners, plan.p)
    lane, row = iota(shape, 1), iota(shape, 0)
    sums = []
    for k in range(3):
        first = k * plan.owners + row
        hits = (lane == first) | (lane == first + 3 * plan.owners) | (lane == first + 6 * plan.owners)
        sums.append(jnp.where(hits & inside[k], 1.0, 0.0))

    def picked(place, i, at):
        ident = jnp.broadcast_to(owner_column(plan, maps[place], i, at), shape)
        out = jnp.zeros(shape, F32)
        for o in range(plan.owners):
            out = jnp.where(ident == float(o), sums[place][o : o + 1], out)
        return out

    below = [[picked(k, i, plan.half_y - 1) for i in range(plan.half_x)] for k in range(3)]
    above = [[picked(k, i, 0) for i in range(plan.half_x)] for k in range(3)]

    def of_plane(plane, choices):
        out = jnp.zeros(shape, F32)
        for k in range(3):
            out = jnp.where(plane == h + (k - 1), choices[k], out)
        return out

    up = even("gx")
    size = 4 * plan.slot_parts
    for plane in range(plan.groups):
        main = of_plane(plane, sums)
        beside = []
        for i in range(plan.half_x):
            beside.append((plan.low_row + i, of_plane(plane - 1, [k[i] for k in below])))
            beside.append((plan.high_row + i, of_plane(plane + 1, [k[i] for k in above])))
        beside += [(at, jnp.zeros(shape, F32)) for at in range(plan.high_row + plan.half_x, size)]
        for pair in range(plan.owners // 2):
            base = (pair * plan.groups + plane) * size
            pick_out[pl.ds(base, plan.owners), :] = main
            for at, values in beside:
                mine = jnp.where(up, values[2 * pair : 2 * pair + 1], values[2 * pair + 1 : 2 * pair + 2])
                pick_out[pl.ds(base + at, 1), :] = mine


def slots_kernel(plan, pick_ref, own_ref, other_ref, total_out):
    rows = pl.ds(plan.sums_row, 3 * plan.owners)
    terms = three_terms(own_ref[rows, :] + other_ref[rows, :])
    blank = jnp.zeros((plan.p - 9 * plan.owners, plan.p), F32)
    terms = jnp.concatenate([terms, blank], axis=0)
    out = lax.dot_general(
        pick_ref[...].astype(BF16),
        terms.astype(BF16),
        (((1,), (0,)), ((), ())),
        preferred_element_type=F32,
    )
    for slot in range(plan.slots):
        for part in range(plan.slot_parts):
            begin = 4 * (slot * plan.slot_parts + part)
            total_out[slot, part] = out[begin : begin + 4]


def coarse_solve(packed, planes):
    lane = iota(packed.shape, 1)
    even = lane & 1 == 0
    mass_mean = jnp.where(even, packed, pltpu.roll(packed, 1, 1))
    pot_mean = jnp.where(even, pltpu.roll(packed, planes - 1, 1), packed)

    def neighbour_sum(values):
        return jnp.where(lane >= 2, pltpu.roll(values, 2, 1), 0.0) + jnp.where(
            lane < planes - 2, pltpu.roll(values, planes - 2, 1), 0.0
        )

    coarse_conc = jnp.zeros_like(mass_mean)
    coarse_pot = jnp.zeros_like(pot_mean)
    for _ in range(CSWEEP):
        mass_gap = mass_mean - (
            coarse_conc + coarse_flux * (2.0 * coarse_pot - neighbour_sum(coarse_pot))
        )
        pot_gap = pot_mean - (
            coarse_pot
            - split_slope * coarse_conc
            + coarse_bend * (neighbour_sum(coarse_conc) - 2.0 * coarse_conc)
        )
        coarse_conc = coarse_conc + (relax_coarse / coarse_det) * (
            mass_gap - 2.0 * coarse_flux * pot_gap
        )
        coarse_pot = coarse_pot + (relax_coarse / coarse_det) * (
            pot_gap + (split_slope + 2.0 * coarse_bend) * mass_gap
        )
    return coarse_conc, coarse_pot


def beside_kernel(
    plan, mob_ref, raw_ref, x_near_msg, x_far_msg, y_near_msg, y_far_msg, x_near_ref, x_far_ref,
    faces_out, diagonal_out, scale_out, ends_out,
):
    mobility = mob_ref[...]
    sides = received("gx", x_near_msg, x_far_msg)
    ends = received("gy", y_near_msg, y_far_msg)
    halo = tuple(side_rows(plan, rows, 2) for rows in sides) + tuple(
        side_columns(plan, rows, 2) for rows in ends
    )
    faces, diagonal = faces_of(mobility, neighbours(mobility, halo))
    for i, face in enumerate(faces):
        faces_out[i] = face
    diagonal_out[...] = diagonal
    scale_out[...] = scale_from(diagonal)

    corners = received("gx", x_near_ref, x_far_ref)
    h = lax.axis_index("gy")
    inside = (h > 0, h < plan.groups - 1)
    own_mob = [
        jnp.concatenate([mobility[x, y : y + 1] for x in range(plan.x)], axis=0)
        for y in (0, plan.y - 1)
    ]
    for end, rows in enumerate(ends):

        def row(which):
            return rows[which * plan.x : (which + 1) * plan.x]

        def beside(which, own):
            here = row(which)
            at = 2 * plan.y + 2 * which + end
            wide = jnp.concatenate([corners[0][at : at + 1], here, corners[1][at : at + 1]], axis=0)
            return (
                wide[: plan.x], wide[2:], own, row(which + 3),
                *(part[0] for part in plane_pair(here[None])),
            )

        raw = [
            raw_ref[pl.ds((2 * which + end) * plan.x, plan.x), :] for which in range(2)
        ]
        faces, diagonal = faces_of(row(2), beside(2, own_mob[end]))
        excess = excess_of(
            row(0), row(1), beside(0, raw[0]), beside(1, raw[1]), faces, diagonal, row(6), row(7)
        )
        new = relax_pair(row(0), row(1), *excess, diagonal, scale_from(diagonal))
        for which, values in enumerate(new):
            ends_out[pl.ds((2 * which + end) * plan.x, plan.x), :] = jnp.where(
                inside[end], values, 0.0
            )


def last_kernel(
    plan, conc_ref, pot_ref, mass_ref, pots_ref, faces_ref, diagonal_ref, scale_ref,
    x_near_ref, x_far_ref, ends_ref, spread_ref, total_ref,
    conc_hbm, pot_hbm, conc_out, pot_out, sems,
):
    parts = []
    for part in range(plan.slot_parts):
        mean = total_ref[0, part]
        for slot in range(1, total_ref.shape[0]):
            mean = mean + total_ref[slot, part]
        parts.append(mean)
    solved = jnp.concatenate(
        coarse_solve(jnp.concatenate(parts, axis=0), plan.p), axis=1
    )
    own = lax.dot_general(
        spread_ref[...].astype(BF16),
        three_terms(solved[: plan.owners]).astype(BF16),
        (((1,), (0,)), ((), ())),
        preferred_element_type=F32,
    )
    sides = received("gx", x_near_ref, x_far_ref)

    def updated(which, ref):
        lanes = slice(which * plan.p, (which + 1) * plan.p)
        corr = own[:, lanes]
        slabs = [side_rows(plan, sides[0], which)]
        slabs += [ref[pl.ds(x, 1)] for x in range(plan.x)]
        slabs.append(side_rows(plan, sides[1], which))
        order = [plan.half_x, *[x >> 1 for x in range(plan.x)], plan.half_x + 1]
        slabs = [
            slab + corr[x * plan.y : (x + 1) * plan.y][None] for slab, x in zip(slabs, order)
        ]
        ends = []
        for end, begin in enumerate((plan.low_row, plan.high_row)):
            rows = ends_ref[pl.ds((2 * which + end) * plan.x, plan.x), :]
            ends.append([
                (rows[x : x + 1] + solved[begin + (x >> 1) : begin + (x >> 1) + 1, lanes])[None]
                for x in range(plan.x)
            ])
        return slabs, ends

    conc, conc_ends = updated(0, conc_ref)
    pot, pot_ends = updated(1, pot_ref)

    def beside(slabs, ends, x):
        here = slabs[x + 1]
        return (
            slabs[x], slabs[x + 2], *y_pair(here, ends[0][x], ends[1][x]), *plane_pair(here)
        )

    copies = []
    for x in range(plan.x):
        one = pl.ds(x, 1)
        diagonal = diagonal_ref[one]
        excess = excess_of(
            conc[x + 1], pot[x + 1], beside(conc, conc_ends, x), beside(pot, pot_ends, x),
            [faces_ref[i, one] for i in range(6)], diagonal, mass_ref[one], pots_ref[one],
        )
        conc_out[one], pot_out[one] = relax_pair(
            conc[x + 1], pot[x + 1], *excess, diagonal, scale_ref[one]
        )
        for source, target in ((conc_out, conc_hbm), (pot_out, pot_hbm)):
            copies.append(
                pltpu.make_async_copy(source.at[one], target.at[one], sems.at[len(copies)])
            )
            copies[-1].start()
    for copy in copies:
        copy.wait()


def call(kernel, plan, outs, args, far=(), smem=(), scratch=(), limit=VMEM_LIMIT, out_far=False):
    def space(i):
        return pl.ANY if i in far else pltpu.SMEM if i in smem else pltpu.VMEM

    return pl.pallas_call(
        functools.partial(kernel, plan),
        out_shape=[jax.ShapeDtypeStruct(shape, F32) for shape in outs],
        in_specs=[pl.BlockSpec(memory_space=space(i)) for i in range(len(args))],
        out_specs=[pl.BlockSpec(memory_space=pl.ANY if out_far else pltpu.VMEM)] * len(outs),
        scratch_shapes=list(scratch),
        compiler_params=pltpu.CompilerParams(vmem_limit_bytes=limit),
    )(*args)


def swap_near(axis, rows, begin=0):
    pairs = [(i, i + 1) for i in range(begin, lax.axis_size(axis) - 1, 2)]
    return lax.ppermute(rows, axis, pairs + [(j, i) for i, j in pairs])


def swap_far(axis, rows):
    return swap_near(axis, rows, 1)


def gather_totals(plan, total, y_near, y_far):
    if plan.slots:
        groups = [
            [g * plan.groups + h for g in range(core, plan.owners, 2) for h in range(plan.groups)]
            for core in range(2)
        ]
        return lax.all_to_all(
            total, ("gx", "gy"), split_axis=0, concat_axis=0, axis_index_groups=groups, tiled=True
        )
    shape = (plan.groups, 3, plan.owners, plan.p)
    parts = lax.all_gather(lax.psum(total, "gx"), "gy").reshape(shape)
    blank = jnp.zeros((1, plan.owners, plan.p), F32)
    to_below, own, to_above = (parts[:, k] for k in range(3))
    own = own + jnp.concatenate([blank, to_above[:-1]]) + jnp.concatenate([to_below[1:], blank])
    own = jnp.concatenate([blank, own, blank])
    g, h = lax.axis_index("gx"), lax.axis_index("gy")
    rows = [lax.dynamic_index_in_dim(own, h + 1, 0, False)]
    up = lax.rem(h, 2) == 0
    for place, at, msg in (
        (h, plan.half_y - 1, jnp.where(up, y_far, y_near)),
        (h + 2, 0, jnp.where(up, y_near, y_far)),
    ):
        ident = lax.dynamic_index_in_dim(msg, plan.map_row + g, 0, False).astype(jnp.int32)
        ident = jnp.stack([ident[i * plan.half_y + at] for i in range(plan.half_x)])
        rows.append(lax.dynamic_index_in_dim(own, place, 0, False)[ident])
    rows = jnp.concatenate(rows)
    rows = jnp.pad(rows, ((0, 4 * plan.slot_parts - rows.shape[0]), (0, 0)))
    return rows.reshape(1, plan.slot_parts, 4, plan.p)


def on_device(conc, pot, mass_source, pot_source, mask, kind, table, owner_map):
    plan = Plan(conc.shape, lax.axis_size("gx"), lax.axis_size("gy"))
    block = conc.shape
    fields = [conc, pot, mask, kind, mass_source, pot_source]
    messages = call(
        prepare_kernel,
        plan,
        [*[(3 * plan.y, plan.p)] * 2, *[(plan.y_rows, plan.p)] * 2],
        [*fields, owner_map, table],
        far=range(8),
        limit=LARGE_LIMIT,
        scratch=(
            *[pltpu.VMEM((2, plan.y, plan.p), field.dtype) for field in fields[:4]],
            *[pltpu.VMEM((2, plan.x, 8, plan.p), field.dtype) for field in fields],
            pltpu.VMEM(owner_map.shape, owner_map.dtype),
            pltpu.SMEM(table.shape, table.dtype),
            pltpu.SemaphoreType.DMA((22,)),
        ),
    )
    old = [
        swap_near("gx", messages[0]), swap_far("gx", messages[1]),
        swap_near("gy", messages[2]), swap_far("gy", messages[3]),
    ]
    old[0], mask, kind = lax.optimization_barrier((old[0], mask, kind))
    mob, gather, spread, scale = call(
        local_kernel,
        plan,
        [block, (plan.owners, plan.rows), (plan.rows, 3 * plan.owners), (plan.owners, plan.p)],
        [mask, kind, table, owner_map],
        smem=(2,),
    )
    conc, pot, raw, near, far = call(
        first_kernel,
        plan,
        [
            block,
            block,
            (4 * plan.x, plan.p),
            (plan.sums_row + 3 * plan.owners, plan.p),
            (plan.sums_row, plan.p),
        ],
        [conc, pot, mob, mass_source, pot_source, gather, scale, owner_map, *old],
    )
    new_near = swap_near("gx", near)
    if plan.slots:
        raw, owner_map = lax.optimization_barrier((raw, owner_map))
        size = 4 * plan.slot_parts
        (pick,) = call(
            pick_kernel, plan, [(plan.slots * size, plan.p)], [owner_map, *old[2:]]
        )
        (total,) = call(
            slots_kernel, plan, [(plan.slots, plan.slot_parts, 4, plan.p)], [pick, near, new_near]
        )
        total, far = lax.optimization_barrier((total, far))
    else:
        total = near[plan.sums_row :]
    total = gather_totals(plan, total, *old[2:])
    new = [new_near, swap_far("gx", far)]
    faces, diagonal, scale, ends = call(
        beside_kernel,
        plan,
        [(6, *block), block, block, (4 * plan.x, plan.p)],
        [mob, raw, *old, *new],
    )
    return tuple(
        call(
            last_kernel,
            plan,
            [block, block],
            [conc, pot, mass_source, pot_source, faces, diagonal, scale, *new, ends, spread, total],
            out_far=True,
            scratch=(
                pltpu.VMEM(block, F32),
                pltpu.VMEM(block, F32),
                pltpu.SemaphoreType.DMA((2 * plan.x,)),
            ),
        )
    )


def solution(mesh):
    grid = P("gx", "gy", None)
    return jax.shard_map(
        on_device,
        mesh=mesh,
        in_specs=(grid,) * 6 + (P(), P(None, "gy")),
        out_specs=(grid, grid),
        check_vma=False,
    )
```

```python
import functools

import jax
import jax.numpy as jnp
from jax import lax
from jax.experimental import pallas as pl
from jax.experimental.pallas import tpu as pltpu
from jax.sharding import PartitionSpec as P

CSWEEP = 3

time_step = 0.25
split_slope = 1.0
interface = 0.5
relax_fine = 0.6
relax_coarse = 0.6
coarse_flux = 0.0625
coarse_bend = 0.125
coarse_det = 1.0 + 2.0 * coarse_flux * (split_slope + 2.0 * coarse_bend)

F32 = jnp.float32
BF16 = jnp.bfloat16
VMEM_LIMIT = 48 * 1024 * 1024


def iota(shape, dim):
    return lax.broadcasted_iota(jnp.int32, shape, dim)


def x_pair(field, low, high):
    return (
        jnp.concatenate([low, field[:-1]], axis=0),
        jnp.concatenate([field[1:], high], axis=0),
    )


def y_pair(field, low, high):
    size = field.shape[1]
    where = iota(field.shape, 1)
    return (
        jnp.where(where == 0, low, pltpu.roll(field, 1, 1)),
        jnp.where(where == size - 1, high, pltpu.roll(field, size - 1, 1)),
    )


def plane_pair(field):
    size = field.shape[2]
    where = iota(field.shape, 2)
    return (
        jnp.where(where == 0, 0.0, pltpu.roll(field, 1, 2)),
        jnp.where(where == size - 1, 0.0, pltpu.roll(field, size - 1, 2)),
    )


def neighbours(field, halo):
    xm, xp, ym, yp = halo
    return (*x_pair(field, xm, xp), *y_pair(field, ym, yp), *plane_pair(field))


def excess_of(conc, pot, conc_beside, pot_beside, faces, diagonal, mass_source, pot_source):
    excess_mass = (mass_source - conc) - diagonal * pot
    for face, other in zip(faces, pot_beside):
        excess_mass = excess_mass + face * other
    beside = conc_beside[0]
    for other in conc_beside[1:]:
        beside = beside + other
    excess_pot = (pot_source - pot) + (split_slope + 6.0 * interface) * conc - interface * beside
    return excess_mass, excess_pot


def scale_from(diagonal):
    return relax_fine / (1.0 + (split_slope + 6.0 * interface) * diagonal)


def relax_pair(conc, pot, excess_mass, excess_pot, diagonal, scale):
    new_conc = conc + (excess_mass - diagonal * excess_pot) * scale
    new_pot = pot + (excess_pot + (split_slope + 6.0 * interface) * excess_mass) * scale
    return new_conc, new_pot


def faces_of(mobility, beside):
    faces = tuple((0.5 * time_step) * (mobility + other) for other in beside)
    diagonal = faces[0]
    for face in faces[1:]:
        diagonal = diagonal + face
    return faces, diagonal


def split_dot(ones, values, contract):
    dims = (contract, ((), ()))
    total = None
    rest = values
    for _ in range(3):
        term = rest.astype(BF16)
        rest = rest - term.astype(F32)
        part = lax.dot_general(ones, term, dims, preferred_element_type=F32)
        total = part if total is None else total + part
    return total


def three_terms(values):
    out = []
    for _ in range(3):
        out.append(values.astype(BF16).astype(F32))
        values = values - out[-1]
    return jnp.concatenate(out, axis=0)


def round_up(value, unit):
    return -(-value // unit) * unit


class Plan:
    def __init__(self, shape, owners, groups):
        self.x, self.y, self.p = shape
        self.owners, self.groups = owners, groups
        self.half_x, self.half_y = self.x // 2, self.y // 2
        self.columns = self.half_x * self.half_y
        self.map_row = round_up(8 * self.x, 8)
        self.y_rows = self.map_row + owners
        self.cells = self.x * self.y
        self.rows = (self.half_x + 2) * self.y
        self.low_row = owners
        self.high_row = owners + self.half_x
        self.slot_parts = -(-(owners + 2 * self.half_x) // 4)
        slots = owners * groups
        self.slots = slots if slots <= 64 else 0


def side_rows(plan, rows, which):
    return rows[which * plan.y : (which + 1) * plan.y][None]


def side_columns(plan, rows, which):
    return rows[which * plan.x : (which + 1) * plan.x][:, None]


def membership(plan, owner_ref):
    g = lax.axis_index("gx")
    last = plan.owners - 1
    owner = iota((plan.owners, plan.columns), 0)
    low, high = plan.half_x, plan.half_x + 1
    shape = (plan.half_x + 2, plan.y, plan.columns)
    x, y, column = iota(shape, 0), iota(shape, 1), iota(shape, 2)
    half = jnp.where(x < low, x, jnp.where(x == low, plan.half_x - 1, 0))
    place = column == half * plan.half_y + (y >> 1)
    sides = (
        (x < low, g, True),
        (x == low, jnp.maximum(g - 1, 0), g > 0),
        (x == high, jnp.minimum(g + 1, last), g < last),
    )
    gather, spread = None, None
    for part, row, inside in sides:
        hits = ((owner_ref[pl.ds(row, 1), :] == owner) & inside).astype(F32).astype(BF16)
        where = (place & part).astype(F32).reshape(plan.rows, plan.columns).astype(BF16)
        nt = (((1,), (1,)), ((), ()))
        some = lax.dot_general(hits, where, nt, preferred_element_type=F32)
        gather = some if gather is None else gather + some
        some = lax.dot_general(where, hits, nt, preferred_element_type=F32)
        spread = some if spread is None else spread + some
    return gather, jnp.concatenate([spread] * 3, axis=1)


def scale_of(plan, owners):
    owner = iota((plan.owners, plan.columns), 0).astype(owners.dtype)
    hits = jnp.zeros((plan.owners, plan.columns), F32)
    for g in range(plan.owners):
        hits = hits + (owners[g : g + 1] == owner).astype(F32)
    count = jnp.sum(hits, axis=1, keepdims=True)
    return jnp.broadcast_to(0.125 / jnp.maximum(count, 1.0), (plan.owners, plan.p))


def mobility_of(mask, kind, table):
    values = jnp.zeros(kind.shape, F32)
    for marker, value in enumerate(table):
        values = jnp.where(kind == marker, value, values)
    return mask.astype(F32) * values


def even(axis):
    return lax.rem(lax.axis_index(axis), 2) == 0


def put_x(plan, lows, highs, near, far):
    up = even("gx")
    for which, (low, high) in enumerate(zip(lows, highs)):
        near[pl.ds(which * plan.y, plan.y), :] = jnp.where(up, high, low)
        far[pl.ds(which * plan.y, plan.y), :] = jnp.where(up, low, high)


def received(axis, near_ref, far_ref):
    up = even(axis)
    rows = pl.ds(0, min(near_ref.shape[0], far_ref.shape[0]))
    near, far = near_ref[rows, :], far_ref[rows, :]
    return jnp.where(up, far, near), jnp.where(up, near, far)


def prepare_kernel(plan, *refs):
    hbm, refs = refs[:8], refs[8:]
    x_near_ref, x_far_ref, y_near_ref, y_far_ref = refs[:4]
    x_refs, y_refs, (owner_ref, table_ref, sems) = refs[4:8], refs[8:14], refs[14:]
    copies = []

    def start(source, target):
        copies.append(pltpu.make_async_copy(source, target, sems.at[len(copies)]))
        copies[-1].start()

    start(hbm[7], table_ref)
    start(hbm[6], owner_ref)
    for source, target in zip(hbm[:4], x_refs):
        start(source.at[0], target.at[0])
        start(source.at[plan.x - 1], target.at[1])
    for source, target in zip(hbm[:6], y_refs):
        start(source.at[:, pl.ds(0, 8)], target.at[0])
        start(source.at[:, pl.ds(plan.y - 8, 8)], target.at[1])
    for copy in copies:
        copy.wait()
    table = [table_ref[marker] for marker in range(table_ref.shape[0])]
    conc, pot, mask, kind = (ref[...] for ref in x_refs)
    fields = (conc, pot, mobility_of(mask, kind, table))
    put_x(plan, [f[0] for f in fields], [f[1] for f in fields], x_near_ref, x_far_ref)
    conc, pot, mask, kind, mass, pots = (ref[...] for ref in y_refs)
    fields = (conc, pot, mobility_of(mask, kind, table))
    up = even("gy")
    rows = [(field, at) for at in range(2) for field in fields] + [(mass, 0), (pots, 0)]
    for which, (field, at) in enumerate(rows):
        for x in range(plan.x):
            low, high = field[0, x, at : at + 1], field[1, x, 7 - at : 8 - at]
            y_near_ref[pl.ds(which * plan.x + x, 1), :] = jnp.where(up, high, low)
            y_far_ref[pl.ds(which * plan.x + x, 1), :] = jnp.where(up, low, high)
    used = 8 * plan.x
    for ref in (y_near_ref, y_far_ref):
        ref[pl.ds(used, plan.y_rows - used), :] = jnp.zeros((plan.y_rows - used, plan.p), F32)
        ref[pl.ds(plan.map_row, plan.owners), pl.ds(0, plan.columns)] = owner_ref[...].astype(F32)


def local_kernel(
    plan, mask_ref, class_ref, table_ref, owner_ref, mob_ref, gather_ref, spread_ref, scale_ref
):
    table = [table_ref[marker] for marker in range(table_ref.shape[0])]
    mob_ref[...] = mobility_of(mask_ref[...], class_ref[...], table)
    gather_ref[...], spread_ref[...] = membership(plan, owner_ref)
    scale_ref[...] = scale_of(plan, owner_ref[...])


def first_kernel(
    plan, x_far_ref, y_far_ref, y_near_ref, x_near_ref,
    conc_ref, pot_ref, mob_ref, mass_ref, pots_ref, gather_ref, scale_ref, owner_ref,
    conc_out, pot_out, total_out, raw_out, x_near_out, x_far_out,
):
    sides = received("gx", x_near_ref, x_far_ref)
    ends = received("gy", y_near_ref, y_far_ref)

    def halo(which):
        return tuple(side_rows(plan, rows, which) for rows in sides) + tuple(
            side_columns(plan, rows, which) for rows in ends
        )

    mobility, mob_halo = mob_ref[...], halo(2)
    faces, diagonal = faces_of(mobility, neighbours(mobility, mob_halo))
    mass_source, pot_source = mass_ref[...], pots_ref[...]
    conc, pot = conc_ref[...], pot_ref[...]
    for at, field in enumerate((conc, pot)):
        for x in range(plan.x):
            raw_out[pl.ds(2 * at * plan.x + x, 1), :] = field[x, 0:1]
            raw_out[pl.ds((2 * at + 1) * plan.x + x, 1), :] = field[x, plan.y - 1 : plan.y]
    excess = excess_of(
        conc, pot, neighbours(conc, halo(0)), neighbours(pot, halo(1)), faces, diagonal,
        mass_source, pot_source,
    )
    conc, pot = relax_pair(conc, pot, *excess, diagonal, scale_from(diagonal))
    conc_out[...] = conc
    pot_out[...] = pot
    put_x(plan, (conc[0], pot[0]), (conc[plan.x - 1], pot[plan.x - 1]), x_near_out, x_far_out)
    up = even("gx")
    base = 2 * plan.y
    for which in range(3):
        for end, rows in enumerate(ends):
            low = rows[which * plan.x : which * plan.x + 1]
            high = rows[(which + 1) * plan.x - 1 : (which + 1) * plan.x]
            x_near_out[pl.ds(base + 2 * which + end, 1), :] = jnp.where(up, high, low)
            x_far_out[pl.ds(base + 2 * which + end, 1), :] = jnp.where(up, low, high)
    for ref in (x_near_out, x_far_out):
        ref[pl.ds(base + 6, 2), :] = jnp.zeros((2, plan.p), F32)

    nothing = tuple(jnp.zeros_like(part) for part in mob_halo)
    own_mass, own_pot = excess_of(
        conc, pot, neighbours(conc, nothing), neighbours(pot, nothing), faces, diagonal,
        mass_source, pot_source,
    )
    give_mass, give_pot = (
        [field[x] + field[x + 1] for x in range(0, plan.x, 2)] for field in (own_mass, own_pot)
    )
    for x, side in ((0, 0), (plan.x - 1, 1)):
        face = 0.5 * (mobility[x] + mob_halo[side][0])
        give_mass.append(time_step * face * pot[x])
        give_pot.append(-interface * conc[x])

    def packed(mass, other):
        first = iota(mass.shape, 1) & 1 == 0
        return jnp.where(
            first, mass + pltpu.roll(mass, plan.p - 1, 1), other + pltpu.roll(other, 1, 1)
        )

    give = packed(jnp.concatenate(give_mass, axis=0), jnp.concatenate(give_pot, axis=0))
    h = lax.axis_index("gy")
    inside = (h > 0, None, h < plan.groups - 1)
    maps = [rows[plan.map_row : plan.map_row + plan.owners, : plan.columns] for rows in ends]
    maps.insert(1, owner_ref[...].astype(F32))
    owner = iota((plan.owners, 1), 0)
    is_mine = owner == lax.axis_index("gx")

    sums = [None, split_dot(gather_ref[...].astype(BF16), give, ((1,), (0,))), None]
    sums[1] = sums[1] * scale_ref[...]
    for place, y, at, side in ((0, 0, plan.half_y - 1, 2), (2, plan.y - 1, 0, 3)):
        edge_mob, edge_pot, edge_conc = (
            jnp.concatenate([field[x, y : y + 1] for x in range(plan.x)], axis=0)
            for field in (mobility, pot, conc)
        )
        face = 0.5 * (edge_mob + mob_halo[side][:, 0])
        both = packed(time_step * face * edge_pot, -interface * edge_conc)
        part = jnp.zeros((plan.owners, plan.p), F32)
        for i in range(plan.half_x):
            column = owner_column(plan, maps[place], i, at)
            ident = jnp.sum(jnp.where(is_mine, column, 0.0), axis=0, keepdims=True)
            pair = both[2 * i : 2 * i + 1] + both[2 * i + 1 : 2 * i + 2]
            part = part + jnp.where((owner.astype(F32) == ident) & inside[place], pair, 0.0)
        sums[place] = part * scale_of(plan, maps[place])
    if not plan.slots:
        total_out[...] = jnp.concatenate(sums, axis=0)
        return

    def picked(place, i, at):
        column = owner_column(plan, maps[place], i, at)
        ident = jnp.broadcast_to(column, (plan.owners, plan.p))
        out = jnp.zeros((plan.owners, plan.p), F32)
        for o in range(plan.owners):
            out = jnp.where(ident == float(o), sums[place][o : o + 1], out)
        return out

    below = [[picked(k, i, plan.half_y - 1) for i in range(plan.half_x)] for k in range(3)]
    above = [[picked(k, i, 0) for i in range(plan.half_x)] for k in range(3)]

    def of_plane(plane, choices):
        out = jnp.zeros((plan.owners, plan.p), F32)
        for k in range(3):
            out = jnp.where(plane == h + (k - 1), choices[k], out)
        return out

    size = 4 * plan.slot_parts
    for plane in range(plan.groups):
        main = of_plane(plane, sums)
        beside = []
        for i in range(plan.half_x):
            beside.append((plan.low_row + i, of_plane(plane - 1, [k[i] for k in below])))
            beside.append((plan.high_row + i, of_plane(plane + 1, [k[i] for k in above])))
        beside += [(at, jnp.zeros_like(main)) for at in range(plan.high_row + plan.half_x, size)]
        for g in range(plan.owners):
            slot = g * plan.groups + plane
            for part in range(plan.owners // 4):
                total_out[slot, part] = main[4 * part : 4 * part + 4]
            for row, values in beside:
                total_out[slot, row // 4, pl.ds(row % 4, 1), :] = values[g : g + 1]


def owner_column(plan, owners, i, at):
    b = i * plan.half_y + at
    return owners[:, b : b + 1]


def coarse_solve(packed, planes):
    lane = iota(packed.shape, 1)
    even = lane & 1 == 0
    mass_mean = jnp.where(even, packed, pltpu.roll(packed, 1, 1))
    pot_mean = jnp.where(even, pltpu.roll(packed, planes - 1, 1), packed)

    def neighbour_sum(values):
        return jnp.where(lane >= 2, pltpu.roll(values, 2, 1), 0.0) + jnp.where(
            lane < planes - 2, pltpu.roll(values, planes - 2, 1), 0.0
        )

    coarse_conc = jnp.zeros_like(mass_mean)
    coarse_pot = jnp.zeros_like(pot_mean)
    for _ in range(CSWEEP):
        mass_gap = mass_mean - (
            coarse_conc + coarse_flux * (2.0 * coarse_pot - neighbour_sum(coarse_pot))
        )
        pot_gap = pot_mean - (
            coarse_pot
            - split_slope * coarse_conc
            + coarse_bend * (neighbour_sum(coarse_conc) - 2.0 * coarse_conc)
        )
        coarse_conc = coarse_conc + (relax_coarse / coarse_det) * (
            mass_gap - 2.0 * coarse_flux * pot_gap
        )
        coarse_pot = coarse_pot + (relax_coarse / coarse_det) * (
            pot_gap + (split_slope + 2.0 * coarse_bend) * mass_gap
        )
    return coarse_conc, coarse_pot


def beside_kernel(
    plan, x_far_ref, x_near_ref, mob_ref, raw_ref, x_near_msg, x_far_msg, y_near_msg, y_far_msg,
    faces_out, diagonal_out, scale_out, ends_out,
):
    mobility = mob_ref[...]
    sides = received("gx", x_near_msg, x_far_msg)
    ends = received("gy", y_near_msg, y_far_msg)
    halo = tuple(side_rows(plan, rows, 2) for rows in sides) + tuple(
        side_columns(plan, rows, 2) for rows in ends
    )
    faces, diagonal = faces_of(mobility, neighbours(mobility, halo))
    for i, face in enumerate(faces):
        faces_out[i] = face
    diagonal_out[...] = diagonal
    scale_out[...] = scale_from(diagonal)

    corners = received("gx", x_near_ref, x_far_ref)
    h = lax.axis_index("gy")
    inside = (h > 0, h < plan.groups - 1)
    own_mob = [
        jnp.concatenate([mobility[x, y : y + 1] for x in range(plan.x)], axis=0)
        for y in (0, plan.y - 1)
    ]
    for end, rows in enumerate(ends):

        def row(which):
            return rows[which * plan.x : (which + 1) * plan.x]

        def beside(which, own):
            here = row(which)
            at = 2 * plan.y + 2 * which + end
            wide = jnp.concatenate([corners[0][at : at + 1], here, corners[1][at : at + 1]], axis=0)
            return (
                wide[: plan.x], wide[2:], own, row(which + 3),
                *(part[0] for part in plane_pair(here[None])),
            )

        raw = [
            raw_ref[pl.ds((2 * which + end) * plan.x, plan.x), :] for which in range(2)
        ]
        faces, diagonal = faces_of(row(2), beside(2, own_mob[end]))
        excess = excess_of(
            row(0), row(1), beside(0, raw[0]), beside(1, raw[1]), faces, diagonal, row(6), row(7)
        )
        new = relax_pair(row(0), row(1), *excess, diagonal, scale_from(diagonal))
        for which, values in enumerate(new):
            ends_out[pl.ds((2 * which + end) * plan.x, plan.x), :] = jnp.where(
                inside[end], values, 0.0
            )


def last_kernel(
    plan, conc_ref, pot_ref, mass_ref, pots_ref, faces_ref, diagonal_ref, scale_ref,
    x_near_ref, x_far_ref, ends_ref, spread_ref, total_ref,
    conc_hbm, pot_hbm, conc_out, pot_out, sems,
):
    parts = []
    for part in range(plan.slot_parts):
        mean = total_ref[0, part]
        for slot in range(1, total_ref.shape[0]):
            mean = mean + total_ref[slot, part]
        parts.append(mean)
    solved = jnp.concatenate(
        coarse_solve(jnp.concatenate(parts, axis=0), plan.p), axis=1
    )
    own = lax.dot_general(
        spread_ref[...].astype(BF16),
        three_terms(solved[: plan.owners]).astype(BF16),
        (((1,), (0,)), ((), ())),
        preferred_element_type=F32,
    )
    sides = received("gx", x_near_ref, x_far_ref)

    def updated(which, ref):
        lanes = slice(which * plan.p, (which + 1) * plan.p)
        corr = own[:, lanes]
        slabs = [side_rows(plan, sides[0], which)]
        slabs += [ref[pl.ds(x, 1)] for x in range(plan.x)]
        slabs.append(side_rows(plan, sides[1], which))
        order = [plan.half_x, *[x >> 1 for x in range(plan.x)], plan.half_x + 1]
        slabs = [
            slab + corr[x * plan.y : (x + 1) * plan.y][None] for slab, x in zip(slabs, order)
        ]
        ends = []
        for end, begin in enumerate((plan.low_row, plan.high_row)):
            rows = ends_ref[pl.ds((2 * which + end) * plan.x, plan.x), :]
            ends.append([
                (rows[x : x + 1] + solved[begin + (x >> 1) : begin + (x >> 1) + 1, lanes])[None]
                for x in range(plan.x)
            ])
        return slabs, ends

    conc, conc_ends = updated(0, conc_ref)
    pot, pot_ends = updated(1, pot_ref)

    def beside(slabs, ends, x):
        here = slabs[x + 1]
        return (
            slabs[x], slabs[x + 2], *y_pair(here, ends[0][x], ends[1][x]), *plane_pair(here)
        )

    copies = []
    for x in range(plan.x):
        one = pl.ds(x, 1)
        diagonal = diagonal_ref[one]
        excess = excess_of(
            conc[x + 1], pot[x + 1], beside(conc, conc_ends, x), beside(pot, pot_ends, x),
            [faces_ref[i, one] for i in range(6)], diagonal, mass_ref[one], pots_ref[one],
        )
        conc_out[one], pot_out[one] = relax_pair(
            conc[x + 1], pot[x + 1], *excess, diagonal, scale_ref[one]
        )
        for source, target in ((conc_out, conc_hbm), (pot_out, pot_hbm)):
            copies.append(
                pltpu.make_async_copy(source.at[one], target.at[one], sems.at[len(copies)])
            )
            copies[-1].start()
    for copy in copies:
        copy.wait()


def call(kernel, plan, outs, args, far=(), smem=(), scratch=(), out_far=False):
    def space(i):
        return pl.ANY if i in far else pltpu.SMEM if i in smem else pltpu.VMEM

    return pl.pallas_call(
        functools.partial(kernel, plan),
        out_shape=[jax.ShapeDtypeStruct(shape, F32) for shape in outs],
        in_specs=[pl.BlockSpec(memory_space=space(i)) for i in range(len(args))],
        out_specs=[pl.BlockSpec(memory_space=pl.ANY if out_far else pltpu.VMEM)] * len(outs),
        scratch_shapes=list(scratch),
        compiler_params=pltpu.CompilerParams(vmem_limit_bytes=VMEM_LIMIT),
    )(*[
        pltpu.with_memory_space_constraint(arg, pltpu.HBM) if i in far else arg
        for i, arg in enumerate(args)
    ])


def swap_near(axis, rows, begin=0):
    pairs = [(i, i + 1) for i in range(begin, lax.axis_size(axis) - 1, 2)]
    return lax.ppermute(rows, axis, pairs + [(j, i) for i, j in pairs])


def swap_far(axis, rows):
    return swap_near(axis, rows, 1)


def gather_totals(plan, total, y_near, y_far):
    if plan.slots:
        return lax.all_to_all(total, ("gx", "gy"), split_axis=0, concat_axis=0, tiled=True)
    shape = (plan.groups, 3, plan.owners, plan.p)
    parts = lax.all_gather(lax.psum(total, "gx"), "gy").reshape(shape)
    blank = jnp.zeros((1, plan.owners, plan.p), F32)
    to_below, own, to_above = (parts[:, k] for k in range(3))
    own = own + jnp.concatenate([blank, to_above[:-1]]) + jnp.concatenate([to_below[1:], blank])
    own = jnp.concatenate([blank, own, blank])
    g, h = lax.axis_index("gx"), lax.axis_index("gy")
    rows = [lax.dynamic_index_in_dim(own, h + 1, 0, False)]
    up = lax.rem(h, 2) == 0
    for place, at, msg in (
        (h, plan.half_y - 1, jnp.where(up, y_far, y_near)),
        (h + 2, 0, jnp.where(up, y_near, y_far)),
    ):
        ident = lax.dynamic_index_in_dim(msg, plan.map_row + g, 0, False).astype(jnp.int32)
        ident = jnp.stack([ident[i * plan.half_y + at] for i in range(plan.half_x)])
        rows.append(lax.dynamic_index_in_dim(own, place, 0, False)[ident])
    rows = jnp.concatenate(rows)
    rows = jnp.pad(rows, ((0, 4 * plan.slot_parts - rows.shape[0]), (0, 0)))
    return rows.reshape(1, plan.slot_parts, 4, plan.p)


def on_device(conc, pot, mass_source, pot_source, mask, kind, table, owner_map):
    plan = Plan(conc.shape, lax.axis_size("gx"), lax.axis_size("gy"))
    block = conc.shape
    fields = [conc, pot, mask, kind, mass_source, pot_source]
    messages = call(
        prepare_kernel,
        plan,
        [*[(3 * plan.y, plan.p)] * 2, *[(plan.y_rows, plan.p)] * 2],
        [*fields, owner_map, table],
        far=range(8),
        scratch=(
            *[pltpu.VMEM((2, plan.y, plan.p), field.dtype) for field in fields[:4]],
            *[pltpu.VMEM((2, plan.x, 8, plan.p), field.dtype) for field in fields],
            pltpu.VMEM(owner_map.shape, owner_map.dtype),
            pltpu.SMEM(table.shape, table.dtype),
            pltpu.SemaphoreType.DMA((22,)),
        ),
    )
    x_far = swap_far("gx", messages[1])
    y_far = swap_far("gy", messages[3])
    y_near = swap_near("gy", messages[2])
    x_far, x_near, mask, kind = lax.optimization_barrier((x_far, messages[0], mask, kind))
    x_near = swap_near("gx", x_near)
    mob, gather, spread, scale = call(
        local_kernel,
        plan,
        [block, (plan.owners, plan.rows), (plan.rows, 3 * plan.owners), (plan.owners, plan.p)],
        [mask, kind, table, owner_map],
        smem=(2,),
    )
    slots = (plan.slots, plan.slot_parts, 4, plan.p)
    conc, pot, total, raw, near, far = call(
        first_kernel,
        plan,
        [
            block,
            block,
            slots if plan.slots else (3 * plan.owners, plan.p),
            (4 * plan.x, plan.p),
            *[(2 * plan.y + 8, plan.p)] * 2,
        ],
        [
            x_far, y_far, y_near, x_near,
            conc, pot, mob, mass_source, pot_source, gather, scale, owner_map,
        ],
    )
    total = gather_totals(plan, total, y_near, y_far)
    far = swap_far("gx", far)
    near = swap_near("gx", near)
    faces, diagonal, scale, ends = call(
        beside_kernel,
        plan,
        [(6, *block), block, block, (4 * plan.x, plan.p)],
        [far, near, mob, raw, x_near, x_far, y_near, y_far],
    )
    return tuple(
        call(
            last_kernel,
            plan,
            [block, block],
            [conc, pot, mass_source, pot_source, faces, diagonal, scale, near, far, ends, spread, total],
            out_far=True,
            scratch=(
                pltpu.VMEM(block, F32),
                pltpu.VMEM(block, F32),
                pltpu.SemaphoreType.DMA((2 * plan.x,)),
            ),
        )
    )


def solution(mesh):
    grid = P("gx", "gy", None)
    return jax.shard_map(
        on_device,
        mesh=mesh,
        in_specs=(grid,) * 6 + (P(), P(None, "gy")),
        out_specs=(grid, grid),
        check_vma=False,
    )
```

```python
import functools

import jax
import jax.numpy as jnp
from jax import lax
from jax.experimental import pallas as pl
from jax.experimental.pallas import tpu as pltpu
from jax.sharding import PartitionSpec as P

CSWEEP = 3

time_step = 0.25
split_slope = 1.0
interface = 0.5
relax_fine = 0.6
relax_coarse = 0.6
coarse_flux = 0.0625
coarse_bend = 0.125
coarse_det = 1.0 + 2.0 * coarse_flux * (split_slope + 2.0 * coarse_bend)

F32 = jnp.float32
BF16 = jnp.bfloat16
VMEM_LIMIT = 48 * 1024 * 1024


def iota(shape, dim):
    return lax.broadcasted_iota(jnp.int32, shape, dim)


def x_pair(field, low, high):
    return (
        jnp.concatenate([low, field[:-1]], axis=0),
        jnp.concatenate([field[1:], high], axis=0),
    )


def y_pair(field, low, high):
    size = field.shape[1]
    where = iota(field.shape, 1)
    return (
        jnp.where(where == 0, low, pltpu.roll(field, 1, 1)),
        jnp.where(where == size - 1, high, pltpu.roll(field, size - 1, 1)),
    )


def plane_pair(field):
    size = field.shape[2]
    where = iota(field.shape, 2)
    return (
        jnp.where(where == 0, 0.0, pltpu.roll(field, 1, 2)),
        jnp.where(where == size - 1, 0.0, pltpu.roll(field, size - 1, 2)),
    )


def neighbours(field, halo):
    xm, xp, ym, yp = halo
    return (*x_pair(field, xm, xp), *y_pair(field, ym, yp), *plane_pair(field))


def excess_of(conc, pot, conc_beside, pot_beside, faces, diagonal, mass_source, pot_source):
    excess_mass = (mass_source - conc) - diagonal * pot
    for face, other in zip(faces, pot_beside):
        excess_mass = excess_mass + face * other
    beside = conc_beside[0]
    for other in conc_beside[1:]:
        beside = beside + other
    excess_pot = (pot_source - pot) + (split_slope + 6.0 * interface) * conc - interface * beside
    return excess_mass, excess_pot


def scale_from(diagonal):
    return relax_fine / (1.0 + (split_slope + 6.0 * interface) * diagonal)


def relax_pair(conc, pot, excess_mass, excess_pot, diagonal, scale):
    new_conc = conc + (excess_mass - diagonal * excess_pot) * scale
    new_pot = pot + (excess_pot + (split_slope + 6.0 * interface) * excess_mass) * scale
    return new_conc, new_pot


def faces_of(mobility, beside):
    faces = tuple((0.5 * time_step) * (mobility + other) for other in beside)
    diagonal = faces[0]
    for face in faces[1:]:
        diagonal = diagonal + face
    return faces, diagonal


def split_dot(ones, values, contract):
    dims = (contract, ((), ()))
    total = None
    rest = values
    for _ in range(3):
        term = rest.astype(BF16)
        rest = rest - term.astype(F32)
        part = lax.dot_general(ones, term, dims, preferred_element_type=F32)
        total = part if total is None else total + part
    return total


def three_terms(values):
    out = []
    for _ in range(3):
        out.append(values.astype(BF16).astype(F32))
        values = values - out[-1]
    return jnp.concatenate(out, axis=0)


def round_up(value, unit):
    return -(-value // unit) * unit


class Plan:
    def __init__(self, shape, owners, groups):
        self.x, self.y, self.p = shape
        self.owners, self.groups = owners, groups
        self.half_x, self.half_y = self.x // 2, self.y // 2
        self.columns = self.half_x * self.half_y
        self.map_row = round_up(8 * self.x, 8)
        self.y_rows = self.map_row + owners
        self.cells = self.x * self.y
        self.rows = (self.half_x + 2) * self.y
        self.low_row = owners
        self.high_row = owners + self.half_x
        self.slot_parts = -(-(owners + 2 * self.half_x) // 4)
        slots = owners * groups
        self.slots = slots if slots <= 64 else 0


def side_rows(plan, rows, which):
    return rows[which * plan.y : (which + 1) * plan.y][None]


def side_columns(plan, rows, which):
    return rows[which * plan.x : (which + 1) * plan.x][:, None]


def membership(plan, owner_ref):
    g = lax.axis_index("gx")
    last = plan.owners - 1
    owner = iota((plan.owners, plan.columns), 0)
    low, high = plan.half_x, plan.half_x + 1
    shape = (plan.half_x + 2, plan.y, plan.columns)
    x, y, column = iota(shape, 0), iota(shape, 1), iota(shape, 2)
    half = jnp.where(x < low, x, jnp.where(x == low, plan.half_x - 1, 0))
    place = column == half * plan.half_y + (y >> 1)
    sides = (
        (x < low, g, True),
        (x == low, jnp.maximum(g - 1, 0), g > 0),
        (x == high, jnp.minimum(g + 1, last), g < last),
    )
    gather, spread = None, None
    for part, row, inside in sides:
        hits = ((owner_ref[pl.ds(row, 1), :] == owner) & inside).astype(F32).astype(BF16)
        where = (place & part).astype(F32).reshape(plan.rows, plan.columns).astype(BF16)
        nt = (((1,), (1,)), ((), ()))
        some = lax.dot_general(hits, where, nt, preferred_element_type=F32)
        gather = some if gather is None else gather + some
        some = lax.dot_general(where, hits, nt, preferred_element_type=F32)
        spread = some if spread is None else spread + some
    return gather, jnp.concatenate([spread] * 3, axis=1)


def scale_of(plan, owners):
    owner = iota((plan.owners, plan.columns), 0).astype(owners.dtype)
    hits = jnp.zeros((plan.owners, plan.columns), F32)
    for g in range(plan.owners):
        hits = hits + (owners[g : g + 1] == owner).astype(F32)
    count = jnp.sum(hits, axis=1, keepdims=True)
    return jnp.broadcast_to(0.125 / jnp.maximum(count, 1.0), (plan.owners, plan.p))


def mobility_of(mask, kind, table):
    values = jnp.zeros(kind.shape, F32)
    for marker, value in enumerate(table):
        values = jnp.where(kind == marker, value, values)
    return mask.astype(F32) * values


def even(axis):
    return lax.rem(lax.axis_index(axis), 2) == 0


def put_x(plan, lows, highs, near, far):
    up = even("gx")
    for which, (low, high) in enumerate(zip(lows, highs)):
        near[pl.ds(which * plan.y, plan.y), :] = jnp.where(up, high, low)
        far[pl.ds(which * plan.y, plan.y), :] = jnp.where(up, low, high)


def received(axis, near_ref, far_ref):
    up = even(axis)
    rows = pl.ds(0, min(near_ref.shape[0], far_ref.shape[0]))
    near, far = near_ref[rows, :], far_ref[rows, :]
    return jnp.where(up, far, near), jnp.where(up, near, far)


def prepare_kernel(plan, *refs):
    hbm, refs = refs[:8], refs[8:]
    x_near_ref, x_far_ref, y_near_ref, y_far_ref = refs[:4]
    x_refs, y_refs, (owner_ref, table_ref, sems) = refs[4:8], refs[8:14], refs[14:]
    copies = []

    def start(source, target):
        copies.append(pltpu.make_async_copy(source, target, sems.at[len(copies)]))
        copies[-1].start()

    start(hbm[7], table_ref)
    start(hbm[6], owner_ref)
    for source, target in zip(hbm[:4], x_refs):
        start(source.at[0], target.at[0])
        start(source.at[plan.x - 1], target.at[1])
    for source, target in zip(hbm[:6], y_refs):
        start(source.at[:, pl.ds(0, 8)], target.at[0])
        start(source.at[:, pl.ds(plan.y - 8, 8)], target.at[1])
    for copy in copies:
        copy.wait()
    table = [table_ref[marker] for marker in range(table_ref.shape[0])]
    conc, pot, mask, kind = (ref[...] for ref in x_refs)
    fields = (conc, pot, mobility_of(mask, kind, table))
    put_x(plan, [f[0] for f in fields], [f[1] for f in fields], x_near_ref, x_far_ref)
    conc, pot, mask, kind, mass, pots = (ref[...] for ref in y_refs)
    fields = (conc, pot, mobility_of(mask, kind, table))
    up = even("gy")
    rows = [(field, at) for at in range(2) for field in fields] + [(mass, 0), (pots, 0)]
    for which, (field, at) in enumerate(rows):
        for x in range(plan.x):
            low, high = field[0, x, at : at + 1], field[1, x, 7 - at : 8 - at]
            y_near_ref[pl.ds(which * plan.x + x, 1), :] = jnp.where(up, high, low)
            y_far_ref[pl.ds(which * plan.x + x, 1), :] = jnp.where(up, low, high)
    used = 8 * plan.x
    for ref in (y_near_ref, y_far_ref):
        ref[pl.ds(used, plan.y_rows - used), :] = jnp.zeros((plan.y_rows - used, plan.p), F32)
        ref[pl.ds(plan.map_row, plan.owners), pl.ds(0, plan.columns)] = owner_ref[...].astype(F32)


def local_kernel(
    plan, mask_ref, class_ref, table_ref, owner_ref, mob_ref, gather_ref, spread_ref, scale_ref
):
    table = [table_ref[marker] for marker in range(table_ref.shape[0])]
    mob_ref[...] = mobility_of(mask_ref[...], class_ref[...], table)
    gather_ref[...], spread_ref[...] = membership(plan, owner_ref)
    scale_ref[...] = scale_of(plan, owner_ref[...])


def first_kernel(
    plan, x_near_ref, x_far_ref, y_near_ref, y_far_ref,
    conc_ref, pot_ref, mob_ref, mass_ref, pots_ref, gather_ref, scale_ref, owner_ref,
    conc_out, pot_out, total_hbm, raw_out, x_near_out, x_far_out, total_out, sems,
):
    sides = received("gx", x_near_ref, x_far_ref)
    ends = received("gy", y_near_ref, y_far_ref)

    def halo(which):
        return tuple(side_rows(plan, rows, which) for rows in sides) + tuple(
            side_columns(plan, rows, which) for rows in ends
        )

    mobility, mob_halo = mob_ref[...], halo(2)
    faces, diagonal = faces_of(mobility, neighbours(mobility, mob_halo))
    mass_source, pot_source = mass_ref[...], pots_ref[...]
    conc, pot = conc_ref[...], pot_ref[...]
    for at, field in enumerate((conc, pot)):
        for x in range(plan.x):
            raw_out[pl.ds(2 * at * plan.x + x, 1), :] = field[x, 0:1]
            raw_out[pl.ds((2 * at + 1) * plan.x + x, 1), :] = field[x, plan.y - 1 : plan.y]
    excess = excess_of(
        conc, pot, neighbours(conc, halo(0)), neighbours(pot, halo(1)), faces, diagonal,
        mass_source, pot_source,
    )
    conc, pot = relax_pair(conc, pot, *excess, diagonal, scale_from(diagonal))
    conc_out[...] = conc
    pot_out[...] = pot
    put_x(plan, (conc[0], pot[0]), (conc[plan.x - 1], pot[plan.x - 1]), x_near_out, x_far_out)
    up = even("gx")
    base = 2 * plan.y
    for which in range(3):
        for end, rows in enumerate(ends):
            low = rows[which * plan.x : which * plan.x + 1]
            high = rows[(which + 1) * plan.x - 1 : (which + 1) * plan.x]
            x_near_out[pl.ds(base + 2 * which + end, 1), :] = jnp.where(up, high, low)
            x_far_out[pl.ds(base + 2 * which + end, 1), :] = jnp.where(up, low, high)
    for ref in (x_near_out, x_far_out):
        ref[pl.ds(base + 6, 2), :] = jnp.zeros((2, plan.p), F32)

    nothing = tuple(jnp.zeros_like(part) for part in mob_halo)
    own_mass, own_pot = excess_of(
        conc, pot, neighbours(conc, nothing), neighbours(pot, nothing), faces, diagonal,
        mass_source, pot_source,
    )
    give_mass, give_pot = (
        [field[x] + field[x + 1] for x in range(0, plan.x, 2)] for field in (own_mass, own_pot)
    )
    for x, side in ((0, 0), (plan.x - 1, 1)):
        face = 0.5 * (mobility[x] + mob_halo[side][0])
        give_mass.append(time_step * face * pot[x])
        give_pot.append(-interface * conc[x])

    def packed(mass, other):
        first = iota(mass.shape, 1) & 1 == 0
        return jnp.where(
            first, mass + pltpu.roll(mass, plan.p - 1, 1), other + pltpu.roll(other, 1, 1)
        )

    give = packed(jnp.concatenate(give_mass, axis=0), jnp.concatenate(give_pot, axis=0))
    h = lax.axis_index("gy")
    inside = (h > 0, None, h < plan.groups - 1)
    maps = [rows[plan.map_row : plan.map_row + plan.owners, : plan.columns] for rows in ends]
    maps.insert(1, owner_ref[...].astype(F32))
    owner = iota((plan.owners, 1), 0)
    is_mine = owner == lax.axis_index("gx")

    sums = [None, split_dot(gather_ref[...].astype(BF16), give, ((1,), (0,))), None]
    sums[1] = sums[1] * scale_ref[...]
    for place, y, at, side in ((0, 0, plan.half_y - 1, 2), (2, plan.y - 1, 0, 3)):
        edge_mob, edge_pot, edge_conc = (
            jnp.concatenate([field[x, y : y + 1] for x in range(plan.x)], axis=0)
            for field in (mobility, pot, conc)
        )
        face = 0.5 * (edge_mob + mob_halo[side][:, 0])
        both = packed(time_step * face * edge_pot, -interface * edge_conc)
        part = jnp.zeros((plan.owners, plan.p), F32)
        for i in range(plan.half_x):
            column = owner_column(plan, maps[place], i, at)
            ident = jnp.sum(jnp.where(is_mine, column, 0.0), axis=0, keepdims=True)
            pair = both[2 * i : 2 * i + 1] + both[2 * i + 1 : 2 * i + 2]
            part = part + jnp.where((owner.astype(F32) == ident) & inside[place], pair, 0.0)
        sums[place] = part * scale_of(plan, maps[place])
    if not plan.slots:
        total_out[...] = jnp.concatenate(sums, axis=0)
        copy = pltpu.make_async_copy(total_out, total_hbm, sems.at[0])
        copy.start()
        copy.wait()
        return

    def picked(place, i, at):
        column = owner_column(plan, maps[place], i, at)
        ident = jnp.broadcast_to(column, (plan.owners, plan.p))
        out = jnp.zeros((plan.owners, plan.p), F32)
        for o in range(plan.owners):
            out = jnp.where(ident == float(o), sums[place][o : o + 1], out)
        return out

    below = [[picked(k, i, plan.half_y - 1) for i in range(plan.half_x)] for k in range(3)]
    above = [[picked(k, i, 0) for i in range(plan.half_x)] for k in range(3)]

    def of_plane(plane, choices):
        out = jnp.zeros((plan.owners, plan.p), F32)
        for k in range(3):
            out = jnp.where(plane == h + (k - 1), choices[k], out)
        return out

    size = 4 * plan.slot_parts
    rows = []
    for plane in range(plan.groups):
        beside = []
        for i in range(plan.half_x):
            beside.append((plan.low_row + i, of_plane(plane - 1, [k[i] for k in below])))
            beside.append((plan.high_row + i, of_plane(plane + 1, [k[i] for k in above])))
        blank = jnp.zeros((plan.owners, plan.p), F32)
        beside += [(at, blank) for at in range(plan.high_row + plan.half_x, size)]
        rows.append((of_plane(plane, sums), beside))
    copies = []
    for g in range(plan.owners):
        for plane, (main, beside) in enumerate(rows):
            slot = g * plan.groups + plane
            for part in range(plan.owners // 4):
                total_out[slot, part] = main[4 * part : 4 * part + 4]
            for row, values in beside:
                total_out[slot, row // 4, pl.ds(row % 4, 1), :] = values[g : g + 1]
        if g % 2:
            some = pl.ds((g - 1) * plan.groups, 2 * plan.groups)
            copies.append(
                pltpu.make_async_copy(total_out.at[some], total_hbm.at[some], sems.at[g // 2])
            )
            copies[-1].start()
    for copy in copies:
        copy.wait()


def owner_column(plan, owners, i, at):
    b = i * plan.half_y + at
    return owners[:, b : b + 1]


def coarse_solve(packed, planes):
    lane = iota(packed.shape, 1)
    even = lane & 1 == 0
    mass_mean = jnp.where(even, packed, pltpu.roll(packed, 1, 1))
    pot_mean = jnp.where(even, pltpu.roll(packed, planes - 1, 1), packed)

    def neighbour_sum(values):
        return jnp.where(lane >= 2, pltpu.roll(values, 2, 1), 0.0) + jnp.where(
            lane < planes - 2, pltpu.roll(values, planes - 2, 1), 0.0
        )

    def step(mass_gap, pot_gap):
        scale = relax_coarse / coarse_det
        return (
            scale * (mass_gap - 2.0 * coarse_flux * pot_gap),
            scale * (pot_gap + (split_slope + 2.0 * coarse_bend) * mass_gap),
        )

    coarse_conc, coarse_pot = step(mass_mean, pot_mean)
    for _ in range(CSWEEP - 1):
        mass_gap = mass_mean - (
            coarse_conc + coarse_flux * (2.0 * coarse_pot - neighbour_sum(coarse_pot))
        )
        pot_gap = pot_mean - (
            coarse_pot
            - split_slope * coarse_conc
            + coarse_bend * (neighbour_sum(coarse_conc) - 2.0 * coarse_conc)
        )
        more_conc, more_pot = step(mass_gap, pot_gap)
        coarse_conc, coarse_pot = coarse_conc + more_conc, coarse_pot + more_pot
    return coarse_conc, coarse_pot


def beside_kernel(
    plan, x_near_ref, x_far_ref, mob_ref, raw_ref, x_near_msg, x_far_msg, y_near_msg, y_far_msg,
    faces_out, diagonal_out, scale_out, ends_out,
):
    mobility = mob_ref[...]
    sides = received("gx", x_near_msg, x_far_msg)
    ends = received("gy", y_near_msg, y_far_msg)
    halo = tuple(side_rows(plan, rows, 2) for rows in sides) + tuple(
        side_columns(plan, rows, 2) for rows in ends
    )
    faces, diagonal = faces_of(mobility, neighbours(mobility, halo))
    for i, face in enumerate(faces):
        faces_out[i] = face
    diagonal_out[...] = diagonal
    scale_out[...] = scale_from(diagonal)

    corners = received("gx", x_near_ref, x_far_ref)
    h = lax.axis_index("gy")
    inside = (h > 0, h < plan.groups - 1)
    own_mob = [
        jnp.concatenate([mobility[x, y : y + 1] for x in range(plan.x)], axis=0)
        for y in (0, plan.y - 1)
    ]
    for end, rows in enumerate(ends):

        def row(which):
            return rows[which * plan.x : (which + 1) * plan.x]

        def beside(which, own):
            here = row(which)
            at = 2 * plan.y + 2 * which + end
            wide = jnp.concatenate([corners[0][at : at + 1], here, corners[1][at : at + 1]], axis=0)
            return (
                wide[: plan.x], wide[2:], own, row(which + 3),
                *(part[0] for part in plane_pair(here[None])),
            )

        raw = [
            raw_ref[pl.ds((2 * which + end) * plan.x, plan.x), :] for which in range(2)
        ]
        faces, diagonal = faces_of(row(2), beside(2, own_mob[end]))
        excess = excess_of(
            row(0), row(1), beside(0, raw[0]), beside(1, raw[1]), faces, diagonal, row(6), row(7)
        )
        new = relax_pair(row(0), row(1), *excess, diagonal, scale_from(diagonal))
        for which, values in enumerate(new):
            ends_out[pl.ds((2 * which + end) * plan.x, plan.x), :] = jnp.where(
                inside[end], values, 0.0
            )


def last_kernel(
    plan, conc_ref, pot_ref, mass_ref, pots_ref, faces_ref, diagonal_ref, scale_ref,
    x_near_ref, x_far_ref, ends_ref, spread_ref, total_ref,
    conc_hbm, pot_hbm, conc_out, pot_out, sems,
):
    parts = []
    for part in range(plan.slot_parts):
        terms = [total_ref[slot, part] for slot in range(total_ref.shape[0])]
        while len(terms) > 1:
            pairs = [a + b for a, b in zip(terms[::2], terms[1::2])]
            terms = pairs + terms[len(pairs) * 2 :]
        parts.append(terms[0])
    solved = jnp.concatenate(
        coarse_solve(jnp.concatenate(parts, axis=0), plan.p), axis=1
    )
    own = lax.dot_general(
        spread_ref[...].astype(BF16),
        three_terms(solved[: plan.owners]).astype(BF16),
        (((1,), (0,)), ((), ())),
        preferred_element_type=F32,
    )
    sides = received("gx", x_near_ref, x_far_ref)

    def updated(which, ref):
        lanes = slice(which * plan.p, (which + 1) * plan.p)
        corr = own[:, lanes]
        slabs = [side_rows(plan, sides[0], which)]
        slabs += [ref[pl.ds(x, 1)] for x in range(plan.x)]
        slabs.append(side_rows(plan, sides[1], which))
        order = [plan.half_x, *[x >> 1 for x in range(plan.x)], plan.half_x + 1]
        slabs = [
            slab + corr[x * plan.y : (x + 1) * plan.y][None] for slab, x in zip(slabs, order)
        ]
        ends = []
        for end, begin in enumerate((plan.low_row, plan.high_row)):
            rows = ends_ref[pl.ds((2 * which + end) * plan.x, plan.x), :]
            ends.append([
                (rows[x : x + 1] + solved[begin + (x >> 1) : begin + (x >> 1) + 1, lanes])[None]
                for x in range(plan.x)
            ])
        return slabs, ends

    conc, conc_ends = updated(0, conc_ref)
    pot, pot_ends = updated(1, pot_ref)

    def beside(slabs, ends, x):
        here = slabs[x + 1]
        return (
            slabs[x], slabs[x + 2], *y_pair(here, ends[0][x], ends[1][x]), *plane_pair(here)
        )

    copies = []
    for x in range(plan.x):
        one = pl.ds(x, 1)
        diagonal = diagonal_ref[one]
        excess = excess_of(
            conc[x + 1], pot[x + 1], beside(conc, conc_ends, x), beside(pot, pot_ends, x),
            [faces_ref[i, one] for i in range(6)], diagonal, mass_ref[one], pots_ref[one],
        )
        conc_out[one], pot_out[one] = relax_pair(
            conc[x + 1], pot[x + 1], *excess, diagonal, scale_ref[one]
        )
        for source, target in ((conc_out, conc_hbm), (pot_out, pot_hbm)):
            copies.append(
                pltpu.make_async_copy(source.at[one], target.at[one], sems.at[len(copies)])
            )
            copies[-1].start()
    for copy in copies:
        copy.wait()


def call(kernel, plan, outs, args, far=(), smem=(), scratch=(), out_far=()):
    def space(i):
        return pl.ANY if i in far else pltpu.SMEM if i in smem else pltpu.VMEM

    return pl.pallas_call(
        functools.partial(kernel, plan),
        out_shape=[jax.ShapeDtypeStruct(shape, F32) for shape in outs],
        in_specs=[pl.BlockSpec(memory_space=space(i)) for i in range(len(args))],
        out_specs=[
            pl.BlockSpec(memory_space=pl.ANY if i in out_far else pltpu.VMEM)
            for i in range(len(outs))
        ],
        scratch_shapes=list(scratch),
        compiler_params=pltpu.CompilerParams(vmem_limit_bytes=VMEM_LIMIT),
    )(*[
        pltpu.with_memory_space_constraint(arg, pltpu.HBM) if i in far else arg
        for i, arg in enumerate(args)
    ])


def swap_near(axis, rows, begin=0):
    pairs = [(i, i + 1) for i in range(begin, lax.axis_size(axis) - 1, 2)]
    return lax.ppermute(rows, axis, pairs + [(j, i) for i, j in pairs])


def swap_far(axis, rows):
    return swap_near(axis, rows, 1)


def gather_totals(plan, total, y_near, y_far):
    if plan.slots:
        return lax.all_to_all(total, ("gx", "gy"), split_axis=0, concat_axis=0, tiled=True)
    shape = (plan.groups, 3, plan.owners, plan.p)
    parts = lax.all_gather(lax.psum(total, "gx"), "gy").reshape(shape)
    blank = jnp.zeros((1, plan.owners, plan.p), F32)
    to_below, own, to_above = (parts[:, k] for k in range(3))
    own = own + jnp.concatenate([blank, to_above[:-1]]) + jnp.concatenate([to_below[1:], blank])
    own = jnp.concatenate([blank, own, blank])
    g, h = lax.axis_index("gx"), lax.axis_index("gy")
    rows = [lax.dynamic_index_in_dim(own, h + 1, 0, False)]
    up = lax.rem(h, 2) == 0
    for place, at, msg in (
        (h, plan.half_y - 1, jnp.where(up, y_far, y_near)),
        (h + 2, 0, jnp.where(up, y_near, y_far)),
    ):
        ident = lax.dynamic_index_in_dim(msg, plan.map_row + g, 0, False).astype(jnp.int32)
        ident = jnp.stack([ident[i * plan.half_y + at] for i in range(plan.half_x)])
        rows.append(lax.dynamic_index_in_dim(own, place, 0, False)[ident])
    rows = jnp.concatenate(rows)
    rows = jnp.pad(rows, ((0, 4 * plan.slot_parts - rows.shape[0]), (0, 0)))
    return rows.reshape(1, plan.slot_parts, 4, plan.p)


def on_device(conc, pot, mass_source, pot_source, mask, kind, table, owner_map):
    plan = Plan(conc.shape, lax.axis_size("gx"), lax.axis_size("gy"))
    block = conc.shape
    fields = [conc, pot, mask, kind, mass_source, pot_source]
    messages = call(
        prepare_kernel,
        plan,
        [*[(3 * plan.y, plan.p)] * 2, *[(plan.y_rows, plan.p)] * 2],
        [*fields, owner_map, table],
        far=range(8),
        scratch=(
            *[pltpu.VMEM((2, plan.y, plan.p), field.dtype) for field in fields[:4]],
            *[pltpu.VMEM((2, plan.x, 8, plan.p), field.dtype) for field in fields],
            pltpu.VMEM(owner_map.shape, owner_map.dtype),
            pltpu.SMEM(table.shape, table.dtype),
            pltpu.SemaphoreType.DMA((22,)),
        ),
    )
    x_near, x_far = swap_near("gx", messages[0]), swap_far("gx", messages[1])
    y_near, y_far = swap_near("gy", messages[2]), swap_far("gy", messages[3])
    x_near, mask, kind = lax.optimization_barrier((x_near, mask, kind))
    mob, gather, spread, scale = call(
        local_kernel,
        plan,
        [block, (plan.owners, plan.rows), (plan.rows, 3 * plan.owners), (plan.owners, plan.p)],
        [mask, kind, table, owner_map],
        smem=(2,),
    )
    slots = (plan.slots, plan.slot_parts, 4, plan.p) if plan.slots else (3 * plan.owners, plan.p)
    conc, pot, total, raw, near, far = call(
        first_kernel,
        plan,
        [
            block,
            block,
            slots,
            (4 * plan.x, plan.p),
            *[(2 * plan.y + 8, plan.p)] * 2,
        ],
        [
            x_near, x_far, y_near, y_far,
            conc, pot, mob, mass_source, pot_source, gather, scale, owner_map,
        ],
        out_far=(2,),
        scratch=(pltpu.VMEM(slots, F32), pltpu.SemaphoreType.DMA((plan.owners // 2,))),
    )
    total = gather_totals(plan, total, y_near, y_far)
    far = swap_far("gx", far)
    near = swap_near("gx", near)
    faces, diagonal, scale, ends = call(
        beside_kernel,
        plan,
        [(6, *block), block, block, (4 * plan.x, plan.p)],
        [near, far, mob, raw, x_near, x_far, y_near, y_far],
    )
    return tuple(
        call(
            last_kernel,
            plan,
            [block, block],
            [conc, pot, mass_source, pot_source, faces, diagonal, scale, near, far, ends, spread, total],
            out_far=(0, 1),
            scratch=(
                pltpu.VMEM(block, F32),
                pltpu.VMEM(block, F32),
                pltpu.SemaphoreType.DMA((2 * plan.x,)),
            ),
        )
    )


def solution(mesh):
    grid = P("gx", "gy", None)
    return jax.shard_map(
        on_device,
        mesh=mesh,
        in_specs=(grid,) * 6 + (P(), P(None, "gy")),
        out_specs=(grid, grid),
        check_vma=False,
    )
```

```python
import functools

import jax
import jax.numpy as jnp
from jax import lax
from jax.experimental import pallas as pl
from jax.experimental.pallas import tpu as pltpu
from jax.sharding import PartitionSpec as P

CSWEEP = 3

time_step = 0.25
split_slope = 1.0
interface = 0.5
relax_fine = 0.6
relax_coarse = 0.6
coarse_flux = 0.0625
coarse_bend = 0.125
coarse_det = 1.0 + 2.0 * coarse_flux * (split_slope + 2.0 * coarse_bend)

F32 = jnp.float32
BF16 = jnp.bfloat16
VMEM_LIMIT = 48 * 1024 * 1024


def iota(shape, dim):
    return lax.broadcasted_iota(jnp.int32, shape, dim)


def x_pair(field, low, high):
    return (
        jnp.concatenate([low, field[:-1]], axis=0),
        jnp.concatenate([field[1:], high], axis=0),
    )


def y_pair(field, low, high):
    size = field.shape[1]
    where = iota(field.shape, 1)
    return (
        jnp.where(where == 0, low, pltpu.roll(field, 1, 1)),
        jnp.where(where == size - 1, high, pltpu.roll(field, size - 1, 1)),
    )


def plane_pair(field):
    size = field.shape[2]
    where = iota(field.shape, 2)
    return (
        jnp.where(where == 0, 0.0, pltpu.roll(field, 1, 2)),
        jnp.where(where == size - 1, 0.0, pltpu.roll(field, size - 1, 2)),
    )


def neighbours(field, halo):
    xm, xp, ym, yp = halo
    return (*x_pair(field, xm, xp), *y_pair(field, ym, yp), *plane_pair(field))


def excess_of(conc, pot, conc_beside, pot_beside, faces, diagonal, mass_source, pot_source):
    excess_mass = (mass_source - conc) - diagonal * pot
    for face, other in zip(faces, pot_beside):
        excess_mass = excess_mass + face * other
    beside = conc_beside[0]
    for other in conc_beside[1:]:
        beside = beside + other
    excess_pot = (pot_source - pot) + (split_slope + 6.0 * interface) * conc - interface * beside
    return excess_mass, excess_pot


def scale_from(diagonal):
    return relax_fine / (1.0 + (split_slope + 6.0 * interface) * diagonal)


def relax_pair(conc, pot, excess_mass, excess_pot, diagonal, scale):
    new_conc = conc + (excess_mass - diagonal * excess_pot) * scale
    new_pot = pot + (excess_pot + (split_slope + 6.0 * interface) * excess_mass) * scale
    return new_conc, new_pot


def faces_of(mobility, beside):
    faces = tuple((0.5 * time_step) * (mobility + other) for other in beside)
    diagonal = faces[0]
    for face in faces[1:]:
        diagonal = diagonal + face
    return faces, diagonal


def split_dot(ones, values, contract):
    dims = (contract, ((), ()))
    total = None
    rest = values
    for _ in range(3):
        term = rest.astype(BF16)
        rest = rest - term.astype(F32)
        part = lax.dot_general(ones, term, dims, preferred_element_type=F32)
        total = part if total is None else total + part
    return total


def three_terms(values):
    out = []
    for _ in range(3):
        out.append(values.astype(BF16).astype(F32))
        values = values - out[-1]
    return jnp.concatenate(out, axis=0)


def round_up(value, unit):
    return -(-value // unit) * unit


class Plan:
    def __init__(self, shape, owners, groups):
        self.x, self.y, self.p = shape
        self.owners, self.groups = owners, groups
        self.half_x, self.half_y = self.x // 2, self.y // 2
        self.columns = self.half_x * self.half_y
        self.map_row = round_up(8 * self.x, 8)
        self.y_rows = self.map_row + owners
        self.y_near_rows = max(self.y_rows, 3 * self.y + 8)
        self.cells = self.x * self.y
        self.rows = (self.half_x + 2) * self.y
        self.low_row = owners
        self.high_row = owners + self.half_x
        self.slot_parts = -(-(owners + 2 * self.half_x) // 4)
        slots = owners * groups
        self.slots = slots if slots <= 64 else 0


def side_rows(plan, rows, which):
    return rows[which * plan.y : (which + 1) * plan.y][None]


def side_columns(plan, rows, which):
    return rows[which * plan.x : (which + 1) * plan.x][:, None]


def membership(plan, owner_ref):
    g = lax.axis_index("gx")
    last = plan.owners - 1
    owner = iota((plan.owners, plan.columns), 0)
    low, high = plan.half_x, plan.half_x + 1
    shape = (plan.half_x + 2, plan.y, plan.columns)
    x, y, column = iota(shape, 0), iota(shape, 1), iota(shape, 2)
    half = jnp.where(x < low, x, jnp.where(x == low, plan.half_x - 1, 0))
    place = column == half * plan.half_y + (y >> 1)
    sides = (
        (x < low, g, True),
        (x == low, jnp.maximum(g - 1, 0), g > 0),
        (x == high, jnp.minimum(g + 1, last), g < last),
    )
    gather, spread = None, None
    for part, row, inside in sides:
        hits = ((owner_ref[pl.ds(row, 1), :] == owner) & inside).astype(F32).astype(BF16)
        where = (place & part).astype(F32).reshape(plan.rows, plan.columns).astype(BF16)
        nt = (((1,), (1,)), ((), ()))
        some = lax.dot_general(hits, where, nt, preferred_element_type=F32)
        gather = some if gather is None else gather + some
        some = lax.dot_general(where, hits, nt, preferred_element_type=F32)
        spread = some if spread is None else spread + some
    return gather, jnp.concatenate([spread] * 3, axis=1)


def scale_of(plan, owners):
    owner = iota((plan.owners, plan.columns), 0).astype(owners.dtype)
    hits = jnp.zeros((plan.owners, plan.columns), F32)
    for g in range(plan.owners):
        hits = hits + (owners[g : g + 1] == owner).astype(F32)
    count = jnp.sum(hits, axis=1, keepdims=True)
    return jnp.broadcast_to(0.125 / jnp.maximum(count, 1.0), (plan.owners, plan.p))


def mobility_of(mask, kind, table):
    values = jnp.zeros(kind.shape, F32)
    for marker, value in enumerate(table):
        values = jnp.where(kind == marker, value, values)
    return mask.astype(F32) * values


def even(axis):
    return lax.rem(lax.axis_index(axis), 2) == 0


def put_x(plan, lows, highs, near, far):
    up = even("gx")
    for which, (low, high) in enumerate(zip(lows, highs)):
        near[pl.ds(which * plan.y, plan.y), :] = jnp.where(up, high, low)
        far[pl.ds(which * plan.y, plan.y), :] = jnp.where(up, low, high)


def received(axis, near_ref, far_ref):
    up = even(axis)
    rows = pl.ds(0, min(near_ref.shape[0], far_ref.shape[0]))
    near, far = near_ref[rows, :], far_ref[rows, :]
    return jnp.where(up, far, near), jnp.where(up, near, far)


def prepare_kernel(plan, *refs):
    hbm, refs = refs[:8], refs[8:]
    x_near_ref, x_far_ref, y_near_ref, y_far_ref = refs[:4]
    x_refs, y_refs, (owner_ref, table_ref, sems) = refs[4:8], refs[8:14], refs[14:]
    copies = []

    def start(source, target):
        copies.append(pltpu.make_async_copy(source, target, sems.at[len(copies)]))
        copies[-1].start()

    start(hbm[7], table_ref)
    start(hbm[6], owner_ref)
    for source, target in zip(hbm[:4], x_refs):
        start(source.at[0], target.at[0])
        start(source.at[plan.x - 1], target.at[1])
    for source, target in zip(hbm[:6], y_refs):
        start(source.at[:, pl.ds(0, 8)], target.at[0])
        start(source.at[:, pl.ds(plan.y - 8, 8)], target.at[1])
    for copy in copies:
        copy.wait()
    table = [table_ref[marker] for marker in range(table_ref.shape[0])]
    conc, pot, mask, kind = (ref[...] for ref in x_refs)
    fields = (conc, pot, mobility_of(mask, kind, table))
    put_x(plan, [f[0] for f in fields], [f[1] for f in fields], x_near_ref, x_far_ref)
    conc, pot, mask, kind, mass, pots = (ref[...] for ref in y_refs)
    fields = (conc, pot, mobility_of(mask, kind, table))
    up = even("gy")
    rows = [(field, at) for at in range(2) for field in fields] + [(mass, 0), (pots, 0)]
    for which, (field, at) in enumerate(rows):
        for x in range(plan.x):
            low, high = field[0, x, at : at + 1], field[1, x, 7 - at : 8 - at]
            y_near_ref[pl.ds(which * plan.x + x, 1), :] = jnp.where(up, high, low)
            y_far_ref[pl.ds(which * plan.x + x, 1), :] = jnp.where(up, low, high)
    used = 8 * plan.x
    for ref, rows in ((y_near_ref, plan.y_near_rows), (y_far_ref, plan.y_rows)):
        ref[pl.ds(used, rows - used), :] = jnp.zeros((rows - used, plan.p), F32)
        ref[pl.ds(plan.map_row, plan.owners), pl.ds(0, plan.columns)] = owner_ref[...].astype(F32)


def local_kernel(
    plan, mask_ref, class_ref, table_ref, owner_ref, mob_ref, gather_ref, spread_ref, scale_ref
):
    table = [table_ref[marker] for marker in range(table_ref.shape[0])]
    mob_ref[...] = mobility_of(mask_ref[...], class_ref[...], table)
    gather_ref[...], spread_ref[...] = membership(plan, owner_ref)
    scale_ref[...] = scale_of(plan, owner_ref[...])


def first_kernel(
    plan, x_far_ref, x_near_ref, y_far_ref, y_near_ref,
    conc_ref, pot_ref, mob_ref, mass_ref, pots_ref, gather_ref, scale_ref, owner_ref,
    conc_out, pot_out, total_hbm, raw_out, x_near_out, x_far_out, total_out, sems,
):
    sides = received("gx", x_near_ref, x_far_ref)
    ends = received("gy", y_near_ref, y_far_ref)

    def halo(which):
        return tuple(side_rows(plan, rows, which) for rows in sides) + tuple(
            side_columns(plan, rows, which) for rows in ends
        )

    mobility, mob_halo = mob_ref[...], halo(2)
    faces, diagonal = faces_of(mobility, neighbours(mobility, mob_halo))
    mass_source, pot_source = mass_ref[...], pots_ref[...]
    conc, pot = conc_ref[...], pot_ref[...]
    for at, field in enumerate((conc, pot)):
        for x in range(plan.x):
            raw_out[pl.ds(2 * at * plan.x + x, 1), :] = field[x, 0:1]
            raw_out[pl.ds((2 * at + 1) * plan.x + x, 1), :] = field[x, plan.y - 1 : plan.y]
    excess = excess_of(
        conc, pot, neighbours(conc, halo(0)), neighbours(pot, halo(1)), faces, diagonal,
        mass_source, pot_source,
    )
    conc, pot = relax_pair(conc, pot, *excess, diagonal, scale_from(diagonal))
    conc_out[...] = conc
    pot_out[...] = pot
    put_x(plan, (conc[0], pot[0]), (conc[plan.x - 1], pot[plan.x - 1]), x_near_out, x_far_out)
    up = even("gx")
    base = 2 * plan.y
    for which in range(3):
        for end, rows in enumerate(ends):
            low = rows[which * plan.x : which * plan.x + 1]
            high = rows[(which + 1) * plan.x - 1 : (which + 1) * plan.x]
            x_near_out[pl.ds(base + 2 * which + end, 1), :] = jnp.where(up, high, low)
            x_far_out[pl.ds(base + 2 * which + end, 1), :] = jnp.where(up, low, high)
    for ref in (x_near_out, x_far_out):
        ref[pl.ds(base + 6, 2), :] = jnp.zeros((2, plan.p), F32)

    nothing = tuple(jnp.zeros_like(part) for part in mob_halo)
    own_mass, own_pot = excess_of(
        conc, pot, neighbours(conc, nothing), neighbours(pot, nothing), faces, diagonal,
        mass_source, pot_source,
    )
    give_mass, give_pot = (
        [field[x] + field[x + 1] for x in range(0, plan.x, 2)] for field in (own_mass, own_pot)
    )
    for x, side in ((0, 0), (plan.x - 1, 1)):
        face = 0.5 * (mobility[x] + mob_halo[side][0])
        give_mass.append(time_step * face * pot[x])
        give_pot.append(-interface * conc[x])

    def packed(mass, other):
        first = iota(mass.shape, 1) & 1 == 0
        return jnp.where(
            first, mass + pltpu.roll(mass, plan.p - 1, 1), other + pltpu.roll(other, 1, 1)
        )

    give = packed(jnp.concatenate(give_mass, axis=0), jnp.concatenate(give_pot, axis=0))
    h = lax.axis_index("gy")
    inside = (h > 0, None, h < plan.groups - 1)
    maps = [rows[plan.map_row : plan.map_row + plan.owners, : plan.columns] for rows in ends]
    maps.insert(1, owner_ref[...].astype(F32))
    owner = iota((plan.owners, 1), 0)
    is_mine = owner == lax.axis_index("gx")

    sums = [None, split_dot(gather_ref[...].astype(BF16), give, ((1,), (0,))), None]
    sums[1] = sums[1] * scale_ref[...]
    for place, y, at, side in ((0, 0, plan.half_y - 1, 2), (2, plan.y - 1, 0, 3)):
        edge_mob, edge_pot, edge_conc = (
            jnp.concatenate([field[x, y : y + 1] for x in range(plan.x)], axis=0)
            for field in (mobility, pot, conc)
        )
        face = 0.5 * (edge_mob + mob_halo[side][:, 0])
        both = packed(time_step * face * edge_pot, -interface * edge_conc)
        part = jnp.zeros((plan.owners, plan.p), F32)
        for i in range(plan.half_x):
            column = owner_column(plan, maps[place], i, at)
            ident = jnp.sum(jnp.where(is_mine, column, 0.0), axis=0, keepdims=True)
            pair = both[2 * i : 2 * i + 1] + both[2 * i + 1 : 2 * i + 2]
            part = part + jnp.where((owner.astype(F32) == ident) & inside[place], pair, 0.0)
        sums[place] = part * scale_of(plan, maps[place])
    if not plan.slots:
        total_out[...] = jnp.concatenate(sums, axis=0)
        copy = pltpu.make_async_copy(total_out, total_hbm, sems.at[0])
        copy.start()
        copy.wait()
        return

    def picked(place, i, at):
        column = owner_column(plan, maps[place], i, at)
        ident = jnp.broadcast_to(column, (plan.owners, plan.p))
        out = jnp.zeros((plan.owners, plan.p), F32)
        for o in range(plan.owners):
            out = jnp.where(ident == float(o), sums[place][o : o + 1], out)
        return out

    below = [[picked(k, i, plan.half_y - 1) for i in range(plan.half_x)] for k in range(3)]
    above = [[picked(k, i, 0) for i in range(plan.half_x)] for k in range(3)]

    def of_plane(plane, choices):
        out = jnp.zeros((plan.owners, plan.p), F32)
        for k in range(3):
            out = jnp.where(plane == h + (k - 1), choices[k], out)
        return out

    size = 4 * plan.slot_parts
    rows = []
    for plane in range(plan.groups):
        beside = []
        for i in range(plan.half_x):
            beside.append((plan.low_row + i, of_plane(plane - 1, [k[i] for k in below])))
            beside.append((plan.high_row + i, of_plane(plane + 1, [k[i] for k in above])))
        blank = jnp.zeros((plan.owners, plan.p), F32)
        beside += [(at, blank) for at in range(plan.high_row + plan.half_x, size)]
        rows.append((of_plane(plane, sums), beside))
    copies = []
    for g in range(plan.owners):
        for plane, (main, beside) in enumerate(rows):
            slot = g * plan.groups + plane
            for part in range(plan.owners // 4):
                total_out[slot, part] = main[4 * part : 4 * part + 4]
            for row, values in beside:
                total_out[slot, row // 4, pl.ds(row % 4, 1), :] = values[g : g + 1]
        if g % 2:
            some = pl.ds((g - 1) * plan.groups, 2 * plan.groups)
            copies.append(
                pltpu.make_async_copy(total_out.at[some], total_hbm.at[some], sems.at[g // 2])
            )
            copies[-1].start()
    for copy in copies:
        copy.wait()


def owner_column(plan, owners, i, at):
    b = i * plan.half_y + at
    return owners[:, b : b + 1]


def coarse_solve(packed, planes):
    lane = iota(packed.shape, 1)
    even = lane & 1 == 0
    mass_mean = jnp.where(even, packed, pltpu.roll(packed, 1, 1))
    pot_mean = jnp.where(even, pltpu.roll(packed, planes - 1, 1), packed)

    def neighbour_sum(values):
        return jnp.where(lane >= 2, pltpu.roll(values, 2, 1), 0.0) + jnp.where(
            lane < planes - 2, pltpu.roll(values, planes - 2, 1), 0.0
        )

    def step(mass_gap, pot_gap):
        scale = relax_coarse / coarse_det
        return (
            scale * (mass_gap - 2.0 * coarse_flux * pot_gap),
            scale * (pot_gap + (split_slope + 2.0 * coarse_bend) * mass_gap),
        )

    coarse_conc, coarse_pot = step(mass_mean, pot_mean)
    for _ in range(CSWEEP - 1):
        mass_gap = mass_mean - (
            coarse_conc + coarse_flux * (2.0 * coarse_pot - neighbour_sum(coarse_pot))
        )
        pot_gap = pot_mean - (
            coarse_pot
            - split_slope * coarse_conc
            + coarse_bend * (neighbour_sum(coarse_conc) - 2.0 * coarse_conc)
        )
        more_conc, more_pot = step(mass_gap, pot_gap)
        coarse_conc, coarse_pot = coarse_conc + more_conc, coarse_pot + more_pot
    return coarse_conc, coarse_pot


def beside_kernel(
    plan, x_near_ref, x_far_ref, mob_ref, raw_ref, x_near_msg, x_far_msg, y_near_msg, y_far_msg,
    faces_out, diagonal_out, scale_out, ends_out,
):
    mobility = mob_ref[...]
    sides = received("gx", x_near_msg, x_far_msg)
    ends = received("gy", y_near_msg, y_far_msg)
    halo = tuple(side_rows(plan, rows, 2) for rows in sides) + tuple(
        side_columns(plan, rows, 2) for rows in ends
    )
    faces, diagonal = faces_of(mobility, neighbours(mobility, halo))
    for i, face in enumerate(faces):
        faces_out[i] = face
    diagonal_out[...] = diagonal
    scale_out[...] = scale_from(diagonal)

    corners = received("gx", x_near_ref, x_far_ref)
    h = lax.axis_index("gy")
    inside = (h > 0, h < plan.groups - 1)
    own_mob = [
        jnp.concatenate([mobility[x, y : y + 1] for x in range(plan.x)], axis=0)
        for y in (0, plan.y - 1)
    ]
    for end, rows in enumerate(ends):

        def row(which):
            return rows[which * plan.x : (which + 1) * plan.x]

        def beside(which, own):
            here = row(which)
            at = 2 * plan.y + 2 * which + end
            wide = jnp.concatenate([corners[0][at : at + 1], here, corners[1][at : at + 1]], axis=0)
            return (
                wide[: plan.x], wide[2:], own, row(which + 3),
                *(part[0] for part in plane_pair(here[None])),
            )

        raw = [
            raw_ref[pl.ds((2 * which + end) * plan.x, plan.x), :] for which in range(2)
        ]
        faces, diagonal = faces_of(row(2), beside(2, own_mob[end]))
        excess = excess_of(
            row(0), row(1), beside(0, raw[0]), beside(1, raw[1]), faces, diagonal, row(6), row(7)
        )
        new = relax_pair(row(0), row(1), *excess, diagonal, scale_from(diagonal))
        for which, values in enumerate(new):
            ends_out[pl.ds((2 * which + end) * plan.x, plan.x), :] = jnp.where(
                inside[end], values, 0.0
            )


def last_kernel(
    plan, conc_ref, pot_ref, mass_ref, pots_ref, faces_ref, diagonal_ref, scale_ref,
    x_near_ref, x_far_ref, ends_ref, spread_ref, total_ref,
    conc_hbm, pot_hbm, conc_out, pot_out, sems,
):
    parts = []
    for part in range(plan.slot_parts):
        terms = [total_ref[slot, part] for slot in range(total_ref.shape[0])]
        while len(terms) > 1:
            pairs = [a + b for a, b in zip(terms[::2], terms[1::2])]
            terms = pairs + terms[len(pairs) * 2 :]
        parts.append(terms[0])
    solved = jnp.concatenate(
        coarse_solve(jnp.concatenate(parts, axis=0), plan.p), axis=1
    )
    own = lax.dot_general(
        spread_ref[...].astype(BF16),
        three_terms(solved[: plan.owners]).astype(BF16),
        (((1,), (0,)), ((), ())),
        preferred_element_type=F32,
    )
    sides = received("gx", x_near_ref, x_far_ref)

    def updated(which, ref):
        lanes = slice(which * plan.p, (which + 1) * plan.p)
        corr = own[:, lanes]
        slabs = [side_rows(plan, sides[0], which)]
        slabs += [ref[pl.ds(x, 1)] for x in range(plan.x)]
        slabs.append(side_rows(plan, sides[1], which))
        order = [plan.half_x, *[x >> 1 for x in range(plan.x)], plan.half_x + 1]
        slabs = [
            slab + corr[x * plan.y : (x + 1) * plan.y][None] for slab, x in zip(slabs, order)
        ]
        ends = []
        for end, begin in enumerate((plan.low_row, plan.high_row)):
            rows = ends_ref[pl.ds((2 * which + end) * plan.x, plan.x), :]
            ends.append([
                (rows[x : x + 1] + solved[begin + (x >> 1) : begin + (x >> 1) + 1, lanes])[None]
                for x in range(plan.x)
            ])
        return slabs, ends

    conc, conc_ends = updated(0, conc_ref)
    pot, pot_ends = updated(1, pot_ref)

    def beside(slabs, ends, x):
        here = slabs[x + 1]
        return (
            slabs[x], slabs[x + 2], *y_pair(here, ends[0][x], ends[1][x]), *plane_pair(here)
        )

    copies = []
    for x in range(plan.x):
        one = pl.ds(x, 1)
        diagonal = diagonal_ref[one]
        excess = excess_of(
            conc[x + 1], pot[x + 1], beside(conc, conc_ends, x), beside(pot, pot_ends, x),
            [faces_ref[i, one] for i in range(6)], diagonal, mass_ref[one], pots_ref[one],
        )
        conc_out[one], pot_out[one] = relax_pair(
            conc[x + 1], pot[x + 1], *excess, diagonal, scale_ref[one]
        )
        for source, target in ((conc_out, conc_hbm), (pot_out, pot_hbm)):
            copies.append(
                pltpu.make_async_copy(source.at[one], target.at[one], sems.at[len(copies)])
            )
            copies[-1].start()
    for copy in copies:
        copy.wait()


def call(kernel, plan, outs, args, far=(), smem=(), scratch=(), out_far=()):
    def space(i):
        return pl.ANY if i in far else pltpu.SMEM if i in smem else pltpu.VMEM

    return pl.pallas_call(
        functools.partial(kernel, plan),
        out_shape=[jax.ShapeDtypeStruct(shape, F32) for shape in outs],
        in_specs=[pl.BlockSpec(memory_space=space(i)) for i in range(len(args))],
        out_specs=[
            pl.BlockSpec(memory_space=pl.ANY if i in out_far else pltpu.VMEM)
            for i in range(len(outs))
        ],
        scratch_shapes=list(scratch),
        compiler_params=pltpu.CompilerParams(vmem_limit_bytes=VMEM_LIMIT),
    )(*[
        pltpu.with_memory_space_constraint(arg, pltpu.HBM) if i in far else arg
        for i, arg in enumerate(args)
    ])


def swap_near(axis, rows, begin=0):
    pairs = [(i, i + 1) for i in range(begin, lax.axis_size(axis) - 1, 2)]
    return lax.ppermute(rows, axis, pairs + [(j, i) for i, j in pairs])


def swap_far(axis, rows):
    return swap_near(axis, rows, 1)


def gather_totals(plan, total, y_near, y_far):
    if plan.slots:
        return lax.all_to_all(total, ("gx", "gy"), split_axis=0, concat_axis=0, tiled=True)
    shape = (plan.groups, 3, plan.owners, plan.p)
    parts = lax.all_gather(lax.psum(total, "gx"), "gy").reshape(shape)
    blank = jnp.zeros((1, plan.owners, plan.p), F32)
    to_below, own, to_above = (parts[:, k] for k in range(3))
    own = own + jnp.concatenate([blank, to_above[:-1]]) + jnp.concatenate([to_below[1:], blank])
    own = jnp.concatenate([blank, own, blank])
    g, h = lax.axis_index("gx"), lax.axis_index("gy")
    rows = [lax.dynamic_index_in_dim(own, h + 1, 0, False)]
    up = lax.rem(h, 2) == 0
    near = y_near[: y_far.shape[0]]
    for place, at, msg in (
        (h, plan.half_y - 1, jnp.where(up, y_far, near)),
        (h + 2, 0, jnp.where(up, near, y_far)),
    ):
        ident = lax.dynamic_index_in_dim(msg, plan.map_row + g, 0, False).astype(jnp.int32)
        ident = jnp.stack([ident[i * plan.half_y + at] for i in range(plan.half_x)])
        rows.append(lax.dynamic_index_in_dim(own, place, 0, False)[ident])
    rows = jnp.concatenate(rows)
    rows = jnp.pad(rows, ((0, 4 * plan.slot_parts - rows.shape[0]), (0, 0)))
    return rows.reshape(1, plan.slot_parts, 4, plan.p)


def on_device(conc, pot, mass_source, pot_source, mask, kind, table, owner_map):
    plan = Plan(conc.shape, lax.axis_size("gx"), lax.axis_size("gy"))
    block = conc.shape
    fields = [conc, pot, mask, kind, mass_source, pot_source]
    messages = call(
        prepare_kernel,
        plan,
        [*[(3 * plan.y, plan.p)] * 2, (plan.y_near_rows, plan.p), (plan.y_rows, plan.p)],
        [*fields, owner_map, table],
        far=range(8),
        scratch=(
            *[pltpu.VMEM((2, plan.y, plan.p), field.dtype) for field in fields[:4]],
            *[pltpu.VMEM((2, plan.x, 8, plan.p), field.dtype) for field in fields],
            pltpu.VMEM(owner_map.shape, owner_map.dtype),
            pltpu.SMEM(table.shape, table.dtype),
            pltpu.SemaphoreType.DMA((22,)),
        ),
    )
    x_near, x_far = swap_near("gx", messages[0]), swap_far("gx", messages[1])
    y_near, y_far = swap_near("gy", messages[2]), swap_far("gy", messages[3])
    y_near, mask, kind = lax.optimization_barrier((y_near, mask, kind))
    mob, gather, spread, scale = call(
        local_kernel,
        plan,
        [block, (plan.owners, plan.rows), (plan.rows, 3 * plan.owners), (plan.owners, plan.p)],
        [mask, kind, table, owner_map],
        smem=(2,),
    )
    slots = (plan.slots, plan.slot_parts, 4, plan.p) if plan.slots else (3 * plan.owners, plan.p)
    conc, pot, total, raw, near, far = call(
        first_kernel,
        plan,
        [
            block,
            block,
            slots,
            (4 * plan.x, plan.p),
            *[(2 * plan.y + 8, plan.p)] * 2,
        ],
        [
            x_far, x_near, y_far, y_near,
            conc, pot, mob, mass_source, pot_source, gather, scale, owner_map,
        ],
        out_far=(2,),
        scratch=(pltpu.VMEM(slots, F32), pltpu.SemaphoreType.DMA((plan.owners // 2,))),
    )
    total = gather_totals(plan, total, y_near, y_far)
    far = swap_far("gx", far)
    near = swap_near("gx", near)
    faces, diagonal, scale, ends = call(
        beside_kernel,
        plan,
        [(6, *block), block, block, (4 * plan.x, plan.p)],
        [near, far, mob, raw, x_near, x_far, y_near, y_far],
    )
    return tuple(
        call(
            last_kernel,
            plan,
            [block, block],
            [conc, pot, mass_source, pot_source, faces, diagonal, scale, near, far, ends, spread, total],
            out_far=(0, 1),
            scratch=(
                pltpu.VMEM(block, F32),
                pltpu.VMEM(block, F32),
                pltpu.SemaphoreType.DMA((2 * plan.x,)),
            ),
        )
    )


def solution(mesh):
    grid = P("gx", "gy", None)
    return jax.shard_map(
        on_device,
        mesh=mesh,
        in_specs=(grid,) * 6 + (P(), P(None, "gy")),
        out_specs=(grid, grid),
        check_vma=False,
    )
```

```python
import functools

import jax
import jax.numpy as jnp
from jax import lax
from jax.experimental import pallas as pl
from jax.experimental.pallas import tpu as pltpu
from jax.sharding import PartitionSpec as P

CSWEEP = 3

time_step = 0.25
split_slope = 1.0
interface = 0.5
relax_fine = 0.6
relax_coarse = 0.6
coarse_flux = 0.0625
coarse_bend = 0.125
coarse_det = 1.0 + 2.0 * coarse_flux * (split_slope + 2.0 * coarse_bend)

F32 = jnp.float32
BF16 = jnp.bfloat16
VMEM_LIMIT = 48 * 1024 * 1024


def iota(shape, dim):
    return lax.broadcasted_iota(jnp.int32, shape, dim)


def x_pair(field, low, high):
    return (
        jnp.concatenate([low, field[:-1]], axis=0),
        jnp.concatenate([field[1:], high], axis=0),
    )


def y_pair(field, low, high):
    size = field.shape[1]
    where = iota(field.shape, 1)
    return (
        jnp.where(where == 0, low, pltpu.roll(field, 1, 1)),
        jnp.where(where == size - 1, high, pltpu.roll(field, size - 1, 1)),
    )


def plane_pair(field):
    size = field.shape[2]
    where = iota(field.shape, 2)
    return (
        jnp.where(where == 0, 0.0, pltpu.roll(field, 1, 2)),
        jnp.where(where == size - 1, 0.0, pltpu.roll(field, size - 1, 2)),
    )


def neighbours(field, halo):
    xm, xp, ym, yp = halo
    return (*x_pair(field, xm, xp), *y_pair(field, ym, yp), *plane_pair(field))


def excess_of(conc, pot, conc_beside, pot_beside, faces, diagonal, mass_source, pot_source):
    excess_mass = (mass_source - conc) - diagonal * pot
    for face, other in zip(faces, pot_beside):
        excess_mass = excess_mass + face * other
    beside = conc_beside[0]
    for other in conc_beside[1:]:
        beside = beside + other
    excess_pot = (pot_source - pot) + (split_slope + 6.0 * interface) * conc - interface * beside
    return excess_mass, excess_pot


def scale_from(diagonal):
    return relax_fine / (1.0 + (split_slope + 6.0 * interface) * diagonal)


def relax_pair(conc, pot, excess_mass, excess_pot, diagonal, scale):
    new_conc = conc + (excess_mass - diagonal * excess_pot) * scale
    new_pot = pot + (excess_pot + (split_slope + 6.0 * interface) * excess_mass) * scale
    return new_conc, new_pot


def faces_of(mobility, beside):
    faces = tuple((0.5 * time_step) * (mobility + other) for other in beside)
    diagonal = faces[0]
    for face in faces[1:]:
        diagonal = diagonal + face
    return faces, diagonal


def split_dot(ones, values, contract):
    dims = (contract, ((), ()))
    total = None
    rest = values
    for _ in range(3):
        term = rest.astype(BF16)
        rest = rest - term.astype(F32)
        part = lax.dot_general(ones, term, dims, preferred_element_type=F32)
        total = part if total is None else total + part
    return total


def three_terms(values):
    out = []
    for _ in range(3):
        out.append(values.astype(BF16).astype(F32))
        values = values - out[-1]
    return jnp.concatenate(out, axis=0)


def round_up(value, unit):
    return -(-value // unit) * unit


class Plan:
    def __init__(self, shape, owners, groups):
        self.x, self.y, self.p = shape
        self.owners, self.groups = owners, groups
        self.half_x, self.half_y = self.x // 2, self.y // 2
        self.columns = self.half_x * self.half_y
        self.map_row = round_up(8 * self.x, 8)
        self.y_rows = self.map_row + owners
        self.y_far_rows = max(self.y_rows, 3 * self.y + 8)
        self.cells = self.x * self.y
        self.rows = (self.half_x + 2) * self.y
        self.low_row = owners
        self.high_row = owners + self.half_x
        self.slot_parts = -(-(owners + 2 * self.half_x) // 4)
        slots = owners * groups
        self.slots = slots if slots <= 64 else 0


def side_rows(plan, rows, which):
    return rows[which * plan.y : (which + 1) * plan.y][None]


def side_columns(plan, rows, which):
    return rows[which * plan.x : (which + 1) * plan.x][:, None]


def membership(plan, owner_ref):
    g = lax.axis_index("gx")
    last = plan.owners - 1
    owner = iota((plan.owners, plan.columns), 0)
    low, high = plan.half_x, plan.half_x + 1
    shape = (plan.half_x + 2, plan.y, plan.columns)
    x, y, column = iota(shape, 0), iota(shape, 1), iota(shape, 2)
    half = jnp.where(x < low, x, jnp.where(x == low, plan.half_x - 1, 0))
    place = column == half * plan.half_y + (y >> 1)
    sides = (
        (x < low, g, True),
        (x == low, jnp.maximum(g - 1, 0), g > 0),
        (x == high, jnp.minimum(g + 1, last), g < last),
    )
    gather, spread = None, None
    for part, row, inside in sides:
        hits = ((owner_ref[pl.ds(row, 1), :] == owner) & inside).astype(F32).astype(BF16)
        where = (place & part).astype(F32).reshape(plan.rows, plan.columns).astype(BF16)
        nt = (((1,), (1,)), ((), ()))
        some = lax.dot_general(hits, where, nt, preferred_element_type=F32)
        gather = some if gather is None else gather + some
        some = lax.dot_general(where, hits, nt, preferred_element_type=F32)
        spread = some if spread is None else spread + some
    return gather, jnp.concatenate([spread] * 3, axis=1)


def scale_of(plan, owners):
    owner = iota((plan.owners, plan.columns), 0).astype(owners.dtype)
    hits = jnp.zeros((plan.owners, plan.columns), F32)
    for g in range(plan.owners):
        hits = hits + (owners[g : g + 1] == owner).astype(F32)
    count = jnp.sum(hits, axis=1, keepdims=True)
    return jnp.broadcast_to(0.125 / jnp.maximum(count, 1.0), (plan.owners, plan.p))


def mobility_of(mask, kind, table):
    values = jnp.zeros(kind.shape, F32)
    for marker, value in enumerate(table):
        values = jnp.where(kind == marker, value, values)
    return mask.astype(F32) * values


def even(axis):
    return lax.rem(lax.axis_index(axis), 2) == 0


def put_x(plan, lows, highs, near, far):
    up = even("gx")
    for which, (low, high) in enumerate(zip(lows, highs)):
        near[pl.ds(which * plan.y, plan.y), :] = jnp.where(up, high, low)
        far[pl.ds(which * plan.y, plan.y), :] = jnp.where(up, low, high)


def received(axis, near_ref, far_ref):
    up = even(axis)
    rows = pl.ds(0, min(near_ref.shape[0], far_ref.shape[0]))
    near, far = near_ref[rows, :], far_ref[rows, :]
    return jnp.where(up, far, near), jnp.where(up, near, far)


def prepare_kernel(plan, *refs):
    hbm, refs = refs[:8], refs[8:]
    x_near_ref, x_far_ref, y_near_ref, y_far_ref = refs[:4]
    x_refs, y_refs, (owner_ref, table_ref, sems) = refs[4:8], refs[8:14], refs[14:]
    copies = []

    def start(source, target):
        copies.append(pltpu.make_async_copy(source, target, sems.at[len(copies)]))
        copies[-1].start()

    start(hbm[7], table_ref)
    start(hbm[6], owner_ref)
    for source, target in zip(hbm[:4], x_refs):
        start(source.at[0], target.at[0])
        start(source.at[plan.x - 1], target.at[1])
    for source, target in zip(hbm[:6], y_refs):
        start(source.at[:, pl.ds(0, 8)], target.at[0])
        start(source.at[:, pl.ds(plan.y - 8, 8)], target.at[1])
    for copy in copies:
        copy.wait()
    table = [table_ref[marker] for marker in range(table_ref.shape[0])]
    conc, pot, mask, kind = (ref[...] for ref in x_refs)
    fields = (conc, pot, mobility_of(mask, kind, table))
    put_x(plan, [f[0] for f in fields], [f[1] for f in fields], x_near_ref, x_far_ref)
    conc, pot, mask, kind, mass, pots = (ref[...] for ref in y_refs)
    fields = (conc, pot, mobility_of(mask, kind, table))
    up = even("gy")
    rows = [(field, at) for at in range(2) for field in fields] + [(mass, 0), (pots, 0)]
    for which, (field, at) in enumerate(rows):
        for x in range(plan.x):
            low, high = field[0, x, at : at + 1], field[1, x, 7 - at : 8 - at]
            y_near_ref[pl.ds(which * plan.x + x, 1), :] = jnp.where(up, high, low)
            y_far_ref[pl.ds(which * plan.x + x, 1), :] = jnp.where(up, low, high)
    used = 8 * plan.x
    for ref, rows in ((y_near_ref, plan.y_rows), (y_far_ref, plan.y_far_rows)):
        ref[pl.ds(used, rows - used), :] = jnp.zeros((rows - used, plan.p), F32)
        ref[pl.ds(plan.map_row, plan.owners), pl.ds(0, plan.columns)] = owner_ref[...].astype(F32)


def local_kernel(
    plan, mask_ref, class_ref, table_ref, owner_ref, mob_ref, gather_ref, spread_ref, scale_ref
):
    table = [table_ref[marker] for marker in range(table_ref.shape[0])]
    mob_ref[...] = mobility_of(mask_ref[...], class_ref[...], table)
    gather_ref[...], spread_ref[...] = membership(plan, owner_ref)
    scale_ref[...] = scale_of(plan, owner_ref[...])


def first_kernel(
    plan, x_far_ref, x_near_ref, y_far_ref, y_near_ref,
    conc_ref, pot_ref, mob_ref, mass_ref, pots_ref, gather_ref, scale_ref, owner_ref,
    conc_out, pot_out, total_hbm, raw_out, x_near_out, x_far_out, total_out, sems,
):
    sides = received("gx", x_near_ref, x_far_ref)
    ends = received("gy", y_near_ref, y_far_ref)

    def halo(which):
        return tuple(side_rows(plan, rows, which) for rows in sides) + tuple(
            side_columns(plan, rows, which) for rows in ends
        )

    mobility, mob_halo = mob_ref[...], halo(2)
    faces, diagonal = faces_of(mobility, neighbours(mobility, mob_halo))
    mass_source, pot_source = mass_ref[...], pots_ref[...]
    conc, pot = conc_ref[...], pot_ref[...]
    for at, field in enumerate((conc, pot)):
        for x in range(plan.x):
            raw_out[pl.ds(2 * at * plan.x + x, 1), :] = field[x, 0:1]
            raw_out[pl.ds((2 * at + 1) * plan.x + x, 1), :] = field[x, plan.y - 1 : plan.y]
    excess = excess_of(
        conc, pot, neighbours(conc, halo(0)), neighbours(pot, halo(1)), faces, diagonal,
        mass_source, pot_source,
    )
    conc, pot = relax_pair(conc, pot, *excess, diagonal, scale_from(diagonal))
    conc_out[...] = conc
    pot_out[...] = pot
    put_x(plan, (conc[0], pot[0]), (conc[plan.x - 1], pot[plan.x - 1]), x_near_out, x_far_out)
    up = even("gx")
    base = 2 * plan.y
    for which in range(3):
        for end, rows in enumerate(ends):
            low = rows[which * plan.x : which * plan.x + 1]
            high = rows[(which + 1) * plan.x - 1 : (which + 1) * plan.x]
            x_near_out[pl.ds(base + 2 * which + end, 1), :] = jnp.where(up, high, low)
            x_far_out[pl.ds(base + 2 * which + end, 1), :] = jnp.where(up, low, high)
    for ref in (x_near_out, x_far_out):
        ref[pl.ds(base + 6, 2), :] = jnp.zeros((2, plan.p), F32)

    nothing = tuple(jnp.zeros_like(part) for part in mob_halo)
    own_mass, own_pot = excess_of(
        conc, pot, neighbours(conc, nothing), neighbours(pot, nothing), faces, diagonal,
        mass_source, pot_source,
    )
    give_mass, give_pot = (
        [field[x] + field[x + 1] for x in range(0, plan.x, 2)] for field in (own_mass, own_pot)
    )
    for x, side in ((0, 0), (plan.x - 1, 1)):
        face = 0.5 * (mobility[x] + mob_halo[side][0])
        give_mass.append(time_step * face * pot[x])
        give_pot.append(-interface * conc[x])

    def packed(mass, other):
        first = iota(mass.shape, 1) & 1 == 0
        return jnp.where(
            first, mass + pltpu.roll(mass, plan.p - 1, 1), other + pltpu.roll(other, 1, 1)
        )

    give = packed(jnp.concatenate(give_mass, axis=0), jnp.concatenate(give_pot, axis=0))
    h = lax.axis_index("gy")
    inside = (h > 0, None, h < plan.groups - 1)
    maps = [rows[plan.map_row : plan.map_row + plan.owners, : plan.columns] for rows in ends]
    maps.insert(1, owner_ref[...].astype(F32))
    owner = iota((plan.owners, 1), 0)
    is_mine = owner == lax.axis_index("gx")

    sums = [None, split_dot(gather_ref[...].astype(BF16), give, ((1,), (0,))), None]
    sums[1] = sums[1] * scale_ref[...]
    for place, y, at, side in ((0, 0, plan.half_y - 1, 2), (2, plan.y - 1, 0, 3)):
        edge_mob, edge_pot, edge_conc = (
            jnp.concatenate([field[x, y : y + 1] for x in range(plan.x)], axis=0)
            for field in (mobility, pot, conc)
        )
        face = 0.5 * (edge_mob + mob_halo[side][:, 0])
        both = packed(time_step * face * edge_pot, -interface * edge_conc)
        part = jnp.zeros((plan.owners, plan.p), F32)
        for i in range(plan.half_x):
            column = owner_column(plan, maps[place], i, at)
            ident = jnp.sum(jnp.where(is_mine, column, 0.0), axis=0, keepdims=True)
            pair = both[2 * i : 2 * i + 1] + both[2 * i + 1 : 2 * i + 2]
            part = part + jnp.where((owner.astype(F32) == ident) & inside[place], pair, 0.0)
        sums[place] = part * scale_of(plan, maps[place])
    if not plan.slots:
        total_out[...] = jnp.concatenate(sums, axis=0)
        copy = pltpu.make_async_copy(total_out, total_hbm, sems.at[0])
        copy.start()
        copy.wait()
        return

    def picked(place, i, at):
        column = owner_column(plan, maps[place], i, at)
        ident = jnp.broadcast_to(column, (plan.owners, plan.p))
        out = jnp.zeros((plan.owners, plan.p), F32)
        for o in range(plan.owners):
            out = jnp.where(ident == float(o), sums[place][o : o + 1], out)
        return out

    below = [[picked(k, i, plan.half_y - 1) for i in range(plan.half_x)] for k in range(3)]
    above = [[picked(k, i, 0) for i in range(plan.half_x)] for k in range(3)]

    def of_plane(plane, choices):
        out = jnp.zeros((plan.owners, plan.p), F32)
        for k in range(3):
            out = jnp.where(plane == h + (k - 1), choices[k], out)
        return out

    size = 4 * plan.slot_parts
    rows = []
    for plane in range(plan.groups):
        beside = []
        for i in range(plan.half_x):
            beside.append((plan.low_row + i, of_plane(plane - 1, [k[i] for k in below])))
            beside.append((plan.high_row + i, of_plane(plane + 1, [k[i] for k in above])))
        blank = jnp.zeros((plan.owners, plan.p), F32)
        beside += [(at, blank) for at in range(plan.high_row + plan.half_x, size)]
        rows.append((of_plane(plane, sums), beside))
    copies = []
    for g in range(plan.owners):
        for plane, (main, beside) in enumerate(rows):
            slot = g * plan.groups + plane
            for part in range(plan.owners // 4):
                total_out[slot, part] = main[4 * part : 4 * part + 4]
            for row, values in beside:
                total_out[slot, row // 4, pl.ds(row % 4, 1), :] = values[g : g + 1]
        if g % 2:
            some = pl.ds((g - 1) * plan.groups, 2 * plan.groups)
            copies.append(
                pltpu.make_async_copy(total_out.at[some], total_hbm.at[some], sems.at[g // 2])
            )
            copies[-1].start()
    for copy in copies:
        copy.wait()


def owner_column(plan, owners, i, at):
    b = i * plan.half_y + at
    return owners[:, b : b + 1]


def coarse_solve(packed, planes):
    lane = iota(packed.shape, 1)
    even = lane & 1 == 0
    mass_mean = jnp.where(even, packed, pltpu.roll(packed, 1, 1))
    pot_mean = jnp.where(even, pltpu.roll(packed, planes - 1, 1), packed)

    def neighbour_sum(values):
        return jnp.where(lane >= 2, pltpu.roll(values, 2, 1), 0.0) + jnp.where(
            lane < planes - 2, pltpu.roll(values, planes - 2, 1), 0.0
        )

    def step(mass_gap, pot_gap):
        scale = relax_coarse / coarse_det
        return (
            scale * (mass_gap - 2.0 * coarse_flux * pot_gap),
            scale * (pot_gap + (split_slope + 2.0 * coarse_bend) * mass_gap),
        )

    coarse_conc, coarse_pot = step(mass_mean, pot_mean)
    for _ in range(CSWEEP - 1):
        mass_gap = mass_mean - (
            coarse_conc + coarse_flux * (2.0 * coarse_pot - neighbour_sum(coarse_pot))
        )
        pot_gap = pot_mean - (
            coarse_pot
            - split_slope * coarse_conc
            + coarse_bend * (neighbour_sum(coarse_conc) - 2.0 * coarse_conc)
        )
        more_conc, more_pot = step(mass_gap, pot_gap)
        coarse_conc, coarse_pot = coarse_conc + more_conc, coarse_pot + more_pot
    return coarse_conc, coarse_pot


def beside_kernel(
    plan, x_near_ref, x_far_ref, mob_ref, raw_ref, x_near_msg, x_far_msg, y_near_msg, y_far_msg,
    faces_out, diagonal_out, scale_out, ends_out,
):
    mobility = mob_ref[...]
    sides = received("gx", x_near_msg, x_far_msg)
    ends = received("gy", y_near_msg, y_far_msg)
    halo = tuple(side_rows(plan, rows, 2) for rows in sides) + tuple(
        side_columns(plan, rows, 2) for rows in ends
    )
    faces, diagonal = faces_of(mobility, neighbours(mobility, halo))
    for i, face in enumerate(faces):
        faces_out[i] = face
    diagonal_out[...] = diagonal
    scale_out[...] = scale_from(diagonal)

    corners = received("gx", x_near_ref, x_far_ref)
    h = lax.axis_index("gy")
    inside = (h > 0, h < plan.groups - 1)
    own_mob = [
        jnp.concatenate([mobility[x, y : y + 1] for x in range(plan.x)], axis=0)
        for y in (0, plan.y - 1)
    ]
    for end, rows in enumerate(ends):

        def row(which):
            return rows[which * plan.x : (which + 1) * plan.x]

        def beside(which, own):
            here = row(which)
            at = 2 * plan.y + 2 * which + end
            wide = jnp.concatenate([corners[0][at : at + 1], here, corners[1][at : at + 1]], axis=0)
            return (
                wide[: plan.x], wide[2:], own, row(which + 3),
                *(part[0] for part in plane_pair(here[None])),
            )

        raw = [
            raw_ref[pl.ds((2 * which + end) * plan.x, plan.x), :] for which in range(2)
        ]
        faces, diagonal = faces_of(row(2), beside(2, own_mob[end]))
        excess = excess_of(
            row(0), row(1), beside(0, raw[0]), beside(1, raw[1]), faces, diagonal, row(6), row(7)
        )
        new = relax_pair(row(0), row(1), *excess, diagonal, scale_from(diagonal))
        for which, values in enumerate(new):
            ends_out[pl.ds((2 * which + end) * plan.x, plan.x), :] = jnp.where(
                inside[end], values, 0.0
            )


def last_kernel(
    plan, conc_ref, pot_ref, mass_ref, pots_ref, faces_ref, diagonal_ref, scale_ref,
    x_near_ref, x_far_ref, ends_ref, spread_ref, total_ref,
    conc_hbm, pot_hbm, conc_out, pot_out, sems,
):
    parts = []
    for part in range(plan.slot_parts):
        terms = [total_ref[slot, part] for slot in range(total_ref.shape[0])]
        while len(terms) > 1:
            pairs = [a + b for a, b in zip(terms[::2], terms[1::2])]
            terms = pairs + terms[len(pairs) * 2 :]
        parts.append(terms[0])
    solved = jnp.concatenate(
        coarse_solve(jnp.concatenate(parts, axis=0), plan.p), axis=1
    )
    own = lax.dot_general(
        spread_ref[...].astype(BF16),
        three_terms(solved[: plan.owners]).astype(BF16),
        (((1,), (0,)), ((), ())),
        preferred_element_type=F32,
    )
    sides = received("gx", x_near_ref, x_far_ref)

    def updated(which, ref):
        lanes = slice(which * plan.p, (which + 1) * plan.p)
        corr = own[:, lanes]
        slabs = [side_rows(plan, sides[0], which)]
        slabs += [ref[pl.ds(x, 1)] for x in range(plan.x)]
        slabs.append(side_rows(plan, sides[1], which))
        order = [plan.half_x, *[x >> 1 for x in range(plan.x)], plan.half_x + 1]
        slabs = [
            slab + corr[x * plan.y : (x + 1) * plan.y][None] for slab, x in zip(slabs, order)
        ]
        ends = []
        for end, begin in enumerate((plan.low_row, plan.high_row)):
            rows = ends_ref[pl.ds((2 * which + end) * plan.x, plan.x), :]
            ends.append([
                (rows[x : x + 1] + solved[begin + (x >> 1) : begin + (x >> 1) + 1, lanes])[None]
                for x in range(plan.x)
            ])
        return slabs, ends

    conc, conc_ends = updated(0, conc_ref)
    pot, pot_ends = updated(1, pot_ref)

    def beside(slabs, ends, x):
        here = slabs[x + 1]
        return (
            slabs[x], slabs[x + 2], *y_pair(here, ends[0][x], ends[1][x]), *plane_pair(here)
        )

    copies = []
    for x in range(plan.x):
        one = pl.ds(x, 1)
        diagonal = diagonal_ref[one]
        excess = excess_of(
            conc[x + 1], pot[x + 1], beside(conc, conc_ends, x), beside(pot, pot_ends, x),
            [faces_ref[i, one] for i in range(6)], diagonal, mass_ref[one], pots_ref[one],
        )
        conc_out[one], pot_out[one] = relax_pair(
            conc[x + 1], pot[x + 1], *excess, diagonal, scale_ref[one]
        )
        for source, target in ((conc_out, conc_hbm), (pot_out, pot_hbm)):
            copies.append(
                pltpu.make_async_copy(source.at[one], target.at[one], sems.at[len(copies)])
            )
            copies[-1].start()
    for copy in copies:
        copy.wait()


def call(kernel, plan, outs, args, far=(), smem=(), scratch=(), out_far=()):
    def space(i):
        return pl.ANY if i in far else pltpu.SMEM if i in smem else pltpu.VMEM

    return pl.pallas_call(
        functools.partial(kernel, plan),
        out_shape=[jax.ShapeDtypeStruct(shape, F32) for shape in outs],
        in_specs=[pl.BlockSpec(memory_space=space(i)) for i in range(len(args))],
        out_specs=[
            pl.BlockSpec(memory_space=pl.ANY if i in out_far else pltpu.VMEM)
            for i in range(len(outs))
        ],
        scratch_shapes=list(scratch),
        compiler_params=pltpu.CompilerParams(vmem_limit_bytes=VMEM_LIMIT),
    )(*[
        pltpu.with_memory_space_constraint(arg, pltpu.HBM) if i in far else arg
        for i, arg in enumerate(args)
    ])


def swap_near(axis, rows, begin=0):
    pairs = [(i, i + 1) for i in range(begin, lax.axis_size(axis) - 1, 2)]
    return lax.ppermute(rows, axis, pairs + [(j, i) for i, j in pairs])


def swap_far(axis, rows):
    return swap_near(axis, rows, 1)


def gather_totals(plan, total, y_near, y_far):
    if plan.slots:
        return lax.all_to_all(total, ("gx", "gy"), split_axis=0, concat_axis=0, tiled=True)
    shape = (plan.groups, 3, plan.owners, plan.p)
    parts = lax.all_gather(lax.psum(total, "gx"), "gy").reshape(shape)
    blank = jnp.zeros((1, plan.owners, plan.p), F32)
    to_below, own, to_above = (parts[:, k] for k in range(3))
    own = own + jnp.concatenate([blank, to_above[:-1]]) + jnp.concatenate([to_below[1:], blank])
    own = jnp.concatenate([blank, own, blank])
    g, h = lax.axis_index("gx"), lax.axis_index("gy")
    rows = [lax.dynamic_index_in_dim(own, h + 1, 0, False)]
    up = lax.rem(h, 2) == 0
    far = y_far[: y_near.shape[0]]
    for place, at, msg in (
        (h, plan.half_y - 1, jnp.where(up, far, y_near)),
        (h + 2, 0, jnp.where(up, y_near, far)),
    ):
        ident = lax.dynamic_index_in_dim(msg, plan.map_row + g, 0, False).astype(jnp.int32)
        ident = jnp.stack([ident[i * plan.half_y + at] for i in range(plan.half_x)])
        rows.append(lax.dynamic_index_in_dim(own, place, 0, False)[ident])
    rows = jnp.concatenate(rows)
    rows = jnp.pad(rows, ((0, 4 * plan.slot_parts - rows.shape[0]), (0, 0)))
    return rows.reshape(1, plan.slot_parts, 4, plan.p)


def on_device(conc, pot, mass_source, pot_source, mask, kind, table, owner_map):
    plan = Plan(conc.shape, lax.axis_size("gx"), lax.axis_size("gy"))
    block = conc.shape
    fields = [conc, pot, mask, kind, mass_source, pot_source]
    messages = call(
        prepare_kernel,
        plan,
        [*[(3 * plan.y, plan.p)] * 2, (plan.y_rows, plan.p), (plan.y_far_rows, plan.p)],
        [*fields, owner_map, table],
        far=range(8),
        scratch=(
            *[pltpu.VMEM((2, plan.y, plan.p), field.dtype) for field in fields[:4]],
            *[pltpu.VMEM((2, plan.x, 8, plan.p), field.dtype) for field in fields],
            pltpu.VMEM(owner_map.shape, owner_map.dtype),
            pltpu.SMEM(table.shape, table.dtype),
            pltpu.SemaphoreType.DMA((22,)),
        ),
    )
    x_near, x_far = swap_near("gx", messages[0]), swap_far("gx", messages[1])
    y_near, y_far = swap_near("gy", messages[2]), swap_far("gy", messages[3])
    y_far, mask, kind = lax.optimization_barrier((y_far, mask, kind))
    mob, gather, spread, scale = call(
        local_kernel,
        plan,
        [block, (plan.owners, plan.rows), (plan.rows, 3 * plan.owners), (plan.owners, plan.p)],
        [mask, kind, table, owner_map],
        smem=(2,),
    )
    slots = (plan.slots, plan.slot_parts, 4, plan.p) if plan.slots else (3 * plan.owners, plan.p)
    conc, pot, total, raw, near, far = call(
        first_kernel,
        plan,
        [
            block,
            block,
            slots,
            (4 * plan.x, plan.p),
            *[(2 * plan.y + 8, plan.p)] * 2,
        ],
        [
            x_far, x_near, y_far, y_near,
            conc, pot, mob, mass_source, pot_source, gather, scale, owner_map,
        ],
        out_far=(2,),
        scratch=(pltpu.VMEM(slots, F32), pltpu.SemaphoreType.DMA((plan.owners // 2,))),
    )
    total = gather_totals(plan, total, y_near, y_far)
    far = swap_far("gx", far)
    near = swap_near("gx", near)
    faces, diagonal, scale, ends = call(
        beside_kernel,
        plan,
        [(6, *block), block, block, (4 * plan.x, plan.p)],
        [near, far, mob, raw, x_near, x_far, y_near, y_far],
    )
    return tuple(
        call(
            last_kernel,
            plan,
            [block, block],
            [conc, pot, mass_source, pot_source, faces, diagonal, scale, near, far, ends, spread, total],
            out_far=(0, 1),
            scratch=(
                pltpu.VMEM(block, F32),
                pltpu.VMEM(block, F32),
                pltpu.SemaphoreType.DMA((2 * plan.x,)),
            ),
        )
    )


def solution(mesh):
    grid = P("gx", "gy", None)
    return jax.shard_map(
        on_device,
        mesh=mesh,
        in_specs=(grid,) * 6 + (P(), P(None, "gy")),
        out_specs=(grid, grid),
        check_vma=False,
    )
```

```python
import functools

import jax
import jax.numpy as jnp
from jax import lax
from jax.experimental import pallas as pl
from jax.experimental.pallas import tpu as pltpu
from jax.sharding import PartitionSpec as P

CSWEEP = 3

time_step = 0.25
split_slope = 1.0
interface = 0.5
relax_fine = 0.6
relax_coarse = 0.6
coarse_flux = 0.0625
coarse_bend = 0.125
coarse_det = 1.0 + 2.0 * coarse_flux * (split_slope + 2.0 * coarse_bend)

F32 = jnp.float32
BF16 = jnp.bfloat16
VMEM_LIMIT = 48 * 1024 * 1024


def iota(shape, dim):
    return lax.broadcasted_iota(jnp.int32, shape, dim)


def x_pair(field, low, high):
    return (
        jnp.concatenate([low, field[:-1]], axis=0),
        jnp.concatenate([field[1:], high], axis=0),
    )


def y_pair(field, low, high):
    size = field.shape[1]
    where = iota(field.shape, 1)
    return (
        jnp.where(where == 0, low, pltpu.roll(field, 1, 1)),
        jnp.where(where == size - 1, high, pltpu.roll(field, size - 1, 1)),
    )


def plane_pair(field):
    size = field.shape[2]
    where = iota(field.shape, 2)
    return (
        jnp.where(where == 0, 0.0, pltpu.roll(field, 1, 2)),
        jnp.where(where == size - 1, 0.0, pltpu.roll(field, size - 1, 2)),
    )


def neighbours(field, halo):
    xm, xp, ym, yp = halo
    return (*x_pair(field, xm, xp), *y_pair(field, ym, yp), *plane_pair(field))


def excess_of(conc, pot, conc_beside, pot_beside, faces, diagonal, mass_source, pot_source):
    excess_mass = (mass_source - conc) - diagonal * pot
    for face, other in zip(faces, pot_beside):
        excess_mass = excess_mass + face * other
    beside = conc_beside[0]
    for other in conc_beside[1:]:
        beside = beside + other
    excess_pot = (pot_source - pot) + (split_slope + 6.0 * interface) * conc - interface * beside
    return excess_mass, excess_pot


def scale_from(diagonal):
    return relax_fine / (1.0 + (split_slope + 6.0 * interface) * diagonal)


def relax_pair(conc, pot, excess_mass, excess_pot, diagonal, scale):
    new_conc = conc + (excess_mass - diagonal * excess_pot) * scale
    new_pot = pot + (excess_pot + (split_slope + 6.0 * interface) * excess_mass) * scale
    return new_conc, new_pot


def faces_of(mobility, beside):
    faces = tuple((0.5 * time_step) * (mobility + other) for other in beside)
    diagonal = faces[0]
    for face in faces[1:]:
        diagonal = diagonal + face
    return faces, diagonal


def split_dot(ones, values, contract):
    dims = (contract, ((), ()))
    total = None
    rest = values
    for _ in range(3):
        term = rest.astype(BF16)
        rest = rest - term.astype(F32)
        part = lax.dot_general(ones, term, dims, preferred_element_type=F32)
        total = part if total is None else total + part
    return total


def three_terms(values):
    out = []
    for _ in range(3):
        out.append(values.astype(BF16).astype(F32))
        values = values - out[-1]
    return jnp.concatenate(out, axis=0)


def round_up(value, unit):
    return -(-value // unit) * unit


class Plan:
    def __init__(self, shape, owners, groups):
        self.x, self.y, self.p = shape
        self.owners, self.groups = owners, groups
        self.half_x, self.half_y = self.x // 2, self.y // 2
        self.columns = self.half_x * self.half_y
        self.map_row = round_up(8 * self.x, 8)
        self.y_rows = self.map_row + owners
        self.y_far_rows = max(self.y_rows, 3 * self.y + 8)
        self.cells = self.x * self.y
        self.rows = (self.half_x + 2) * self.y
        self.low_row = owners
        self.high_row = owners + self.half_x
        self.slot_parts = -(-(owners + 2 * self.half_x) // 4)
        slots = owners * groups
        self.slots = slots if slots <= 64 else 0


def side_rows(plan, rows, which):
    return rows[which * plan.y : (which + 1) * plan.y][None]


def side_columns(plan, rows, which):
    return rows[which * plan.x : (which + 1) * plan.x][:, None]


def membership(plan, owner_ref):
    g = lax.axis_index("gx")
    last = plan.owners - 1
    owner = iota((plan.owners, plan.columns), 0)
    low, high = plan.half_x, plan.half_x + 1
    shape = (plan.half_x + 2, plan.y, plan.columns)
    x, y, column = iota(shape, 0), iota(shape, 1), iota(shape, 2)
    half = jnp.where(x < low, x, jnp.where(x == low, plan.half_x - 1, 0))
    place = column == half * plan.half_y + (y >> 1)
    sides = (
        (x < low, g, True),
        (x == low, jnp.maximum(g - 1, 0), g > 0),
        (x == high, jnp.minimum(g + 1, last), g < last),
    )
    gather, spread = None, None
    for part, row, inside in sides:
        hits = ((owner_ref[pl.ds(row, 1), :] == owner) & inside).astype(F32).astype(BF16)
        where = (place & part).astype(F32).reshape(plan.rows, plan.columns).astype(BF16)
        nt = (((1,), (1,)), ((), ()))
        some = lax.dot_general(hits, where, nt, preferred_element_type=F32)
        gather = some if gather is None else gather + some
        some = lax.dot_general(where, hits, nt, preferred_element_type=F32)
        spread = some if spread is None else spread + some
    return gather, jnp.concatenate([spread] * 3, axis=1)


def scale_of(plan, owners):
    owner = iota((plan.owners, plan.columns), 0).astype(owners.dtype)
    hits = jnp.zeros((plan.owners, plan.columns), F32)
    for g in range(plan.owners):
        hits = hits + (owners[g : g + 1] == owner).astype(F32)
    count = jnp.sum(hits, axis=1, keepdims=True)
    return jnp.broadcast_to(0.125 / jnp.maximum(count, 1.0), (plan.owners, plan.p))


def mobility_of(mask, kind, table):
    values = jnp.zeros(kind.shape, F32)
    for marker, value in enumerate(table):
        values = jnp.where(kind == marker, value, values)
    return mask.astype(F32) * values


def even(axis):
    return lax.rem(lax.axis_index(axis), 2) == 0


def put_x(plan, lows, highs, near, far):
    up = even("gx")
    for which, (low, high) in enumerate(zip(lows, highs)):
        near[pl.ds(which * plan.y, plan.y), :] = jnp.where(up, high, low)
        far[pl.ds(which * plan.y, plan.y), :] = jnp.where(up, low, high)


def received(axis, near_ref, far_ref):
    up = even(axis)
    rows = pl.ds(0, min(near_ref.shape[0], far_ref.shape[0]))
    near, far = near_ref[rows, :], far_ref[rows, :]
    return jnp.where(up, far, near), jnp.where(up, near, far)


def prepare_kernel(plan, *refs):
    hbm, refs = refs[:8], refs[8:]
    x_near_ref, x_far_ref, y_near_ref, y_far_ref = refs[:4]
    x_refs, y_refs, (owner_ref, table_ref, sems) = refs[4:8], refs[8:14], refs[14:]
    copies = []

    def start(source, target):
        copies.append(pltpu.make_async_copy(source, target, sems.at[len(copies)]))
        copies[-1].start()

    start(hbm[7], table_ref)
    start(hbm[6], owner_ref)
    for source, target in zip(hbm[:4], x_refs):
        start(source.at[0], target.at[0])
        start(source.at[plan.x - 1], target.at[1])
    for source, target in zip(hbm[:6], y_refs):
        start(source.at[:, pl.ds(0, 8)], target.at[0])
        start(source.at[:, pl.ds(plan.y - 8, 8)], target.at[1])
    for copy in copies:
        copy.wait()
    table = [table_ref[marker] for marker in range(table_ref.shape[0])]
    conc, pot, mask, kind = (ref[...] for ref in x_refs)
    fields = (conc, pot, mobility_of(mask, kind, table))
    put_x(plan, [f[0] for f in fields], [f[1] for f in fields], x_near_ref, x_far_ref)
    conc, pot, mask, kind, mass, pots = (ref[...] for ref in y_refs)
    fields = (conc, pot, mobility_of(mask, kind, table))
    up = even("gy")
    rows = [(field, at) for at in range(2) for field in fields] + [(mass, 0), (pots, 0)]
    for which, (field, at) in enumerate(rows):
        for x in range(plan.x):
            low, high = field[0, x, at : at + 1], field[1, x, 7 - at : 8 - at]
            y_near_ref[pl.ds(which * plan.x + x, 1), :] = jnp.where(up, high, low)
            y_far_ref[pl.ds(which * plan.x + x, 1), :] = jnp.where(up, low, high)
    used = 8 * plan.x
    for ref, rows in ((y_near_ref, plan.y_rows), (y_far_ref, plan.y_far_rows)):
        ref[pl.ds(used, rows - used), :] = jnp.zeros((rows - used, plan.p), F32)
        ref[pl.ds(plan.map_row, plan.owners), pl.ds(0, plan.columns)] = owner_ref[...].astype(F32)


def inner_faces(mobility):
    half = 0.5 * time_step
    shape = mobility.shape
    y, plane = iota(shape, 1), iota(shape, 2)
    to_x = jnp.concatenate(
        [half * (mobility[:-1] + mobility[1:]), jnp.zeros_like(mobility[:1])], axis=0
    )
    out = [to_x]
    for dim, where, shift, edge in (
        (1, y, 1, 0), (1, y, shape[1] - 1, shape[1] - 1),
        (2, plane, 1, 0), (2, plane, shape[2] - 1, shape[2] - 1),
    ):
        face = half * (mobility + pltpu.roll(mobility, shift, dim))
        out.append(jnp.where(where == edge, 0.0, face))
    return out


def inner_flux(faces, field):
    to_x, y_low, y_high, plane_low, plane_high = faces
    size_y, size_p = field.shape[1:]
    from_x = to_x[:-1]
    blank = jnp.zeros_like(field[:1])
    flux = jnp.concatenate([from_x * field[1:], blank], axis=0)
    flux = flux + jnp.concatenate([blank, from_x * field[:-1]], axis=0)
    flux = flux + y_low * pltpu.roll(field, 1, 1) + y_high * pltpu.roll(field, size_y - 1, 1)
    return flux + plane_low * pltpu.roll(field, 1, 2) + plane_high * pltpu.roll(field, size_p - 1, 2)


def inner_excess(conc, pot, faces, diagonal, mass_source, pot_source):
    excess_mass = (mass_source - conc) - diagonal * pot + inner_flux(faces, pot)
    nothing = [jnp.zeros_like(conc[:1])] * 2 + [jnp.zeros_like(conc[:, :1])] * 2
    beside = None
    for other in neighbours(conc, nothing):
        beside = other if beside is None else beside + other
    excess_pot = (pot_source - pot) + (split_slope + 6.0 * interface) * conc - interface * beside
    return excess_mass, excess_pot


def add_edges(field, x_low, x_high, y_low, y_high):
    field = jnp.concatenate(
        [(field[0] + x_low)[None], field[1:-1], (field[-1] + x_high)[None]], axis=0
    )
    row = iota((field.shape[0], 8, field.shape[2]), 1)
    size = field.shape[1]
    low = field[:, :8] + jnp.where(row == 0, y_low, 0.0)
    high = field[:, size - 8 :] + jnp.where(row == 7, y_high, 0.0)
    return jnp.concatenate([low, field[:, 8 : size - 8], high], axis=1)


def local_kernel(
    plan, conc_ref, pot_ref, mask_ref, class_ref, mass_ref, pots_ref, table_ref, owner_ref,
    mob_ref, gather_ref, spread_ref, scale_ref, faces_ref, diagonal_ref, mass_out, pots_out,
):
    table = [table_ref[marker] for marker in range(table_ref.shape[0])]
    mobility = mobility_of(mask_ref[...], class_ref[...], table)
    mob_ref[...] = mobility
    gather_ref[...], spread_ref[...] = membership(plan, owner_ref)
    scale_ref[...] = scale_of(plan, owner_ref[...])
    faces = inner_faces(mobility)
    diagonal = faces[0] + jnp.concatenate([jnp.zeros_like(mobility[:1]), faces[0][:-1]], axis=0)
    for face in faces[1:]:
        diagonal = diagonal + face
    plane = iota(mobility.shape, 2)
    ends = (plane == 0) | (plane == plan.p - 1)
    diagonal = diagonal + jnp.where(ends, (0.5 * time_step) * mobility, 0.0)
    for i, face in enumerate(faces):
        faces_ref[i] = face
    diagonal_ref[...] = diagonal
    mass_out[...], pots_out[...] = inner_excess(
        conc_ref[...], pot_ref[...], faces, diagonal, mass_ref[...], pots_ref[...]
    )


def first_kernel(
    plan, x_far_ref, x_near_ref, y_far_ref, y_near_ref,
    conc_ref, pot_ref, mob_ref, mass_ref, pots_ref, gather_ref, scale_ref, owner_ref,
    faces_ref, diagonal_ref, mass_part_ref, pot_part_ref,
    conc_out, pot_out, total_hbm, raw_out, x_near_out, x_far_out, total_out, sems,
):
    sides = received("gx", x_near_ref, x_far_ref)
    ends = received("gy", y_near_ref, y_far_ref)
    last_x, last_y = plan.x - 1, plan.y - 1

    def halo(which):
        return tuple(side_rows(plan, rows, which)[0] for rows in sides) + tuple(
            side_columns(plan, rows, which) for rows in ends
        )

    def edges(field):
        return field[0], field[last_x], field[:, :1], field[:, last_y:]

    mobility = mob_ref[...]
    raw_conc, raw_pot = conc_ref[...], pot_ref[...]
    outer = [
        (0.5 * time_step) * (own + other) for own, other in zip(edges(mobility), halo(2))
    ]
    diagonal = add_edges(diagonal_ref[...], *outer)
    excess_mass = add_edges(
        mass_part_ref[...],
        *(f * (other - own) for f, own, other in zip(outer, edges(raw_pot), halo(1))),
    )
    excess_pot = add_edges(pot_part_ref[...], *(-interface * other for other in halo(0)))
    conc, pot = relax_pair(
        raw_conc, raw_pot, excess_mass, excess_pot, diagonal, scale_from(diagonal)
    )

    own_mass, own_pot = inner_excess(
        conc, pot, [faces_ref[i] for i in range(5)], diagonal, mass_ref[...], pots_ref[...]
    )
    give_mass, give_pot = (
        [field[x] + field[x + 1] for x in range(0, plan.x, 2)] for field in (own_mass, own_pot)
    )
    for x, side in ((0, 0), (last_x, 1)):
        give_mass.append(outer[side] * pot[x])
        give_pot.append(-interface * conc[x])

    def packed(mass, other):
        first = iota(mass.shape, 1) & 1 == 0
        return jnp.where(
            first, mass + pltpu.roll(mass, plan.p - 1, 1), other + pltpu.roll(other, 1, 1)
        )

    give = packed(jnp.concatenate(give_mass, axis=0), jnp.concatenate(give_pot, axis=0))
    h = lax.axis_index("gy")
    inside = (h > 0, None, h < plan.groups - 1)
    maps = [rows[plan.map_row : plan.map_row + plan.owners, : plan.columns] for rows in ends]
    maps.insert(1, owner_ref[...].astype(F32))
    owner = iota((plan.owners, 1), 0)
    is_mine = owner == lax.axis_index("gx")

    sums = [None, split_dot(gather_ref[...].astype(BF16), give, ((1,), (0,))), None]
    sums[1] = sums[1] * scale_ref[...]
    for place, y, at, side in ((0, 0, plan.half_y - 1, 2), (2, plan.y - 1, 0, 3)):
        edge_pot, edge_conc = (
            jnp.concatenate([field[x, y : y + 1] for x in range(plan.x)], axis=0)
            for field in (pot, conc)
        )
        both = packed(outer[side][:, 0] * edge_pot, -interface * edge_conc)
        part = jnp.zeros((plan.owners, plan.p), F32)
        for i in range(plan.half_x):
            column = owner_column(plan, maps[place], i, at)
            ident = jnp.sum(jnp.where(is_mine, column, 0.0), axis=0, keepdims=True)
            pair = both[2 * i : 2 * i + 1] + both[2 * i + 1 : 2 * i + 2]
            part = part + jnp.where((owner.astype(F32) == ident) & inside[place], pair, 0.0)
        sums[place] = part * scale_of(plan, maps[place])
    def store_fields():
        conc_out[...] = conc
        pot_out[...] = pot
        for at, field in enumerate((raw_conc, raw_pot)):
            for x in range(plan.x):
                raw_out[pl.ds(2 * at * plan.x + x, 1), :] = field[x, 0:1]
                raw_out[pl.ds((2 * at + 1) * plan.x + x, 1), :] = field[x, last_y : last_y + 1]
        put_x(plan, (conc[0], pot[0]), (conc[last_x], pot[last_x]), x_near_out, x_far_out)
        up = even("gx")
        base = 2 * plan.y
        for which in range(3):
            for end, rows in enumerate(ends):
                low = rows[which * plan.x : which * plan.x + 1]
                high = rows[(which + 1) * plan.x - 1 : (which + 1) * plan.x]
                x_near_out[pl.ds(base + 2 * which + end, 1), :] = jnp.where(up, high, low)
                x_far_out[pl.ds(base + 2 * which + end, 1), :] = jnp.where(up, low, high)
        for ref in (x_near_out, x_far_out):
            ref[pl.ds(base + 6, 2), :] = jnp.zeros((2, plan.p), F32)

    if not plan.slots:
        total_out[...] = jnp.concatenate(sums, axis=0)
        copies = [pltpu.make_async_copy(total_out, total_hbm, sems.at[0])]
        copies[0].start()
        store_fields()
        copies[0].wait()
        return

    def picked(place, i, at):
        column = owner_column(plan, maps[place], i, at)
        ident = jnp.broadcast_to(column, (plan.owners, plan.p))
        out = jnp.zeros((plan.owners, plan.p), F32)
        for o in range(plan.owners):
            out = jnp.where(ident == float(o), sums[place][o : o + 1], out)
        return out

    below = [[picked(k, i, plan.half_y - 1) for i in range(plan.half_x)] for k in range(3)]
    above = [[picked(k, i, 0) for i in range(plan.half_x)] for k in range(3)]

    def of_plane(plane, choices):
        out = jnp.zeros((plan.owners, plan.p), F32)
        for k in range(3):
            out = jnp.where(plane == h + (k - 1), choices[k], out)
        return out

    size = 4 * plan.slot_parts
    rows = []
    for plane in range(plan.groups):
        beside = []
        for i in range(plan.half_x):
            beside.append((plan.low_row + i, of_plane(plane - 1, [k[i] for k in below])))
            beside.append((plan.high_row + i, of_plane(plane + 1, [k[i] for k in above])))
        blank = jnp.zeros((plan.owners, plan.p), F32)
        beside += [(at, blank) for at in range(plan.high_row + plan.half_x, size)]
        rows.append((of_plane(plane, sums), beside))
    copies = []
    for g in range(plan.owners):
        for plane, (main, beside) in enumerate(rows):
            slot = g * plan.groups + plane
            for part in range(plan.owners // 4):
                total_out[slot, part] = main[4 * part : 4 * part + 4]
            for row, values in beside:
                total_out[slot, row // 4, pl.ds(row % 4, 1), :] = values[g : g + 1]
        if g % 2:
            some = pl.ds((g - 1) * plan.groups, 2 * plan.groups)
            copies.append(
                pltpu.make_async_copy(total_out.at[some], total_hbm.at[some], sems.at[g // 2])
            )
            copies[-1].start()
    store_fields()
    for copy in copies:
        copy.wait()


def owner_column(plan, owners, i, at):
    b = i * plan.half_y + at
    return owners[:, b : b + 1]


def coarse_solve(packed, planes):
    lane = iota(packed.shape, 1)
    even = lane & 1 == 0
    mass_mean = jnp.where(even, packed, pltpu.roll(packed, 1, 1))
    pot_mean = jnp.where(even, pltpu.roll(packed, planes - 1, 1), packed)

    def neighbour_sum(values):
        return jnp.where(lane >= 2, pltpu.roll(values, 2, 1), 0.0) + jnp.where(
            lane < planes - 2, pltpu.roll(values, planes - 2, 1), 0.0
        )

    def step(mass_gap, pot_gap):
        scale = relax_coarse / coarse_det
        return (
            scale * (mass_gap - 2.0 * coarse_flux * pot_gap),
            scale * (pot_gap + (split_slope + 2.0 * coarse_bend) * mass_gap),
        )

    coarse_conc, coarse_pot = step(mass_mean, pot_mean)
    for _ in range(CSWEEP - 1):
        mass_gap = mass_mean - (
            coarse_conc + coarse_flux * (2.0 * coarse_pot - neighbour_sum(coarse_pot))
        )
        pot_gap = pot_mean - (
            coarse_pot
            - split_slope * coarse_conc
            + coarse_bend * (neighbour_sum(coarse_conc) - 2.0 * coarse_conc)
        )
        more_conc, more_pot = step(mass_gap, pot_gap)
        coarse_conc, coarse_pot = coarse_conc + more_conc, coarse_pot + more_pot
    return coarse_conc, coarse_pot


def beside_kernel(
    plan, x_near_ref, x_far_ref, mob_ref, raw_ref, x_near_msg, x_far_msg, y_near_msg, y_far_msg,
    faces_out, diagonal_out, scale_out, ends_out,
):
    mobility = mob_ref[...]
    sides = received("gx", x_near_msg, x_far_msg)
    ends = received("gy", y_near_msg, y_far_msg)
    halo = tuple(side_rows(plan, rows, 2) for rows in sides) + tuple(
        side_columns(plan, rows, 2) for rows in ends
    )
    faces, diagonal = faces_of(mobility, neighbours(mobility, halo))
    for i, face in enumerate(faces):
        faces_out[i] = face
    diagonal_out[...] = diagonal
    scale_out[...] = scale_from(diagonal)

    corners = received("gx", x_near_ref, x_far_ref)
    h = lax.axis_index("gy")
    inside = (h > 0, h < plan.groups - 1)
    own_mob = [
        jnp.concatenate([mobility[x, y : y + 1] for x in range(plan.x)], axis=0)
        for y in (0, plan.y - 1)
    ]
    for end, rows in enumerate(ends):

        def row(which):
            return rows[which * plan.x : (which + 1) * plan.x]

        def beside(which, own):
            here = row(which)
            at = 2 * plan.y + 2 * which + end
            wide = jnp.concatenate([corners[0][at : at + 1], here, corners[1][at : at + 1]], axis=0)
            return (
                wide[: plan.x], wide[2:], own, row(which + 3),
                *(part[0] for part in plane_pair(here[None])),
            )

        raw = [
            raw_ref[pl.ds((2 * which + end) * plan.x, plan.x), :] for which in range(2)
        ]
        faces, diagonal = faces_of(row(2), beside(2, own_mob[end]))
        excess = excess_of(
            row(0), row(1), beside(0, raw[0]), beside(1, raw[1]), faces, diagonal, row(6), row(7)
        )
        new = relax_pair(row(0), row(1), *excess, diagonal, scale_from(diagonal))
        for which, values in enumerate(new):
            ends_out[pl.ds((2 * which + end) * plan.x, plan.x), :] = jnp.where(
                inside[end], values, 0.0
            )


def last_kernel(
    plan, conc_ref, pot_ref, mass_ref, pots_ref, faces_ref, diagonal_ref, scale_ref,
    x_near_ref, x_far_ref, ends_ref, spread_ref, total_ref,
    conc_hbm, pot_hbm, conc_out, pot_out, sems,
):
    parts = []
    for part in range(plan.slot_parts):
        terms = [total_ref[slot, part] for slot in range(total_ref.shape[0])]
        while len(terms) > 1:
            pairs = [a + b for a, b in zip(terms[::2], terms[1::2])]
            terms = pairs + terms[len(pairs) * 2 :]
        parts.append(terms[0])
    solved = jnp.concatenate(
        coarse_solve(jnp.concatenate(parts, axis=0), plan.p), axis=1
    )
    own = lax.dot_general(
        spread_ref[...].astype(BF16),
        three_terms(solved[: plan.owners]).astype(BF16),
        (((1,), (0,)), ((), ())),
        preferred_element_type=F32,
    )
    sides = received("gx", x_near_ref, x_far_ref)

    def updated(which, ref):
        lanes = slice(which * plan.p, (which + 1) * plan.p)
        corr = own[:, lanes]
        slabs = [side_rows(plan, sides[0], which)]
        slabs += [ref[pl.ds(x, 1)] for x in range(plan.x)]
        slabs.append(side_rows(plan, sides[1], which))
        order = [plan.half_x, *[x >> 1 for x in range(plan.x)], plan.half_x + 1]
        slabs = [
            slab + corr[x * plan.y : (x + 1) * plan.y][None] for slab, x in zip(slabs, order)
        ]
        ends = []
        for end, begin in enumerate((plan.low_row, plan.high_row)):
            rows = ends_ref[pl.ds((2 * which + end) * plan.x, plan.x), :]
            ends.append([
                (rows[x : x + 1] + solved[begin + (x >> 1) : begin + (x >> 1) + 1, lanes])[None]
                for x in range(plan.x)
            ])
        return slabs, ends

    conc, conc_ends = updated(0, conc_ref)
    pot, pot_ends = updated(1, pot_ref)

    def beside(slabs, ends, x):
        here = slabs[x + 1]
        return (
            slabs[x], slabs[x + 2], *y_pair(here, ends[0][x], ends[1][x]), *plane_pair(here)
        )

    copies = []
    for x in range(plan.x):
        one = pl.ds(x, 1)
        diagonal = diagonal_ref[one]
        excess = excess_of(
            conc[x + 1], pot[x + 1], beside(conc, conc_ends, x), beside(pot, pot_ends, x),
            [faces_ref[i, one] for i in range(6)], diagonal, mass_ref[one], pots_ref[one],
        )
        conc_out[one], pot_out[one] = relax_pair(
            conc[x + 1], pot[x + 1], *excess, diagonal, scale_ref[one]
        )
        for source, target in ((conc_out, conc_hbm), (pot_out, pot_hbm)):
            copies.append(
                pltpu.make_async_copy(source.at[one], target.at[one], sems.at[len(copies)])
            )
            copies[-1].start()
    for copy in copies:
        copy.wait()


def call(kernel, plan, outs, args, far=(), smem=(), scratch=(), out_far=()):
    def space(i):
        return pl.ANY if i in far else pltpu.SMEM if i in smem else pltpu.VMEM

    return pl.pallas_call(
        functools.partial(kernel, plan),
        out_shape=[jax.ShapeDtypeStruct(shape, F32) for shape in outs],
        in_specs=[pl.BlockSpec(memory_space=space(i)) for i in range(len(args))],
        out_specs=[
            pl.BlockSpec(memory_space=pl.ANY if i in out_far else pltpu.VMEM)
            for i in range(len(outs))
        ],
        scratch_shapes=list(scratch),
        compiler_params=pltpu.CompilerParams(vmem_limit_bytes=VMEM_LIMIT),
    )(*[
        pltpu.with_memory_space_constraint(arg, pltpu.HBM) if i in far else arg
        for i, arg in enumerate(args)
    ])


def swap_near(axis, rows, begin=0):
    pairs = [(i, i + 1) for i in range(begin, lax.axis_size(axis) - 1, 2)]
    return lax.ppermute(rows, axis, pairs + [(j, i) for i, j in pairs])


def swap_far(axis, rows):
    return swap_near(axis, rows, 1)


def gather_totals(plan, total, y_near, y_far):
    if plan.slots:
        return lax.all_to_all(total, ("gx", "gy"), split_axis=0, concat_axis=0, tiled=True)
    shape = (plan.groups, 3, plan.owners, plan.p)
    parts = lax.all_gather(lax.psum(total, "gx"), "gy").reshape(shape)
    blank = jnp.zeros((1, plan.owners, plan.p), F32)
    to_below, own, to_above = (parts[:, k] for k in range(3))
    own = own + jnp.concatenate([blank, to_above[:-1]]) + jnp.concatenate([to_below[1:], blank])
    own = jnp.concatenate([blank, own, blank])
    g, h = lax.axis_index("gx"), lax.axis_index("gy")
    rows = [lax.dynamic_index_in_dim(own, h + 1, 0, False)]
    up = lax.rem(h, 2) == 0
    far = y_far[: y_near.shape[0]]
    for place, at, msg in (
        (h, plan.half_y - 1, jnp.where(up, far, y_near)),
        (h + 2, 0, jnp.where(up, y_near, far)),
    ):
        ident = lax.dynamic_index_in_dim(msg, plan.map_row + g, 0, False).astype(jnp.int32)
        ident = jnp.stack([ident[i * plan.half_y + at] for i in range(plan.half_x)])
        rows.append(lax.dynamic_index_in_dim(own, place, 0, False)[ident])
    rows = jnp.concatenate(rows)
    rows = jnp.pad(rows, ((0, 4 * plan.slot_parts - rows.shape[0]), (0, 0)))
    return rows.reshape(1, plan.slot_parts, 4, plan.p)


def on_device(conc, pot, mass_source, pot_source, mask, kind, table, owner_map):
    plan = Plan(conc.shape, lax.axis_size("gx"), lax.axis_size("gy"))
    block = conc.shape
    fields = [conc, pot, mask, kind, mass_source, pot_source]
    messages = call(
        prepare_kernel,
        plan,
        [*[(3 * plan.y, plan.p)] * 2, (plan.y_rows, plan.p), (plan.y_far_rows, plan.p)],
        [*fields, owner_map, table],
        far=range(8),
        scratch=(
            *[pltpu.VMEM((2, plan.y, plan.p), field.dtype) for field in fields[:4]],
            *[pltpu.VMEM((2, plan.x, 8, plan.p), field.dtype) for field in fields],
            pltpu.VMEM(owner_map.shape, owner_map.dtype),
            pltpu.SMEM(table.shape, table.dtype),
            pltpu.SemaphoreType.DMA((22,)),
        ),
    )
    x_near, x_far = swap_near("gx", messages[0]), swap_far("gx", messages[1])
    y_near, y_far = swap_near("gy", messages[2]), swap_far("gy", messages[3])
    y_far, mask, kind = lax.optimization_barrier((y_far, mask, kind))
    mob, gather, spread, scale, *parts = call(
        local_kernel,
        plan,
        [
            block, (plan.owners, plan.rows), (plan.rows, 3 * plan.owners), (plan.owners, plan.p),
            (5, *block), block, block, block,
        ],
        [conc, pot, mask, kind, mass_source, pot_source, table, owner_map],
        smem=(6,),
    )
    slots = (plan.slots, plan.slot_parts, 4, plan.p) if plan.slots else (3 * plan.owners, plan.p)
    conc, pot, total, raw, near, far = call(
        first_kernel,
        plan,
        [
            block,
            block,
            slots,
            (4 * plan.x, plan.p),
            *[(2 * plan.y + 8, plan.p)] * 2,
        ],
        [
            x_far, x_near, y_far, y_near,
            conc, pot, mob, mass_source, pot_source, gather, scale, owner_map, *parts,
        ],
        out_far=(2,),
        scratch=(pltpu.VMEM(slots, F32), pltpu.SemaphoreType.DMA((plan.owners // 2,))),
    )
    total = gather_totals(plan, total, y_near, y_far)
    far = swap_far("gx", far)
    near = swap_near("gx", near)
    faces, diagonal, scale, ends = call(
        beside_kernel,
        plan,
        [(6, *block), block, block, (4 * plan.x, plan.p)],
        [near, far, mob, raw, x_near, x_far, y_near, y_far],
    )
    return tuple(
        call(
            last_kernel,
            plan,
            [block, block],
            [conc, pot, mass_source, pot_source, faces, diagonal, scale, near, far, ends, spread, total],
            out_far=(0, 1),
            scratch=(
                pltpu.VMEM(block, F32),
                pltpu.VMEM(block, F32),
                pltpu.SemaphoreType.DMA((2 * plan.x,)),
            ),
        )
    )


def solution(mesh):
    grid = P("gx", "gy", None)
    return jax.shard_map(
        on_device,
        mesh=mesh,
        in_specs=(grid,) * 6 + (P(), P(None, "gy")),
        out_specs=(grid, grid),
        check_vma=False,
    )
```

```python
import functools

import jax
import jax.numpy as jnp
from jax import lax
from jax.experimental import pallas as pl
from jax.experimental.pallas import tpu as pltpu
from jax.sharding import PartitionSpec as P

CSWEEP = 3

time_step = 0.25
split_slope = 1.0
interface = 0.5
relax_fine = 0.6
relax_coarse = 0.6
coarse_flux = 0.0625
coarse_bend = 0.125
coarse_det = 1.0 + 2.0 * coarse_flux * (split_slope + 2.0 * coarse_bend)

F32 = jnp.float32
BF16 = jnp.bfloat16
VMEM_LIMIT = 48 * 1024 * 1024


def iota(shape, dim):
    return lax.broadcasted_iota(jnp.int32, shape, dim)


def x_pair(field, low, high):
    return (
        jnp.concatenate([low, field[:-1]], axis=0),
        jnp.concatenate([field[1:], high], axis=0),
    )


def y_pair(field, low, high):
    size = field.shape[1]
    where = iota(field.shape, 1)
    return (
        jnp.where(where == 0, low, pltpu.roll(field, 1, 1)),
        jnp.where(where == size - 1, high, pltpu.roll(field, size - 1, 1)),
    )


def plane_pair(field):
    size = field.shape[2]
    where = iota(field.shape, 2)
    return (
        jnp.where(where == 0, 0.0, pltpu.roll(field, 1, 2)),
        jnp.where(where == size - 1, 0.0, pltpu.roll(field, size - 1, 2)),
    )


def neighbours(field, halo):
    xm, xp, ym, yp = halo
    return (*x_pair(field, xm, xp), *y_pair(field, ym, yp), *plane_pair(field))


def excess_of(conc, pot, conc_beside, pot_beside, faces, diagonal, mass_source, pot_source):
    excess_mass = (mass_source - conc) - diagonal * pot
    for face, other in zip(faces, pot_beside):
        excess_mass = excess_mass + face * other
    beside = conc_beside[0]
    for other in conc_beside[1:]:
        beside = beside + other
    excess_pot = (pot_source - pot) + (split_slope + 6.0 * interface) * conc - interface * beside
    return excess_mass, excess_pot


def scale_from(diagonal):
    return relax_fine / (1.0 + (split_slope + 6.0 * interface) * diagonal)


def relax_pair(conc, pot, excess_mass, excess_pot, diagonal, scale):
    new_conc = conc + (excess_mass - diagonal * excess_pot) * scale
    new_pot = pot + (excess_pot + (split_slope + 6.0 * interface) * excess_mass) * scale
    return new_conc, new_pot


def faces_of(mobility, beside):
    faces = tuple((0.5 * time_step) * (mobility + other) for other in beside)
    diagonal = faces[0]
    for face in faces[1:]:
        diagonal = diagonal + face
    return faces, diagonal


def split_dot(ones, values, contract):
    dims = (contract, ((), ()))
    total = None
    rest = values
    for _ in range(3):
        term = rest.astype(BF16)
        rest = rest - term.astype(F32)
        part = lax.dot_general(ones, term, dims, preferred_element_type=F32)
        total = part if total is None else total + part
    return total


def three_terms(values):
    out = []
    for _ in range(3):
        out.append(values.astype(BF16).astype(F32))
        values = values - out[-1]
    return jnp.concatenate(out, axis=0)


def round_up(value, unit):
    return -(-value // unit) * unit


class Plan:
    def __init__(self, shape, owners, groups):
        self.x, self.y, self.p = shape
        self.owners, self.groups = owners, groups
        self.half_x, self.half_y = self.x // 2, self.y // 2
        self.columns = self.half_x * self.half_y
        self.map_row = round_up(8 * self.x, 8)
        self.y_rows = self.map_row + owners
        self.y_far_rows = max(self.y_rows, 3 * self.y + 8)
        self.cells = self.x * self.y
        self.rows = (self.half_x + 2) * self.y
        self.low_row = owners
        self.high_row = owners + self.half_x
        self.slot_parts = -(-(owners + 2 * self.half_x) // 4)
        slots = owners * groups
        self.slots = slots if slots <= 64 else 0

    def slot_of(self, g, h):
        return (-h % self.groups) * self.owners + g


def side_rows(plan, rows, which):
    return rows[which * plan.y : (which + 1) * plan.y][None]


def side_columns(plan, rows, which):
    return rows[which * plan.x : (which + 1) * plan.x][:, None]


def membership(plan, owner_ref):
    g = lax.axis_index("gx")
    last = plan.owners - 1
    owner = iota((plan.owners, plan.columns), 0)
    low, high = plan.half_x, plan.half_x + 1
    shape = (plan.half_x + 2, plan.y, plan.columns)
    x, y, column = iota(shape, 0), iota(shape, 1), iota(shape, 2)
    half = jnp.where(x < low, x, jnp.where(x == low, plan.half_x - 1, 0))
    place = column == half * plan.half_y + (y >> 1)
    sides = (
        (x < low, g, True),
        (x == low, jnp.maximum(g - 1, 0), g > 0),
        (x == high, jnp.minimum(g + 1, last), g < last),
    )
    gather, spread = None, None
    for part, row, inside in sides:
        hits = ((owner_ref[pl.ds(row, 1), :] == owner) & inside).astype(F32).astype(BF16)
        where = (place & part).astype(F32).reshape(plan.rows, plan.columns).astype(BF16)
        nt = (((1,), (1,)), ((), ()))
        some = lax.dot_general(hits, where, nt, preferred_element_type=F32)
        gather = some if gather is None else gather + some
        some = lax.dot_general(where, hits, nt, preferred_element_type=F32)
        spread = some if spread is None else spread + some
    return gather, jnp.concatenate([spread] * 3, axis=1)


def scale_of(plan, owners):
    owner = iota((plan.owners, plan.columns), 0).astype(owners.dtype)
    hits = jnp.zeros((plan.owners, plan.columns), F32)
    for g in range(plan.owners):
        hits = hits + (owners[g : g + 1] == owner).astype(F32)
    count = jnp.sum(hits, axis=1, keepdims=True)
    return jnp.broadcast_to(0.125 / jnp.maximum(count, 1.0), (plan.owners, plan.p))


def mobility_of(mask, kind, table):
    values = jnp.zeros(kind.shape, F32)
    for marker, value in enumerate(table):
        values = jnp.where(kind == marker, value, values)
    return mask.astype(F32) * values


def even(axis):
    return lax.rem(lax.axis_index(axis), 2) == 0


def put_x(plan, lows, highs, near, far):
    up = even("gx")
    for which, (low, high) in enumerate(zip(lows, highs)):
        near[pl.ds(which * plan.y, plan.y), :] = jnp.where(up, high, low)
        far[pl.ds(which * plan.y, plan.y), :] = jnp.where(up, low, high)


def received(axis, near_ref, far_ref):
    up = even(axis)
    rows = pl.ds(0, min(near_ref.shape[0], far_ref.shape[0]))
    near, far = near_ref[rows, :], far_ref[rows, :]
    return jnp.where(up, far, near), jnp.where(up, near, far)


def prepare_kernel(plan, *refs):
    hbm, refs = refs[:8], refs[8:]
    x_near_ref, x_far_ref, y_near_ref, y_far_ref = refs[:4]
    x_refs, y_refs, (owner_ref, table_ref, sems) = refs[4:8], refs[8:14], refs[14:]
    copies = []

    def start(source, target):
        copies.append(pltpu.make_async_copy(source, target, sems.at[len(copies)]))
        copies[-1].start()

    start(hbm[7], table_ref)
    start(hbm[6], owner_ref)
    for source, target in zip(hbm[:4], x_refs):
        start(source.at[0], target.at[0])
        start(source.at[plan.x - 1], target.at[1])
    for source, target in zip(hbm[:6], y_refs):
        start(source.at[:, pl.ds(0, 8)], target.at[0])
        start(source.at[:, pl.ds(plan.y - 8, 8)], target.at[1])
    for copy in copies:
        copy.wait()
    table = [table_ref[marker] for marker in range(table_ref.shape[0])]
    conc, pot, mask, kind = (ref[...] for ref in x_refs)
    fields = (conc, pot, mobility_of(mask, kind, table))
    put_x(plan, [f[0] for f in fields], [f[1] for f in fields], x_near_ref, x_far_ref)
    conc, pot, mask, kind, mass, pots = (ref[...] for ref in y_refs)
    fields = (conc, pot, mobility_of(mask, kind, table))
    up = even("gy")
    rows = [(field, at) for at in range(2) for field in fields] + [(mass, 0), (pots, 0)]
    for which, (field, at) in enumerate(rows):
        for x in range(plan.x):
            low, high = field[0, x, at : at + 1], field[1, x, 7 - at : 8 - at]
            y_near_ref[pl.ds(which * plan.x + x, 1), :] = jnp.where(up, high, low)
            y_far_ref[pl.ds(which * plan.x + x, 1), :] = jnp.where(up, low, high)
    used = 8 * plan.x
    for ref, rows in ((y_near_ref, plan.y_rows), (y_far_ref, plan.y_far_rows)):
        ref[pl.ds(used, rows - used), :] = jnp.zeros((rows - used, plan.p), F32)
        ref[pl.ds(plan.map_row, plan.owners), pl.ds(0, plan.columns)] = owner_ref[...].astype(F32)


def inner_faces(mobility):
    half = 0.5 * time_step
    shape = mobility.shape
    y, plane = iota(shape, 1), iota(shape, 2)
    to_x = jnp.concatenate(
        [half * (mobility[:-1] + mobility[1:]), jnp.zeros_like(mobility[:1])], axis=0
    )
    out = [to_x]
    for dim, where, shift, edge in (
        (1, y, 1, 0), (1, y, shape[1] - 1, shape[1] - 1),
        (2, plane, 1, 0), (2, plane, shape[2] - 1, shape[2] - 1),
    ):
        face = half * (mobility + pltpu.roll(mobility, shift, dim))
        out.append(jnp.where(where == edge, 0.0, face))
    return out


def inner_flux(faces, field):
    to_x, y_low, y_high, plane_low, plane_high = faces
    size_y, size_p = field.shape[1:]
    from_x = to_x[:-1]
    blank = jnp.zeros_like(field[:1])
    flux = jnp.concatenate([from_x * field[1:], blank], axis=0)
    flux = flux + jnp.concatenate([blank, from_x * field[:-1]], axis=0)
    flux = flux + y_low * pltpu.roll(field, 1, 1) + y_high * pltpu.roll(field, size_y - 1, 1)
    return flux + plane_low * pltpu.roll(field, 1, 2) + plane_high * pltpu.roll(field, size_p - 1, 2)


def inner_excess(conc, pot, faces, diagonal, mass_source, pot_source):
    excess_mass = (mass_source - conc) - diagonal * pot + inner_flux(faces, pot)
    nothing = [jnp.zeros_like(conc[:1])] * 2 + [jnp.zeros_like(conc[:, :1])] * 2
    beside = None
    for other in neighbours(conc, nothing):
        beside = other if beside is None else beside + other
    excess_pot = (pot_source - pot) + (split_slope + 6.0 * interface) * conc - interface * beside
    return excess_mass, excess_pot


def add_edges(field, x_low, x_high, y_low, y_high):
    field = jnp.concatenate(
        [(field[0] + x_low)[None], field[1:-1], (field[-1] + x_high)[None]], axis=0
    )
    row = iota((field.shape[0], 8, field.shape[2]), 1)
    size = field.shape[1]
    low = field[:, :8] + jnp.where(row == 0, y_low, 0.0)
    high = field[:, size - 8 :] + jnp.where(row == 7, y_high, 0.0)
    return jnp.concatenate([low, field[:, 8 : size - 8], high], axis=1)


def local_kernel(
    plan, conc_ref, pot_ref, mask_ref, class_ref, mass_ref, pots_ref, table_ref, owner_ref,
    mob_ref, gather_ref, spread_ref, scale_ref, faces_ref, diagonal_ref, mass_out, pots_out,
):
    table = [table_ref[marker] for marker in range(table_ref.shape[0])]
    mobility = mobility_of(mask_ref[...], class_ref[...], table)
    mob_ref[...] = mobility
    gather_ref[...], spread_ref[...] = membership(plan, owner_ref)
    scale_ref[...] = scale_of(plan, owner_ref[...])
    faces = inner_faces(mobility)
    diagonal = faces[0] + jnp.concatenate([jnp.zeros_like(mobility[:1]), faces[0][:-1]], axis=0)
    for face in faces[1:]:
        diagonal = diagonal + face
    plane = iota(mobility.shape, 2)
    ends = (plane == 0) | (plane == plan.p - 1)
    diagonal = diagonal + jnp.where(ends, (0.5 * time_step) * mobility, 0.0)
    for i, face in enumerate(faces):
        faces_ref[i] = face
    diagonal_ref[...] = diagonal
    mass_out[...], pots_out[...] = inner_excess(
        conc_ref[...], pot_ref[...], faces, diagonal, mass_ref[...], pots_ref[...]
    )


def first_kernel(
    plan, x_far_ref, x_near_ref, y_far_ref, y_near_ref,
    conc_ref, pot_ref, mob_ref, mass_ref, pots_ref, gather_ref, scale_ref, owner_ref,
    faces_ref, diagonal_ref, mass_part_ref, pot_part_ref,
    conc_out, pot_out, total_hbm, raw_out, x_near_out, x_far_out, total_out, sems,
):
    sides = received("gx", x_near_ref, x_far_ref)
    ends = received("gy", y_near_ref, y_far_ref)
    last_x, last_y = plan.x - 1, plan.y - 1

    def halo(which):
        return tuple(side_rows(plan, rows, which)[0] for rows in sides) + tuple(
            side_columns(plan, rows, which) for rows in ends
        )

    def edges(field):
        return field[0], field[last_x], field[:, :1], field[:, last_y:]

    mobility = mob_ref[...]
    raw_conc, raw_pot = conc_ref[...], pot_ref[...]
    outer = [
        (0.5 * time_step) * (own + other) for own, other in zip(edges(mobility), halo(2))
    ]
    diagonal = add_edges(diagonal_ref[...], *outer)
    excess_mass = add_edges(
        mass_part_ref[...],
        *(f * (other - own) for f, own, other in zip(outer, edges(raw_pot), halo(1))),
    )
    excess_pot = add_edges(pot_part_ref[...], *(-interface * other for other in halo(0)))
    conc, pot = relax_pair(
        raw_conc, raw_pot, excess_mass, excess_pot, diagonal, scale_from(diagonal)
    )

    own_mass, own_pot = inner_excess(
        conc, pot, [faces_ref[i] for i in range(5)], diagonal, mass_ref[...], pots_ref[...]
    )
    give_mass, give_pot = (
        [field[x] + field[x + 1] for x in range(0, plan.x, 2)] for field in (own_mass, own_pot)
    )
    for x, side in ((0, 0), (last_x, 1)):
        give_mass.append(outer[side] * pot[x])
        give_pot.append(-interface * conc[x])

    def packed(mass, other):
        first = iota(mass.shape, 1) & 1 == 0
        return jnp.where(
            first, mass + pltpu.roll(mass, plan.p - 1, 1), other + pltpu.roll(other, 1, 1)
        )

    give = packed(jnp.concatenate(give_mass, axis=0), jnp.concatenate(give_pot, axis=0))
    h = lax.axis_index("gy")
    inside = (h > 0, None, h < plan.groups - 1)
    maps = [rows[plan.map_row : plan.map_row + plan.owners, : plan.columns] for rows in ends]
    maps.insert(1, owner_ref[...].astype(F32))
    owner = iota((plan.owners, 1), 0)
    is_mine = owner == lax.axis_index("gx")

    sums = [None, split_dot(gather_ref[...].astype(BF16), give, ((1,), (0,))), None]
    sums[1] = sums[1] * scale_ref[...]
    for place, y, at, side in ((0, 0, plan.half_y - 1, 2), (2, plan.y - 1, 0, 3)):
        edge_pot, edge_conc = (
            jnp.concatenate([field[x, y : y + 1] for x in range(plan.x)], axis=0)
            for field in (pot, conc)
        )
        both = packed(outer[side][:, 0] * edge_pot, -interface * edge_conc)
        part = jnp.zeros((plan.owners, plan.p), F32)
        for i in range(plan.half_x):
            column = owner_column(plan, maps[place], i, at)
            ident = jnp.sum(jnp.where(is_mine, column, 0.0), axis=0, keepdims=True)
            pair = both[2 * i : 2 * i + 1] + both[2 * i + 1 : 2 * i + 2]
            part = part + jnp.where((owner.astype(F32) == ident) & inside[place], pair, 0.0)
        sums[place] = part * scale_of(plan, maps[place])
    def store_fields():
        conc_out[...] = conc
        pot_out[...] = pot
        for at, field in enumerate((raw_conc, raw_pot)):
            for x in range(plan.x):
                raw_out[pl.ds(2 * at * plan.x + x, 1), :] = field[x, 0:1]
                raw_out[pl.ds((2 * at + 1) * plan.x + x, 1), :] = field[x, last_y : last_y + 1]
        put_x(plan, (conc[0], pot[0]), (conc[last_x], pot[last_x]), x_near_out, x_far_out)
        up = even("gx")
        base = 2 * plan.y
        for which in range(3):
            for end, rows in enumerate(ends):
                low = rows[which * plan.x : which * plan.x + 1]
                high = rows[(which + 1) * plan.x - 1 : (which + 1) * plan.x]
                x_near_out[pl.ds(base + 2 * which + end, 1), :] = jnp.where(up, high, low)
                x_far_out[pl.ds(base + 2 * which + end, 1), :] = jnp.where(up, low, high)
        for ref in (x_near_out, x_far_out):
            ref[pl.ds(base + 6, 2), :] = jnp.zeros((2, plan.p), F32)

    if not plan.slots:
        total_out[...] = jnp.concatenate(sums, axis=0)
        copies = [pltpu.make_async_copy(total_out, total_hbm, sems.at[0])]
        copies[0].start()
        store_fields()
        copies[0].wait()
        return

    def picked(place, i, at):
        column = owner_column(plan, maps[place], i, at)
        ident = jnp.broadcast_to(column, (plan.owners, plan.p))
        out = jnp.zeros((plan.owners, plan.p), F32)
        for o in range(plan.owners):
            out = jnp.where(ident == float(o), sums[place][o : o + 1], out)
        return out

    below = [[picked(k, i, plan.half_y - 1) for i in range(plan.half_x)] for k in range(3)]
    above = [[picked(k, i, 0) for i in range(plan.half_x)] for k in range(3)]

    def of_plane(plane, choices):
        out = jnp.zeros((plan.owners, plan.p), F32)
        for k in range(3):
            out = jnp.where(plane == h + (k - 1), choices[k], out)
        return out

    size = 4 * plan.slot_parts
    rows = []
    for plane in range(plan.groups):
        beside = []
        for i in range(plan.half_x):
            beside.append((plan.low_row + i, of_plane(plane - 1, [k[i] for k in below])))
            beside.append((plan.high_row + i, of_plane(plane + 1, [k[i] for k in above])))
        blank = jnp.zeros((plan.owners, plan.p), F32)
        beside += [(at, blank) for at in range(plan.high_row + plan.half_x, size)]
        rows.append((of_plane(plane, sums), beside))
    copies = []
    for plane, (main, beside) in enumerate(rows):
        for g in range(plan.owners):
            slot = plan.slot_of(g, plane)
            for part in range(plan.owners // 4):
                total_out[slot, part] = main[4 * part : 4 * part + 4]
            for row, values in beside:
                total_out[slot, row // 4, pl.ds(row % 4, 1), :] = values[g : g + 1]
        some = pl.ds(plan.slot_of(0, plane), plan.owners)
        copies.append(
            pltpu.make_async_copy(total_out.at[some], total_hbm.at[some], sems.at[plane])
        )
        copies[-1].start()
    store_fields()
    for copy in copies:
        copy.wait()


def owner_column(plan, owners, i, at):
    b = i * plan.half_y + at
    return owners[:, b : b + 1]


def coarse_solve(packed, planes):
    lane = iota(packed.shape, 1)
    even = lane & 1 == 0
    mass_mean = jnp.where(even, packed, pltpu.roll(packed, 1, 1))
    pot_mean = jnp.where(even, pltpu.roll(packed, planes - 1, 1), packed)

    def neighbour_sum(values):
        return jnp.where(lane >= 2, pltpu.roll(values, 2, 1), 0.0) + jnp.where(
            lane < planes - 2, pltpu.roll(values, planes - 2, 1), 0.0
        )

    def step(mass_gap, pot_gap):
        scale = relax_coarse / coarse_det
        return (
            scale * (mass_gap - 2.0 * coarse_flux * pot_gap),
            scale * (pot_gap + (split_slope + 2.0 * coarse_bend) * mass_gap),
        )

    coarse_conc, coarse_pot = step(mass_mean, pot_mean)
    for _ in range(CSWEEP - 1):
        mass_gap = mass_mean - (
            coarse_conc + coarse_flux * (2.0 * coarse_pot - neighbour_sum(coarse_pot))
        )
        pot_gap = pot_mean - (
            coarse_pot
            - split_slope * coarse_conc
            + coarse_bend * (neighbour_sum(coarse_conc) - 2.0 * coarse_conc)
        )
        more_conc, more_pot = step(mass_gap, pot_gap)
        coarse_conc, coarse_pot = coarse_conc + more_conc, coarse_pot + more_pot
    return coarse_conc, coarse_pot


def beside_kernel(
    plan, x_near_ref, x_far_ref, mob_ref, raw_ref, x_near_msg, x_far_msg, y_near_msg, y_far_msg,
    faces_out, diagonal_out, scale_out, ends_out,
):
    mobility = mob_ref[...]
    sides = received("gx", x_near_msg, x_far_msg)
    ends = received("gy", y_near_msg, y_far_msg)
    halo = tuple(side_rows(plan, rows, 2) for rows in sides) + tuple(
        side_columns(plan, rows, 2) for rows in ends
    )
    faces, diagonal = faces_of(mobility, neighbours(mobility, halo))
    for i, face in enumerate(faces):
        faces_out[i] = face
    diagonal_out[...] = diagonal
    scale_out[...] = scale_from(diagonal)

    corners = received("gx", x_near_ref, x_far_ref)
    h = lax.axis_index("gy")
    inside = (h > 0, h < plan.groups - 1)
    own_mob = [
        jnp.concatenate([mobility[x, y : y + 1] for x in range(plan.x)], axis=0)
        for y in (0, plan.y - 1)
    ]
    for end, rows in enumerate(ends):

        def row(which):
            return rows[which * plan.x : (which + 1) * plan.x]

        def beside(which, own):
            here = row(which)
            at = 2 * plan.y + 2 * which + end
            wide = jnp.concatenate([corners[0][at : at + 1], here, corners[1][at : at + 1]], axis=0)
            return (
                wide[: plan.x], wide[2:], own, row(which + 3),
                *(part[0] for part in plane_pair(here[None])),
            )

        raw = [
            raw_ref[pl.ds((2 * which + end) * plan.x, plan.x), :] for which in range(2)
        ]
        faces, diagonal = faces_of(row(2), beside(2, own_mob[end]))
        excess = excess_of(
            row(0), row(1), beside(0, raw[0]), beside(1, raw[1]), faces, diagonal, row(6), row(7)
        )
        new = relax_pair(row(0), row(1), *excess, diagonal, scale_from(diagonal))
        for which, values in enumerate(new):
            ends_out[pl.ds((2 * which + end) * plan.x, plan.x), :] = jnp.where(
                inside[end], values, 0.0
            )


def last_kernel(
    plan, conc_ref, pot_ref, mass_ref, pots_ref, faces_ref, diagonal_ref, scale_ref,
    x_near_ref, x_far_ref, ends_ref, spread_ref, total_ref,
    conc_hbm, pot_hbm, conc_out, pot_out, sems,
):
    parts = []
    for part in range(plan.slot_parts):
        terms = [total_ref[slot, part] for slot in range(total_ref.shape[0])]
        while len(terms) > 1:
            pairs = [a + b for a, b in zip(terms[::2], terms[1::2])]
            terms = pairs + terms[len(pairs) * 2 :]
        parts.append(terms[0])
    solved = jnp.concatenate(
        coarse_solve(jnp.concatenate(parts, axis=0), plan.p), axis=1
    )
    own = lax.dot_general(
        spread_ref[...].astype(BF16),
        three_terms(solved[: plan.owners]).astype(BF16),
        (((1,), (0,)), ((), ())),
        preferred_element_type=F32,
    )
    sides = received("gx", x_near_ref, x_far_ref)

    def updated(which, ref):
        lanes = slice(which * plan.p, (which + 1) * plan.p)
        corr = own[:, lanes]
        slabs = [side_rows(plan, sides[0], which)]
        slabs += [ref[pl.ds(x, 1)] for x in range(plan.x)]
        slabs.append(side_rows(plan, sides[1], which))
        order = [plan.half_x, *[x >> 1 for x in range(plan.x)], plan.half_x + 1]
        slabs = [
            slab + corr[x * plan.y : (x + 1) * plan.y][None] for slab, x in zip(slabs, order)
        ]
        ends = []
        for end, begin in enumerate((plan.low_row, plan.high_row)):
            rows = ends_ref[pl.ds((2 * which + end) * plan.x, plan.x), :]
            ends.append([
                (rows[x : x + 1] + solved[begin + (x >> 1) : begin + (x >> 1) + 1, lanes])[None]
                for x in range(plan.x)
            ])
        return slabs, ends

    conc, conc_ends = updated(0, conc_ref)
    pot, pot_ends = updated(1, pot_ref)

    def beside(slabs, ends, x):
        here = slabs[x + 1]
        return (
            slabs[x], slabs[x + 2], *y_pair(here, ends[0][x], ends[1][x]), *plane_pair(here)
        )

    copies = []
    for x in range(plan.x):
        one = pl.ds(x, 1)
        diagonal = diagonal_ref[one]
        excess = excess_of(
            conc[x + 1], pot[x + 1], beside(conc, conc_ends, x), beside(pot, pot_ends, x),
            [faces_ref[i, one] for i in range(6)], diagonal, mass_ref[one], pots_ref[one],
        )
        conc_out[one], pot_out[one] = relax_pair(
            conc[x + 1], pot[x + 1], *excess, diagonal, scale_ref[one]
        )
        for source, target in ((conc_out, conc_hbm), (pot_out, pot_hbm)):
            copies.append(
                pltpu.make_async_copy(source.at[one], target.at[one], sems.at[len(copies)])
            )
            copies[-1].start()
    for copy in copies:
        copy.wait()


def call(kernel, plan, outs, args, far=(), smem=(), scratch=(), out_far=()):
    def space(i):
        return pl.ANY if i in far else pltpu.SMEM if i in smem else pltpu.VMEM

    return pl.pallas_call(
        functools.partial(kernel, plan),
        out_shape=[jax.ShapeDtypeStruct(shape, F32) for shape in outs],
        in_specs=[pl.BlockSpec(memory_space=space(i)) for i in range(len(args))],
        out_specs=[
            pl.BlockSpec(memory_space=pl.ANY if i in out_far else pltpu.VMEM)
            for i in range(len(outs))
        ],
        scratch_shapes=list(scratch),
        compiler_params=pltpu.CompilerParams(vmem_limit_bytes=VMEM_LIMIT),
    )(*[
        pltpu.with_memory_space_constraint(arg, pltpu.HBM) if i in far else arg
        for i, arg in enumerate(args)
    ])


def swap_near(axis, rows, begin=0):
    pairs = [(i, i + 1) for i in range(begin, lax.axis_size(axis) - 1, 2)]
    return lax.ppermute(rows, axis, pairs + [(j, i) for i, j in pairs])


def swap_far(axis, rows):
    return swap_near(axis, rows, 1)


def gather_totals(plan, total, y_near, y_far):
    if plan.slots:
        order = [0] * plan.slots
        for g in range(plan.owners):
            for h in range(plan.groups):
                order[plan.slot_of(g, h)] = g * plan.groups + h
        return lax.all_to_all(
            total, ("gx", "gy"), split_axis=0, concat_axis=0, axis_index_groups=[order], tiled=True
        )
    shape = (plan.groups, 3, plan.owners, plan.p)
    parts = lax.all_gather(lax.psum(total, "gx"), "gy").reshape(shape)
    blank = jnp.zeros((1, plan.owners, plan.p), F32)
    to_below, own, to_above = (parts[:, k] for k in range(3))
    own = own + jnp.concatenate([blank, to_above[:-1]]) + jnp.concatenate([to_below[1:], blank])
    own = jnp.concatenate([blank, own, blank])
    g, h = lax.axis_index("gx"), lax.axis_index("gy")
    rows = [lax.dynamic_index_in_dim(own, h + 1, 0, False)]
    up = lax.rem(h, 2) == 0
    far = y_far[: y_near.shape[0]]
    for place, at, msg in (
        (h, plan.half_y - 1, jnp.where(up, far, y_near)),
        (h + 2, 0, jnp.where(up, y_near, far)),
    ):
        ident = lax.dynamic_index_in_dim(msg, plan.map_row + g, 0, False).astype(jnp.int32)
        ident = jnp.stack([ident[i * plan.half_y + at] for i in range(plan.half_x)])
        rows.append(lax.dynamic_index_in_dim(own, place, 0, False)[ident])
    rows = jnp.concatenate(rows)
    rows = jnp.pad(rows, ((0, 4 * plan.slot_parts - rows.shape[0]), (0, 0)))
    return rows.reshape(1, plan.slot_parts, 4, plan.p)


def on_device(conc, pot, mass_source, pot_source, mask, kind, table, owner_map):
    plan = Plan(conc.shape, lax.axis_size("gx"), lax.axis_size("gy"))
    block = conc.shape
    fields = [conc, pot, mask, kind, mass_source, pot_source]
    messages = call(
        prepare_kernel,
        plan,
        [*[(3 * plan.y, plan.p)] * 2, (plan.y_rows, plan.p), (plan.y_far_rows, plan.p)],
        [*fields, owner_map, table],
        far=range(8),
        scratch=(
            *[pltpu.VMEM((2, plan.y, plan.p), field.dtype) for field in fields[:4]],
            *[pltpu.VMEM((2, plan.x, 8, plan.p), field.dtype) for field in fields],
            pltpu.VMEM(owner_map.shape, owner_map.dtype),
            pltpu.SMEM(table.shape, table.dtype),
            pltpu.SemaphoreType.DMA((22,)),
        ),
    )
    x_near, x_far = swap_near("gx", messages[0]), swap_far("gx", messages[1])
    y_near, y_far = swap_near("gy", messages[2]), swap_far("gy", messages[3])
    y_far, mask, kind = lax.optimization_barrier((y_far, mask, kind))
    mob, gather, spread, scale, *parts = call(
        local_kernel,
        plan,
        [
            block, (plan.owners, plan.rows), (plan.rows, 3 * plan.owners), (plan.owners, plan.p),
            (5, *block), block, block, block,
        ],
        [conc, pot, mask, kind, mass_source, pot_source, table, owner_map],
        smem=(6,),
    )
    slots = (plan.slots, plan.slot_parts, 4, plan.p) if plan.slots else (3 * plan.owners, plan.p)
    conc, pot, total, raw, near, far = call(
        first_kernel,
        plan,
        [
            block,
            block,
            slots,
            (4 * plan.x, plan.p),
            *[(2 * plan.y + 8, plan.p)] * 2,
        ],
        [
            x_far, x_near, y_far, y_near,
            conc, pot, mob, mass_source, pot_source, gather, scale, owner_map, *parts,
        ],
        out_far=(2,),
        scratch=(pltpu.VMEM(slots, F32), pltpu.SemaphoreType.DMA((plan.groups,))),
    )
    total = gather_totals(plan, total, y_near, y_far)
    far = swap_far("gx", far)
    near = swap_near("gx", near)
    faces, diagonal, scale, ends = call(
        beside_kernel,
        plan,
        [(6, *block), block, block, (4 * plan.x, plan.p)],
        [near, far, mob, raw, x_near, x_far, y_near, y_far],
    )
    return tuple(
        call(
            last_kernel,
            plan,
            [block, block],
            [conc, pot, mass_source, pot_source, faces, diagonal, scale, near, far, ends, spread, total],
            out_far=(0, 1),
            scratch=(
                pltpu.VMEM(block, F32),
                pltpu.VMEM(block, F32),
                pltpu.SemaphoreType.DMA((2 * plan.x,)),
            ),
        )
    )


def solution(mesh):
    grid = P("gx", "gy", None)
    return jax.shard_map(
        on_device,
        mesh=mesh,
        in_specs=(grid,) * 6 + (P(), P(None, "gy")),
        out_specs=(grid, grid),
        check_vma=False,
    )
```

```python
import functools

import jax
import jax.numpy as jnp
from jax import lax
from jax.experimental import pallas as pl
from jax.experimental.pallas import tpu as pltpu
from jax.sharding import PartitionSpec as P

CSWEEP = 3

time_step = 0.25
split_slope = 1.0
interface = 0.5
relax_fine = 0.6
relax_coarse = 0.6
coarse_flux = 0.0625
coarse_bend = 0.125
coarse_det = 1.0 + 2.0 * coarse_flux * (split_slope + 2.0 * coarse_bend)

F32 = jnp.float32
BF16 = jnp.bfloat16
VMEM_LIMIT = 48 * 1024 * 1024


def iota(shape, dim):
    return lax.broadcasted_iota(jnp.int32, shape, dim)


def x_pair(field, low, high):
    return (
        jnp.concatenate([low, field[:-1]], axis=0),
        jnp.concatenate([field[1:], high], axis=0),
    )


def y_pair(field, low, high):
    size = field.shape[1]
    where = iota(field.shape, 1)
    return (
        jnp.where(where == 0, low, pltpu.roll(field, 1, 1)),
        jnp.where(where == size - 1, high, pltpu.roll(field, size - 1, 1)),
    )


def plane_pair(field):
    size = field.shape[2]
    where = iota(field.shape, 2)
    return (
        jnp.where(where == 0, 0.0, pltpu.roll(field, 1, 2)),
        jnp.where(where == size - 1, 0.0, pltpu.roll(field, size - 1, 2)),
    )


def neighbours(field, halo):
    xm, xp, ym, yp = halo
    return (*x_pair(field, xm, xp), *y_pair(field, ym, yp), *plane_pair(field))


def excess_of(conc, pot, conc_beside, pot_beside, faces, diagonal, mass_source, pot_source):
    excess_mass = (mass_source - conc) - diagonal * pot
    for face, other in zip(faces, pot_beside):
        excess_mass = excess_mass + face * other
    beside = conc_beside[0]
    for other in conc_beside[1:]:
        beside = beside + other
    excess_pot = (pot_source - pot) + (split_slope + 6.0 * interface) * conc - interface * beside
    return excess_mass, excess_pot


def scale_from(diagonal):
    return relax_fine / (1.0 + (split_slope + 6.0 * interface) * diagonal)


def relax_pair(conc, pot, excess_mass, excess_pot, diagonal, scale):
    new_conc = conc + (excess_mass - diagonal * excess_pot) * scale
    new_pot = pot + (excess_pot + (split_slope + 6.0 * interface) * excess_mass) * scale
    return new_conc, new_pot


def faces_of(mobility, beside):
    faces = tuple((0.5 * time_step) * (mobility + other) for other in beside)
    diagonal = faces[0]
    for face in faces[1:]:
        diagonal = diagonal + face
    return faces, diagonal


def split_dot(ones, values, contract):
    dims = (contract, ((), ()))
    total = None
    rest = values
    for _ in range(3):
        term = rest.astype(BF16)
        rest = rest - term.astype(F32)
        part = lax.dot_general(ones, term, dims, preferred_element_type=F32)
        total = part if total is None else total + part
    return total


def three_terms(values):
    out = []
    for _ in range(3):
        out.append(values.astype(BF16).astype(F32))
        values = values - out[-1]
    return jnp.concatenate(out, axis=0)


def round_up(value, unit):
    return -(-value // unit) * unit


class Plan:
    def __init__(self, shape, owners, groups):
        self.x, self.y, self.p = shape
        self.owners, self.groups = owners, groups
        self.half_x, self.half_y = self.x // 2, self.y // 2
        self.columns = self.half_x * self.half_y
        self.map_row = round_up(8 * self.x, 8)
        self.y_rows = self.map_row + owners
        self.y_far_rows = max(self.y_rows, 3 * self.y + 8)
        self.cells = self.x * self.y
        self.rows = (self.half_x + 2) * self.y
        self.low_row = owners
        self.high_row = owners + self.half_x
        self.slot_parts = -(-(owners + 2 * self.half_x) // 4)
        slots = owners * groups
        self.slots = slots if slots <= 64 else 0

    def slot_of(self, g, h):
        return (-h % self.groups) * self.owners + self.owners - 1 - g


def side_rows(plan, rows, which):
    return rows[which * plan.y : (which + 1) * plan.y][None]


def side_columns(plan, rows, which):
    return rows[which * plan.x : (which + 1) * plan.x][:, None]


def membership(plan, owner_ref):
    g = lax.axis_index("gx")
    last = plan.owners - 1
    owner = iota((plan.owners, plan.columns), 0)
    low, high = plan.half_x, plan.half_x + 1
    shape = (plan.half_x + 2, plan.y, plan.columns)
    x, y, column = iota(shape, 0), iota(shape, 1), iota(shape, 2)
    half = jnp.where(x < low, x, jnp.where(x == low, plan.half_x - 1, 0))
    place = column == half * plan.half_y + (y >> 1)
    sides = (
        (x < low, g, True),
        (x == low, jnp.maximum(g - 1, 0), g > 0),
        (x == high, jnp.minimum(g + 1, last), g < last),
    )
    gather, spread = None, None
    for part, row, inside in sides:
        hits = ((owner_ref[pl.ds(row, 1), :] == owner) & inside).astype(F32).astype(BF16)
        where = (place & part).astype(F32).reshape(plan.rows, plan.columns).astype(BF16)
        nt = (((1,), (1,)), ((), ()))
        some = lax.dot_general(hits, where, nt, preferred_element_type=F32)
        gather = some if gather is None else gather + some
        some = lax.dot_general(where, hits, nt, preferred_element_type=F32)
        spread = some if spread is None else spread + some
    return gather, jnp.concatenate([spread] * 3, axis=1)


def scale_of(plan, owners):
    owner = iota((plan.owners, plan.columns), 0).astype(owners.dtype)
    hits = jnp.zeros((plan.owners, plan.columns), F32)
    for g in range(plan.owners):
        hits = hits + (owners[g : g + 1] == owner).astype(F32)
    count = jnp.sum(hits, axis=1, keepdims=True)
    return jnp.broadcast_to(0.125 / jnp.maximum(count, 1.0), (plan.owners, plan.p))


def mobility_of(mask, kind, table):
    values = jnp.zeros(kind.shape, F32)
    for marker, value in enumerate(table):
        values = jnp.where(kind == marker, value, values)
    return mask.astype(F32) * values


def even(axis):
    return lax.rem(lax.axis_index(axis), 2) == 0


def put_x(plan, lows, highs, near, far):
    up = even("gx")
    for which, (low, high) in enumerate(zip(lows, highs)):
        near[pl.ds(which * plan.y, plan.y), :] = jnp.where(up, high, low)
        far[pl.ds(which * plan.y, plan.y), :] = jnp.where(up, low, high)


def received(axis, near_ref, far_ref):
    up = even(axis)
    rows = pl.ds(0, min(near_ref.shape[0], far_ref.shape[0]))
    near, far = near_ref[rows, :], far_ref[rows, :]
    return jnp.where(up, far, near), jnp.where(up, near, far)


def prepare_kernel(plan, *refs):
    hbm, refs = refs[:8], refs[8:]
    x_near_ref, x_far_ref, y_near_ref, y_far_ref = refs[:4]
    x_refs, y_refs, (owner_ref, table_ref, sems) = refs[4:8], refs[8:14], refs[14:]
    copies = []

    def start(source, target):
        copies.append(pltpu.make_async_copy(source, target, sems.at[len(copies)]))
        copies[-1].start()

    start(hbm[7], table_ref)
    start(hbm[6], owner_ref)
    for source, target in zip(hbm[:4], x_refs):
        start(source.at[0], target.at[0])
        start(source.at[plan.x - 1], target.at[1])
    for source, target in zip(hbm[:6], y_refs):
        start(source.at[:, pl.ds(0, 8)], target.at[0])
        start(source.at[:, pl.ds(plan.y - 8, 8)], target.at[1])
    for copy in copies:
        copy.wait()
    table = [table_ref[marker] for marker in range(table_ref.shape[0])]
    conc, pot, mask, kind = (ref[...] for ref in x_refs)
    fields = (conc, pot, mobility_of(mask, kind, table))
    put_x(plan, [f[0] for f in fields], [f[1] for f in fields], x_near_ref, x_far_ref)
    conc, pot, mask, kind, mass, pots = (ref[...] for ref in y_refs)
    fields = (conc, pot, mobility_of(mask, kind, table))
    up = even("gy")
    rows = [(field, at) for at in range(2) for field in fields] + [(mass, 0), (pots, 0)]
    for which, (field, at) in enumerate(rows):
        for x in range(plan.x):
            low, high = field[0, x, at : at + 1], field[1, x, 7 - at : 8 - at]
            y_near_ref[pl.ds(which * plan.x + x, 1), :] = jnp.where(up, high, low)
            y_far_ref[pl.ds(which * plan.x + x, 1), :] = jnp.where(up, low, high)
    used = 8 * plan.x
    for ref, rows in ((y_near_ref, plan.y_rows), (y_far_ref, plan.y_far_rows)):
        ref[pl.ds(used, rows - used), :] = jnp.zeros((rows - used, plan.p), F32)
        ref[pl.ds(plan.map_row, plan.owners), pl.ds(0, plan.columns)] = owner_ref[...].astype(F32)


def inner_faces(mobility):
    half = 0.5 * time_step
    shape = mobility.shape
    y, plane = iota(shape, 1), iota(shape, 2)
    to_x = jnp.concatenate(
        [half * (mobility[:-1] + mobility[1:]), jnp.zeros_like(mobility[:1])], axis=0
    )
    out = [to_x]
    for dim, where, shift, edge in (
        (1, y, 1, 0), (1, y, shape[1] - 1, shape[1] - 1),
        (2, plane, 1, 0), (2, plane, shape[2] - 1, shape[2] - 1),
    ):
        face = half * (mobility + pltpu.roll(mobility, shift, dim))
        out.append(jnp.where(where == edge, 0.0, face))
    return out


def inner_flux(faces, field):
    to_x, y_low, y_high, plane_low, plane_high = faces
    size_y, size_p = field.shape[1:]
    from_x = to_x[:-1]
    blank = jnp.zeros_like(field[:1])
    flux = jnp.concatenate([from_x * field[1:], blank], axis=0)
    flux = flux + jnp.concatenate([blank, from_x * field[:-1]], axis=0)
    flux = flux + y_low * pltpu.roll(field, 1, 1) + y_high * pltpu.roll(field, size_y - 1, 1)
    return flux + plane_low * pltpu.roll(field, 1, 2) + plane_high * pltpu.roll(field, size_p - 1, 2)


def inner_excess(conc, pot, faces, diagonal, mass_source, pot_source):
    excess_mass = (mass_source - conc) - diagonal * pot + inner_flux(faces, pot)
    nothing = [jnp.zeros_like(conc[:1])] * 2 + [jnp.zeros_like(conc[:, :1])] * 2
    beside = None
    for other in neighbours(conc, nothing):
        beside = other if beside is None else beside + other
    excess_pot = (pot_source - pot) + (split_slope + 6.0 * interface) * conc - interface * beside
    return excess_mass, excess_pot


def add_edges(field, x_low, x_high, y_low, y_high):
    field = jnp.concatenate(
        [(field[0] + x_low)[None], field[1:-1], (field[-1] + x_high)[None]], axis=0
    )
    row = iota((field.shape[0], 8, field.shape[2]), 1)
    size = field.shape[1]
    low = field[:, :8] + jnp.where(row == 0, y_low, 0.0)
    high = field[:, size - 8 :] + jnp.where(row == 7, y_high, 0.0)
    return jnp.concatenate([low, field[:, 8 : size - 8], high], axis=1)


def local_kernel(
    plan, conc_ref, pot_ref, mask_ref, class_ref, mass_ref, pots_ref, table_ref, owner_ref,
    mob_ref, gather_ref, spread_ref, scale_ref, faces_ref, diagonal_ref, mass_out, pots_out,
):
    table = [table_ref[marker] for marker in range(table_ref.shape[0])]
    mobility = mobility_of(mask_ref[...], class_ref[...], table)
    mob_ref[...] = mobility
    gather_ref[...], spread_ref[...] = membership(plan, owner_ref)
    scale_ref[...] = scale_of(plan, owner_ref[...])
    faces = inner_faces(mobility)
    diagonal = faces[0] + jnp.concatenate([jnp.zeros_like(mobility[:1]), faces[0][:-1]], axis=0)
    for face in faces[1:]:
        diagonal = diagonal + face
    plane = iota(mobility.shape, 2)
    ends = (plane == 0) | (plane == plan.p - 1)
    diagonal = diagonal + jnp.where(ends, (0.5 * time_step) * mobility, 0.0)
    for i, face in enumerate(faces):
        faces_ref[i] = face
    diagonal_ref[...] = diagonal
    mass_out[...], pots_out[...] = inner_excess(
        conc_ref[...], pot_ref[...], faces, diagonal, mass_ref[...], pots_ref[...]
    )


def first_kernel(
    plan, x_far_ref, x_near_ref, y_far_ref, y_near_ref,
    conc_ref, pot_ref, mob_ref, mass_ref, pots_ref, gather_ref, scale_ref, owner_ref,
    faces_ref, diagonal_ref, mass_part_ref, pot_part_ref,
    conc_out, pot_out, total_hbm, raw_out, x_near_out, x_far_out, total_out, sems,
):
    sides = received("gx", x_near_ref, x_far_ref)
    ends = received("gy", y_near_ref, y_far_ref)
    last_x, last_y = plan.x - 1, plan.y - 1

    def halo(which):
        return tuple(side_rows(plan, rows, which)[0] for rows in sides) + tuple(
            side_columns(plan, rows, which) for rows in ends
        )

    def edges(field):
        return field[0], field[last_x], field[:, :1], field[:, last_y:]

    mobility = mob_ref[...]
    raw_conc, raw_pot = conc_ref[...], pot_ref[...]
    outer = [
        (0.5 * time_step) * (own + other) for own, other in zip(edges(mobility), halo(2))
    ]
    diagonal = add_edges(diagonal_ref[...], *outer)
    excess_mass = add_edges(
        mass_part_ref[...],
        *(f * (other - own) for f, own, other in zip(outer, edges(raw_pot), halo(1))),
    )
    excess_pot = add_edges(pot_part_ref[...], *(-interface * other for other in halo(0)))
    conc, pot = relax_pair(
        raw_conc, raw_pot, excess_mass, excess_pot, diagonal, scale_from(diagonal)
    )

    own_mass, own_pot = inner_excess(
        conc, pot, [faces_ref[i] for i in range(5)], diagonal, mass_ref[...], pots_ref[...]
    )
    give_mass, give_pot = (
        [field[x] + field[x + 1] for x in range(0, plan.x, 2)] for field in (own_mass, own_pot)
    )
    for x, side in ((0, 0), (last_x, 1)):
        give_mass.append(outer[side] * pot[x])
        give_pot.append(-interface * conc[x])

    def packed(mass, other):
        first = iota(mass.shape, 1) & 1 == 0
        return jnp.where(
            first, mass + pltpu.roll(mass, plan.p - 1, 1), other + pltpu.roll(other, 1, 1)
        )

    give = packed(jnp.concatenate(give_mass, axis=0), jnp.concatenate(give_pot, axis=0))
    h = lax.axis_index("gy")
    inside = (h > 0, None, h < plan.groups - 1)
    maps = [rows[plan.map_row : plan.map_row + plan.owners, : plan.columns] for rows in ends]
    maps.insert(1, owner_ref[...].astype(F32))
    owner = iota((plan.owners, 1), 0)
    is_mine = owner == lax.axis_index("gx")

    sums = [None, split_dot(gather_ref[...].astype(BF16), give, ((1,), (0,))), None]
    sums[1] = sums[1] * scale_ref[...]
    for place, y, at, side in ((0, 0, plan.half_y - 1, 2), (2, plan.y - 1, 0, 3)):
        edge_pot, edge_conc = (
            jnp.concatenate([field[x, y : y + 1] for x in range(plan.x)], axis=0)
            for field in (pot, conc)
        )
        both = packed(outer[side][:, 0] * edge_pot, -interface * edge_conc)
        part = jnp.zeros((plan.owners, plan.p), F32)
        for i in range(plan.half_x):
            column = owner_column(plan, maps[place], i, at)
            ident = jnp.sum(jnp.where(is_mine, column, 0.0), axis=0, keepdims=True)
            pair = both[2 * i : 2 * i + 1] + both[2 * i + 1 : 2 * i + 2]
            part = part + jnp.where((owner.astype(F32) == ident) & inside[place], pair, 0.0)
        sums[place] = part * scale_of(plan, maps[place])
    def store_fields():
        conc_out[...] = conc
        pot_out[...] = pot
        for at, field in enumerate((raw_conc, raw_pot)):
            for x in range(plan.x):
                raw_out[pl.ds(2 * at * plan.x + x, 1), :] = field[x, 0:1]
                raw_out[pl.ds((2 * at + 1) * plan.x + x, 1), :] = field[x, last_y : last_y + 1]
        put_x(plan, (conc[0], pot[0]), (conc[last_x], pot[last_x]), x_near_out, x_far_out)
        up = even("gx")
        base = 2 * plan.y
        for which in range(3):
            for end, rows in enumerate(ends):
                low = rows[which * plan.x : which * plan.x + 1]
                high = rows[(which + 1) * plan.x - 1 : (which + 1) * plan.x]
                x_near_out[pl.ds(base + 2 * which + end, 1), :] = jnp.where(up, high, low)
                x_far_out[pl.ds(base + 2 * which + end, 1), :] = jnp.where(up, low, high)
        for ref in (x_near_out, x_far_out):
            ref[pl.ds(base + 6, 2), :] = jnp.zeros((2, plan.p), F32)

    if not plan.slots:
        total_out[...] = jnp.concatenate(sums, axis=0)
        copies = [pltpu.make_async_copy(total_out, total_hbm, sems.at[0])]
        copies[0].start()
        store_fields()
        copies[0].wait()
        return

    def picked(place, i, at):
        column = owner_column(plan, maps[place], i, at)
        ident = jnp.broadcast_to(column, (plan.owners, plan.p))
        out = jnp.zeros((plan.owners, plan.p), F32)
        for o in range(plan.owners):
            out = jnp.where(ident == float(o), sums[place][o : o + 1], out)
        return out

    below = [[picked(k, i, plan.half_y - 1) for i in range(plan.half_x)] for k in range(3)]
    above = [[picked(k, i, 0) for i in range(plan.half_x)] for k in range(3)]

    def of_plane(plane, choices):
        out = jnp.zeros((plan.owners, plan.p), F32)
        for k in range(3):
            out = jnp.where(plane == h + (k - 1), choices[k], out)
        return out

    size = 4 * plan.slot_parts
    rows = []
    for plane in range(plan.groups):
        beside = []
        for i in range(plan.half_x):
            beside.append((plan.low_row + i, of_plane(plane - 1, [k[i] for k in below])))
            beside.append((plan.high_row + i, of_plane(plane + 1, [k[i] for k in above])))
        blank = jnp.zeros((plan.owners, plan.p), F32)
        beside += [(at, blank) for at in range(plan.high_row + plan.half_x, size)]
        rows.append((of_plane(plane, sums), beside))
    copies = []
    for plane, (main, beside) in enumerate(rows):
        for g in range(plan.owners):
            slot = plan.slot_of(g, plane)
            for part in range(plan.owners // 4):
                total_out[slot, part] = main[4 * part : 4 * part + 4]
            for row, values in beside:
                total_out[slot, row // 4, pl.ds(row % 4, 1), :] = values[g : g + 1]
        some = pl.ds(plan.slot_of(plan.owners - 1, plane), plan.owners)
        copies.append(
            pltpu.make_async_copy(total_out.at[some], total_hbm.at[some], sems.at[plane])
        )
        copies[-1].start()
    store_fields()
    for copy in copies:
        copy.wait()


def owner_column(plan, owners, i, at):
    b = i * plan.half_y + at
    return owners[:, b : b + 1]


def coarse_solve(packed, planes):
    lane = iota(packed.shape, 1)
    even = lane & 1 == 0
    mass_mean = jnp.where(even, packed, pltpu.roll(packed, 1, 1))
    pot_mean = jnp.where(even, pltpu.roll(packed, planes - 1, 1), packed)

    def neighbour_sum(values):
        return jnp.where(lane >= 2, pltpu.roll(values, 2, 1), 0.0) + jnp.where(
            lane < planes - 2, pltpu.roll(values, planes - 2, 1), 0.0
        )

    def step(mass_gap, pot_gap):
        scale = relax_coarse / coarse_det
        return (
            scale * (mass_gap - 2.0 * coarse_flux * pot_gap),
            scale * (pot_gap + (split_slope + 2.0 * coarse_bend) * mass_gap),
        )

    coarse_conc, coarse_pot = step(mass_mean, pot_mean)
    for _ in range(CSWEEP - 1):
        mass_gap = mass_mean - (
            coarse_conc + coarse_flux * (2.0 * coarse_pot - neighbour_sum(coarse_pot))
        )
        pot_gap = pot_mean - (
            coarse_pot
            - split_slope * coarse_conc
            + coarse_bend * (neighbour_sum(coarse_conc) - 2.0 * coarse_conc)
        )
        more_conc, more_pot = step(mass_gap, pot_gap)
        coarse_conc, coarse_pot = coarse_conc + more_conc, coarse_pot + more_pot
    return coarse_conc, coarse_pot


def beside_kernel(
    plan, x_near_ref, x_far_ref, conc_ref, pot_ref, mass_ref, pots_ref, mob_ref, raw_ref,
    x_near_msg, x_far_msg, y_near_msg, y_far_msg,
    faces_out, diagonal_out, scale_out, mass_out, pots_out,
):
    mobility = mob_ref[...]
    sides = received("gx", x_near_msg, x_far_msg)
    ends = received("gy", y_near_msg, y_far_msg)
    halo = tuple(side_rows(plan, rows, 2) for rows in sides) + tuple(
        side_columns(plan, rows, 2) for rows in ends
    )
    faces, diagonal = faces_of(mobility, neighbours(mobility, halo))
    block_terms = faces, diagonal, mass_ref[...], pots_ref[...]
    for i, face in enumerate(faces):
        faces_out[i] = face
    diagonal_out[...] = diagonal
    scale_out[...] = scale_from(diagonal)

    corners = received("gx", x_near_ref, x_far_ref)
    h = lax.axis_index("gy")
    inside = (h > 0, h < plan.groups - 1)
    own_mob = [
        jnp.concatenate([mobility[x, y : y + 1] for x in range(plan.x)], axis=0)
        for y in (0, plan.y - 1)
    ]
    halos = [[side_rows(plan, rows, which) for rows in corners] for which in range(2)]
    for end, rows in enumerate(ends):

        def row(which):
            return rows[which * plan.x : (which + 1) * plan.x]

        def beside(which, own):
            here = row(which)
            at = 2 * plan.y + 2 * which + end
            wide = jnp.concatenate([corners[0][at : at + 1], here, corners[1][at : at + 1]], axis=0)
            return (
                wide[: plan.x], wide[2:], own, row(which + 3),
                *(part[0] for part in plane_pair(here[None])),
            )

        raw = [
            raw_ref[pl.ds((2 * which + end) * plan.x, plan.x), :] for which in range(2)
        ]
        faces, diagonal = faces_of(row(2), beside(2, own_mob[end]))
        excess = excess_of(
            row(0), row(1), beside(0, raw[0]), beside(1, raw[1]), faces, diagonal, row(6), row(7)
        )
        new = relax_pair(row(0), row(1), *excess, diagonal, scale_from(diagonal))
        for which, values in enumerate(new):
            halos[which].append(jnp.where(inside[end], values, 0.0)[:, None])
    conc, pot = conc_ref[...], pot_ref[...]
    mass_out[...], pots_out[...] = excess_of(
        conc, pot, neighbours(conc, halos[0]), neighbours(pot, halos[1]), *block_terms
    )


def last_kernel(
    plan, conc_ref, pot_ref, mass_ref, pots_ref, faces_ref, diagonal_ref, scale_ref,
    spread_ref, total_ref,
    conc_hbm, pot_hbm, conc_out, pot_out, sems,
):
    parts = []
    for part in range(plan.slot_parts):
        terms = [total_ref[slot, part] for slot in range(total_ref.shape[0])]
        while len(terms) > 1:
            pairs = [a + b for a, b in zip(terms[::2], terms[1::2])]
            terms = pairs + terms[len(pairs) * 2 :]
        parts.append(terms[0])
    solved = jnp.concatenate(
        coarse_solve(jnp.concatenate(parts, axis=0), plan.p), axis=1
    )
    own = lax.dot_general(
        spread_ref[...].astype(BF16),
        three_terms(solved[: plan.owners]).astype(BF16),
        (((1,), (0,)), ((), ())),
        preferred_element_type=F32,
    )

    def shifted(which):
        lanes = slice(which * plan.p, (which + 1) * plan.p)
        rows = [own[i * plan.y : (i + 1) * plan.y, lanes][None] for i in range(plan.half_x + 2)]
        beside = []
        for i in range(plan.half_x):
            ends = [
                solved[begin + i : begin + i + 1, lanes][None]
                for begin in (plan.low_row, plan.high_row)
            ]
            beside.append((*y_pair(rows[i], *ends), *plane_pair(rows[i])))
        return [rows[plan.half_x], *rows[: plan.half_x], rows[plan.half_x + 1]], beside

    conc_rows, conc_beside = shifted(0)
    pot_rows, pot_beside = shifted(1)
    conc_sums = [a + b + c + d for a, b, c, d in conc_beside]
    copies = []
    for x in range(plan.x):
        one = pl.ds(x, 1)
        i = x >> 1
        low, high = (i, i + 1) if x % 2 == 0 else (i + 1, i + 2)
        diagonal = diagonal_ref[one]
        conc, pot = conc_rows[i + 1], pot_rows[i + 1]
        excess_mass = mass_ref[one] - conc - diagonal * pot
        beside = (pot_rows[low], pot_rows[high], *pot_beside[i])
        for k, other in enumerate(beside):
            excess_mass = excess_mass + faces_ref[k, one] * other
        excess_pot = (pots_ref[one] - pot) + (split_slope + 6.0 * interface) * conc
        excess_pot = excess_pot - interface * (conc_rows[low] + conc_rows[high] + conc_sums[i])
        conc_out[one], pot_out[one] = relax_pair(
            conc_ref[one] + conc, pot_ref[one] + pot, excess_mass, excess_pot, diagonal, scale_ref[one]
        )
        for source, target in ((conc_out, conc_hbm), (pot_out, pot_hbm)):
            copies.append(
                pltpu.make_async_copy(source.at[one], target.at[one], sems.at[len(copies)])
            )
            copies[-1].start()
    for copy in copies:
        copy.wait()


def call(kernel, plan, outs, args, far=(), smem=(), scratch=(), out_far=()):
    def space(i):
        return pl.ANY if i in far else pltpu.SMEM if i in smem else pltpu.VMEM

    return pl.pallas_call(
        functools.partial(kernel, plan),
        out_shape=[jax.ShapeDtypeStruct(shape, F32) for shape in outs],
        in_specs=[pl.BlockSpec(memory_space=space(i)) for i in range(len(args))],
        out_specs=[
            pl.BlockSpec(memory_space=pl.ANY if i in out_far else pltpu.VMEM)
            for i in range(len(outs))
        ],
        scratch_shapes=list(scratch),
        compiler_params=pltpu.CompilerParams(vmem_limit_bytes=VMEM_LIMIT),
    )(*[
        pltpu.with_memory_space_constraint(arg, pltpu.HBM) if i in far else arg
        for i, arg in enumerate(args)
    ])


def swap_near(axis, rows, begin=0):
    pairs = [(i, i + 1) for i in range(begin, lax.axis_size(axis) - 1, 2)]
    return lax.ppermute(rows, axis, pairs + [(j, i) for i, j in pairs])


def swap_far(axis, rows):
    return swap_near(axis, rows, 1)


def gather_totals(plan, total, y_near, y_far):
    if plan.slots:
        order = [0] * plan.slots
        for g in range(plan.owners):
            for h in range(plan.groups):
                order[plan.slot_of(g, h)] = g * plan.groups + h
        return lax.all_to_all(
            total, ("gx", "gy"), split_axis=0, concat_axis=0, axis_index_groups=[order], tiled=True
        )
    shape = (plan.groups, 3, plan.owners, plan.p)
    parts = lax.all_gather(lax.psum(total, "gx"), "gy").reshape(shape)
    blank = jnp.zeros((1, plan.owners, plan.p), F32)
    to_below, own, to_above = (parts[:, k] for k in range(3))
    own = own + jnp.concatenate([blank, to_above[:-1]]) + jnp.concatenate([to_below[1:], blank])
    own = jnp.concatenate([blank, own, blank])
    g, h = lax.axis_index("gx"), lax.axis_index("gy")
    rows = [lax.dynamic_index_in_dim(own, h + 1, 0, False)]
    up = lax.rem(h, 2) == 0
    far = y_far[: y_near.shape[0]]
    for place, at, msg in (
        (h, plan.half_y - 1, jnp.where(up, far, y_near)),
        (h + 2, 0, jnp.where(up, y_near, far)),
    ):
        ident = lax.dynamic_index_in_dim(msg, plan.map_row + g, 0, False).astype(jnp.int32)
        ident = jnp.stack([ident[i * plan.half_y + at] for i in range(plan.half_x)])
        rows.append(lax.dynamic_index_in_dim(own, place, 0, False)[ident])
    rows = jnp.concatenate(rows)
    rows = jnp.pad(rows, ((0, 4 * plan.slot_parts - rows.shape[0]), (0, 0)))
    return rows.reshape(1, plan.slot_parts, 4, plan.p)


def on_device(conc, pot, mass_source, pot_source, mask, kind, table, owner_map):
    plan = Plan(conc.shape, lax.axis_size("gx"), lax.axis_size("gy"))
    block = conc.shape
    fields = [conc, pot, mask, kind, mass_source, pot_source]
    messages = call(
        prepare_kernel,
        plan,
        [*[(3 * plan.y, plan.p)] * 2, (plan.y_rows, plan.p), (plan.y_far_rows, plan.p)],
        [*fields, owner_map, table],
        far=range(8),
        scratch=(
            *[pltpu.VMEM((2, plan.y, plan.p), field.dtype) for field in fields[:4]],
            *[pltpu.VMEM((2, plan.x, 8, plan.p), field.dtype) for field in fields],
            pltpu.VMEM(owner_map.shape, owner_map.dtype),
            pltpu.SMEM(table.shape, table.dtype),
            pltpu.SemaphoreType.DMA((22,)),
        ),
    )
    x_near, x_far = swap_near("gx", messages[0]), swap_far("gx", messages[1])
    y_near, y_far = swap_near("gy", messages[2]), swap_far("gy", messages[3])
    y_far, mask, kind = lax.optimization_barrier((y_far, mask, kind))
    mob, gather, spread, scale, *parts = call(
        local_kernel,
        plan,
        [
            block, (plan.owners, plan.rows), (plan.rows, 3 * plan.owners), (plan.owners, plan.p),
            (5, *block), block, block, block,
        ],
        [conc, pot, mask, kind, mass_source, pot_source, table, owner_map],
        smem=(6,),
    )
    slots = (plan.slots, plan.slot_parts, 4, plan.p) if plan.slots else (3 * plan.owners, plan.p)
    conc, pot, total, raw, near, far = call(
        first_kernel,
        plan,
        [
            block,
            block,
            slots,
            (4 * plan.x, plan.p),
            *[(2 * plan.y + 8, plan.p)] * 2,
        ],
        [
            x_far, x_near, y_far, y_near,
            conc, pot, mob, mass_source, pot_source, gather, scale, owner_map, *parts,
        ],
        out_far=(2,),
        scratch=(pltpu.VMEM(slots, F32), pltpu.SemaphoreType.DMA((plan.groups,))),
    )
    total = gather_totals(plan, total, y_near, y_far)
    far = swap_far("gx", far)
    near = swap_near("gx", near)
    faces, diagonal, scale, mass_part, pot_part = call(
        beside_kernel,
        plan,
        [(6, *block), block, block, block, block],
        [
            near, far, conc, pot, mass_source, pot_source, mob, raw,
            x_near, x_far, y_near, y_far,
        ],
    )
    return tuple(
        call(
            last_kernel,
            plan,
            [block, block],
            [conc, pot, mass_part, pot_part, faces, diagonal, scale, spread, total],
            out_far=(0, 1),
            scratch=(
                pltpu.VMEM(block, F32),
                pltpu.VMEM(block, F32),
                pltpu.SemaphoreType.DMA((2 * plan.x,)),
            ),
        )
    )


def solution(mesh):
    grid = P("gx", "gy", None)
    return jax.shard_map(
        on_device,
        mesh=mesh,
        in_specs=(grid,) * 6 + (P(), P(None, "gy")),
        out_specs=(grid, grid),
        check_vma=False,
    )
```

```python
import functools

import jax
import jax.numpy as jnp
from jax import lax
from jax.experimental import pallas as pl
from jax.experimental.pallas import tpu as pltpu
from jax.sharding import PartitionSpec as P

CSWEEP = 3

time_step = 0.25
split_slope = 1.0
interface = 0.5
relax_fine = 0.6
relax_coarse = 0.6
coarse_flux = 0.0625
coarse_bend = 0.125
coarse_det = 1.0 + 2.0 * coarse_flux * (split_slope + 2.0 * coarse_bend)

F32 = jnp.float32
BF16 = jnp.bfloat16
VMEM_LIMIT = 48 * 1024 * 1024


def iota(shape, dim):
    return lax.broadcasted_iota(jnp.int32, shape, dim)


def x_pair(field, low, high):
    return (
        jnp.concatenate([low, field[:-1]], axis=0),
        jnp.concatenate([field[1:], high], axis=0),
    )


def y_pair(field, low, high):
    size = field.shape[1]
    where = iota(field.shape, 1)
    return (
        jnp.where(where == 0, low, pltpu.roll(field, 1, 1)),
        jnp.where(where == size - 1, high, pltpu.roll(field, size - 1, 1)),
    )


def plane_pair(field):
    size = field.shape[2]
    where = iota(field.shape, 2)
    return (
        jnp.where(where == 0, 0.0, pltpu.roll(field, 1, 2)),
        jnp.where(where == size - 1, 0.0, pltpu.roll(field, size - 1, 2)),
    )


def neighbours(field, halo):
    xm, xp, ym, yp = halo
    return (*x_pair(field, xm, xp), *y_pair(field, ym, yp), *plane_pair(field))


def excess_of(conc, pot, conc_beside, pot_beside, faces, diagonal, mass_source, pot_source):
    excess_mass = (mass_source - conc) - diagonal * pot
    for face, other in zip(faces, pot_beside):
        excess_mass = excess_mass + face * other
    beside = conc_beside[0]
    for other in conc_beside[1:]:
        beside = beside + other
    excess_pot = (pot_source - pot) + (split_slope + 6.0 * interface) * conc - interface * beside
    return excess_mass, excess_pot


def scale_from(diagonal):
    return relax_fine / (1.0 + (split_slope + 6.0 * interface) * diagonal)


def relax_pair(conc, pot, excess_mass, excess_pot, diagonal, scale):
    new_conc = conc + (excess_mass - diagonal * excess_pot) * scale
    new_pot = pot + (excess_pot + (split_slope + 6.0 * interface) * excess_mass) * scale
    return new_conc, new_pot


def faces_of(mobility, beside):
    faces = tuple((0.5 * time_step) * (mobility + other) for other in beside)
    diagonal = faces[0]
    for face in faces[1:]:
        diagonal = diagonal + face
    return faces, diagonal


def split_dot(ones, values, contract):
    dims = (contract, ((), ()))
    total = None
    rest = values
    for _ in range(3):
        term = rest.astype(BF16)
        rest = rest - term.astype(F32)
        part = lax.dot_general(ones, term, dims, preferred_element_type=F32)
        total = part if total is None else total + part
    return total


def three_terms(values):
    out = []
    for _ in range(3):
        out.append(values.astype(BF16).astype(F32))
        values = values - out[-1]
    return jnp.concatenate(out, axis=0)


def round_up(value, unit):
    return -(-value // unit) * unit


class Plan:
    def __init__(self, shape, owners, groups):
        self.x, self.y, self.p = shape
        self.owners, self.groups = owners, groups
        self.half_x, self.half_y = self.x // 2, self.y // 2
        self.columns = self.half_x * self.half_y
        self.map_row = round_up(8 * self.x, 8)
        self.y_rows = self.map_row + owners
        self.y_far_rows = max(self.y_rows, 3 * self.y + 8)
        self.cells = self.x * self.y
        self.rows = (self.half_x + 2) * self.y
        self.low_row = owners
        self.high_row = owners + self.half_x
        self.slot_parts = -(-(owners + 2 * self.half_x) // 4)
        slots = owners * groups
        self.slots = slots if slots <= 64 else 0

    def slot_of(self, g, h):
        last = self.groups - 1
        place = 0 if h == 0 else 1 if h == last else h + 1
        return place * self.owners + self.owners - 1 - g


def side_rows(plan, rows, which):
    return rows[which * plan.y : (which + 1) * plan.y][None]


def side_columns(plan, rows, which):
    return rows[which * plan.x : (which + 1) * plan.x][:, None]


def membership(plan, owner_ref):
    g = lax.axis_index("gx")
    last = plan.owners - 1
    owner = iota((plan.owners, plan.columns), 0)
    low, high = plan.half_x, plan.half_x + 1
    shape = (plan.half_x + 2, plan.y, plan.columns)
    x, y, column = iota(shape, 0), iota(shape, 1), iota(shape, 2)
    half = jnp.where(x < low, x, jnp.where(x == low, plan.half_x - 1, 0))
    place = column == half * plan.half_y + (y >> 1)
    sides = (
        (x < low, g, True),
        (x == low, jnp.maximum(g - 1, 0), g > 0),
        (x == high, jnp.minimum(g + 1, last), g < last),
    )
    gather, spread = None, None
    for part, row, inside in sides:
        hits = ((owner_ref[pl.ds(row, 1), :] == owner) & inside).astype(F32).astype(BF16)
        where = (place & part).astype(F32).reshape(plan.rows, plan.columns).astype(BF16)
        nt = (((1,), (1,)), ((), ()))
        some = lax.dot_general(hits, where, nt, preferred_element_type=F32)
        gather = some if gather is None else gather + some
        some = lax.dot_general(where, hits, nt, preferred_element_type=F32)
        spread = some if spread is None else spread + some
    return gather, jnp.concatenate([spread] * 3, axis=1)


def scale_of(plan, owners):
    owner = iota((plan.owners, plan.columns), 0).astype(owners.dtype)
    hits = jnp.zeros((plan.owners, plan.columns), F32)
    for g in range(plan.owners):
        hits = hits + (owners[g : g + 1] == owner).astype(F32)
    count = jnp.sum(hits, axis=1, keepdims=True)
    return jnp.broadcast_to(0.125 / jnp.maximum(count, 1.0), (plan.owners, plan.p))


def mobility_of(mask, kind, table):
    values = jnp.zeros(kind.shape, F32)
    for marker, value in enumerate(table):
        values = jnp.where(kind == marker, value, values)
    return mask.astype(F32) * values


def even(axis):
    return lax.rem(lax.axis_index(axis), 2) == 0


def put_x(plan, lows, highs, near, far):
    up = even("gx")
    for which, (low, high) in enumerate(zip(lows, highs)):
        near[pl.ds(which * plan.y, plan.y), :] = jnp.where(up, high, low)
        far[pl.ds(which * plan.y, plan.y), :] = jnp.where(up, low, high)


def received(axis, near_ref, far_ref):
    up = even(axis)
    rows = pl.ds(0, min(near_ref.shape[0], far_ref.shape[0]))
    near, far = near_ref[rows, :], far_ref[rows, :]
    return jnp.where(up, far, near), jnp.where(up, near, far)


def prepare_kernel(plan, *refs):
    hbm, refs = refs[:8], refs[8:]
    x_near_ref, x_far_ref, y_near_ref, y_far_ref = refs[:4]
    x_refs, y_refs, (owner_ref, table_ref, sems) = refs[4:8], refs[8:14], refs[14:]
    copies = []

    def start(source, target):
        copies.append(pltpu.make_async_copy(source, target, sems.at[len(copies)]))
        copies[-1].start()

    start(hbm[7], table_ref)
    start(hbm[6], owner_ref)
    for source, target in zip(hbm[:4], x_refs):
        start(source.at[0], target.at[0])
        start(source.at[plan.x - 1], target.at[1])
    for source, target in zip(hbm[:6], y_refs):
        start(source.at[:, pl.ds(0, 8)], target.at[0])
        start(source.at[:, pl.ds(plan.y - 8, 8)], target.at[1])
    for copy in copies:
        copy.wait()
    table = [table_ref[marker] for marker in range(table_ref.shape[0])]
    conc, pot, mask, kind = (ref[...] for ref in x_refs)
    fields = (conc, pot, mobility_of(mask, kind, table))
    put_x(plan, [f[0] for f in fields], [f[1] for f in fields], x_near_ref, x_far_ref)
    conc, pot, mask, kind, mass, pots = (ref[...] for ref in y_refs)
    fields = (conc, pot, mobility_of(mask, kind, table))
    up = even("gy")
    rows = [(field, at) for at in range(2) for field in fields] + [(mass, 0), (pots, 0)]
    for which, (field, at) in enumerate(rows):
        for x in range(plan.x):
            low, high = field[0, x, at : at + 1], field[1, x, 7 - at : 8 - at]
            y_near_ref[pl.ds(which * plan.x + x, 1), :] = jnp.where(up, high, low)
            y_far_ref[pl.ds(which * plan.x + x, 1), :] = jnp.where(up, low, high)
    used = 8 * plan.x
    for ref, rows in ((y_near_ref, plan.y_rows), (y_far_ref, plan.y_far_rows)):
        ref[pl.ds(used, rows - used), :] = jnp.zeros((rows - used, plan.p), F32)
        ref[pl.ds(plan.map_row, plan.owners), pl.ds(0, plan.columns)] = owner_ref[...].astype(F32)


def inner_faces(mobility):
    half = 0.5 * time_step
    shape = mobility.shape
    y, plane = iota(shape, 1), iota(shape, 2)
    to_x = jnp.concatenate(
        [half * (mobility[:-1] + mobility[1:]), jnp.zeros_like(mobility[:1])], axis=0
    )
    out = [to_x]
    for dim, where, shift, edge in (
        (1, y, 1, 0), (1, y, shape[1] - 1, shape[1] - 1),
        (2, plane, 1, 0), (2, plane, shape[2] - 1, shape[2] - 1),
    ):
        face = half * (mobility + pltpu.roll(mobility, shift, dim))
        out.append(jnp.where(where == edge, 0.0, face))
    return out


def inner_flux(faces, field):
    to_x, y_low, y_high, plane_low, plane_high = faces
    size_y, size_p = field.shape[1:]
    from_x = to_x[:-1]
    blank = jnp.zeros_like(field[:1])
    flux = jnp.concatenate([from_x * field[1:], blank], axis=0)
    flux = flux + jnp.concatenate([blank, from_x * field[:-1]], axis=0)
    flux = flux + y_low * pltpu.roll(field, 1, 1) + y_high * pltpu.roll(field, size_y - 1, 1)
    return flux + plane_low * pltpu.roll(field, 1, 2) + plane_high * pltpu.roll(field, size_p - 1, 2)


def inner_excess(conc, pot, faces, diagonal, mass_source, pot_source):
    excess_mass = (mass_source - conc) - diagonal * pot + inner_flux(faces, pot)
    nothing = [jnp.zeros_like(conc[:1])] * 2 + [jnp.zeros_like(conc[:, :1])] * 2
    beside = None
    for other in neighbours(conc, nothing):
        beside = other if beside is None else beside + other
    excess_pot = (pot_source - pot) + (split_slope + 6.0 * interface) * conc - interface * beside
    return excess_mass, excess_pot


def add_edges(field, x_low, x_high, y_low, y_high):
    field = jnp.concatenate(
        [(field[0] + x_low)[None], field[1:-1], (field[-1] + x_high)[None]], axis=0
    )
    row = iota((field.shape[0], 8, field.shape[2]), 1)
    size = field.shape[1]
    low = field[:, :8] + jnp.where(row == 0, y_low, 0.0)
    high = field[:, size - 8 :] + jnp.where(row == 7, y_high, 0.0)
    return jnp.concatenate([low, field[:, 8 : size - 8], high], axis=1)


def local_kernel(
    plan, conc_ref, pot_ref, mask_ref, class_ref, mass_ref, pots_ref, table_ref, owner_ref,
    mob_ref, gather_ref, spread_ref, scale_ref, faces_ref, diagonal_ref, mass_out, pots_out,
):
    table = [table_ref[marker] for marker in range(table_ref.shape[0])]
    mobility = mobility_of(mask_ref[...], class_ref[...], table)
    mob_ref[...] = mobility
    gather_ref[...], spread_ref[...] = membership(plan, owner_ref)
    scale_ref[...] = scale_of(plan, owner_ref[...])
    faces = inner_faces(mobility)
    diagonal = faces[0] + jnp.concatenate([jnp.zeros_like(mobility[:1]), faces[0][:-1]], axis=0)
    for face in faces[1:]:
        diagonal = diagonal + face
    plane = iota(mobility.shape, 2)
    ends = (plane == 0) | (plane == plan.p - 1)
    diagonal = diagonal + jnp.where(ends, (0.5 * time_step) * mobility, 0.0)
    for i, face in enumerate(faces):
        faces_ref[i] = face
    diagonal_ref[...] = diagonal
    mass_out[...], pots_out[...] = inner_excess(
        conc_ref[...], pot_ref[...], faces, diagonal, mass_ref[...], pots_ref[...]
    )


def first_kernel(
    plan, x_far_ref, x_near_ref, y_far_ref, y_near_ref,
    conc_ref, pot_ref, mob_ref, mass_ref, pots_ref, gather_ref, scale_ref, owner_ref,
    faces_ref, diagonal_ref, mass_part_ref, pot_part_ref,
    conc_out, pot_out, total_hbm, raw_out, x_near_out, x_far_out, total_out, sems,
):
    sides = received("gx", x_near_ref, x_far_ref)
    ends = received("gy", y_near_ref, y_far_ref)
    last_x, last_y = plan.x - 1, plan.y - 1

    def halo(which):
        return tuple(side_rows(plan, rows, which)[0] for rows in sides) + tuple(
            side_columns(plan, rows, which) for rows in ends
        )

    def edges(field):
        return field[0], field[last_x], field[:, :1], field[:, last_y:]

    mobility = mob_ref[...]
    raw_conc, raw_pot = conc_ref[...], pot_ref[...]
    outer = [
        (0.5 * time_step) * (own + other) for own, other in zip(edges(mobility), halo(2))
    ]
    diagonal = add_edges(diagonal_ref[...], *outer)
    excess_mass = add_edges(
        mass_part_ref[...],
        *(f * (other - own) for f, own, other in zip(outer, edges(raw_pot), halo(1))),
    )
    excess_pot = add_edges(pot_part_ref[...], *(-interface * other for other in halo(0)))
    conc, pot = relax_pair(
        raw_conc, raw_pot, excess_mass, excess_pot, diagonal, scale_from(diagonal)
    )

    own_mass, own_pot = inner_excess(
        conc, pot, [faces_ref[i] for i in range(5)], diagonal, mass_ref[...], pots_ref[...]
    )
    give_mass, give_pot = (
        [field[x] + field[x + 1] for x in range(0, plan.x, 2)] for field in (own_mass, own_pot)
    )
    for x, side in ((0, 0), (last_x, 1)):
        give_mass.append(outer[side] * pot[x])
        give_pot.append(-interface * conc[x])

    def packed(mass, other):
        first = iota(mass.shape, 1) & 1 == 0
        return jnp.where(
            first, mass + pltpu.roll(mass, plan.p - 1, 1), other + pltpu.roll(other, 1, 1)
        )

    give = packed(jnp.concatenate(give_mass, axis=0), jnp.concatenate(give_pot, axis=0))
    h = lax.axis_index("gy")
    inside = (h > 0, None, h < plan.groups - 1)
    maps = [rows[plan.map_row : plan.map_row + plan.owners, : plan.columns] for rows in ends]
    maps.insert(1, owner_ref[...].astype(F32))
    owner = iota((plan.owners, 1), 0)
    is_mine = owner == lax.axis_index("gx")

    sums = [None, split_dot(gather_ref[...].astype(BF16), give, ((1,), (0,))), None]
    sums[1] = sums[1] * scale_ref[...]
    for place, y, at, side in ((0, 0, plan.half_y - 1, 2), (2, plan.y - 1, 0, 3)):
        edge_pot, edge_conc = (
            jnp.concatenate([field[x, y : y + 1] for x in range(plan.x)], axis=0)
            for field in (pot, conc)
        )
        both = packed(outer[side][:, 0] * edge_pot, -interface * edge_conc)
        part = jnp.zeros((plan.owners, plan.p), F32)
        for i in range(plan.half_x):
            column = owner_column(plan, maps[place], i, at)
            ident = jnp.sum(jnp.where(is_mine, column, 0.0), axis=0, keepdims=True)
            pair = both[2 * i : 2 * i + 1] + both[2 * i + 1 : 2 * i + 2]
            part = part + jnp.where((owner.astype(F32) == ident) & inside[place], pair, 0.0)
        sums[place] = part * scale_of(plan, maps[place])
    def store_fields():
        conc_out[...] = conc
        pot_out[...] = pot
        for at, field in enumerate((raw_conc, raw_pot)):
            for x in range(plan.x):
                raw_out[pl.ds(2 * at * plan.x + x, 1), :] = field[x, 0:1]
                raw_out[pl.ds((2 * at + 1) * plan.x + x, 1), :] = field[x, last_y : last_y + 1]
        put_x(plan, (conc[0], pot[0]), (conc[last_x], pot[last_x]), x_near_out, x_far_out)
        up = even("gx")
        base = 2 * plan.y
        for which in range(3):
            for end, rows in enumerate(ends):
                low = rows[which * plan.x : which * plan.x + 1]
                high = rows[(which + 1) * plan.x - 1 : (which + 1) * plan.x]
                x_near_out[pl.ds(base + 2 * which + end, 1), :] = jnp.where(up, high, low)
                x_far_out[pl.ds(base + 2 * which + end, 1), :] = jnp.where(up, low, high)
        for ref in (x_near_out, x_far_out):
            ref[pl.ds(base + 6, 2), :] = jnp.zeros((2, plan.p), F32)

    if not plan.slots:
        total_out[...] = jnp.concatenate(sums, axis=0)
        copies = [pltpu.make_async_copy(total_out, total_hbm, sems.at[0])]
        copies[0].start()
        store_fields()
        copies[0].wait()
        return

    def picked(place, i, at):
        column = owner_column(plan, maps[place], i, at)
        ident = jnp.broadcast_to(column, (plan.owners, plan.p))
        out = jnp.zeros((plan.owners, plan.p), F32)
        for o in range(plan.owners):
            out = jnp.where(ident == float(o), sums[place][o : o + 1], out)
        return out

    below = [[picked(k, i, plan.half_y - 1) for i in range(plan.half_x)] for k in range(3)]
    above = [[picked(k, i, 0) for i in range(plan.half_x)] for k in range(3)]

    def of_plane(plane, choices):
        out = jnp.zeros((plan.owners, plan.p), F32)
        for k in range(3):
            out = jnp.where(plane == h + (k - 1), choices[k], out)
        return out

    size = 4 * plan.slot_parts
    rows = []
    for plane in range(plan.groups):
        beside = []
        for i in range(plan.half_x):
            beside.append((plan.low_row + i, of_plane(plane - 1, [k[i] for k in below])))
            beside.append((plan.high_row + i, of_plane(plane + 1, [k[i] for k in above])))
        blank = jnp.zeros((plan.owners, plan.p), F32)
        beside += [(at, blank) for at in range(plan.high_row + plan.half_x, size)]
        rows.append((of_plane(plane, sums), beside))
    copies = []
    for plane, (main, beside) in enumerate(rows):
        for g in range(plan.owners):
            slot = plan.slot_of(g, plane)
            for part in range(plan.owners // 4):
                total_out[slot, part] = main[4 * part : 4 * part + 4]
            for row, values in beside:
                total_out[slot, row // 4, pl.ds(row % 4, 1), :] = values[g : g + 1]
        some = pl.ds(plan.slot_of(plan.owners - 1, plane), plan.owners)
        copies.append(
            pltpu.make_async_copy(total_out.at[some], total_hbm.at[some], sems.at[plane])
        )
        copies[-1].start()
    store_fields()
    for copy in copies:
        copy.wait()


def owner_column(plan, owners, i, at):
    b = i * plan.half_y + at
    return owners[:, b : b + 1]


def coarse_solve(packed, planes):
    lane = iota(packed.shape, 1)
    even = lane & 1 == 0
    mass_mean = jnp.where(even, packed, pltpu.roll(packed, 1, 1))
    pot_mean = jnp.where(even, pltpu.roll(packed, planes - 1, 1), packed)

    def neighbour_sum(values):
        return jnp.where(lane >= 2, pltpu.roll(values, 2, 1), 0.0) + jnp.where(
            lane < planes - 2, pltpu.roll(values, planes - 2, 1), 0.0
        )

    def step(mass_gap, pot_gap):
        scale = relax_coarse / coarse_det
        return (
            scale * (mass_gap - 2.0 * coarse_flux * pot_gap),
            scale * (pot_gap + (split_slope + 2.0 * coarse_bend) * mass_gap),
        )

    coarse_conc, coarse_pot = step(mass_mean, pot_mean)
    for _ in range(CSWEEP - 1):
        mass_gap = mass_mean - (
            coarse_conc + coarse_flux * (2.0 * coarse_pot - neighbour_sum(coarse_pot))
        )
        pot_gap = pot_mean - (
            coarse_pot
            - split_slope * coarse_conc
            + coarse_bend * (neighbour_sum(coarse_conc) - 2.0 * coarse_conc)
        )
        more_conc, more_pot = step(mass_gap, pot_gap)
        coarse_conc, coarse_pot = coarse_conc + more_conc, coarse_pot + more_pot
    return coarse_conc, coarse_pot


def beside_kernel(
    plan, x_near_ref, x_far_ref, conc_ref, pot_ref, mass_ref, pots_ref, mob_ref, raw_ref,
    x_near_msg, x_far_msg, y_near_msg, y_far_msg,
    faces_out, diagonal_out, scale_out, mass_out, pots_out,
):
    mobility = mob_ref[...]
    sides = received("gx", x_near_msg, x_far_msg)
    ends = received("gy", y_near_msg, y_far_msg)
    halo = tuple(side_rows(plan, rows, 2) for rows in sides) + tuple(
        side_columns(plan, rows, 2) for rows in ends
    )
    faces, diagonal = faces_of(mobility, neighbours(mobility, halo))
    block_terms = faces, diagonal, mass_ref[...], pots_ref[...]
    for i, face in enumerate(faces):
        faces_out[i] = face
    diagonal_out[...] = diagonal
    scale_out[...] = scale_from(diagonal)

    corners = received("gx", x_near_ref, x_far_ref)
    h = lax.axis_index("gy")
    inside = (h > 0, h < plan.groups - 1)
    own_mob = [
        jnp.concatenate([mobility[x, y : y + 1] for x in range(plan.x)], axis=0)
        for y in (0, plan.y - 1)
    ]
    halos = [[side_rows(plan, rows, which) for rows in corners] for which in range(2)]
    for end, rows in enumerate(ends):

        def row(which):
            return rows[which * plan.x : (which + 1) * plan.x]

        def beside(which, own):
            here = row(which)
            at = 2 * plan.y + 2 * which + end
            wide = jnp.concatenate([corners[0][at : at + 1], here, corners[1][at : at + 1]], axis=0)
            return (
                wide[: plan.x], wide[2:], own, row(which + 3),
                *(part[0] for part in plane_pair(here[None])),
            )

        raw = [
            raw_ref[pl.ds((2 * which + end) * plan.x, plan.x), :] for which in range(2)
        ]
        faces, diagonal = faces_of(row(2), beside(2, own_mob[end]))
        excess = excess_of(
            row(0), row(1), beside(0, raw[0]), beside(1, raw[1]), faces, diagonal, row(6), row(7)
        )
        new = relax_pair(row(0), row(1), *excess, diagonal, scale_from(diagonal))
        for which, values in enumerate(new):
            halos[which].append(jnp.where(inside[end], values, 0.0)[:, None])
    conc, pot = conc_ref[...], pot_ref[...]
    mass_out[...], pots_out[...] = excess_of(
        conc, pot, neighbours(conc, halos[0]), neighbours(pot, halos[1]), *block_terms
    )


def last_kernel(
    plan, conc_ref, pot_ref, mass_ref, pots_ref, faces_ref, diagonal_ref, scale_ref,
    spread_ref, total_ref,
    conc_hbm, pot_hbm, conc_out, pot_out, sems,
):
    parts = []
    for part in range(plan.slot_parts):
        terms = [total_ref[slot, part] for slot in range(total_ref.shape[0])]
        while len(terms) > 1:
            pairs = [a + b for a, b in zip(terms[::2], terms[1::2])]
            terms = pairs + terms[len(pairs) * 2 :]
        parts.append(terms[0])
    solved = jnp.concatenate(
        coarse_solve(jnp.concatenate(parts, axis=0), plan.p), axis=1
    )
    own = lax.dot_general(
        spread_ref[...].astype(BF16),
        three_terms(solved[: plan.owners]).astype(BF16),
        (((1,), (0,)), ((), ())),
        preferred_element_type=F32,
    )

    def shifted(which):
        lanes = slice(which * plan.p, (which + 1) * plan.p)
        rows = [own[i * plan.y : (i + 1) * plan.y, lanes][None] for i in range(plan.half_x + 2)]
        beside = []
        for i in range(plan.half_x):
            ends = [
                solved[begin + i : begin + i + 1, lanes][None]
                for begin in (plan.low_row, plan.high_row)
            ]
            beside.append((*y_pair(rows[i], *ends), *plane_pair(rows[i])))
        return [rows[plan.half_x], *rows[: plan.half_x], rows[plan.half_x + 1]], beside

    conc_rows, conc_beside = shifted(0)
    pot_rows, pot_beside = shifted(1)
    conc_sums = [a + b + c + d for a, b, c, d in conc_beside]
    copies = []
    for x in range(plan.x):
        one = pl.ds(x, 1)
        i = x >> 1
        low, high = (i, i + 1) if x % 2 == 0 else (i + 1, i + 2)
        diagonal = diagonal_ref[one]
        conc, pot = conc_rows[i + 1], pot_rows[i + 1]
        excess_mass = mass_ref[one] - conc - diagonal * pot
        beside = (pot_rows[low], pot_rows[high], *pot_beside[i])
        for k, other in enumerate(beside):
            excess_mass = excess_mass + faces_ref[k, one] * other
        excess_pot = (pots_ref[one] - pot) + (split_slope + 6.0 * interface) * conc
        excess_pot = excess_pot - interface * (conc_rows[low] + conc_rows[high] + conc_sums[i])
        conc_out[one], pot_out[one] = relax_pair(
            conc_ref[one] + conc, pot_ref[one] + pot, excess_mass, excess_pot, diagonal, scale_ref[one]
        )
        for source, target in ((conc_out, conc_hbm), (pot_out, pot_hbm)):
            copies.append(
                pltpu.make_async_copy(source.at[one], target.at[one], sems.at[len(copies)])
            )
            copies[-1].start()
    for copy in copies:
        copy.wait()


def call(kernel, plan, outs, args, far=(), smem=(), scratch=(), out_far=()):
    def space(i):
        return pl.ANY if i in far else pltpu.SMEM if i in smem else pltpu.VMEM

    return pl.pallas_call(
        functools.partial(kernel, plan),
        out_shape=[jax.ShapeDtypeStruct(shape, F32) for shape in outs],
        in_specs=[pl.BlockSpec(memory_space=space(i)) for i in range(len(args))],
        out_specs=[
            pl.BlockSpec(memory_space=pl.ANY if i in out_far else pltpu.VMEM)
            for i in range(len(outs))
        ],
        scratch_shapes=list(scratch),
        compiler_params=pltpu.CompilerParams(vmem_limit_bytes=VMEM_LIMIT),
    )(*[
        pltpu.with_memory_space_constraint(arg, pltpu.HBM) if i in far else arg
        for i, arg in enumerate(args)
    ])


def swap_near(axis, rows, begin=0):
    pairs = [(i, i + 1) for i in range(begin, lax.axis_size(axis) - 1, 2)]
    return lax.ppermute(rows, axis, pairs + [(j, i) for i, j in pairs])


def swap_far(axis, rows):
    return swap_near(axis, rows, 1)


def gather_totals(plan, total, y_near, y_far):
    if plan.slots:
        order = [0] * plan.slots
        for g in range(plan.owners):
            for h in range(plan.groups):
                order[plan.slot_of(g, h)] = g * plan.groups + h
        return lax.all_to_all(
            total, ("gx", "gy"), split_axis=0, concat_axis=0, axis_index_groups=[order], tiled=True
        )
    shape = (plan.groups, 3, plan.owners, plan.p)
    parts = lax.all_gather(lax.psum(total, "gx"), "gy").reshape(shape)
    blank = jnp.zeros((1, plan.owners, plan.p), F32)
    to_below, own, to_above = (parts[:, k] for k in range(3))
    own = own + jnp.concatenate([blank, to_above[:-1]]) + jnp.concatenate([to_below[1:], blank])
    own = jnp.concatenate([blank, own, blank])
    g, h = lax.axis_index("gx"), lax.axis_index("gy")
    rows = [lax.dynamic_index_in_dim(own, h + 1, 0, False)]
    up = lax.rem(h, 2) == 0
    far = y_far[: y_near.shape[0]]
    for place, at, msg in (
        (h, plan.half_y - 1, jnp.where(up, far, y_near)),
        (h + 2, 0, jnp.where(up, y_near, far)),
    ):
        ident = lax.dynamic_index_in_dim(msg, plan.map_row + g, 0, False).astype(jnp.int32)
        ident = jnp.stack([ident[i * plan.half_y + at] for i in range(plan.half_x)])
        rows.append(lax.dynamic_index_in_dim(own, place, 0, False)[ident])
    rows = jnp.concatenate(rows)
    rows = jnp.pad(rows, ((0, 4 * plan.slot_parts - rows.shape[0]), (0, 0)))
    return rows.reshape(1, plan.slot_parts, 4, plan.p)


def on_device(conc, pot, mass_source, pot_source, mask, kind, table, owner_map):
    plan = Plan(conc.shape, lax.axis_size("gx"), lax.axis_size("gy"))
    block = conc.shape
    fields = [conc, pot, mask, kind, mass_source, pot_source]
    messages = call(
        prepare_kernel,
        plan,
        [*[(3 * plan.y, plan.p)] * 2, (plan.y_rows, plan.p), (plan.y_far_rows, plan.p)],
        [*fields, owner_map, table],
        far=range(8),
        scratch=(
            *[pltpu.VMEM((2, plan.y, plan.p), field.dtype) for field in fields[:4]],
            *[pltpu.VMEM((2, plan.x, 8, plan.p), field.dtype) for field in fields],
            pltpu.VMEM(owner_map.shape, owner_map.dtype),
            pltpu.SMEM(table.shape, table.dtype),
            pltpu.SemaphoreType.DMA((22,)),
        ),
    )
    x_near, x_far = swap_near("gx", messages[0]), swap_far("gx", messages[1])
    y_near, y_far = swap_near("gy", messages[2]), swap_far("gy", messages[3])
    y_far, mask, kind = lax.optimization_barrier((y_far, mask, kind))
    mob, gather, spread, scale, *parts = call(
        local_kernel,
        plan,
        [
            block, (plan.owners, plan.rows), (plan.rows, 3 * plan.owners), (plan.owners, plan.p),
            (5, *block), block, block, block,
        ],
        [conc, pot, mask, kind, mass_source, pot_source, table, owner_map],
        smem=(6,),
    )
    slots = (plan.slots, plan.slot_parts, 4, plan.p) if plan.slots else (3 * plan.owners, plan.p)
    conc, pot, total, raw, near, far = call(
        first_kernel,
        plan,
        [
            block,
            block,
            slots,
            (4 * plan.x, plan.p),
            *[(2 * plan.y + 8, plan.p)] * 2,
        ],
        [
            x_far, x_near, y_far, y_near,
            conc, pot, mob, mass_source, pot_source, gather, scale, owner_map, *parts,
        ],
        out_far=(2,),
        scratch=(pltpu.VMEM(slots, F32), pltpu.SemaphoreType.DMA((plan.groups,))),
    )
    total = gather_totals(plan, total, y_near, y_far)
    far = swap_far("gx", far)
    near = swap_near("gx", near)
    faces, diagonal, scale, mass_part, pot_part = call(
        beside_kernel,
        plan,
        [(6, *block), block, block, block, block],
        [
            near, far, conc, pot, mass_source, pot_source, mob, raw,
            x_near, x_far, y_near, y_far,
        ],
    )
    return tuple(
        call(
            last_kernel,
            plan,
            [block, block],
            [conc, pot, mass_part, pot_part, faces, diagonal, scale, spread, total],
            out_far=(0, 1),
            scratch=(
                pltpu.VMEM(block, F32),
                pltpu.VMEM(block, F32),
                pltpu.SemaphoreType.DMA((2 * plan.x,)),
            ),
        )
    )


def solution(mesh):
    grid = P("gx", "gy", None)
    return jax.shard_map(
        on_device,
        mesh=mesh,
        in_specs=(grid,) * 6 + (P(), P(None, "gy")),
        out_specs=(grid, grid),
        check_vma=False,
    )
```

```python
import functools

import jax
import jax.numpy as jnp
from jax import lax
from jax.experimental import pallas as pl
from jax.experimental.pallas import tpu as pltpu
from jax.sharding import PartitionSpec as P

CSWEEP = 3

time_step = 0.25
split_slope = 1.0
interface = 0.5
relax_fine = 0.6
relax_coarse = 0.6
coarse_flux = 0.0625
coarse_bend = 0.125
coarse_det = 1.0 + 2.0 * coarse_flux * (split_slope + 2.0 * coarse_bend)

F32 = jnp.float32
BF16 = jnp.bfloat16
VMEM_LIMIT = 48 * 1024 * 1024


def iota(shape, dim):
    return lax.broadcasted_iota(jnp.int32, shape, dim)


def x_pair(field, low, high):
    return (
        jnp.concatenate([low, field[:-1]], axis=0),
        jnp.concatenate([field[1:], high], axis=0),
    )


def y_pair(field, low, high):
    size = field.shape[1]
    where = iota(field.shape, 1)
    return (
        jnp.where(where == 0, low, pltpu.roll(field, 1, 1)),
        jnp.where(where == size - 1, high, pltpu.roll(field, size - 1, 1)),
    )


def plane_pair(field):
    size = field.shape[2]
    where = iota(field.shape, 2)
    return (
        jnp.where(where == 0, 0.0, pltpu.roll(field, 1, 2)),
        jnp.where(where == size - 1, 0.0, pltpu.roll(field, size - 1, 2)),
    )


def neighbours(field, halo):
    xm, xp, ym, yp = halo
    return (*x_pair(field, xm, xp), *y_pair(field, ym, yp), *plane_pair(field))


def excess_of(conc, pot, conc_beside, pot_beside, faces, diagonal, mass_source, pot_source):
    excess_mass = (mass_source - conc) - diagonal * pot
    for face, other in zip(faces, pot_beside):
        excess_mass = excess_mass + face * other
    beside = conc_beside[0]
    for other in conc_beside[1:]:
        beside = beside + other
    excess_pot = (pot_source - pot) + (split_slope + 6.0 * interface) * conc - interface * beside
    return excess_mass, excess_pot


def scale_from(diagonal):
    return relax_fine / (1.0 + (split_slope + 6.0 * interface) * diagonal)


def relax_pair(conc, pot, excess_mass, excess_pot, diagonal, scale):
    new_conc = conc + (excess_mass - diagonal * excess_pot) * scale
    new_pot = pot + (excess_pot + (split_slope + 6.0 * interface) * excess_mass) * scale
    return new_conc, new_pot


def faces_of(mobility, beside):
    faces = tuple((0.5 * time_step) * (mobility + other) for other in beside)
    diagonal = faces[0]
    for face in faces[1:]:
        diagonal = diagonal + face
    return faces, diagonal


def three_terms(values, dim=0):
    out = []
    for _ in range(3):
        out.append(values.astype(BF16).astype(F32))
        values = values - out[-1]
    return jnp.concatenate(out, axis=dim)


def round_up(value, unit):
    return -(-value // unit) * unit


class Plan:
    def __init__(self, shape, owners, groups):
        self.x, self.y, self.p = shape
        self.owners, self.groups = owners, groups
        self.half_x, self.half_y = self.x // 2, self.y // 2
        self.columns = self.half_x * self.half_y
        self.map_row = round_up(8 * self.x, 8)
        self.y_rows = self.map_row + owners
        self.y_far_rows = max(self.y_rows, 3 * self.y + 8)
        self.cells = self.x * self.y
        self.rows = (self.half_x + 2) * self.y
        self.low_row = owners
        self.high_row = owners + self.half_x
        self.slot_parts = -(-(owners + 2 * self.half_x) // 4)
        slots = owners * groups
        self.slots = slots if slots <= 64 else 0

    def slot_of(self, g, h):
        last = self.groups - 1
        place = 0 if h == 0 else 1 if h == last else h + 1
        return place * self.owners + self.owners - 1 - (g ^ 1)


def side_rows(plan, rows, which):
    return rows[which * plan.y : (which + 1) * plan.y][None]


def side_columns(plan, rows, which):
    return rows[which * plan.x : (which + 1) * plan.x][:, None]


def membership(plan, owner_ref):
    g = lax.axis_index("gx")
    last = plan.owners - 1
    owner = iota((plan.owners, plan.columns), 0)
    low, high = plan.half_x, plan.half_x + 1
    shape = (plan.half_x + 2, plan.y, plan.columns)
    x, y, column = iota(shape, 0), iota(shape, 1), iota(shape, 2)
    half = jnp.where(x < low, x, jnp.where(x == low, plan.half_x - 1, 0))
    place = column == half * plan.half_y + (y >> 1)
    sides = (
        (x < low, g, True),
        (x == low, jnp.maximum(g - 1, 0), g > 0),
        (x == high, jnp.minimum(g + 1, last), g < last),
    )
    gather, spread = None, None
    for part, row, inside in sides:
        hits = ((owner_ref[pl.ds(row, 1), :] == owner) & inside).astype(F32).astype(BF16)
        where = (place & part).astype(F32).reshape(plan.rows, plan.columns).astype(BF16)
        nt = (((1,), (1,)), ((), ()))
        some = lax.dot_general(hits, where, nt, preferred_element_type=F32)
        gather = some if gather is None else gather + some
        some = lax.dot_general(where, hits, nt, preferred_element_type=F32)
        spread = some if spread is None else spread + some
    return gather, jnp.concatenate([spread] * 3, axis=1)


def scale_of(plan, owners):
    owner = iota((plan.owners, plan.columns), 0).astype(owners.dtype)
    hits = jnp.zeros((plan.owners, plan.columns), F32)
    for g in range(plan.owners):
        hits = hits + (owners[g : g + 1] == owner).astype(F32)
    count = jnp.sum(hits, axis=1, keepdims=True)
    return jnp.broadcast_to(0.125 / jnp.maximum(count, 1.0), (plan.owners, plan.p))


def mobility_of(mask, kind, table):
    values = jnp.zeros(kind.shape, F32)
    for marker, value in enumerate(table):
        values = jnp.where(kind == marker, value, values)
    return mask.astype(F32) * values


def even(axis):
    return lax.rem(lax.axis_index(axis), 2) == 0


def put_x(plan, lows, highs, near, far):
    up = even("gx")
    for which, (low, high) in enumerate(zip(lows, highs)):
        near[pl.ds(which * plan.y, plan.y), :] = jnp.where(up, high, low)
        far[pl.ds(which * plan.y, plan.y), :] = jnp.where(up, low, high)


def received(axis, near_ref, far_ref):
    up = even(axis)
    rows = pl.ds(0, min(near_ref.shape[0], far_ref.shape[0]))
    near, far = near_ref[rows, :], far_ref[rows, :]
    return jnp.where(up, far, near), jnp.where(up, near, far)


def prepare_kernel(plan, *refs):
    hbm, refs = refs[:8], refs[8:]
    x_near_ref, x_far_ref, y_near_ref, y_far_ref = refs[:4]
    x_refs, y_refs, (owner_ref, table_ref, sems) = refs[4:8], refs[8:14], refs[14:]
    copies = []

    def start(source, target):
        copies.append(pltpu.make_async_copy(source, target, sems.at[len(copies)]))
        copies[-1].start()

    start(hbm[7], table_ref)
    start(hbm[6], owner_ref)
    for source, target in zip(hbm[:4], x_refs):
        start(source.at[0], target.at[0])
        start(source.at[plan.x - 1], target.at[1])
    for source, target in zip(hbm[:6], y_refs):
        start(source.at[:, pl.ds(0, 8)], target.at[0])
        start(source.at[:, pl.ds(plan.y - 8, 8)], target.at[1])
    for copy in copies:
        copy.wait()
    table = [table_ref[marker] for marker in range(table_ref.shape[0])]
    conc, pot, mask, kind = (ref[...] for ref in x_refs)
    fields = (conc, pot, mobility_of(mask, kind, table))
    put_x(plan, [f[0] for f in fields], [f[1] for f in fields], x_near_ref, x_far_ref)
    conc, pot, mask, kind, mass, pots = (ref[...] for ref in y_refs)
    fields = (conc, pot, mobility_of(mask, kind, table))
    up = even("gy")
    rows = [(field, at) for at in range(2) for field in fields] + [(mass, 0), (pots, 0)]
    for which, (field, at) in enumerate(rows):
        for x in range(plan.x):
            low, high = field[0, x, at : at + 1], field[1, x, 7 - at : 8 - at]
            y_near_ref[pl.ds(which * plan.x + x, 1), :] = jnp.where(up, high, low)
            y_far_ref[pl.ds(which * plan.x + x, 1), :] = jnp.where(up, low, high)
    used = 8 * plan.x
    for ref, rows in ((y_near_ref, plan.y_rows), (y_far_ref, plan.y_far_rows)):
        ref[pl.ds(used, rows - used), :] = jnp.zeros((rows - used, plan.p), F32)
        ref[pl.ds(plan.map_row, plan.owners), pl.ds(0, plan.columns)] = owner_ref[...].astype(F32)


def inner_faces(mobility):
    half = 0.5 * time_step
    shape = mobility.shape
    y, plane = iota(shape, 1), iota(shape, 2)
    to_x = jnp.concatenate(
        [half * (mobility[:-1] + mobility[1:]), jnp.zeros_like(mobility[:1])], axis=0
    )
    out = [to_x]
    for dim, where, shift, edge in (
        (1, y, 1, 0), (1, y, shape[1] - 1, shape[1] - 1),
        (2, plane, 1, 0), (2, plane, shape[2] - 1, shape[2] - 1),
    ):
        face = half * (mobility + pltpu.roll(mobility, shift, dim))
        out.append(jnp.where(where == edge, 0.0, face))
    return out


def inner_flux(faces, field):
    to_x, y_low, y_high, plane_low, plane_high = faces
    size_y, size_p = field.shape[1:]
    from_x = to_x[:-1]
    blank = jnp.zeros_like(field[:1])
    flux = jnp.concatenate([from_x * field[1:], blank], axis=0)
    flux = flux + jnp.concatenate([blank, from_x * field[:-1]], axis=0)
    flux = flux + y_low * pltpu.roll(field, 1, 1) + y_high * pltpu.roll(field, size_y - 1, 1)
    return flux + plane_low * pltpu.roll(field, 1, 2) + plane_high * pltpu.roll(field, size_p - 1, 2)


def inner_excess(conc, pot, faces, diagonal, mass_source, pot_source):
    excess_mass = (mass_source - conc) - diagonal * pot + inner_flux(faces, pot)
    nothing = [jnp.zeros_like(conc[:1])] * 2 + [jnp.zeros_like(conc[:, :1])] * 2
    beside = None
    for other in neighbours(conc, nothing):
        beside = other if beside is None else beside + other
    excess_pot = (pot_source - pot) + (split_slope + 6.0 * interface) * conc - interface * beside
    return excess_mass, excess_pot


def add_edges(field, x_low, x_high, y_low, y_high):
    field = jnp.concatenate(
        [(field[0] + x_low)[None], field[1:-1], (field[-1] + x_high)[None]], axis=0
    )
    row = iota((field.shape[0], 8, field.shape[2]), 1)
    size = field.shape[1]
    low = field[:, :8] + jnp.where(row == 0, y_low, 0.0)
    high = field[:, size - 8 :] + jnp.where(row == 7, y_high, 0.0)
    return jnp.concatenate([low, field[:, 8 : size - 8], high], axis=1)


def local_kernel(
    plan, conc_ref, pot_ref, mask_ref, class_ref, mass_ref, pots_ref, table_ref, owner_ref,
    mob_ref, gather_ref, spread_ref, scale_ref, faces_ref, diagonal_ref, mass_out, pots_out,
):
    table = [table_ref[marker] for marker in range(table_ref.shape[0])]
    mobility = mobility_of(mask_ref[...], class_ref[...], table)
    mob_ref[...] = mobility
    gather_ref[...], spread_ref[...] = membership(plan, owner_ref)
    scale_ref[...] = scale_of(plan, owner_ref[...])
    faces = inner_faces(mobility)
    diagonal = faces[0] + jnp.concatenate([jnp.zeros_like(mobility[:1]), faces[0][:-1]], axis=0)
    for face in faces[1:]:
        diagonal = diagonal + face
    plane = iota(mobility.shape, 2)
    ends = (plane == 0) | (plane == plan.p - 1)
    diagonal = diagonal + jnp.where(ends, (0.5 * time_step) * mobility, 0.0)
    for i, face in enumerate(faces):
        faces_ref[i] = face
    diagonal_ref[...] = diagonal
    mass_out[...], pots_out[...] = inner_excess(
        conc_ref[...], pot_ref[...], faces, diagonal, mass_ref[...], pots_ref[...]
    )


def first_kernel(
    plan, x_far_ref, x_near_ref, y_far_ref, y_near_ref,
    conc_ref, pot_ref, mob_ref, mass_ref, pots_ref, gather_ref, scale_ref, owner_ref,
    faces_ref, diagonal_ref, mass_part_ref, pot_part_ref,
    conc_out, pot_out, total_hbm, raw_out, x_near_out, x_far_out, total_out, sems,
):
    sides = received("gx", x_near_ref, x_far_ref)
    ends = received("gy", y_near_ref, y_far_ref)
    last_x, last_y = plan.x - 1, plan.y - 1

    def halo(which):
        return tuple(side_rows(plan, rows, which)[0] for rows in sides) + tuple(
            side_columns(plan, rows, which) for rows in ends
        )

    def edges(field):
        return field[0], field[last_x], field[:, :1], field[:, last_y:]

    mobility = mob_ref[...]
    raw_conc, raw_pot = conc_ref[...], pot_ref[...]
    outer = [
        (0.5 * time_step) * (own + other) for own, other in zip(edges(mobility), halo(2))
    ]
    diagonal = add_edges(diagonal_ref[...], *outer)
    excess_mass = add_edges(
        mass_part_ref[...],
        *(f * (other - own) for f, own, other in zip(outer, edges(raw_pot), halo(1))),
    )
    excess_pot = add_edges(pot_part_ref[...], *(-interface * other for other in halo(0)))
    conc, pot = relax_pair(
        raw_conc, raw_pot, excess_mass, excess_pot, diagonal, scale_from(diagonal)
    )

    own_mass, own_pot = inner_excess(
        conc, pot, [faces_ref[i] for i in range(5)], diagonal, mass_ref[...], pots_ref[...]
    )
    give_mass, give_pot = (
        [field[x] + field[x + 1] for x in range(0, plan.x, 2)] for field in (own_mass, own_pot)
    )
    for x, side in ((0, 0), (last_x, 1)):
        give_mass.append(outer[side] * pot[x])
        give_pot.append(-interface * conc[x])

    def packed(mass, other):
        first = iota(mass.shape, 1) & 1 == 0
        return jnp.where(
            first, mass + pltpu.roll(mass, plan.p - 1, 1), other + pltpu.roll(other, 1, 1)
        )

    give = packed(jnp.concatenate(give_mass, axis=0), jnp.concatenate(give_pot, axis=0))
    h = lax.axis_index("gy")
    inside = (h > 0, None, h < plan.groups - 1)
    maps = [rows[plan.map_row : plan.map_row + plan.owners, : plan.columns] for rows in ends]
    maps.insert(1, owner_ref[...].astype(F32))
    owner = iota((plan.owners, 1), 0)
    is_mine = owner == lax.axis_index("gx")

    own = lax.dot_general(
        gather_ref[...].astype(BF16),
        three_terms(give, 1).astype(BF16),
        (((1,), (0,)), ((), ())),
        preferred_element_type=F32,
    )
    own = own[:, : plan.p] + own[:, plan.p : 2 * plan.p] + own[:, 2 * plan.p :]
    sums = [None, own * scale_ref[...], None]
    for place, y, at, side in ((0, 0, plan.half_y - 1, 2), (2, plan.y - 1, 0, 3)):
        edge_pot, edge_conc = (
            jnp.concatenate([field[x, y : y + 1] for x in range(plan.x)], axis=0)
            for field in (pot, conc)
        )
        both = packed(outer[side][:, 0] * edge_pot, -interface * edge_conc)
        part = jnp.zeros((plan.owners, plan.p), F32)
        for i in range(plan.half_x):
            column = owner_column(plan, maps[place], i, at)
            ident = jnp.sum(jnp.where(is_mine, column, 0.0), axis=0, keepdims=True)
            pair = both[2 * i : 2 * i + 1] + both[2 * i + 1 : 2 * i + 2]
            part = part + jnp.where((owner.astype(F32) == ident) & inside[place], pair, 0.0)
        sums[place] = part * scale_of(plan, maps[place])
    def store_fields():
        conc_out[...] = conc
        pot_out[...] = pot
        for at, field in enumerate((raw_conc, raw_pot)):
            for x in range(plan.x):
                raw_out[pl.ds(2 * at * plan.x + x, 1), :] = field[x, 0:1]
                raw_out[pl.ds((2 * at + 1) * plan.x + x, 1), :] = field[x, last_y : last_y + 1]
        put_x(plan, (conc[0], pot[0]), (conc[last_x], pot[last_x]), x_near_out, x_far_out)
        up = even("gx")
        base = 2 * plan.y
        for which in range(3):
            for end, rows in enumerate(ends):
                low = rows[which * plan.x : which * plan.x + 1]
                high = rows[(which + 1) * plan.x - 1 : (which + 1) * plan.x]
                x_near_out[pl.ds(base + 2 * which + end, 1), :] = jnp.where(up, high, low)
                x_far_out[pl.ds(base + 2 * which + end, 1), :] = jnp.where(up, low, high)
        for ref in (x_near_out, x_far_out):
            ref[pl.ds(base + 6, 2), :] = jnp.zeros((2, plan.p), F32)

    if not plan.slots:
        total_out[...] = jnp.concatenate(sums, axis=0)
        copies = [pltpu.make_async_copy(total_out, total_hbm, sems.at[0])]
        copies[0].start()
        store_fields()
        copies[0].wait()
        return

    def picked(place, i, at):
        column = owner_column(plan, maps[place], i, at)
        ident = jnp.broadcast_to(column, (plan.owners, plan.p))
        out = jnp.zeros((plan.owners, plan.p), F32)
        for o in range(plan.owners):
            out = jnp.where(ident == float(o), sums[place][o : o + 1], out)
        return out

    below = [[picked(k, i, plan.half_y - 1) for i in range(plan.half_x)] for k in range(3)]
    above = [[picked(k, i, 0) for i in range(plan.half_x)] for k in range(3)]

    def of_plane(plane, choices):
        out = jnp.zeros((plan.owners, plan.p), F32)
        for k in range(3):
            out = jnp.where(plane == h + (k - 1), choices[k], out)
        return out

    size = 4 * plan.slot_parts
    rows = []
    for plane in range(plan.groups):
        beside = []
        for i in range(plan.half_x):
            beside.append((plan.low_row + i, of_plane(plane - 1, [k[i] for k in below])))
            beside.append((plan.high_row + i, of_plane(plane + 1, [k[i] for k in above])))
        blank = jnp.zeros((plan.owners, plan.p), F32)
        beside += [(at, blank) for at in range(plan.high_row + plan.half_x, size)]
        rows.append((of_plane(plane, sums), beside))
    copies = []
    for plane, (main, beside) in enumerate(rows):
        for g in range(plan.owners):
            slot = plan.slot_of(g, plane)
            for part in range(plan.owners // 4):
                total_out[slot, part] = main[4 * part : 4 * part + 4]
            for row, values in beside:
                total_out[slot, row // 4, pl.ds(row % 4, 1), :] = values[g : g + 1]
        some = pl.ds(plan.slot_of(plan.owners - 2, plane), plan.owners)
        copies.append(
            pltpu.make_async_copy(total_out.at[some], total_hbm.at[some], sems.at[plane])
        )
        copies[-1].start()
    store_fields()
    for copy in copies:
        copy.wait()


def owner_column(plan, owners, i, at):
    b = i * plan.half_y + at
    return owners[:, b : b + 1]


def coarse_solve(packed, planes):
    lane = iota(packed.shape, 1)
    even = lane & 1 == 0
    mass_mean = jnp.where(even, packed, pltpu.roll(packed, 1, 1))
    pot_mean = jnp.where(even, pltpu.roll(packed, planes - 1, 1), packed)

    def neighbour_sum(values):
        return jnp.where(lane >= 2, pltpu.roll(values, 2, 1), 0.0) + jnp.where(
            lane < planes - 2, pltpu.roll(values, planes - 2, 1), 0.0
        )

    def step(mass_gap, pot_gap):
        scale = relax_coarse / coarse_det
        return (
            scale * (mass_gap - 2.0 * coarse_flux * pot_gap),
            scale * (pot_gap + (split_slope + 2.0 * coarse_bend) * mass_gap),
        )

    coarse_conc, coarse_pot = step(mass_mean, pot_mean)
    for _ in range(CSWEEP - 1):
        mass_gap = mass_mean - (
            coarse_conc + coarse_flux * (2.0 * coarse_pot - neighbour_sum(coarse_pot))
        )
        pot_gap = pot_mean - (
            coarse_pot
            - split_slope * coarse_conc
            + coarse_bend * (neighbour_sum(coarse_conc) - 2.0 * coarse_conc)
        )
        more_conc, more_pot = step(mass_gap, pot_gap)
        coarse_conc, coarse_pot = coarse_conc + more_conc, coarse_pot + more_pot
    return coarse_conc, coarse_pot


def beside_kernel(
    plan, x_near_ref, x_far_ref, conc_ref, pot_ref, mass_ref, pots_ref, mob_ref, raw_ref,
    x_near_msg, x_far_msg, y_near_msg, y_far_msg,
    faces_out, diagonal_out, scale_out, mass_out, pots_out,
):
    mobility = mob_ref[...]
    sides = received("gx", x_near_msg, x_far_msg)
    ends = received("gy", y_near_msg, y_far_msg)
    halo = tuple(side_rows(plan, rows, 2) for rows in sides) + tuple(
        side_columns(plan, rows, 2) for rows in ends
    )
    faces, diagonal = faces_of(mobility, neighbours(mobility, halo))
    block_terms = faces, diagonal, mass_ref[...], pots_ref[...]
    for i, face in enumerate(faces):
        faces_out[i] = face
    diagonal_out[...] = diagonal
    scale_out[...] = scale_from(diagonal)

    corners = received("gx", x_near_ref, x_far_ref)
    h = lax.axis_index("gy")
    inside = (h > 0, h < plan.groups - 1)
    own_mob = [
        jnp.concatenate([mobility[x, y : y + 1] for x in range(plan.x)], axis=0)
        for y in (0, plan.y - 1)
    ]
    halos = [[side_rows(plan, rows, which) for rows in corners] for which in range(2)]
    for end, rows in enumerate(ends):

        def row(which):
            return rows[which * plan.x : (which + 1) * plan.x]

        def beside(which, own):
            here = row(which)
            at = 2 * plan.y + 2 * which + end
            wide = jnp.concatenate([corners[0][at : at + 1], here, corners[1][at : at + 1]], axis=0)
            return (
                wide[: plan.x], wide[2:], own, row(which + 3),
                *(part[0] for part in plane_pair(here[None])),
            )

        raw = [
            raw_ref[pl.ds((2 * which + end) * plan.x, plan.x), :] for which in range(2)
        ]
        faces, diagonal = faces_of(row(2), beside(2, own_mob[end]))
        excess = excess_of(
            row(0), row(1), beside(0, raw[0]), beside(1, raw[1]), faces, diagonal, row(6), row(7)
        )
        new = relax_pair(row(0), row(1), *excess, diagonal, scale_from(diagonal))
        for which, values in enumerate(new):
            halos[which].append(jnp.where(inside[end], values, 0.0)[:, None])
    conc, pot = conc_ref[...], pot_ref[...]
    mass_out[...], pots_out[...] = excess_of(
        conc, pot, neighbours(conc, halos[0]), neighbours(pot, halos[1]), *block_terms
    )


def last_kernel(
    plan, conc_ref, pot_ref, mass_ref, pots_ref, faces_ref, diagonal_ref, scale_ref,
    spread_ref, total_ref,
    conc_hbm, pot_hbm, conc_out, pot_out, sems,
):
    parts = []
    for part in range(plan.slot_parts):
        terms = [total_ref[slot, part] for slot in range(total_ref.shape[0])]
        while len(terms) > 1:
            pairs = [a + b for a, b in zip(terms[::2], terms[1::2])]
            terms = pairs + terms[len(pairs) * 2 :]
        parts.append(terms[0])
    solved = jnp.concatenate(
        coarse_solve(jnp.concatenate(parts, axis=0), plan.p), axis=1
    )
    own = lax.dot_general(
        spread_ref[...].astype(BF16),
        three_terms(solved[: plan.owners]).astype(BF16),
        (((1,), (0,)), ((), ())),
        preferred_element_type=F32,
    )

    def shifted(which):
        lanes = slice(which * plan.p, (which + 1) * plan.p)
        rows = [own[i * plan.y : (i + 1) * plan.y, lanes][None] for i in range(plan.half_x + 2)]
        beside = []
        for i in range(plan.half_x):
            ends = [
                solved[begin + i : begin + i + 1, lanes][None]
                for begin in (plan.low_row, plan.high_row)
            ]
            beside.append((*y_pair(rows[i], *ends), *plane_pair(rows[i])))
        return [rows[plan.half_x], *rows[: plan.half_x], rows[plan.half_x + 1]], beside

    conc_rows, conc_beside = shifted(0)
    pot_rows, pot_beside = shifted(1)
    conc_sums = [a + b + c + d for a, b, c, d in conc_beside]
    copies = []
    for x in range(plan.x):
        one = pl.ds(x, 1)
        i = x >> 1
        low, high = (i, i + 1) if x % 2 == 0 else (i + 1, i + 2)
        diagonal = diagonal_ref[one]
        conc, pot = conc_rows[i + 1], pot_rows[i + 1]
        excess_mass = mass_ref[one] - conc - diagonal * pot
        beside = (pot_rows[low], pot_rows[high], *pot_beside[i])
        for k, other in enumerate(beside):
            excess_mass = excess_mass + faces_ref[k, one] * other
        excess_pot = (pots_ref[one] - pot) + (split_slope + 6.0 * interface) * conc
        excess_pot = excess_pot - interface * (conc_rows[low] + conc_rows[high] + conc_sums[i])
        conc_out[one], pot_out[one] = relax_pair(
            conc_ref[one] + conc, pot_ref[one] + pot, excess_mass, excess_pot, diagonal, scale_ref[one]
        )
        for source, target in ((conc_out, conc_hbm), (pot_out, pot_hbm)):
            copies.append(
                pltpu.make_async_copy(source.at[one], target.at[one], sems.at[len(copies)])
            )
            copies[-1].start()
    for copy in copies:
        copy.wait()


def call(kernel, plan, outs, args, far=(), smem=(), scratch=(), out_far=()):
    def space(i):
        return pl.ANY if i in far else pltpu.SMEM if i in smem else pltpu.VMEM

    return pl.pallas_call(
        functools.partial(kernel, plan),
        out_shape=[jax.ShapeDtypeStruct(shape, F32) for shape in outs],
        in_specs=[pl.BlockSpec(memory_space=space(i)) for i in range(len(args))],
        out_specs=[
            pl.BlockSpec(memory_space=pl.ANY if i in out_far else pltpu.VMEM)
            for i in range(len(outs))
        ],
        scratch_shapes=list(scratch),
        compiler_params=pltpu.CompilerParams(vmem_limit_bytes=VMEM_LIMIT),
    )(*[
        pltpu.with_memory_space_constraint(arg, pltpu.HBM) if i in far else arg
        for i, arg in enumerate(args)
    ])


def swap_near(axis, rows, begin=0):
    pairs = [(i, i + 1) for i in range(begin, lax.axis_size(axis) - 1, 2)]
    return lax.ppermute(rows, axis, pairs + [(j, i) for i, j in pairs])


def swap_far(axis, rows):
    return swap_near(axis, rows, 1)


def gather_totals(plan, total, y_near, y_far):
    if plan.slots:
        order = [0] * plan.slots
        for g in range(plan.owners):
            for h in range(plan.groups):
                order[plan.slot_of(g, h)] = g * plan.groups + h
        return lax.all_to_all(
            total, ("gx", "gy"), split_axis=0, concat_axis=0, axis_index_groups=[order], tiled=True
        )
    shape = (plan.groups, 3, plan.owners, plan.p)
    parts = lax.all_gather(lax.psum(total, "gx"), "gy").reshape(shape)
    blank = jnp.zeros((1, plan.owners, plan.p), F32)
    to_below, own, to_above = (parts[:, k] for k in range(3))
    own = own + jnp.concatenate([blank, to_above[:-1]]) + jnp.concatenate([to_below[1:], blank])
    own = jnp.concatenate([blank, own, blank])
    g, h = lax.axis_index("gx"), lax.axis_index("gy")
    rows = [lax.dynamic_index_in_dim(own, h + 1, 0, False)]
    up = lax.rem(h, 2) == 0
    far = y_far[: y_near.shape[0]]
    for place, at, msg in (
        (h, plan.half_y - 1, jnp.where(up, far, y_near)),
        (h + 2, 0, jnp.where(up, y_near, far)),
    ):
        ident = lax.dynamic_index_in_dim(msg, plan.map_row + g, 0, False).astype(jnp.int32)
        ident = jnp.stack([ident[i * plan.half_y + at] for i in range(plan.half_x)])
        rows.append(lax.dynamic_index_in_dim(own, place, 0, False)[ident])
    rows = jnp.concatenate(rows)
    rows = jnp.pad(rows, ((0, 4 * plan.slot_parts - rows.shape[0]), (0, 0)))
    return rows.reshape(1, plan.slot_parts, 4, plan.p)


def on_device(conc, pot, mass_source, pot_source, mask, kind, table, owner_map):
    plan = Plan(conc.shape, lax.axis_size("gx"), lax.axis_size("gy"))
    block = conc.shape
    fields = [conc, pot, mask, kind, mass_source, pot_source]
    messages = call(
        prepare_kernel,
        plan,
        [*[(3 * plan.y, plan.p)] * 2, (plan.y_rows, plan.p), (plan.y_far_rows, plan.p)],
        [*fields, owner_map, table],
        far=range(8),
        scratch=(
            *[pltpu.VMEM((2, plan.y, plan.p), field.dtype) for field in fields[:4]],
            *[pltpu.VMEM((2, plan.x, 8, plan.p), field.dtype) for field in fields],
            pltpu.VMEM(owner_map.shape, owner_map.dtype),
            pltpu.SMEM(table.shape, table.dtype),
            pltpu.SemaphoreType.DMA((22,)),
        ),
    )
    x_near, x_far = swap_near("gx", messages[0]), swap_far("gx", messages[1])
    y_near, y_far = swap_near("gy", messages[2]), swap_far("gy", messages[3])
    y_far, mask, kind = lax.optimization_barrier((y_far, mask, kind))
    mob, gather, spread, scale, *parts = call(
        local_kernel,
        plan,
        [
            block, (plan.owners, plan.rows), (plan.rows, 3 * plan.owners), (plan.owners, plan.p),
            (5, *block), block, block, block,
        ],
        [conc, pot, mask, kind, mass_source, pot_source, table, owner_map],
        smem=(6,),
    )
    slots = (plan.slots, plan.slot_parts, 4, plan.p) if plan.slots else (3 * plan.owners, plan.p)
    conc, pot, total, raw, near, far = call(
        first_kernel,
        plan,
        [
            block,
            block,
            slots,
            (4 * plan.x, plan.p),
            *[(2 * plan.y + 8, plan.p)] * 2,
        ],
        [
            x_far, x_near, y_far, y_near,
            conc, pot, mob, mass_source, pot_source, gather, scale, owner_map, *parts,
        ],
        out_far=(2,),
        scratch=(pltpu.VMEM(slots, F32), pltpu.SemaphoreType.DMA((plan.groups,))),
    )
    total = gather_totals(plan, total, y_near, y_far)
    far = swap_far("gx", far)
    near = swap_near("gx", near)
    faces, diagonal, scale, mass_part, pot_part = call(
        beside_kernel,
        plan,
        [(6, *block), block, block, block, block],
        [
            near, far, conc, pot, mass_source, pot_source, mob, raw,
            x_near, x_far, y_near, y_far,
        ],
    )
    return tuple(
        call(
            last_kernel,
            plan,
            [block, block],
            [conc, pot, mass_part, pot_part, faces, diagonal, scale, spread, total],
            out_far=(0, 1),
            scratch=(
                pltpu.VMEM(block, F32),
                pltpu.VMEM(block, F32),
                pltpu.SemaphoreType.DMA((2 * plan.x,)),
            ),
        )
    )


def solution(mesh):
    grid = P("gx", "gy", None)
    return jax.shard_map(
        on_device,
        mesh=mesh,
        in_specs=(grid,) * 6 + (P(), P(None, "gy")),
        out_specs=(grid, grid),
        check_vma=False,
    )
```

```python
import functools

import jax
import jax.numpy as jnp
from jax import lax
from jax.experimental import pallas as pl
from jax.experimental.pallas import tpu as pltpu
from jax.sharding import PartitionSpec as P

CSWEEP = 3

time_step = 0.25
split_slope = 1.0
interface = 0.5
relax_fine = 0.6
relax_coarse = 0.6
coarse_flux = 0.0625
coarse_bend = 0.125
coarse_det = 1.0 + 2.0 * coarse_flux * (split_slope + 2.0 * coarse_bend)

F32 = jnp.float32
BF16 = jnp.bfloat16
VMEM_LIMIT = 48 * 1024 * 1024


def iota(shape, dim):
    return lax.broadcasted_iota(jnp.int32, shape, dim)


def x_pair(field, low, high):
    return (
        jnp.concatenate([low, field[:-1]], axis=0),
        jnp.concatenate([field[1:], high], axis=0),
    )


def y_pair(field, low, high):
    size = field.shape[1]
    where = iota(field.shape, 1)
    return (
        jnp.where(where == 0, low, pltpu.roll(field, 1, 1)),
        jnp.where(where == size - 1, high, pltpu.roll(field, size - 1, 1)),
    )


def plane_pair(field):
    size = field.shape[2]
    where = iota(field.shape, 2)
    return (
        jnp.where(where == 0, 0.0, pltpu.roll(field, 1, 2)),
        jnp.where(where == size - 1, 0.0, pltpu.roll(field, size - 1, 2)),
    )


def neighbours(field, halo):
    xm, xp, ym, yp = halo
    return (*x_pair(field, xm, xp), *y_pair(field, ym, yp), *plane_pair(field))


def excess_of(conc, pot, conc_beside, pot_beside, faces, diagonal, mass_source, pot_source):
    excess_mass = (mass_source - conc) - diagonal * pot
    for face, other in zip(faces, pot_beside):
        excess_mass = excess_mass + face * other
    beside = conc_beside[0]
    for other in conc_beside[1:]:
        beside = beside + other
    excess_pot = (pot_source - pot) + (split_slope + 6.0 * interface) * conc - interface * beside
    return excess_mass, excess_pot


def scale_from(diagonal):
    return relax_fine / (1.0 + (split_slope + 6.0 * interface) * diagonal)


def relax_pair(conc, pot, excess_mass, excess_pot, diagonal, scale):
    new_conc = conc + (excess_mass - diagonal * excess_pot) * scale
    new_pot = pot + (excess_pot + (split_slope + 6.0 * interface) * excess_mass) * scale
    return new_conc, new_pot


def faces_of(mobility, beside):
    faces = tuple((0.5 * time_step) * (mobility + other) for other in beside)
    diagonal = faces[0]
    for face in faces[1:]:
        diagonal = diagonal + face
    return faces, diagonal


def three_terms(values, dim=0):
    out = []
    for _ in range(3):
        out.append(values.astype(BF16).astype(F32))
        values = values - out[-1]
    return jnp.concatenate(out, axis=dim)


def round_up(value, unit):
    return -(-value // unit) * unit


class Plan:
    def __init__(self, shape, owners, groups):
        self.x, self.y, self.p = shape
        self.owners, self.groups = owners, groups
        self.half_x, self.half_y = self.x // 2, self.y // 2
        self.columns = self.half_x * self.half_y
        self.map_row = round_up(8 * self.x, 8)
        self.y_rows = self.map_row + owners
        self.y_far_rows = max(self.y_rows, 3 * self.y + 8)
        self.cells = self.x * self.y
        self.rows = (self.half_x + 2) * self.y
        self.low_row = owners
        self.high_row = owners + self.half_x
        self.slot_parts = -(-(owners + 2 * self.half_x) // 4)
        slots = owners * groups
        self.slots = slots if slots <= 64 else 0

    def slot_of(self, g, h):
        last = self.groups - 1
        place = 0 if h == 0 else 1 if h == last else h + 1
        return place * self.owners + self.owners - 1 - (g ^ 1)


def side_rows(plan, rows, which):
    return rows[which * plan.y : (which + 1) * plan.y][None]


def side_columns(plan, rows, which):
    return rows[which * plan.x : (which + 1) * plan.x][:, None]


def membership(plan, owner_ref):
    g = lax.axis_index("gx")
    last = plan.owners - 1
    owner = iota((plan.owners, plan.columns), 0)
    low, high = plan.half_x, plan.half_x + 1
    shape = (plan.half_x + 2, plan.y, plan.columns)
    x, y, column = iota(shape, 0), iota(shape, 1), iota(shape, 2)
    half = jnp.where(x < low, x, jnp.where(x == low, plan.half_x - 1, 0))
    place = column == half * plan.half_y + (y >> 1)
    sides = (
        (x < low, g, True),
        (x == low, jnp.maximum(g - 1, 0), g > 0),
        (x == high, jnp.minimum(g + 1, last), g < last),
    )
    gather, spread = None, None
    for part, row, inside in sides:
        hits = ((owner_ref[pl.ds(row, 1), :] == owner) & inside).astype(F32).astype(BF16)
        where = (place & part).astype(F32).reshape(plan.rows, plan.columns).astype(BF16)
        nt = (((1,), (1,)), ((), ()))
        some = lax.dot_general(hits, where, nt, preferred_element_type=F32)
        gather = some if gather is None else gather + some
        some = lax.dot_general(where, hits, nt, preferred_element_type=F32)
        spread = some if spread is None else spread + some
    return gather, jnp.concatenate([spread] * 3, axis=1)


def scale_of(plan, owners):
    owner = iota((plan.owners, plan.columns), 0).astype(owners.dtype)
    hits = jnp.zeros((plan.owners, plan.columns), F32)
    for g in range(plan.owners):
        hits = hits + (owners[g : g + 1] == owner).astype(F32)
    count = jnp.sum(hits, axis=1, keepdims=True)
    return jnp.broadcast_to(0.125 / jnp.maximum(count, 1.0), (plan.owners, plan.p))


def mobility_of(mask, kind, table):
    values = jnp.zeros(kind.shape, F32)
    for marker, value in enumerate(table):
        values = jnp.where(kind == marker, value, values)
    return mask.astype(F32) * values


def even(axis):
    return lax.rem(lax.axis_index(axis), 2) == 0


def put_x(plan, lows, highs, near, far):
    up = even("gx")
    for which, (low, high) in enumerate(zip(lows, highs)):
        near[pl.ds(which * plan.y, plan.y), :] = jnp.where(up, high, low)
        far[pl.ds(which * plan.y, plan.y), :] = jnp.where(up, low, high)


def received(axis, near_ref, far_ref):
    up = even(axis)
    rows = pl.ds(0, min(near_ref.shape[0], far_ref.shape[0]))
    near, far = near_ref[rows, :], far_ref[rows, :]
    return jnp.where(up, far, near), jnp.where(up, near, far)


def prepare_kernel(plan, *refs):
    hbm, refs = refs[:8], refs[8:]
    x_near_ref, x_far_ref, y_near_ref, y_far_ref = refs[:4]
    whole_refs, y_refs, (owner_ref, table_ref, sems) = refs[4:8], refs[8:10], refs[10:]
    copies = []

    def start(source, target):
        copies.append(pltpu.make_async_copy(source, target, sems.at[len(copies)]))
        copies[-1].start()

    start(hbm[7], table_ref)
    start(hbm[6], owner_ref)
    for source, target in zip(hbm[:4], whole_refs):
        start(source, target)
    for source, target in zip(hbm[4:6], y_refs):
        start(source.at[:, pl.ds(0, 8)], target.at[0])
        start(source.at[:, pl.ds(plan.y - 8, 8)], target.at[1])
    for copy in copies:
        copy.wait()
    table = [table_ref[marker] for marker in range(table_ref.shape[0])]
    last = plan.x - 1

    def part(pick):
        conc, pot, mask, kind = (pick(ref) for ref in whole_refs)
        return conc, pot, mobility_of(mask, kind, table)

    lows, highs = part(lambda ref: ref[0]), part(lambda ref: ref[last])
    put_x(plan, lows, highs, x_near_ref, x_far_ref)
    lows = part(lambda ref: ref[:, pl.ds(0, 8), :])
    highs = part(lambda ref: ref[:, pl.ds(plan.y - 8, 8), :])
    fields = [*zip(lows, highs)]
    mass, pots = (ref[...] for ref in y_refs)
    up = even("gy")
    rows = [(field, at) for at in range(2) for field in fields] + [(mass, 0), (pots, 0)]
    for which, (field, at) in enumerate(rows):
        for x in range(plan.x):
            low, high = field[0][x, at : at + 1], field[1][x, 7 - at : 8 - at]
            y_near_ref[pl.ds(which * plan.x + x, 1), :] = jnp.where(up, high, low)
            y_far_ref[pl.ds(which * plan.x + x, 1), :] = jnp.where(up, low, high)
    used = 8 * plan.x
    for ref, rows in ((y_near_ref, plan.y_rows), (y_far_ref, plan.y_far_rows)):
        ref[pl.ds(used, rows - used), :] = jnp.zeros((rows - used, plan.p), F32)
        ref[pl.ds(plan.map_row, plan.owners), pl.ds(0, plan.columns)] = owner_ref[...].astype(F32)


def inner_faces(mobility):
    half = 0.5 * time_step
    shape = mobility.shape
    y, plane = iota(shape, 1), iota(shape, 2)
    to_x = jnp.concatenate(
        [half * (mobility[:-1] + mobility[1:]), jnp.zeros_like(mobility[:1])], axis=0
    )
    out = [to_x]
    for dim, where, shift, edge in (
        (1, y, 1, 0), (1, y, shape[1] - 1, shape[1] - 1),
        (2, plane, 1, 0), (2, plane, shape[2] - 1, shape[2] - 1),
    ):
        face = half * (mobility + pltpu.roll(mobility, shift, dim))
        out.append(jnp.where(where == edge, 0.0, face))
    return out


def inner_flux(faces, field):
    to_x, y_low, y_high, plane_low, plane_high = faces
    size_y, size_p = field.shape[1:]
    from_x = to_x[:-1]
    blank = jnp.zeros_like(field[:1])
    flux = jnp.concatenate([from_x * field[1:], blank], axis=0)
    flux = flux + jnp.concatenate([blank, from_x * field[:-1]], axis=0)
    flux = flux + y_low * pltpu.roll(field, 1, 1) + y_high * pltpu.roll(field, size_y - 1, 1)
    return flux + plane_low * pltpu.roll(field, 1, 2) + plane_high * pltpu.roll(field, size_p - 1, 2)


def inner_excess(conc, pot, faces, diagonal, mass_source, pot_source):
    excess_mass = (mass_source - conc) - diagonal * pot + inner_flux(faces, pot)
    nothing = [jnp.zeros_like(conc[:1])] * 2 + [jnp.zeros_like(conc[:, :1])] * 2
    beside = None
    for other in neighbours(conc, nothing):
        beside = other if beside is None else beside + other
    excess_pot = (pot_source - pot) + (split_slope + 6.0 * interface) * conc - interface * beside
    return excess_mass, excess_pot


def add_edges(field, x_low, x_high, y_low, y_high):
    field = jnp.concatenate(
        [(field[0] + x_low)[None], field[1:-1], (field[-1] + x_high)[None]], axis=0
    )
    row = iota((field.shape[0], 8, field.shape[2]), 1)
    size = field.shape[1]
    low = field[:, :8] + jnp.where(row == 0, y_low, 0.0)
    high = field[:, size - 8 :] + jnp.where(row == 7, y_high, 0.0)
    return jnp.concatenate([low, field[:, 8 : size - 8], high], axis=1)


def local_kernel(
    plan, conc_ref, pot_ref, mask_ref, class_ref, mass_ref, pots_ref, table_ref, owner_ref,
    mob_ref, gather_ref, spread_ref, scale_ref, faces_ref, diagonal_ref, mass_out, pots_out,
):
    table = [table_ref[marker] for marker in range(table_ref.shape[0])]
    mobility = mobility_of(mask_ref[...], class_ref[...], table)
    mob_ref[...] = mobility
    gather_ref[...], spread_ref[...] = membership(plan, owner_ref)
    scale_ref[...] = scale_of(plan, owner_ref[...])
    faces = inner_faces(mobility)
    diagonal = faces[0] + jnp.concatenate([jnp.zeros_like(mobility[:1]), faces[0][:-1]], axis=0)
    for face in faces[1:]:
        diagonal = diagonal + face
    plane = iota(mobility.shape, 2)
    ends = (plane == 0) | (plane == plan.p - 1)
    diagonal = diagonal + jnp.where(ends, (0.5 * time_step) * mobility, 0.0)
    for i, face in enumerate(faces):
        faces_ref[i] = face
    diagonal_ref[...] = diagonal
    mass_out[...], pots_out[...] = inner_excess(
        conc_ref[...], pot_ref[...], faces, diagonal, mass_ref[...], pots_ref[...]
    )


def first_kernel(
    plan, x_far_ref, x_near_ref, y_far_ref, y_near_ref,
    conc_ref, pot_ref, mob_ref, mass_ref, pots_ref, gather_ref, scale_ref, owner_ref,
    faces_ref, diagonal_ref, mass_part_ref, pot_part_ref,
    conc_out, pot_out, total_hbm, raw_out, x_near_out, x_far_out, total_out, sems,
):
    sides = received("gx", x_near_ref, x_far_ref)
    ends = received("gy", y_near_ref, y_far_ref)
    last_x, last_y = plan.x - 1, plan.y - 1

    def halo(which):
        return tuple(side_rows(plan, rows, which)[0] for rows in sides) + tuple(
            side_columns(plan, rows, which) for rows in ends
        )

    def edges(field):
        return field[0], field[last_x], field[:, :1], field[:, last_y:]

    mobility = mob_ref[...]
    raw_conc, raw_pot = conc_ref[...], pot_ref[...]
    outer = [
        (0.5 * time_step) * (own + other) for own, other in zip(edges(mobility), halo(2))
    ]
    diagonal = add_edges(diagonal_ref[...], *outer)
    excess_mass = add_edges(
        mass_part_ref[...],
        *(f * (other - own) for f, own, other in zip(outer, edges(raw_pot), halo(1))),
    )
    excess_pot = add_edges(pot_part_ref[...], *(-interface * other for other in halo(0)))
    conc, pot = relax_pair(
        raw_conc, raw_pot, excess_mass, excess_pot, diagonal, scale_from(diagonal)
    )

    own_mass, own_pot = inner_excess(
        conc, pot, [faces_ref[i] for i in range(5)], diagonal, mass_ref[...], pots_ref[...]
    )
    give_mass, give_pot = (
        [field[x] + field[x + 1] for x in range(0, plan.x, 2)] for field in (own_mass, own_pot)
    )
    for x, side in ((0, 0), (last_x, 1)):
        give_mass.append(outer[side] * pot[x])
        give_pot.append(-interface * conc[x])

    def packed(mass, other):
        first = iota(mass.shape, 1) & 1 == 0
        return jnp.where(
            first, mass + pltpu.roll(mass, plan.p - 1, 1), other + pltpu.roll(other, 1, 1)
        )

    give = packed(jnp.concatenate(give_mass, axis=0), jnp.concatenate(give_pot, axis=0))
    h = lax.axis_index("gy")
    inside = (h > 0, None, h < plan.groups - 1)
    maps = [rows[plan.map_row : plan.map_row + plan.owners, : plan.columns] for rows in ends]
    maps.insert(1, owner_ref[...].astype(F32))
    owner = iota((plan.owners, 1), 0)
    is_mine = owner == lax.axis_index("gx")

    own = lax.dot_general(
        gather_ref[...].astype(BF16),
        three_terms(give, 1).astype(BF16),
        (((1,), (0,)), ((), ())),
        preferred_element_type=F32,
    )
    own = own[:, : plan.p] + own[:, plan.p : 2 * plan.p] + own[:, 2 * plan.p :]
    sums = [None, own * scale_ref[...], None]
    for place, y, at, side in ((0, 0, plan.half_y - 1, 2), (2, plan.y - 1, 0, 3)):
        edge_pot, edge_conc = (
            jnp.concatenate([field[x, y : y + 1] for x in range(plan.x)], axis=0)
            for field in (pot, conc)
        )
        both = packed(outer[side][:, 0] * edge_pot, -interface * edge_conc)
        part = jnp.zeros((plan.owners, plan.p), F32)
        for i in range(plan.half_x):
            column = owner_column(plan, maps[place], i, at)
            ident = jnp.sum(jnp.where(is_mine, column, 0.0), axis=0, keepdims=True)
            pair = both[2 * i : 2 * i + 1] + both[2 * i + 1 : 2 * i + 2]
            part = part + jnp.where((owner.astype(F32) == ident) & inside[place], pair, 0.0)
        sums[place] = part * scale_of(plan, maps[place])
    def store_fields():
        conc_out[...] = conc
        pot_out[...] = pot
        for at, field in enumerate((raw_conc, raw_pot)):
            for x in range(plan.x):
                raw_out[pl.ds(2 * at * plan.x + x, 1), :] = field[x, 0:1]
                raw_out[pl.ds((2 * at + 1) * plan.x + x, 1), :] = field[x, last_y : last_y + 1]
        put_x(plan, (conc[0], pot[0]), (conc[last_x], pot[last_x]), x_near_out, x_far_out)
        up = even("gx")
        base = 2 * plan.y
        for which in range(3):
            for end, rows in enumerate(ends):
                low = rows[which * plan.x : which * plan.x + 1]
                high = rows[(which + 1) * plan.x - 1 : (which + 1) * plan.x]
                x_near_out[pl.ds(base + 2 * which + end, 1), :] = jnp.where(up, high, low)
                x_far_out[pl.ds(base + 2 * which + end, 1), :] = jnp.where(up, low, high)
        for ref in (x_near_out, x_far_out):
            ref[pl.ds(base + 6, 2), :] = jnp.zeros((2, plan.p), F32)

    if not plan.slots:
        total_out[...] = jnp.concatenate(sums, axis=0)
        copies = [pltpu.make_async_copy(total_out, total_hbm, sems.at[0])]
        copies[0].start()
        store_fields()
        copies[0].wait()
        return

    def picked(place, i, at):
        column = owner_column(plan, maps[place], i, at)
        ident = jnp.broadcast_to(column, (plan.owners, plan.p))
        out = jnp.zeros((plan.owners, plan.p), F32)
        for o in range(plan.owners):
            out = jnp.where(ident == float(o), sums[place][o : o + 1], out)
        return out

    below = [[picked(k, i, plan.half_y - 1) for i in range(plan.half_x)] for k in range(3)]
    above = [[picked(k, i, 0) for i in range(plan.half_x)] for k in range(3)]

    def of_plane(plane, choices):
        out = jnp.zeros((plan.owners, plan.p), F32)
        for k in range(3):
            out = jnp.where(plane == h + (k - 1), choices[k], out)
        return out

    size = 4 * plan.slot_parts
    rows = []
    for plane in range(plan.groups):
        beside = []
        for i in range(plan.half_x):
            beside.append((plan.low_row + i, of_plane(plane - 1, [k[i] for k in below])))
            beside.append((plan.high_row + i, of_plane(plane + 1, [k[i] for k in above])))
        blank = jnp.zeros((plan.owners, plan.p), F32)
        beside += [(at, blank) for at in range(plan.high_row + plan.half_x, size)]
        rows.append((of_plane(plane, sums), beside))
    copies = []
    for plane, (main, beside) in enumerate(rows):
        for g in range(plan.owners):
            slot = plan.slot_of(g, plane)
            for part in range(plan.owners // 4):
                total_out[slot, part] = main[4 * part : 4 * part + 4]
            for row, values in beside:
                total_out[slot, row // 4, pl.ds(row % 4, 1), :] = values[g : g + 1]
        some = pl.ds(plan.slot_of(plan.owners - 2, plane), plan.owners)
        copies.append(
            pltpu.make_async_copy(total_out.at[some], total_hbm.at[some], sems.at[plane])
        )
        copies[-1].start()
    store_fields()
    for copy in copies:
        copy.wait()


def owner_column(plan, owners, i, at):
    b = i * plan.half_y + at
    return owners[:, b : b + 1]


def coarse_solve(packed, planes):
    lane = iota(packed.shape, 1)
    even = lane & 1 == 0
    mass_mean = jnp.where(even, packed, pltpu.roll(packed, 1, 1))
    pot_mean = jnp.where(even, pltpu.roll(packed, planes - 1, 1), packed)

    def neighbour_sum(values):
        return jnp.where(lane >= 2, pltpu.roll(values, 2, 1), 0.0) + jnp.where(
            lane < planes - 2, pltpu.roll(values, planes - 2, 1), 0.0
        )

    def step(mass_gap, pot_gap):
        scale = relax_coarse / coarse_det
        return (
            scale * (mass_gap - 2.0 * coarse_flux * pot_gap),
            scale * (pot_gap + (split_slope + 2.0 * coarse_bend) * mass_gap),
        )

    coarse_conc, coarse_pot = step(mass_mean, pot_mean)
    for _ in range(CSWEEP - 1):
        mass_gap = mass_mean - (
            coarse_conc + coarse_flux * (2.0 * coarse_pot - neighbour_sum(coarse_pot))
        )
        pot_gap = pot_mean - (
            coarse_pot
            - split_slope * coarse_conc
            + coarse_bend * (neighbour_sum(coarse_conc) - 2.0 * coarse_conc)
        )
        more_conc, more_pot = step(mass_gap, pot_gap)
        coarse_conc, coarse_pot = coarse_conc + more_conc, coarse_pot + more_pot
    return coarse_conc, coarse_pot


def beside_kernel(
    plan, x_near_ref, x_far_ref, conc_ref, pot_ref, mass_ref, pots_ref, mob_ref, raw_ref,
    x_near_msg, x_far_msg, y_near_msg, y_far_msg,
    faces_out, diagonal_out, scale_out, mass_out, pots_out,
):
    mobility = mob_ref[...]
    sides = received("gx", x_near_msg, x_far_msg)
    ends = received("gy", y_near_msg, y_far_msg)
    halo = tuple(side_rows(plan, rows, 2) for rows in sides) + tuple(
        side_columns(plan, rows, 2) for rows in ends
    )
    faces, diagonal = faces_of(mobility, neighbours(mobility, halo))
    block_terms = faces, diagonal, mass_ref[...], pots_ref[...]
    for i, face in enumerate(faces):
        faces_out[i] = face
    diagonal_out[...] = diagonal
    scale_out[...] = scale_from(diagonal)

    corners = received("gx", x_near_ref, x_far_ref)
    h = lax.axis_index("gy")
    inside = (h > 0, h < plan.groups - 1)
    own_mob = [
        jnp.concatenate([mobility[x, y : y + 1] for x in range(plan.x)], axis=0)
        for y in (0, plan.y - 1)
    ]
    halos = [[side_rows(plan, rows, which) for rows in corners] for which in range(2)]
    for end, rows in enumerate(ends):

        def row(which):
            return rows[which * plan.x : (which + 1) * plan.x]

        def beside(which, own):
            here = row(which)
            at = 2 * plan.y + 2 * which + end
            wide = jnp.concatenate([corners[0][at : at + 1], here, corners[1][at : at + 1]], axis=0)
            return (
                wide[: plan.x], wide[2:], own, row(which + 3),
                *(part[0] for part in plane_pair(here[None])),
            )

        raw = [
            raw_ref[pl.ds((2 * which + end) * plan.x, plan.x), :] for which in range(2)
        ]
        faces, diagonal = faces_of(row(2), beside(2, own_mob[end]))
        excess = excess_of(
            row(0), row(1), beside(0, raw[0]), beside(1, raw[1]), faces, diagonal, row(6), row(7)
        )
        new = relax_pair(row(0), row(1), *excess, diagonal, scale_from(diagonal))
        for which, values in enumerate(new):
            halos[which].append(jnp.where(inside[end], values, 0.0)[:, None])
    conc, pot = conc_ref[...], pot_ref[...]
    mass_out[...], pots_out[...] = excess_of(
        conc, pot, neighbours(conc, halos[0]), neighbours(pot, halos[1]), *block_terms
    )


def last_kernel(
    plan, conc_ref, pot_ref, mass_ref, pots_ref, faces_ref, diagonal_ref, scale_ref,
    spread_ref, total_ref,
    conc_hbm, pot_hbm, conc_out, pot_out, sems,
):
    parts = []
    for part in range(plan.slot_parts):
        terms = [total_ref[slot, part] for slot in range(total_ref.shape[0])]
        while len(terms) > 1:
            pairs = [a + b for a, b in zip(terms[::2], terms[1::2])]
            terms = pairs + terms[len(pairs) * 2 :]
        parts.append(terms[0])
    solved = jnp.concatenate(
        coarse_solve(jnp.concatenate(parts, axis=0), plan.p), axis=1
    )
    own = lax.dot_general(
        spread_ref[...].astype(BF16),
        three_terms(solved[: plan.owners]).astype(BF16),
        (((1,), (0,)), ((), ())),
        preferred_element_type=F32,
    )

    def shifted(which):
        lanes = slice(which * plan.p, (which + 1) * plan.p)
        rows = [own[i * plan.y : (i + 1) * plan.y, lanes][None] for i in range(plan.half_x + 2)]
        beside = []
        for i in range(plan.half_x):
            ends = [
                solved[begin + i : begin + i + 1, lanes][None]
                for begin in (plan.low_row, plan.high_row)
            ]
            beside.append((*y_pair(rows[i], *ends), *plane_pair(rows[i])))
        return [rows[plan.half_x], *rows[: plan.half_x], rows[plan.half_x + 1]], beside

    conc_rows, conc_beside = shifted(0)
    pot_rows, pot_beside = shifted(1)
    conc_sums = [a + b + c + d for a, b, c, d in conc_beside]
    copies = []
    for x in range(plan.x):
        one = pl.ds(x, 1)
        i = x >> 1
        low, high = (i, i + 1) if x % 2 == 0 else (i + 1, i + 2)
        diagonal = diagonal_ref[one]
        conc, pot = conc_rows[i + 1], pot_rows[i + 1]
        excess_mass = mass_ref[one] - conc - diagonal * pot
        beside = (pot_rows[low], pot_rows[high], *pot_beside[i])
        for k, other in enumerate(beside):
            excess_mass = excess_mass + faces_ref[k, one] * other
        excess_pot = (pots_ref[one] - pot) + (split_slope + 6.0 * interface) * conc
        excess_pot = excess_pot - interface * (conc_rows[low] + conc_rows[high] + conc_sums[i])
        conc_out[one], pot_out[one] = relax_pair(
            conc_ref[one] + conc, pot_ref[one] + pot, excess_mass, excess_pot, diagonal, scale_ref[one]
        )
        for source, target in ((conc_out, conc_hbm), (pot_out, pot_hbm)):
            copies.append(
                pltpu.make_async_copy(source.at[one], target.at[one], sems.at[len(copies)])
            )
            copies[-1].start()
    for copy in copies:
        copy.wait()


def call(kernel, plan, outs, args, far=(), smem=(), scratch=(), out_far=()):
    def space(i):
        return pl.ANY if i in far else pltpu.SMEM if i in smem else pltpu.VMEM

    return pl.pallas_call(
        functools.partial(kernel, plan),
        out_shape=[jax.ShapeDtypeStruct(shape, F32) for shape in outs],
        in_specs=[pl.BlockSpec(memory_space=space(i)) for i in range(len(args))],
        out_specs=[
            pl.BlockSpec(memory_space=pl.ANY if i in out_far else pltpu.VMEM)
            for i in range(len(outs))
        ],
        scratch_shapes=list(scratch),
        compiler_params=pltpu.CompilerParams(vmem_limit_bytes=VMEM_LIMIT),
    )(*[
        pltpu.with_memory_space_constraint(arg, pltpu.HBM) if i in far else arg
        for i, arg in enumerate(args)
    ])


def swap_near(axis, rows, begin=0):
    pairs = [(i, i + 1) for i in range(begin, lax.axis_size(axis) - 1, 2)]
    return lax.ppermute(rows, axis, pairs + [(j, i) for i, j in pairs])


def swap_far(axis, rows):
    return swap_near(axis, rows, 1)


def gather_totals(plan, total, y_near, y_far):
    if plan.slots:
        order = [0] * plan.slots
        for g in range(plan.owners):
            for h in range(plan.groups):
                order[plan.slot_of(g, h)] = g * plan.groups + h
        return lax.all_to_all(
            total, ("gx", "gy"), split_axis=0, concat_axis=0, axis_index_groups=[order], tiled=True
        )
    shape = (plan.groups, 3, plan.owners, plan.p)
    parts = lax.all_gather(lax.psum(total, "gx"), "gy").reshape(shape)
    blank = jnp.zeros((1, plan.owners, plan.p), F32)
    to_below, own, to_above = (parts[:, k] for k in range(3))
    own = own + jnp.concatenate([blank, to_above[:-1]]) + jnp.concatenate([to_below[1:], blank])
    own = jnp.concatenate([blank, own, blank])
    g, h = lax.axis_index("gx"), lax.axis_index("gy")
    rows = [lax.dynamic_index_in_dim(own, h + 1, 0, False)]
    up = lax.rem(h, 2) == 0
    far = y_far[: y_near.shape[0]]
    for place, at, msg in (
        (h, plan.half_y - 1, jnp.where(up, far, y_near)),
        (h + 2, 0, jnp.where(up, y_near, far)),
    ):
        ident = lax.dynamic_index_in_dim(msg, plan.map_row + g, 0, False).astype(jnp.int32)
        ident = jnp.stack([ident[i * plan.half_y + at] for i in range(plan.half_x)])
        rows.append(lax.dynamic_index_in_dim(own, place, 0, False)[ident])
    rows = jnp.concatenate(rows)
    rows = jnp.pad(rows, ((0, 4 * plan.slot_parts - rows.shape[0]), (0, 0)))
    return rows.reshape(1, plan.slot_parts, 4, plan.p)


def on_device(conc, pot, mass_source, pot_source, mask, kind, table, owner_map):
    plan = Plan(conc.shape, lax.axis_size("gx"), lax.axis_size("gy"))
    block = conc.shape
    fields = [conc, pot, mask, kind, mass_source, pot_source]
    messages = call(
        prepare_kernel,
        plan,
        [*[(3 * plan.y, plan.p)] * 2, (plan.y_rows, plan.p), (plan.y_far_rows, plan.p)],
        [*fields, owner_map, table],
        far=range(8),
        scratch=(
            *[pltpu.VMEM(block, field.dtype) for field in fields[:4]],
            *[pltpu.VMEM((2, plan.x, 8, plan.p), field.dtype) for field in fields[4:]],
            pltpu.VMEM(owner_map.shape, owner_map.dtype),
            pltpu.SMEM(table.shape, table.dtype),
            pltpu.SemaphoreType.DMA((10,)),
        ),
    )
    x_near, x_far = swap_near("gx", messages[0]), swap_far("gx", messages[1])
    y_near, y_far = swap_near("gy", messages[2]), swap_far("gy", messages[3])
    y_far, mask, kind = lax.optimization_barrier((y_far, mask, kind))
    mob, gather, spread, scale, *parts = call(
        local_kernel,
        plan,
        [
            block, (plan.owners, plan.rows), (plan.rows, 3 * plan.owners), (plan.owners, plan.p),
            (5, *block), block, block, block,
        ],
        [conc, pot, mask, kind, mass_source, pot_source, table, owner_map],
        smem=(6,),
    )
    slots = (plan.slots, plan.slot_parts, 4, plan.p) if plan.slots else (3 * plan.owners, plan.p)
    conc, pot, total, raw, near, far = call(
        first_kernel,
        plan,
        [
            block,
            block,
            slots,
            (4 * plan.x, plan.p),
            *[(2 * plan.y + 8, plan.p)] * 2,
        ],
        [
            x_far, x_near, y_far, y_near,
            conc, pot, mob, mass_source, pot_source, gather, scale, owner_map, *parts,
        ],
        out_far=(2,),
        scratch=(pltpu.VMEM(slots, F32), pltpu.SemaphoreType.DMA((plan.groups,))),
    )
    total = gather_totals(plan, total, y_near, y_far)
    far = swap_far("gx", far)
    near = swap_near("gx", near)
    faces, diagonal, scale, mass_part, pot_part = call(
        beside_kernel,
        plan,
        [(6, *block), block, block, block, block],
        [
            near, far, conc, pot, mass_source, pot_source, mob, raw,
            x_near, x_far, y_near, y_far,
        ],
    )
    return tuple(
        call(
            last_kernel,
            plan,
            [block, block],
            [conc, pot, mass_part, pot_part, faces, diagonal, scale, spread, total],
            out_far=(0, 1),
            scratch=(
                pltpu.VMEM(block, F32),
                pltpu.VMEM(block, F32),
                pltpu.SemaphoreType.DMA((2 * plan.x,)),
            ),
        )
    )


def solution(mesh):
    grid = P("gx", "gy", None)
    return jax.shard_map(
        on_device,
        mesh=mesh,
        in_specs=(grid,) * 6 + (P(), P(None, "gy")),
        out_specs=(grid, grid),
        check_vma=False,
    )
```

```python
import functools

import jax
import jax.numpy as jnp
from jax import lax
from jax.experimental import pallas as pl
from jax.experimental.pallas import tpu as pltpu
from jax.sharding import PartitionSpec as P

CSWEEP = 3

time_step = 0.25
split_slope = 1.0
interface = 0.5
relax_fine = 0.6
relax_coarse = 0.6
coarse_flux = 0.0625
coarse_bend = 0.125
coarse_det = 1.0 + 2.0 * coarse_flux * (split_slope + 2.0 * coarse_bend)

F32 = jnp.float32
BF16 = jnp.bfloat16
VMEM_LIMIT = 48 * 1024 * 1024


def iota(shape, dim):
    return lax.broadcasted_iota(jnp.int32, shape, dim)


def x_pair(field, low, high):
    return (
        jnp.concatenate([low, field[:-1]], axis=0),
        jnp.concatenate([field[1:], high], axis=0),
    )


def y_pair(field, low, high):
    size = field.shape[1]
    where = iota(field.shape, 1)
    return (
        jnp.where(where == 0, low, pltpu.roll(field, 1, 1)),
        jnp.where(where == size - 1, high, pltpu.roll(field, size - 1, 1)),
    )


def plane_pair(field):
    size = field.shape[2]
    where = iota(field.shape, 2)
    return (
        jnp.where(where == 0, 0.0, pltpu.roll(field, 1, 2)),
        jnp.where(where == size - 1, 0.0, pltpu.roll(field, size - 1, 2)),
    )


def neighbours(field, halo):
    xm, xp, ym, yp = halo
    return (*x_pair(field, xm, xp), *y_pair(field, ym, yp), *plane_pair(field))


def excess_of(conc, pot, conc_beside, pot_beside, faces, diagonal, mass_source, pot_source):
    excess_mass = (mass_source - conc) - diagonal * pot
    for face, other in zip(faces, pot_beside):
        excess_mass = excess_mass + face * other
    beside = conc_beside[0]
    for other in conc_beside[1:]:
        beside = beside + other
    excess_pot = (pot_source - pot) + (split_slope + 6.0 * interface) * conc - interface * beside
    return excess_mass, excess_pot


def scale_from(diagonal):
    return relax_fine / (1.0 + (split_slope + 6.0 * interface) * diagonal)


def relax_pair(conc, pot, excess_mass, excess_pot, diagonal, scale):
    new_conc = conc + (excess_mass - diagonal * excess_pot) * scale
    new_pot = pot + (excess_pot + (split_slope + 6.0 * interface) * excess_mass) * scale
    return new_conc, new_pot


def faces_of(mobility, beside):
    faces = tuple((0.5 * time_step) * (mobility + other) for other in beside)
    diagonal = faces[0]
    for face in faces[1:]:
        diagonal = diagonal + face
    return faces, diagonal


def three_terms(values, dim=0):
    out = []
    for _ in range(3):
        out.append(values.astype(BF16).astype(F32))
        values = values - out[-1]
    return jnp.concatenate(out, axis=dim)


def round_up(value, unit):
    return -(-value // unit) * unit


class Plan:
    def __init__(self, shape, owners, groups):
        self.x, self.y, self.p = shape
        self.owners, self.groups = owners, groups
        self.half_x, self.half_y = self.x // 2, self.y // 2
        self.columns = self.half_x * self.half_y
        self.map_row = round_up(8 * self.x, 8)
        self.y_rows = self.map_row + owners
        self.y_far_rows = max(self.y_rows, 3 * self.y + 8)
        self.cells = self.x * self.y
        self.rows = (self.half_x + 2) * self.y
        self.low_row = owners
        self.high_row = owners + self.half_x
        self.slot_parts = -(-(owners + 2 * self.half_x) // 4)
        slots = owners * groups
        self.slots = slots if slots <= 64 else 0

    def slot_of(self, g, h):
        last = self.groups - 1
        place = 0 if h == 0 else 1 if h == last else h + 1
        return place * self.owners + self.owners - 1 - (g ^ 1)


def side_rows(plan, rows, which):
    return rows[which * plan.y : (which + 1) * plan.y][None]


def side_columns(plan, rows, which):
    return rows[which * plan.x : (which + 1) * plan.x][:, None]


def membership(plan, owner_ref):
    g = lax.axis_index("gx")
    last = plan.owners - 1
    owner = iota((plan.owners, plan.columns), 0)
    low, high = plan.half_x, plan.half_x + 1
    shape = (plan.half_x + 2, plan.y, plan.columns)
    x, y, column = iota(shape, 0), iota(shape, 1), iota(shape, 2)
    half = jnp.where(x < low, x, jnp.where(x == low, plan.half_x - 1, 0))
    place = column == half * plan.half_y + (y >> 1)
    sides = (
        (x < low, g, True),
        (x == low, jnp.maximum(g - 1, 0), g > 0),
        (x == high, jnp.minimum(g + 1, last), g < last),
    )
    gather, spread = None, None
    for part, row, inside in sides:
        hits = ((owner_ref[pl.ds(row, 1), :] == owner) & inside).astype(F32).astype(BF16)
        where = (place & part).astype(F32).reshape(plan.rows, plan.columns).astype(BF16)
        nt = (((1,), (1,)), ((), ()))
        some = lax.dot_general(hits, where, nt, preferred_element_type=F32)
        gather = some if gather is None else gather + some
        some = lax.dot_general(where, hits, nt, preferred_element_type=F32)
        spread = some if spread is None else spread + some
    return gather, jnp.concatenate([spread] * 3, axis=1)


def scale_of(plan, owners):
    owner = iota((plan.owners, plan.columns), 0).astype(owners.dtype)
    hits = jnp.zeros((plan.owners, plan.columns), F32)
    for g in range(plan.owners):
        hits = hits + (owners[g : g + 1] == owner).astype(F32)
    count = jnp.sum(hits, axis=1, keepdims=True)
    return jnp.broadcast_to(0.125 / jnp.maximum(count, 1.0), (plan.owners, plan.p))


def mobility_of(mask, kind, table):
    values = jnp.zeros(kind.shape, F32)
    for marker, value in enumerate(table):
        values = jnp.where(kind == marker, value, values)
    return mask.astype(F32) * values


def even(axis):
    return lax.rem(lax.axis_index(axis), 2) == 0


def put_x(plan, lows, highs, near, far):
    up = even("gx")
    for which, (low, high) in enumerate(zip(lows, highs)):
        near[pl.ds(which * plan.y, plan.y), :] = jnp.where(up, high, low)
        far[pl.ds(which * plan.y, plan.y), :] = jnp.where(up, low, high)


def received(axis, near_ref, far_ref):
    up = even(axis)
    rows = pl.ds(0, min(near_ref.shape[0], far_ref.shape[0]))
    near, far = near_ref[rows, :], far_ref[rows, :]
    return jnp.where(up, far, near), jnp.where(up, near, far)


def prepare_kernel(plan, *refs):
    hbm, refs = refs[:8], refs[8:]
    x_near_ref, x_far_ref, y_near_ref, y_far_ref = refs[:4]
    x_refs, y_refs, (owner_ref, table_ref, sems) = refs[4:8], refs[8:14], refs[14:]
    copies = []

    def start(source, target):
        copies.append(pltpu.make_async_copy(source, target, sems.at[len(copies)]))
        copies[-1].start()

    start(hbm[7], table_ref)
    start(hbm[6], owner_ref)
    for source, target in zip(hbm[:4], x_refs):
        start(source.at[0], target.at[0])
        start(source.at[plan.x - 1], target.at[1])
    for source, target in zip(hbm[:6], y_refs):
        start(source.at[:, pl.ds(0, 8)], target.at[0])
        start(source.at[:, pl.ds(plan.y - 8, 8)], target.at[1])
    for copy in copies:
        copy.wait()
    table = [table_ref[marker] for marker in range(table_ref.shape[0])]
    conc, pot, mask, kind = (ref[...] for ref in x_refs)
    fields = (conc, pot, mobility_of(mask, kind, table))
    put_x(plan, [f[0] for f in fields], [f[1] for f in fields], x_near_ref, x_far_ref)
    conc, pot, mask, kind, mass, pots = (ref[...] for ref in y_refs)
    fields = (conc, pot, mobility_of(mask, kind, table))
    up = even("gy")
    rows = [(field, at) for at in range(2) for field in fields] + [(mass, 0), (pots, 0)]
    for which, (field, at) in enumerate(rows):
        for x in range(plan.x):
            low, high = field[0, x, at : at + 1], field[1, x, 7 - at : 8 - at]
            y_near_ref[pl.ds(which * plan.x + x, 1), :] = jnp.where(up, high, low)
            y_far_ref[pl.ds(which * plan.x + x, 1), :] = jnp.where(up, low, high)
    used = 8 * plan.x
    for ref, rows in ((y_near_ref, plan.y_rows), (y_far_ref, plan.y_far_rows)):
        ref[pl.ds(used, rows - used), :] = jnp.zeros((rows - used, plan.p), F32)
        ref[pl.ds(plan.map_row, plan.owners), pl.ds(0, plan.columns)] = owner_ref[...].astype(F32)


def inner_faces(mobility):
    half = 0.5 * time_step
    shape = mobility.shape
    y, plane = iota(shape, 1), iota(shape, 2)
    to_x = jnp.concatenate(
        [half * (mobility[:-1] + mobility[1:]), jnp.zeros_like(mobility[:1])], axis=0
    )
    out = [to_x]
    for dim, where, shift, edge in (
        (1, y, 1, 0), (1, y, shape[1] - 1, shape[1] - 1),
        (2, plane, 1, 0), (2, plane, shape[2] - 1, shape[2] - 1),
    ):
        face = half * (mobility + pltpu.roll(mobility, shift, dim))
        out.append(jnp.where(where == edge, 0.0, face))
    return out


def inner_flux(faces, field):
    to_x, y_low, y_high, plane_low, plane_high = faces
    size_y, size_p = field.shape[1:]
    from_x = to_x[:-1]
    blank = jnp.zeros_like(field[:1])
    flux = jnp.concatenate([from_x * field[1:], blank], axis=0)
    flux = flux + jnp.concatenate([blank, from_x * field[:-1]], axis=0)
    flux = flux + y_low * pltpu.roll(field, 1, 1) + y_high * pltpu.roll(field, size_y - 1, 1)
    return flux + plane_low * pltpu.roll(field, 1, 2) + plane_high * pltpu.roll(field, size_p - 1, 2)


def inner_excess(conc, pot, faces, diagonal, mass_source, pot_source):
    excess_mass = (mass_source - conc) - diagonal * pot + inner_flux(faces, pot)
    nothing = [jnp.zeros_like(conc[:1])] * 2 + [jnp.zeros_like(conc[:, :1])] * 2
    beside = None
    for other in neighbours(conc, nothing):
        beside = other if beside is None else beside + other
    excess_pot = (pot_source - pot) + (split_slope + 6.0 * interface) * conc - interface * beside
    return excess_mass, excess_pot


def add_edges(field, x_low, x_high, y_low, y_high):
    field = jnp.concatenate(
        [(field[0] + x_low)[None], field[1:-1], (field[-1] + x_high)[None]], axis=0
    )
    row = iota((field.shape[0], 8, field.shape[2]), 1)
    size = field.shape[1]
    low = field[:, :8] + jnp.where(row == 0, y_low, 0.0)
    high = field[:, size - 8 :] + jnp.where(row == 7, y_high, 0.0)
    return jnp.concatenate([low, field[:, 8 : size - 8], high], axis=1)


def local_kernel(
    plan, conc_ref, pot_ref, mask_ref, class_ref, mass_ref, pots_ref, table_ref, owner_ref,
    mob_ref, gather_ref, spread_ref, faces_ref, diagonal_ref, mass_out, pots_out,
):
    table = [table_ref[marker] for marker in range(table_ref.shape[0])]
    mobility = mobility_of(mask_ref[...], class_ref[...], table)
    mob_ref[...] = mobility
    gather_ref[...], spread_ref[...] = membership(plan, owner_ref)
    faces = inner_faces(mobility)
    diagonal = faces[0] + jnp.concatenate([jnp.zeros_like(mobility[:1]), faces[0][:-1]], axis=0)
    for face in faces[1:]:
        diagonal = diagonal + face
    plane = iota(mobility.shape, 2)
    ends = (plane == 0) | (plane == plan.p - 1)
    diagonal = diagonal + jnp.where(ends, (0.5 * time_step) * mobility, 0.0)
    for i, face in enumerate(faces):
        faces_ref[i] = face
    diagonal_ref[...] = diagonal
    mass_out[...], pots_out[...] = inner_excess(
        conc_ref[...], pot_ref[...], faces, diagonal, mass_ref[...], pots_ref[...]
    )


def first_kernel(
    plan, x_far_ref, x_near_ref, y_far_ref, y_near_ref,
    conc_ref, pot_ref, mob_ref, mass_ref, pots_ref, gather_ref, owner_ref,
    faces_ref, diagonal_ref, mass_part_ref, pot_part_ref,
    conc_out, pot_out, total_hbm, raw_out, x_near_out, x_far_out, total_out, sems,
):
    sides = received("gx", x_near_ref, x_far_ref)
    ends = received("gy", y_near_ref, y_far_ref)
    last_x, last_y = plan.x - 1, plan.y - 1

    def halo(which):
        return tuple(side_rows(plan, rows, which)[0] for rows in sides) + tuple(
            side_columns(plan, rows, which) for rows in ends
        )

    def edges(field):
        return field[0], field[last_x], field[:, :1], field[:, last_y:]

    mobility = mob_ref[...]
    raw_conc, raw_pot = conc_ref[...], pot_ref[...]
    outer = [
        (0.5 * time_step) * (own + other) for own, other in zip(edges(mobility), halo(2))
    ]
    diagonal = add_edges(diagonal_ref[...], *outer)
    excess_mass = add_edges(
        mass_part_ref[...],
        *(f * (other - own) for f, own, other in zip(outer, edges(raw_pot), halo(1))),
    )
    excess_pot = add_edges(pot_part_ref[...], *(-interface * other for other in halo(0)))
    conc, pot = relax_pair(
        raw_conc, raw_pot, excess_mass, excess_pot, diagonal, scale_from(diagonal)
    )

    own_mass, own_pot = inner_excess(
        conc, pot, [faces_ref[i] for i in range(5)], diagonal, mass_ref[...], pots_ref[...]
    )
    give_mass, give_pot = (
        [field[x] + field[x + 1] for x in range(0, plan.x, 2)] for field in (own_mass, own_pot)
    )
    for x, side in ((0, 0), (last_x, 1)):
        give_mass.append(outer[side] * pot[x])
        give_pot.append(-interface * conc[x])

    def packed(mass, other):
        first = iota(mass.shape, 1) & 1 == 0
        return jnp.where(
            first, mass + pltpu.roll(mass, plan.p - 1, 1), other + pltpu.roll(other, 1, 1)
        )

    give = packed(jnp.concatenate(give_mass, axis=0), jnp.concatenate(give_pot, axis=0))
    h = lax.axis_index("gy")
    inside = (h > 0, None, h < plan.groups - 1)
    maps = [rows[plan.map_row : plan.map_row + plan.owners, : plan.columns] for rows in ends]
    maps.insert(1, owner_ref[...].astype(F32))
    owner = iota((plan.owners, 1), 0)
    is_mine = owner == lax.axis_index("gx")

    own = lax.dot_general(
        gather_ref[...].astype(BF16),
        three_terms(give, 1).astype(BF16),
        (((1,), (0,)), ((), ())),
        preferred_element_type=F32,
    )
    own = own[:, : plan.p] + own[:, plan.p : 2 * plan.p] + own[:, 2 * plan.p :]
    sums = [None, own, None]
    for place, y, at, side in ((0, 0, plan.half_y - 1, 2), (2, plan.y - 1, 0, 3)):
        edge_pot, edge_conc = (
            jnp.concatenate([field[x, y : y + 1] for x in range(plan.x)], axis=0)
            for field in (pot, conc)
        )
        both = packed(outer[side][:, 0] * edge_pot, -interface * edge_conc)
        part = jnp.zeros((plan.owners, plan.p), F32)
        for i in range(plan.half_x):
            column = owner_column(plan, maps[place], i, at)
            ident = jnp.sum(jnp.where(is_mine, column, 0.0), axis=0, keepdims=True)
            pair = both[2 * i : 2 * i + 1] + both[2 * i + 1 : 2 * i + 2]
            part = part + jnp.where((owner.astype(F32) == ident) & inside[place], pair, 0.0)
        sums[place] = part
    def store_fields():
        conc_out[...] = conc
        pot_out[...] = pot
        for at, field in enumerate((raw_conc, raw_pot)):
            for x in range(plan.x):
                raw_out[pl.ds(2 * at * plan.x + x, 1), :] = field[x, 0:1]
                raw_out[pl.ds((2 * at + 1) * plan.x + x, 1), :] = field[x, last_y : last_y + 1]
        put_x(plan, (conc[0], pot[0]), (conc[last_x], pot[last_x]), x_near_out, x_far_out)
        up = even("gx")
        base = 2 * plan.y
        for which in range(3):
            for end, rows in enumerate(ends):
                low = rows[which * plan.x : which * plan.x + 1]
                high = rows[(which + 1) * plan.x - 1 : (which + 1) * plan.x]
                x_near_out[pl.ds(base + 2 * which + end, 1), :] = jnp.where(up, high, low)
                x_far_out[pl.ds(base + 2 * which + end, 1), :] = jnp.where(up, low, high)
        for ref in (x_near_out, x_far_out):
            ref[pl.ds(base + 6, 2), :] = jnp.zeros((2, plan.p), F32)

    if not plan.slots:
        total_out[...] = jnp.concatenate(sums, axis=0)
        copies = [pltpu.make_async_copy(total_out, total_hbm, sems.at[0])]
        copies[0].start()
        store_fields()
        copies[0].wait()
        return

    def picked(place, i, at):
        column = owner_column(plan, maps[place], i, at)
        ident = jnp.broadcast_to(column, (plan.owners, plan.p))
        out = jnp.zeros((plan.owners, plan.p), F32)
        for o in range(plan.owners):
            out = jnp.where(ident == float(o), sums[place][o : o + 1], out)
        return out

    below = [[picked(k, i, plan.half_y - 1) for i in range(plan.half_x)] for k in range(3)]
    above = [[picked(k, i, 0) for i in range(plan.half_x)] for k in range(3)]

    def of_plane(plane, choices):
        out = jnp.zeros((plan.owners, plan.p), F32)
        for k in range(3):
            out = jnp.where(plane == h + (k - 1), choices[k], out)
        return out

    size = 4 * plan.slot_parts
    rows = []
    for plane in range(plan.groups):
        beside = []
        for i in range(plan.half_x):
            beside.append((plan.low_row + i, of_plane(plane - 1, [k[i] for k in below])))
            beside.append((plan.high_row + i, of_plane(plane + 1, [k[i] for k in above])))
        blank = jnp.zeros((plan.owners, plan.p), F32)
        beside += [(at, blank) for at in range(plan.high_row + plan.half_x, size)]
        rows.append((of_plane(plane, sums), beside))
    copies = []
    for plane, (main, beside) in enumerate(rows):
        for g in range(plan.owners):
            slot = plan.slot_of(g, plane)
            for part in range(plan.owners // 4):
                total_out[slot, part] = main[4 * part : 4 * part + 4]
            for row, values in beside:
                total_out[slot, row // 4, pl.ds(row % 4, 1), :] = values[g : g + 1]
        some = pl.ds(plan.slot_of(plan.owners - 2, plane), plan.owners)
        copies.append(
            pltpu.make_async_copy(total_out.at[some], total_hbm.at[some], sems.at[plane])
        )
        copies[-1].start()
    store_fields()
    for copy in copies:
        copy.wait()


def owner_column(plan, owners, i, at):
    b = i * plan.half_y + at
    return owners[:, b : b + 1]


def coarse_solve(packed, planes):
    lane = iota(packed.shape, 1)
    even = lane & 1 == 0
    mass_mean = jnp.where(even, packed, pltpu.roll(packed, 1, 1))
    pot_mean = jnp.where(even, pltpu.roll(packed, planes - 1, 1), packed)

    def neighbour_sum(values):
        return jnp.where(lane >= 2, pltpu.roll(values, 2, 1), 0.0) + jnp.where(
            lane < planes - 2, pltpu.roll(values, planes - 2, 1), 0.0
        )

    def step(mass_gap, pot_gap):
        scale = relax_coarse / coarse_det
        return (
            scale * (mass_gap - 2.0 * coarse_flux * pot_gap),
            scale * (pot_gap + (split_slope + 2.0 * coarse_bend) * mass_gap),
        )

    coarse_conc, coarse_pot = step(mass_mean, pot_mean)
    for _ in range(CSWEEP - 1):
        mass_gap = mass_mean - (
            coarse_conc + coarse_flux * (2.0 * coarse_pot - neighbour_sum(coarse_pot))
        )
        pot_gap = pot_mean - (
            coarse_pot
            - split_slope * coarse_conc
            + coarse_bend * (neighbour_sum(coarse_conc) - 2.0 * coarse_conc)
        )
        more_conc, more_pot = step(mass_gap, pot_gap)
        coarse_conc, coarse_pot = coarse_conc + more_conc, coarse_pot + more_pot
    return coarse_conc, coarse_pot


def weights(plan, own_map, ends):
    owner = iota((plan.owners, 1), 0)
    is_mine = owner == lax.axis_index("gx")
    rows = [scale_of(plan, own_map)]
    for end, at in zip(ends, (plan.half_y - 1, 0)):
        owners = end[plan.map_row : plan.map_row + plan.owners, : plan.columns]
        scale = scale_of(plan, owners)
        for i in range(plan.half_x):
            column = owner_column(plan, owners, i, at)
            ident = jnp.sum(jnp.where(is_mine, column, 0.0), axis=0, keepdims=True)
            mine = jnp.where(owner.astype(F32) == ident, scale, 0.0)
            rows.append(jnp.sum(mine, axis=0, keepdims=True))
    blank = 4 * plan.slot_parts - plan.high_row - plan.half_x
    if blank:
        rows.append(jnp.zeros((blank, plan.p), F32))
    return jnp.concatenate(rows, axis=0)


def beside_kernel(
    plan, x_near_ref, x_far_ref, conc_ref, pot_ref, mass_ref, pots_ref, mob_ref, raw_ref,
    x_near_msg, x_far_msg, y_near_msg, y_far_msg, owner_ref,
    faces_out, diagonal_out, scale_out, mass_out, pots_out, weight_out,
):
    mobility = mob_ref[...]
    sides = received("gx", x_near_msg, x_far_msg)
    ends = received("gy", y_near_msg, y_far_msg)
    halo = tuple(side_rows(plan, rows, 2) for rows in sides) + tuple(
        side_columns(plan, rows, 2) for rows in ends
    )
    faces, diagonal = faces_of(mobility, neighbours(mobility, halo))
    weight_out[...] = weights(plan, owner_ref[...].astype(F32), ends)
    block_terms = faces, diagonal, mass_ref[...], pots_ref[...]
    for i, face in enumerate(faces):
        faces_out[i] = face
    diagonal_out[...] = diagonal
    scale_out[...] = scale_from(diagonal)

    corners = received("gx", x_near_ref, x_far_ref)
    h = lax.axis_index("gy")
    inside = (h > 0, h < plan.groups - 1)
    own_mob = [
        jnp.concatenate([mobility[x, y : y + 1] for x in range(plan.x)], axis=0)
        for y in (0, plan.y - 1)
    ]
    halos = [[side_rows(plan, rows, which) for rows in corners] for which in range(2)]
    for end, rows in enumerate(ends):

        def row(which):
            return rows[which * plan.x : (which + 1) * plan.x]

        def beside(which, own):
            here = row(which)
            at = 2 * plan.y + 2 * which + end
            wide = jnp.concatenate([corners[0][at : at + 1], here, corners[1][at : at + 1]], axis=0)
            return (
                wide[: plan.x], wide[2:], own, row(which + 3),
                *(part[0] for part in plane_pair(here[None])),
            )

        raw = [
            raw_ref[pl.ds((2 * which + end) * plan.x, plan.x), :] for which in range(2)
        ]
        faces, diagonal = faces_of(row(2), beside(2, own_mob[end]))
        excess = excess_of(
            row(0), row(1), beside(0, raw[0]), beside(1, raw[1]), faces, diagonal, row(6), row(7)
        )
        new = relax_pair(row(0), row(1), *excess, diagonal, scale_from(diagonal))
        for which, values in enumerate(new):
            halos[which].append(jnp.where(inside[end], values, 0.0)[:, None])
    conc, pot = conc_ref[...], pot_ref[...]
    mass_out[...], pots_out[...] = excess_of(
        conc, pot, neighbours(conc, halos[0]), neighbours(pot, halos[1]), *block_terms
    )


def last_kernel(
    plan, conc_ref, pot_ref, mass_ref, pots_ref, faces_ref, diagonal_ref, scale_ref,
    spread_ref, weight_ref, total_ref,
    conc_hbm, pot_hbm, conc_out, pot_out, sems,
):
    parts = []
    for part in range(plan.slot_parts):
        terms = [total_ref[slot, part] for slot in range(total_ref.shape[0])]
        while len(terms) > 1:
            pairs = [a + b for a, b in zip(terms[::2], terms[1::2])]
            terms = pairs + terms[len(pairs) * 2 :]
        parts.append(terms[0])
    means = jnp.concatenate(parts, axis=0) * weight_ref[...]
    solved = jnp.concatenate(coarse_solve(means, plan.p), axis=1)
    own = lax.dot_general(
        spread_ref[...].astype(BF16),
        three_terms(solved[: plan.owners]).astype(BF16),
        (((1,), (0,)), ((), ())),
        preferred_element_type=F32,
    )

    def shifted(which):
        lanes = slice(which * plan.p, (which + 1) * plan.p)
        rows = [own[i * plan.y : (i + 1) * plan.y, lanes][None] for i in range(plan.half_x + 2)]
        beside = []
        for i in range(plan.half_x):
            ends = [
                solved[begin + i : begin + i + 1, lanes][None]
                for begin in (plan.low_row, plan.high_row)
            ]
            beside.append((*y_pair(rows[i], *ends), *plane_pair(rows[i])))
        return [rows[plan.half_x], *rows[: plan.half_x], rows[plan.half_x + 1]], beside

    conc_rows, conc_beside = shifted(0)
    pot_rows, pot_beside = shifted(1)
    conc_sums = [a + b + c + d for a, b, c, d in conc_beside]
    copies = []
    for x in range(plan.x):
        one = pl.ds(x, 1)
        i = x >> 1
        low, high = (i, i + 1) if x % 2 == 0 else (i + 1, i + 2)
        diagonal = diagonal_ref[one]
        conc, pot = conc_rows[i + 1], pot_rows[i + 1]
        excess_mass = mass_ref[one] - conc - diagonal * pot
        beside = (pot_rows[low], pot_rows[high], *pot_beside[i])
        for k, other in enumerate(beside):
            excess_mass = excess_mass + faces_ref[k, one] * other
        excess_pot = (pots_ref[one] - pot) + (split_slope + 6.0 * interface) * conc
        excess_pot = excess_pot - interface * (conc_rows[low] + conc_rows[high] + conc_sums[i])
        conc_out[one], pot_out[one] = relax_pair(
            conc_ref[one] + conc, pot_ref[one] + pot, excess_mass, excess_pot, diagonal, scale_ref[one]
        )
        for source, target in ((conc_out, conc_hbm), (pot_out, pot_hbm)):
            copies.append(
                pltpu.make_async_copy(source.at[one], target.at[one], sems.at[len(copies)])
            )
            copies[-1].start()
    for copy in copies:
        copy.wait()


def call(kernel, plan, outs, args, far=(), smem=(), scratch=(), out_far=()):
    def space(i):
        return pl.ANY if i in far else pltpu.SMEM if i in smem else pltpu.VMEM

    return pl.pallas_call(
        functools.partial(kernel, plan),
        out_shape=[jax.ShapeDtypeStruct(shape, F32) for shape in outs],
        in_specs=[pl.BlockSpec(memory_space=space(i)) for i in range(len(args))],
        out_specs=[
            pl.BlockSpec(memory_space=pl.ANY if i in out_far else pltpu.VMEM)
            for i in range(len(outs))
        ],
        scratch_shapes=list(scratch),
        compiler_params=pltpu.CompilerParams(vmem_limit_bytes=VMEM_LIMIT),
    )(*[
        pltpu.with_memory_space_constraint(arg, pltpu.HBM) if i in far else arg
        for i, arg in enumerate(args)
    ])


def swap_near(axis, rows, begin=0):
    pairs = [(i, i + 1) for i in range(begin, lax.axis_size(axis) - 1, 2)]
    return lax.ppermute(rows, axis, pairs + [(j, i) for i, j in pairs])


def swap_far(axis, rows):
    return swap_near(axis, rows, 1)


def gather_totals(plan, total, y_near, y_far):
    if plan.slots:
        order = [0] * plan.slots
        for g in range(plan.owners):
            for h in range(plan.groups):
                order[plan.slot_of(g, h)] = g * plan.groups + h
        return lax.all_to_all(
            total, ("gx", "gy"), split_axis=0, concat_axis=0, axis_index_groups=[order], tiled=True
        )
    shape = (plan.groups, 3, plan.owners, plan.p)
    parts = lax.all_gather(lax.psum(total, "gx"), "gy").reshape(shape)
    blank = jnp.zeros((1, plan.owners, plan.p), F32)
    to_below, own, to_above = (parts[:, k] for k in range(3))
    own = own + jnp.concatenate([blank, to_above[:-1]]) + jnp.concatenate([to_below[1:], blank])
    own = jnp.concatenate([blank, own, blank])
    g, h = lax.axis_index("gx"), lax.axis_index("gy")
    rows = [lax.dynamic_index_in_dim(own, h + 1, 0, False)]
    up = lax.rem(h, 2) == 0
    far = y_far[: y_near.shape[0]]
    for place, at, msg in (
        (h, plan.half_y - 1, jnp.where(up, far, y_near)),
        (h + 2, 0, jnp.where(up, y_near, far)),
    ):
        ident = lax.dynamic_index_in_dim(msg, plan.map_row + g, 0, False).astype(jnp.int32)
        ident = jnp.stack([ident[i * plan.half_y + at] for i in range(plan.half_x)])
        rows.append(lax.dynamic_index_in_dim(own, place, 0, False)[ident])
    rows = jnp.concatenate(rows)
    rows = jnp.pad(rows, ((0, 4 * plan.slot_parts - rows.shape[0]), (0, 0)))
    return rows.reshape(1, plan.slot_parts, 4, plan.p)


def on_device(conc, pot, mass_source, pot_source, mask, kind, table, owner_map):
    plan = Plan(conc.shape, lax.axis_size("gx"), lax.axis_size("gy"))
    block = conc.shape
    fields = [conc, pot, mask, kind, mass_source, pot_source]
    messages = call(
        prepare_kernel,
        plan,
        [*[(3 * plan.y, plan.p)] * 2, (plan.y_rows, plan.p), (plan.y_far_rows, plan.p)],
        [*fields, owner_map, table],
        far=range(8),
        scratch=(
            *[pltpu.VMEM((2, plan.y, plan.p), field.dtype) for field in fields[:4]],
            *[pltpu.VMEM((2, plan.x, 8, plan.p), field.dtype) for field in fields],
            pltpu.VMEM(owner_map.shape, owner_map.dtype),
            pltpu.SMEM(table.shape, table.dtype),
            pltpu.SemaphoreType.DMA((22,)),
        ),
    )
    x_near, x_far = swap_near("gx", messages[0]), swap_far("gx", messages[1])
    y_near, y_far = swap_near("gy", messages[2]), swap_far("gy", messages[3])
    y_far, mask, kind = lax.optimization_barrier((y_far, mask, kind))
    mob, gather, spread, *parts = call(
        local_kernel,
        plan,
        [
            block, (plan.owners, plan.rows), (plan.rows, 3 * plan.owners),
            (5, *block), block, block, block,
        ],
        [conc, pot, mask, kind, mass_source, pot_source, table, owner_map],
        smem=(6,),
    )
    slots = (plan.slots, plan.slot_parts, 4, plan.p) if plan.slots else (3 * plan.owners, plan.p)
    conc, pot, total, raw, near, far = call(
        first_kernel,
        plan,
        [
            block,
            block,
            slots,
            (4 * plan.x, plan.p),
            *[(2 * plan.y + 8, plan.p)] * 2,
        ],
        [
            x_far, x_near, y_far, y_near,
            conc, pot, mob, mass_source, pot_source, gather, owner_map, *parts,
        ],
        out_far=(2,),
        scratch=(pltpu.VMEM(slots, F32), pltpu.SemaphoreType.DMA((plan.groups,))),
    )
    total = gather_totals(plan, total, y_near, y_far)
    far = swap_far("gx", far)
    near = swap_near("gx", near)
    faces, diagonal, scale, mass_part, pot_part, weight = call(
        beside_kernel,
        plan,
        [(6, *block), block, block, block, block, (4 * plan.slot_parts, plan.p)],
        [
            near, far, conc, pot, mass_source, pot_source, mob, raw,
            x_near, x_far, y_near, y_far, owner_map,
        ],
    )
    return tuple(
        call(
            last_kernel,
            plan,
            [block, block],
            [conc, pot, mass_part, pot_part, faces, diagonal, scale, spread, weight, total],
            out_far=(0, 1),
            scratch=(
                pltpu.VMEM(block, F32),
                pltpu.VMEM(block, F32),
                pltpu.SemaphoreType.DMA((2 * plan.x,)),
            ),
        )
    )


def solution(mesh):
    grid = P("gx", "gy", None)
    return jax.shard_map(
        on_device,
        mesh=mesh,
        in_specs=(grid,) * 6 + (P(), P(None, "gy")),
        out_specs=(grid, grid),
        check_vma=False,
    )
```

```python
import functools

import jax
import jax.numpy as jnp
from jax import lax
from jax.experimental import pallas as pl
from jax.experimental.pallas import tpu as pltpu
from jax.sharding import PartitionSpec as P

CSWEEP = 3

time_step = 0.25
split_slope = 1.0
interface = 0.5
relax_fine = 0.6
relax_coarse = 0.6
coarse_flux = 0.0625
coarse_bend = 0.125
coarse_det = 1.0 + 2.0 * coarse_flux * (split_slope + 2.0 * coarse_bend)

F32 = jnp.float32
BF16 = jnp.bfloat16
VMEM_LIMIT = 48 * 1024 * 1024


def iota(shape, dim):
    return lax.broadcasted_iota(jnp.int32, shape, dim)


def x_pair(field, low, high):
    return (
        jnp.concatenate([low, field[:-1]], axis=0),
        jnp.concatenate([field[1:], high], axis=0),
    )


def y_pair(field, low, high):
    size = field.shape[1]
    where = iota(field.shape, 1)
    return (
        jnp.where(where == 0, low, pltpu.roll(field, 1, 1)),
        jnp.where(where == size - 1, high, pltpu.roll(field, size - 1, 1)),
    )


def plane_pair(field):
    size = field.shape[2]
    where = iota(field.shape, 2)
    return (
        jnp.where(where == 0, 0.0, pltpu.roll(field, 1, 2)),
        jnp.where(where == size - 1, 0.0, pltpu.roll(field, size - 1, 2)),
    )


def neighbours(field, halo):
    xm, xp, ym, yp = halo
    return (*x_pair(field, xm, xp), *y_pair(field, ym, yp), *plane_pair(field))


def excess_of(conc, pot, conc_beside, pot_beside, faces, diagonal, mass_source, pot_source):
    excess_mass = (mass_source - conc) - diagonal * pot
    for face, other in zip(faces, pot_beside):
        excess_mass = excess_mass + face * other
    beside = conc_beside[0]
    for other in conc_beside[1:]:
        beside = beside + other
    excess_pot = (pot_source - pot) + (split_slope + 6.0 * interface) * conc - interface * beside
    return excess_mass, excess_pot


def scale_from(diagonal):
    return relax_fine / (1.0 + (split_slope + 6.0 * interface) * diagonal)


def relax_pair(conc, pot, excess_mass, excess_pot, diagonal, scale):
    new_conc = conc + (excess_mass - diagonal * excess_pot) * scale
    new_pot = pot + (excess_pot + (split_slope + 6.0 * interface) * excess_mass) * scale
    return new_conc, new_pot


def faces_of(mobility, beside):
    faces = tuple((0.5 * time_step) * (mobility + other) for other in beside)
    diagonal = faces[0]
    for face in faces[1:]:
        diagonal = diagonal + face
    return faces, diagonal


def three_terms(values, dim=0):
    out = []
    for _ in range(3):
        out.append(values.astype(BF16).astype(F32))
        values = values - out[-1]
    return jnp.concatenate(out, axis=dim)


def round_up(value, unit):
    return -(-value // unit) * unit


class Plan:
    def __init__(self, shape, owners, groups):
        self.x, self.y, self.p = shape
        self.owners, self.groups = owners, groups
        self.half_x, self.half_y = self.x // 2, self.y // 2
        self.columns = self.half_x * self.half_y
        self.map_row = round_up(8 * self.x, 8)
        self.y_rows = self.map_row + owners
        self.y_far_rows = max(self.y_rows, 3 * self.y + 8)
        self.cells = self.x * self.y
        self.rows = (self.half_x + 2) * self.y
        self.low_row = owners
        self.high_row = owners + self.half_x
        self.slot_parts = -(-(owners + 2 * self.half_x) // 4)
        slots = owners * groups
        self.slots = slots if slots <= 64 else 0

    def slot_of(self, g, h):
        last = self.groups - 1
        place = 0 if h == 0 else 1 if h == last else h + 1
        low = self.owners - 1 if g == 0 else 0 if g == 1 else self.owners - g
        return place * self.owners + low


def side_rows(plan, rows, which):
    return rows[which * plan.y : (which + 1) * plan.y][None]


def side_columns(plan, rows, which):
    return rows[which * plan.x : (which + 1) * plan.x][:, None]


def membership(plan, owner_ref):
    g = lax.axis_index("gx")
    last = plan.owners - 1
    owner = iota((plan.owners, plan.columns), 0)
    low, high = plan.half_x, plan.half_x + 1
    shape = (plan.half_x + 2, plan.y, plan.columns)
    x, y, column = iota(shape, 0), iota(shape, 1), iota(shape, 2)
    half = jnp.where(x < low, x, jnp.where(x == low, plan.half_x - 1, 0))
    place = column == half * plan.half_y + (y >> 1)
    sides = (
        (x < low, g, True),
        (x == low, jnp.maximum(g - 1, 0), g > 0),
        (x == high, jnp.minimum(g + 1, last), g < last),
    )
    gather, spread = None, None
    for part, row, inside in sides:
        hits = ((owner_ref[pl.ds(row, 1), :] == owner) & inside).astype(F32).astype(BF16)
        where = (place & part).astype(F32).reshape(plan.rows, plan.columns).astype(BF16)
        nt = (((1,), (1,)), ((), ()))
        some = lax.dot_general(hits, where, nt, preferred_element_type=F32)
        gather = some if gather is None else gather + some
        some = lax.dot_general(where, hits, nt, preferred_element_type=F32)
        spread = some if spread is None else spread + some
    return gather, jnp.concatenate([spread] * 3, axis=1)


def scale_of(plan, owners):
    owner = iota((plan.owners, plan.columns), 0).astype(owners.dtype)
    hits = jnp.zeros((plan.owners, plan.columns), F32)
    for g in range(plan.owners):
        hits = hits + (owners[g : g + 1] == owner).astype(F32)
    count = jnp.sum(hits, axis=1, keepdims=True)
    return jnp.broadcast_to(0.125 / jnp.maximum(count, 1.0), (plan.owners, plan.p))


def mobility_of(mask, kind, table):
    values = jnp.zeros(kind.shape, F32)
    for marker, value in enumerate(table):
        values = jnp.where(kind == marker, value, values)
    return mask.astype(F32) * values


def even(axis):
    return lax.rem(lax.axis_index(axis), 2) == 0


def put_x(plan, lows, highs, near, far):
    up = even("gx")
    for which, (low, high) in enumerate(zip(lows, highs)):
        near[pl.ds(which * plan.y, plan.y), :] = jnp.where(up, high, low)
        far[pl.ds(which * plan.y, plan.y), :] = jnp.where(up, low, high)


def received(axis, near_ref, far_ref):
    up = even(axis)
    rows = pl.ds(0, min(near_ref.shape[0], far_ref.shape[0]))
    near, far = near_ref[rows, :], far_ref[rows, :]
    return jnp.where(up, far, near), jnp.where(up, near, far)


def prepare_kernel(plan, *refs):
    hbm, refs = refs[:8], refs[8:]
    x_near_ref, x_far_ref, y_near_ref, y_far_ref = refs[:4]
    x_refs, y_refs, (owner_ref, table_ref, sems) = refs[4:8], refs[8:14], refs[14:]
    copies = []

    def start(source, target):
        copies.append(pltpu.make_async_copy(source, target, sems.at[len(copies)]))
        copies[-1].start()

    start(hbm[7], table_ref)
    start(hbm[6], owner_ref)
    for source, target in zip(hbm[:4], x_refs):
        start(source.at[0], target.at[0])
        start(source.at[plan.x - 1], target.at[1])
    for source, target in zip(hbm[:6], y_refs):
        start(source.at[:, pl.ds(0, 8)], target.at[0])
        start(source.at[:, pl.ds(plan.y - 8, 8)], target.at[1])
    for copy in copies:
        copy.wait()
    table = [table_ref[marker] for marker in range(table_ref.shape[0])]
    conc, pot, mask, kind = (ref[...] for ref in x_refs)
    fields = (conc, pot, mobility_of(mask, kind, table))
    put_x(plan, [f[0] for f in fields], [f[1] for f in fields], x_near_ref, x_far_ref)
    conc, pot, mask, kind, mass, pots = (ref[...] for ref in y_refs)
    fields = (conc, pot, mobility_of(mask, kind, table))
    up = even("gy")
    rows = [(field, at) for at in range(2) for field in fields] + [(mass, 0), (pots, 0)]
    for which, (field, at) in enumerate(rows):
        for x in range(plan.x):
            low, high = field[0, x, at : at + 1], field[1, x, 7 - at : 8 - at]
            y_near_ref[pl.ds(which * plan.x + x, 1), :] = jnp.where(up, high, low)
            y_far_ref[pl.ds(which * plan.x + x, 1), :] = jnp.where(up, low, high)
    used = 8 * plan.x
    for ref, rows in ((y_near_ref, plan.y_rows), (y_far_ref, plan.y_far_rows)):
        ref[pl.ds(used, rows - used), :] = jnp.zeros((rows - used, plan.p), F32)
        ref[pl.ds(plan.map_row, plan.owners), pl.ds(0, plan.columns)] = owner_ref[...].astype(F32)


def inner_faces(mobility):
    half = 0.5 * time_step
    shape = mobility.shape
    y, plane = iota(shape, 1), iota(shape, 2)
    to_x = jnp.concatenate(
        [half * (mobility[:-1] + mobility[1:]), jnp.zeros_like(mobility[:1])], axis=0
    )
    out = [to_x]
    for dim, where, shift, edge in (
        (1, y, 1, 0), (1, y, shape[1] - 1, shape[1] - 1),
        (2, plane, 1, 0), (2, plane, shape[2] - 1, shape[2] - 1),
    ):
        face = half * (mobility + pltpu.roll(mobility, shift, dim))
        out.append(jnp.where(where == edge, 0.0, face))
    return out


def inner_flux(faces, field):
    to_x, y_low, y_high, plane_low, plane_high = faces
    size_y, size_p = field.shape[1:]
    from_x = to_x[:-1]
    blank = jnp.zeros_like(field[:1])
    flux = jnp.concatenate([from_x * field[1:], blank], axis=0)
    flux = flux + jnp.concatenate([blank, from_x * field[:-1]], axis=0)
    flux = flux + y_low * pltpu.roll(field, 1, 1) + y_high * pltpu.roll(field, size_y - 1, 1)
    return flux + plane_low * pltpu.roll(field, 1, 2) + plane_high * pltpu.roll(field, size_p - 1, 2)


def inner_excess(conc, pot, faces, diagonal, mass_source, pot_source):
    excess_mass = (mass_source - conc) - diagonal * pot + inner_flux(faces, pot)
    nothing = [jnp.zeros_like(conc[:1])] * 2 + [jnp.zeros_like(conc[:, :1])] * 2
    beside = None
    for other in neighbours(conc, nothing):
        beside = other if beside is None else beside + other
    excess_pot = (pot_source - pot) + (split_slope + 6.0 * interface) * conc - interface * beside
    return excess_mass, excess_pot


def add_edges(field, x_low, x_high, y_low, y_high):
    field = jnp.concatenate(
        [(field[0] + x_low)[None], field[1:-1], (field[-1] + x_high)[None]], axis=0
    )
    row = iota((field.shape[0], 8, field.shape[2]), 1)
    size = field.shape[1]
    low = field[:, :8] + jnp.where(row == 0, y_low, 0.0)
    high = field[:, size - 8 :] + jnp.where(row == 7, y_high, 0.0)
    return jnp.concatenate([low, field[:, 8 : size - 8], high], axis=1)


def local_kernel(
    plan, conc_ref, pot_ref, mask_ref, class_ref, mass_ref, pots_ref, table_ref, owner_ref,
    mob_ref, gather_ref, spread_ref, scale_ref, faces_ref, diagonal_ref, mass_out, pots_out,
):
    table = [table_ref[marker] for marker in range(table_ref.shape[0])]
    mobility = mobility_of(mask_ref[...], class_ref[...], table)
    mob_ref[...] = mobility
    gather_ref[...], spread_ref[...] = membership(plan, owner_ref)
    scale_ref[...] = scale_of(plan, owner_ref[...])
    faces = inner_faces(mobility)
    diagonal = faces[0] + jnp.concatenate([jnp.zeros_like(mobility[:1]), faces[0][:-1]], axis=0)
    for face in faces[1:]:
        diagonal = diagonal + face
    plane = iota(mobility.shape, 2)
    ends = (plane == 0) | (plane == plan.p - 1)
    diagonal = diagonal + jnp.where(ends, (0.5 * time_step) * mobility, 0.0)
    for i, face in enumerate(faces):
        faces_ref[i] = face
    diagonal_ref[...] = diagonal
    mass_out[...], pots_out[...] = inner_excess(
        conc_ref[...], pot_ref[...], faces, diagonal, mass_ref[...], pots_ref[...]
    )


def first_kernel(
    plan, x_far_ref, x_near_ref, y_far_ref, y_near_ref,
    conc_ref, pot_ref, mob_ref, mass_ref, pots_ref, gather_ref, scale_ref, owner_ref,
    faces_ref, diagonal_ref, mass_part_ref, pot_part_ref,
    conc_out, pot_out, total_hbm, raw_out, x_near_out, x_far_out, total_out, sems,
):
    sides = received("gx", x_near_ref, x_far_ref)
    ends = received("gy", y_near_ref, y_far_ref)
    last_x, last_y = plan.x - 1, plan.y - 1

    def halo(which):
        return tuple(side_rows(plan, rows, which)[0] for rows in sides) + tuple(
            side_columns(plan, rows, which) for rows in ends
        )

    def edges(field):
        return field[0], field[last_x], field[:, :1], field[:, last_y:]

    mobility = mob_ref[...]
    raw_conc, raw_pot = conc_ref[...], pot_ref[...]
    outer = [
        (0.5 * time_step) * (own + other) for own, other in zip(edges(mobility), halo(2))
    ]
    diagonal = add_edges(diagonal_ref[...], *outer)
    excess_mass = add_edges(
        mass_part_ref[...],
        *(f * (other - own) for f, own, other in zip(outer, edges(raw_pot), halo(1))),
    )
    excess_pot = add_edges(pot_part_ref[...], *(-interface * other for other in halo(0)))
    conc, pot = relax_pair(
        raw_conc, raw_pot, excess_mass, excess_pot, diagonal, scale_from(diagonal)
    )

    own_mass, own_pot = inner_excess(
        conc, pot, [faces_ref[i] for i in range(5)], diagonal, mass_ref[...], pots_ref[...]
    )
    give_mass, give_pot = (
        [field[x] + field[x + 1] for x in range(0, plan.x, 2)] for field in (own_mass, own_pot)
    )
    for x, side in ((0, 0), (last_x, 1)):
        give_mass.append(outer[side] * pot[x])
        give_pot.append(-interface * conc[x])

    def packed(mass, other):
        first = iota(mass.shape, 1) & 1 == 0
        return jnp.where(
            first, mass + pltpu.roll(mass, plan.p - 1, 1), other + pltpu.roll(other, 1, 1)
        )

    give = packed(jnp.concatenate(give_mass, axis=0), jnp.concatenate(give_pot, axis=0))
    h = lax.axis_index("gy")
    inside = (h > 0, None, h < plan.groups - 1)
    maps = [rows[plan.map_row : plan.map_row + plan.owners, : plan.columns] for rows in ends]
    maps.insert(1, owner_ref[...].astype(F32))
    owner = iota((plan.owners, 1), 0)
    is_mine = owner == lax.axis_index("gx")

    own = lax.dot_general(
        gather_ref[...].astype(BF16),
        three_terms(give, 1).astype(BF16),
        (((1,), (0,)), ((), ())),
        preferred_element_type=F32,
    )
    own = own[:, : plan.p] + own[:, plan.p : 2 * plan.p] + own[:, 2 * plan.p :]
    sums = [None, own * scale_ref[...], None]
    for place, y, at, side in ((0, 0, plan.half_y - 1, 2), (2, plan.y - 1, 0, 3)):
        edge_pot, edge_conc = (
            jnp.concatenate([field[x, y : y + 1] for x in range(plan.x)], axis=0)
            for field in (pot, conc)
        )
        both = packed(outer[side][:, 0] * edge_pot, -interface * edge_conc)
        part = jnp.zeros((plan.owners, plan.p), F32)
        for i in range(plan.half_x):
            column = owner_column(plan, maps[place], i, at)
            ident = jnp.sum(jnp.where(is_mine, column, 0.0), axis=0, keepdims=True)
            pair = both[2 * i : 2 * i + 1] + both[2 * i + 1 : 2 * i + 2]
            part = part + jnp.where((owner.astype(F32) == ident) & inside[place], pair, 0.0)
        sums[place] = part * scale_of(plan, maps[place])
    def store_fields():
        conc_out[...] = conc
        pot_out[...] = pot
        for at, field in enumerate((raw_conc, raw_pot)):
            for x in range(plan.x):
                raw_out[pl.ds(2 * at * plan.x + x, 1), :] = field[x, 0:1]
                raw_out[pl.ds((2 * at + 1) * plan.x + x, 1), :] = field[x, last_y : last_y + 1]
        put_x(plan, (conc[0], pot[0]), (conc[last_x], pot[last_x]), x_near_out, x_far_out)
        up = even("gx")
        base = 2 * plan.y
        for which in range(3):
            for end, rows in enumerate(ends):
                low = rows[which * plan.x : which * plan.x + 1]
                high = rows[(which + 1) * plan.x - 1 : (which + 1) * plan.x]
                x_near_out[pl.ds(base + 2 * which + end, 1), :] = jnp.where(up, high, low)
                x_far_out[pl.ds(base + 2 * which + end, 1), :] = jnp.where(up, low, high)
        for ref in (x_near_out, x_far_out):
            ref[pl.ds(base + 6, 2), :] = jnp.zeros((2, plan.p), F32)

    if not plan.slots:
        total_out[...] = jnp.concatenate(sums, axis=0)
        copies = [pltpu.make_async_copy(total_out, total_hbm, sems.at[0])]
        copies[0].start()
        store_fields()
        copies[0].wait()
        return

    def picked(place, i, at):
        column = owner_column(plan, maps[place], i, at)
        ident = jnp.broadcast_to(column, (plan.owners, plan.p))
        out = jnp.zeros((plan.owners, plan.p), F32)
        for o in range(plan.owners):
            out = jnp.where(ident == float(o), sums[place][o : o + 1], out)
        return out

    below = [[picked(k, i, plan.half_y - 1) for i in range(plan.half_x)] for k in range(3)]
    above = [[picked(k, i, 0) for i in range(plan.half_x)] for k in range(3)]

    def of_plane(plane, choices):
        out = jnp.zeros((plan.owners, plan.p), F32)
        for k in range(3):
            out = jnp.where(plane == h + (k - 1), choices[k], out)
        return out

    size = 4 * plan.slot_parts
    rows = []
    for plane in range(plan.groups):
        beside = []
        for i in range(plan.half_x):
            beside.append((plan.low_row + i, of_plane(plane - 1, [k[i] for k in below])))
            beside.append((plan.high_row + i, of_plane(plane + 1, [k[i] for k in above])))
        blank = jnp.zeros((plan.owners, plan.p), F32)
        beside += [(at, blank) for at in range(plan.high_row + plan.half_x, size)]
        rows.append((of_plane(plane, sums), beside))
    copies = []
    for plane, (main, beside) in enumerate(rows):
        for g in range(plan.owners):
            slot = plan.slot_of(g, plane)
            for part in range(plan.owners // 4):
                total_out[slot, part] = main[4 * part : 4 * part + 4]
            for row, values in beside:
                total_out[slot, row // 4, pl.ds(row % 4, 1), :] = values[g : g + 1]
        some = pl.ds(plan.slot_of(1, plane), plan.owners)
        copies.append(
            pltpu.make_async_copy(total_out.at[some], total_hbm.at[some], sems.at[plane])
        )
        copies[-1].start()
    store_fields()
    for copy in copies:
        copy.wait()


def owner_column(plan, owners, i, at):
    b = i * plan.half_y + at
    return owners[:, b : b + 1]


def coarse_solve(packed, planes):
    lane = iota(packed.shape, 1)
    even = lane & 1 == 0
    mass_mean = jnp.where(even, packed, pltpu.roll(packed, 1, 1))
    pot_mean = jnp.where(even, pltpu.roll(packed, planes - 1, 1), packed)

    def neighbour_sum(values):
        return jnp.where(lane >= 2, pltpu.roll(values, 2, 1), 0.0) + jnp.where(
            lane < planes - 2, pltpu.roll(values, planes - 2, 1), 0.0
        )

    def step(mass_gap, pot_gap):
        scale = relax_coarse / coarse_det
        return (
            scale * (mass_gap - 2.0 * coarse_flux * pot_gap),
            scale * (pot_gap + (split_slope + 2.0 * coarse_bend) * mass_gap),
        )

    coarse_conc, coarse_pot = step(mass_mean, pot_mean)
    for _ in range(CSWEEP - 1):
        mass_gap = mass_mean - (
            coarse_conc + coarse_flux * (2.0 * coarse_pot - neighbour_sum(coarse_pot))
        )
        pot_gap = pot_mean - (
            coarse_pot
            - split_slope * coarse_conc
            + coarse_bend * (neighbour_sum(coarse_conc) - 2.0 * coarse_conc)
        )
        more_conc, more_pot = step(mass_gap, pot_gap)
        coarse_conc, coarse_pot = coarse_conc + more_conc, coarse_pot + more_pot
    return coarse_conc, coarse_pot


def beside_kernel(
    plan, x_near_ref, x_far_ref, conc_ref, pot_ref, mass_ref, pots_ref, mob_ref, raw_ref,
    x_near_msg, x_far_msg, y_near_msg, y_far_msg,
    faces_out, diagonal_out, scale_out, mass_out, pots_out,
):
    mobility = mob_ref[...]
    sides = received("gx", x_near_msg, x_far_msg)
    ends = received("gy", y_near_msg, y_far_msg)
    halo = tuple(side_rows(plan, rows, 2) for rows in sides) + tuple(
        side_columns(plan, rows, 2) for rows in ends
    )
    faces, diagonal = faces_of(mobility, neighbours(mobility, halo))
    block_terms = faces, diagonal, mass_ref[...], pots_ref[...]
    for i, face in enumerate(faces):
        faces_out[i] = face
    diagonal_out[...] = diagonal
    scale_out[...] = scale_from(diagonal)

    corners = received("gx", x_near_ref, x_far_ref)
    h = lax.axis_index("gy")
    inside = (h > 0, h < plan.groups - 1)
    own_mob = [
        jnp.concatenate([mobility[x, y : y + 1] for x in range(plan.x)], axis=0)
        for y in (0, plan.y - 1)
    ]
    halos = [[side_rows(plan, rows, which) for rows in corners] for which in range(2)]
    for end, rows in enumerate(ends):

        def row(which):
            return rows[which * plan.x : (which + 1) * plan.x]

        def beside(which, own):
            here = row(which)
            at = 2 * plan.y + 2 * which + end
            wide = jnp.concatenate([corners[0][at : at + 1], here, corners[1][at : at + 1]], axis=0)
            return (
                wide[: plan.x], wide[2:], own, row(which + 3),
                *(part[0] for part in plane_pair(here[None])),
            )

        raw = [
            raw_ref[pl.ds((2 * which + end) * plan.x, plan.x), :] for which in range(2)
        ]
        faces, diagonal = faces_of(row(2), beside(2, own_mob[end]))
        excess = excess_of(
            row(0), row(1), beside(0, raw[0]), beside(1, raw[1]), faces, diagonal, row(6), row(7)
        )
        new = relax_pair(row(0), row(1), *excess, diagonal, scale_from(diagonal))
        for which, values in enumerate(new):
            halos[which].append(jnp.where(inside[end], values, 0.0)[:, None])
    conc, pot = conc_ref[...], pot_ref[...]
    mass_out[...], pots_out[...] = excess_of(
        conc, pot, neighbours(conc, halos[0]), neighbours(pot, halos[1]), *block_terms
    )


def last_kernel(
    plan, conc_ref, pot_ref, mass_ref, pots_ref, faces_ref, diagonal_ref, scale_ref,
    spread_ref, total_ref,
    conc_hbm, pot_hbm, conc_out, pot_out, sems,
):
    parts = []
    for part in range(plan.slot_parts):
        terms = [total_ref[slot, part] for slot in range(total_ref.shape[0])]
        while len(terms) > 1:
            pairs = [a + b for a, b in zip(terms[::2], terms[1::2])]
            terms = pairs + terms[len(pairs) * 2 :]
        parts.append(terms[0])
    solved = jnp.concatenate(
        coarse_solve(jnp.concatenate(parts, axis=0), plan.p), axis=1
    )
    own = lax.dot_general(
        spread_ref[...].astype(BF16),
        three_terms(solved[: plan.owners]).astype(BF16),
        (((1,), (0,)), ((), ())),
        preferred_element_type=F32,
    )

    def shifted(which):
        lanes = slice(which * plan.p, (which + 1) * plan.p)
        rows = [own[i * plan.y : (i + 1) * plan.y, lanes][None] for i in range(plan.half_x + 2)]
        beside = []
        for i in range(plan.half_x):
            ends = [
                solved[begin + i : begin + i + 1, lanes][None]
                for begin in (plan.low_row, plan.high_row)
            ]
            beside.append((*y_pair(rows[i], *ends), *plane_pair(rows[i])))
        return [rows[plan.half_x], *rows[: plan.half_x], rows[plan.half_x + 1]], beside

    conc_rows, conc_beside = shifted(0)
    pot_rows, pot_beside = shifted(1)
    conc_sums = [a + b + c + d for a, b, c, d in conc_beside]
    copies = []
    for x in range(plan.x):
        one = pl.ds(x, 1)
        i = x >> 1
        low, high = (i, i + 1) if x % 2 == 0 else (i + 1, i + 2)
        diagonal = diagonal_ref[one]
        conc, pot = conc_rows[i + 1], pot_rows[i + 1]
        excess_mass = mass_ref[one] - conc - diagonal * pot
        beside = (pot_rows[low], pot_rows[high], *pot_beside[i])
        for k, other in enumerate(beside):
            excess_mass = excess_mass + faces_ref[k, one] * other
        excess_pot = (pots_ref[one] - pot) + (split_slope + 6.0 * interface) * conc
        excess_pot = excess_pot - interface * (conc_rows[low] + conc_rows[high] + conc_sums[i])
        conc_out[one], pot_out[one] = relax_pair(
            conc_ref[one] + conc, pot_ref[one] + pot, excess_mass, excess_pot, diagonal, scale_ref[one]
        )
        for source, target in ((conc_out, conc_hbm), (pot_out, pot_hbm)):
            copies.append(
                pltpu.make_async_copy(source.at[one], target.at[one], sems.at[len(copies)])
            )
            copies[-1].start()
    for copy in copies:
        copy.wait()


def call(kernel, plan, outs, args, far=(), smem=(), scratch=(), out_far=()):
    def space(i):
        return pl.ANY if i in far else pltpu.SMEM if i in smem else pltpu.VMEM

    return pl.pallas_call(
        functools.partial(kernel, plan),
        out_shape=[jax.ShapeDtypeStruct(shape, F32) for shape in outs],
        in_specs=[pl.BlockSpec(memory_space=space(i)) for i in range(len(args))],
        out_specs=[
            pl.BlockSpec(memory_space=pl.ANY if i in out_far else pltpu.VMEM)
            for i in range(len(outs))
        ],
        scratch_shapes=list(scratch),
        compiler_params=pltpu.CompilerParams(vmem_limit_bytes=VMEM_LIMIT),
    )(*[
        pltpu.with_memory_space_constraint(arg, pltpu.HBM) if i in far else arg
        for i, arg in enumerate(args)
    ])


def swap_near(axis, rows, begin=0):
    pairs = [(i, i + 1) for i in range(begin, lax.axis_size(axis) - 1, 2)]
    return lax.ppermute(rows, axis, pairs + [(j, i) for i, j in pairs])


def swap_far(axis, rows):
    return swap_near(axis, rows, 1)


def gather_totals(plan, total, y_near, y_far):
    if plan.slots:
        order = [0] * plan.slots
        for g in range(plan.owners):
            for h in range(plan.groups):
                order[plan.slot_of(g, h)] = g * plan.groups + h
        return lax.all_to_all(
            total, ("gx", "gy"), split_axis=0, concat_axis=0, axis_index_groups=[order], tiled=True
        )
    shape = (plan.groups, 3, plan.owners, plan.p)
    parts = lax.all_gather(lax.psum(total, "gx"), "gy").reshape(shape)
    blank = jnp.zeros((1, plan.owners, plan.p), F32)
    to_below, own, to_above = (parts[:, k] for k in range(3))
    own = own + jnp.concatenate([blank, to_above[:-1]]) + jnp.concatenate([to_below[1:], blank])
    own = jnp.concatenate([blank, own, blank])
    g, h = lax.axis_index("gx"), lax.axis_index("gy")
    rows = [lax.dynamic_index_in_dim(own, h + 1, 0, False)]
    up = lax.rem(h, 2) == 0
    far = y_far[: y_near.shape[0]]
    for place, at, msg in (
        (h, plan.half_y - 1, jnp.where(up, far, y_near)),
        (h + 2, 0, jnp.where(up, y_near, far)),
    ):
        ident = lax.dynamic_index_in_dim(msg, plan.map_row + g, 0, False).astype(jnp.int32)
        ident = jnp.stack([ident[i * plan.half_y + at] for i in range(plan.half_x)])
        rows.append(lax.dynamic_index_in_dim(own, place, 0, False)[ident])
    rows = jnp.concatenate(rows)
    rows = jnp.pad(rows, ((0, 4 * plan.slot_parts - rows.shape[0]), (0, 0)))
    return rows.reshape(1, plan.slot_parts, 4, plan.p)


def on_device(conc, pot, mass_source, pot_source, mask, kind, table, owner_map):
    plan = Plan(conc.shape, lax.axis_size("gx"), lax.axis_size("gy"))
    block = conc.shape
    fields = [conc, pot, mask, kind, mass_source, pot_source]
    messages = call(
        prepare_kernel,
        plan,
        [*[(3 * plan.y, plan.p)] * 2, (plan.y_rows, plan.p), (plan.y_far_rows, plan.p)],
        [*fields, owner_map, table],
        far=range(8),
        scratch=(
            *[pltpu.VMEM((2, plan.y, plan.p), field.dtype) for field in fields[:4]],
            *[pltpu.VMEM((2, plan.x, 8, plan.p), field.dtype) for field in fields],
            pltpu.VMEM(owner_map.shape, owner_map.dtype),
            pltpu.SMEM(table.shape, table.dtype),
            pltpu.SemaphoreType.DMA((22,)),
        ),
    )
    x_near, x_far = swap_near("gx", messages[0]), swap_far("gx", messages[1])
    y_near, y_far = swap_near("gy", messages[2]), swap_far("gy", messages[3])
    y_far, mask, kind = lax.optimization_barrier((y_far, mask, kind))
    mob, gather, spread, scale, *parts = call(
        local_kernel,
        plan,
        [
            block, (plan.owners, plan.rows), (plan.rows, 3 * plan.owners), (plan.owners, plan.p),
            (5, *block), block, block, block,
        ],
        [conc, pot, mask, kind, mass_source, pot_source, table, owner_map],
        smem=(6,),
    )
    slots = (plan.slots, plan.slot_parts, 4, plan.p) if plan.slots else (3 * plan.owners, plan.p)
    conc, pot, total, raw, near, far = call(
        first_kernel,
        plan,
        [
            block,
            block,
            slots,
            (4 * plan.x, plan.p),
            *[(2 * plan.y + 8, plan.p)] * 2,
        ],
        [
            x_far, x_near, y_far, y_near,
            conc, pot, mob, mass_source, pot_source, gather, scale, owner_map, *parts,
        ],
        out_far=(2,),
        scratch=(pltpu.VMEM(slots, F32), pltpu.SemaphoreType.DMA((plan.groups,))),
    )
    total = gather_totals(plan, total, y_near, y_far)
    far = swap_far("gx", far)
    near = swap_near("gx", near)
    faces, diagonal, scale, mass_part, pot_part = call(
        beside_kernel,
        plan,
        [(6, *block), block, block, block, block],
        [
            near, far, conc, pot, mass_source, pot_source, mob, raw,
            x_near, x_far, y_near, y_far,
        ],
    )
    return tuple(
        call(
            last_kernel,
            plan,
            [block, block],
            [conc, pot, mass_part, pot_part, faces, diagonal, scale, spread, total],
            out_far=(0, 1),
            scratch=(
                pltpu.VMEM(block, F32),
                pltpu.VMEM(block, F32),
                pltpu.SemaphoreType.DMA((2 * plan.x,)),
            ),
        )
    )


def solution(mesh):
    grid = P("gx", "gy", None)
    return jax.shard_map(
        on_device,
        mesh=mesh,
        in_specs=(grid,) * 6 + (P(), P(None, "gy")),
        out_specs=(grid, grid),
        check_vma=False,
    )
```

```python
import functools

import jax
import jax.numpy as jnp
from jax import lax
from jax.experimental import pallas as pl
from jax.experimental.pallas import tpu as pltpu
from jax.sharding import PartitionSpec as P

CSWEEP = 3

time_step = 0.25
split_slope = 1.0
interface = 0.5
relax_fine = 0.6
relax_coarse = 0.6
coarse_flux = 0.0625
coarse_bend = 0.125
coarse_det = 1.0 + 2.0 * coarse_flux * (split_slope + 2.0 * coarse_bend)

F32 = jnp.float32
BF16 = jnp.bfloat16
VMEM_LIMIT = 48 * 1024 * 1024


def iota(shape, dim):
    return lax.broadcasted_iota(jnp.int32, shape, dim)


def x_pair(field, low, high):
    return (
        jnp.concatenate([low, field[:-1]], axis=0),
        jnp.concatenate([field[1:], high], axis=0),
    )


def y_pair(field, low, high):
    size = field.shape[1]
    where = iota(field.shape, 1)
    return (
        jnp.where(where == 0, low, pltpu.roll(field, 1, 1)),
        jnp.where(where == size - 1, high, pltpu.roll(field, size - 1, 1)),
    )


def plane_pair(field):
    size = field.shape[2]
    where = iota(field.shape, 2)
    return (
        jnp.where(where == 0, 0.0, pltpu.roll(field, 1, 2)),
        jnp.where(where == size - 1, 0.0, pltpu.roll(field, size - 1, 2)),
    )


def neighbours(field, halo):
    xm, xp, ym, yp = halo
    return (*x_pair(field, xm, xp), *y_pair(field, ym, yp), *plane_pair(field))


def excess_of(conc, pot, conc_beside, pot_beside, faces, diagonal, mass_source, pot_source):
    excess_mass = (mass_source - conc) - diagonal * pot
    for face, other in zip(faces, pot_beside):
        excess_mass = excess_mass + face * other
    beside = conc_beside[0]
    for other in conc_beside[1:]:
        beside = beside + other
    excess_pot = (pot_source - pot) + (split_slope + 6.0 * interface) * conc - interface * beside
    return excess_mass, excess_pot


def scale_from(diagonal):
    return relax_fine / (1.0 + (split_slope + 6.0 * interface) * diagonal)


def relax_pair(conc, pot, excess_mass, excess_pot, diagonal, scale):
    new_conc = conc + (excess_mass - diagonal * excess_pot) * scale
    new_pot = pot + (excess_pot + (split_slope + 6.0 * interface) * excess_mass) * scale
    return new_conc, new_pot


def faces_of(mobility, beside):
    faces = tuple((0.5 * time_step) * (mobility + other) for other in beside)
    diagonal = faces[0]
    for face in faces[1:]:
        diagonal = diagonal + face
    return faces, diagonal


def three_terms(values, dim=0):
    out = []
    for _ in range(3):
        out.append(values.astype(BF16).astype(F32))
        values = values - out[-1]
    return jnp.concatenate(out, axis=dim)


def round_up(value, unit):
    return -(-value // unit) * unit


class Plan:
    def __init__(self, shape, owners, groups):
        self.x, self.y, self.p = shape
        self.owners, self.groups = owners, groups
        self.half_x, self.half_y = self.x // 2, self.y // 2
        self.columns = self.half_x * self.half_y
        self.map_row = round_up(8 * self.x, 8)
        self.y_rows = self.map_row + owners
        self.y_far_rows = max(self.y_rows, 3 * self.y + 8)
        self.cells = self.x * self.y
        self.rows = (self.half_x + 2) * self.y
        self.low_row = owners
        self.high_row = owners + self.half_x
        self.slot_parts = -(-(owners + 2 * self.half_x) // 4)
        slots = owners * groups
        self.slots = slots if slots <= 64 else 0

    def slot_of(self, g, h):
        last = self.groups - 1
        place = 0 if h == 0 else 1 if h == last else h + 1
        return place * self.owners + self.owners - 1 - (g ^ 1)


def side_rows(plan, rows, which):
    return rows[which * plan.y : (which + 1) * plan.y][None]


def side_columns(plan, rows, which):
    return rows[which * plan.x : (which + 1) * plan.x][:, None]


def membership(plan, owner_ref):
    g = lax.axis_index("gx")
    last = plan.owners - 1
    owner = iota((plan.owners, plan.columns), 0)
    low, high = plan.half_x, plan.half_x + 1
    shape = (plan.half_x + 2, plan.y, plan.columns)
    x, y, column = iota(shape, 0), iota(shape, 1), iota(shape, 2)
    half = jnp.where(x < low, x, jnp.where(x == low, plan.half_x - 1, 0))
    place = column == half * plan.half_y + (y >> 1)
    sides = (
        (x < low, g, True),
        (x == low, jnp.maximum(g - 1, 0), g > 0),
        (x == high, jnp.minimum(g + 1, last), g < last),
    )
    gather, spread = None, None
    for part, row, inside in sides:
        hits = ((owner_ref[pl.ds(row, 1), :] == owner) & inside).astype(F32).astype(BF16)
        where = (place & part).astype(F32).reshape(plan.rows, plan.columns).astype(BF16)
        nt = (((1,), (1,)), ((), ()))
        some = lax.dot_general(hits, where, nt, preferred_element_type=F32)
        gather = some if gather is None else gather + some
        some = lax.dot_general(where, hits, nt, preferred_element_type=F32)
        spread = some if spread is None else spread + some
    return gather, jnp.concatenate([spread] * 3, axis=1)


def scale_of(plan, owners):
    owner = iota((plan.owners, plan.columns), 0).astype(owners.dtype)
    hits = jnp.zeros((plan.owners, plan.columns), F32)
    for g in range(plan.owners):
        hits = hits + (owners[g : g + 1] == owner).astype(F32)
    count = jnp.sum(hits, axis=1, keepdims=True)
    return jnp.broadcast_to(0.125 / jnp.maximum(count, 1.0), (plan.owners, plan.p))


def mobility_of(mask, kind, table):
    values = jnp.zeros(kind.shape, F32)
    for marker, value in enumerate(table):
        values = jnp.where(kind == marker, value, values)
    return mask.astype(F32) * values


def even(axis):
    return lax.rem(lax.axis_index(axis), 2) == 0


def put_x(plan, lows, highs, near, far):
    up = even("gx")
    for which, (low, high) in enumerate(zip(lows, highs)):
        near[pl.ds(which * plan.y, plan.y), :] = jnp.where(up, high, low)
        far[pl.ds(which * plan.y, plan.y), :] = jnp.where(up, low, high)


def received(axis, near_ref, far_ref):
    up = even(axis)
    rows = pl.ds(0, min(near_ref.shape[0], far_ref.shape[0]))
    near, far = near_ref[rows, :], far_ref[rows, :]
    return jnp.where(up, far, near), jnp.where(up, near, far)


def prepare_kernel(plan, *refs):
    hbm, refs = refs[:8], refs[8:]
    x_near_ref, x_far_ref, y_near_ref, y_far_ref = refs[:4]
    x_refs, y_refs, (owner_ref, table_ref, sems) = refs[4:8], refs[8:14], refs[14:]
    copies = []

    def start(source, target):
        copies.append(pltpu.make_async_copy(source, target, sems.at[len(copies)]))
        copies[-1].start()

    start(hbm[7], table_ref)
    start(hbm[6], owner_ref)
    for source, target in zip(hbm[:4], x_refs):
        start(source.at[0], target.at[0])
        start(source.at[plan.x - 1], target.at[1])
    for source, target in zip(hbm[:6], y_refs):
        start(source.at[:, pl.ds(0, 8)], target.at[0])
        start(source.at[:, pl.ds(plan.y - 8, 8)], target.at[1])
    for copy in copies:
        copy.wait()
    table = [table_ref[marker] for marker in range(table_ref.shape[0])]
    conc, pot, mask, kind = (ref[...] for ref in x_refs)
    fields = (conc, pot, mobility_of(mask, kind, table))
    put_x(plan, [f[0] for f in fields], [f[1] for f in fields], x_near_ref, x_far_ref)
    conc, pot, mask, kind, mass, pots = (ref[...] for ref in y_refs)
    fields = (conc, pot, mobility_of(mask, kind, table))
    up = even("gy")
    rows = [(field, at) for at in range(2) for field in fields] + [(mass, 0), (pots, 0)]
    for which, (field, at) in enumerate(rows):
        for x in range(plan.x):
            low, high = field[0, x, at : at + 1], field[1, x, 7 - at : 8 - at]
            y_near_ref[pl.ds(which * plan.x + x, 1), :] = jnp.where(up, high, low)
            y_far_ref[pl.ds(which * plan.x + x, 1), :] = jnp.where(up, low, high)
    used = 8 * plan.x
    for ref, rows in ((y_near_ref, plan.y_rows), (y_far_ref, plan.y_far_rows)):
        ref[pl.ds(used, rows - used), :] = jnp.zeros((rows - used, plan.p), F32)
        ref[pl.ds(plan.map_row, plan.owners), pl.ds(0, plan.columns)] = owner_ref[...].astype(F32)


def inner_faces(mobility):
    half = 0.5 * time_step
    shape = mobility.shape
    y, plane = iota(shape, 1), iota(shape, 2)
    to_x = jnp.concatenate(
        [half * (mobility[:-1] + mobility[1:]), jnp.zeros_like(mobility[:1])], axis=0
    )
    out = [to_x]
    for dim, where, shift, edge in (
        (1, y, 1, 0), (1, y, shape[1] - 1, shape[1] - 1),
        (2, plane, 1, 0), (2, plane, shape[2] - 1, shape[2] - 1),
    ):
        face = half * (mobility + pltpu.roll(mobility, shift, dim))
        out.append(jnp.where(where == edge, 0.0, face))
    return out


def inner_flux(faces, field):
    to_x, y_low, y_high, plane_low, plane_high = faces
    size_y, size_p = field.shape[1:]
    from_x = to_x[:-1]
    blank = jnp.zeros_like(field[:1])
    flux = jnp.concatenate([from_x * field[1:], blank], axis=0)
    flux = flux + jnp.concatenate([blank, from_x * field[:-1]], axis=0)
    flux = flux + y_low * pltpu.roll(field, 1, 1) + y_high * pltpu.roll(field, size_y - 1, 1)
    return flux + plane_low * pltpu.roll(field, 1, 2) + plane_high * pltpu.roll(field, size_p - 1, 2)


def inner_excess(conc, pot, faces, diagonal, mass_source, pot_source):
    excess_mass = (mass_source - conc) - diagonal * pot + inner_flux(faces, pot)
    nothing = [jnp.zeros_like(conc[:1])] * 2 + [jnp.zeros_like(conc[:, :1])] * 2
    beside = None
    for other in neighbours(conc, nothing):
        beside = other if beside is None else beside + other
    excess_pot = (pot_source - pot) + (split_slope + 6.0 * interface) * conc - interface * beside
    return excess_mass, excess_pot


def add_edges(field, x_low, x_high, y_low, y_high):
    field = jnp.concatenate(
        [(field[0] + x_low)[None], field[1:-1], (field[-1] + x_high)[None]], axis=0
    )
    row = iota((field.shape[0], 8, field.shape[2]), 1)
    size = field.shape[1]
    low = field[:, :8] + jnp.where(row == 0, y_low, 0.0)
    high = field[:, size - 8 :] + jnp.where(row == 7, y_high, 0.0)
    return jnp.concatenate([low, field[:, 8 : size - 8], high], axis=1)


def local_kernel(
    plan, conc_ref, pot_ref, mask_ref, class_ref, mass_ref, pots_ref, table_ref, owner_ref,
    mob_ref, gather_ref, spread_ref, scale_ref, faces_ref, diagonal_ref, mass_out, pots_out,
):
    table = [table_ref[marker] for marker in range(table_ref.shape[0])]
    mobility = mobility_of(mask_ref[...], class_ref[...], table)
    mob_ref[...] = mobility
    gather_ref[...], spread_ref[...] = membership(plan, owner_ref)
    scale_ref[...] = scale_of(plan, owner_ref[...])
    faces = inner_faces(mobility)
    diagonal = faces[0] + jnp.concatenate([jnp.zeros_like(mobility[:1]), faces[0][:-1]], axis=0)
    for face in faces[1:]:
        diagonal = diagonal + face
    plane = iota(mobility.shape, 2)
    ends = (plane == 0) | (plane == plan.p - 1)
    diagonal = diagonal + jnp.where(ends, (0.5 * time_step) * mobility, 0.0)
    for i, face in enumerate(faces):
        faces_ref[i] = face
    diagonal_ref[...] = diagonal
    mass_out[...], pots_out[...] = inner_excess(
        conc_ref[...], pot_ref[...], faces, diagonal, mass_ref[...], pots_ref[...]
    )


def first_kernel(
    plan, x_far_ref, x_near_ref, y_far_ref, y_near_ref,
    conc_ref, pot_ref, mob_ref, mass_ref, pots_ref, gather_ref, scale_ref, owner_ref,
    faces_ref, diagonal_ref, mass_part_ref, pot_part_ref,
    conc_out, pot_out, total_hbm, raw_out, x_near_out, x_far_out, total_out, sems,
):
    sides = received("gx", x_near_ref, x_far_ref)
    ends = received("gy", y_near_ref, y_far_ref)
    last_x, last_y = plan.x - 1, plan.y - 1

    def halo(which):
        return tuple(side_rows(plan, rows, which)[0] for rows in sides) + tuple(
            side_columns(plan, rows, which) for rows in ends
        )

    def edges(field):
        return field[0], field[last_x], field[:, :1], field[:, last_y:]

    mobility = mob_ref[...]
    raw_conc, raw_pot = conc_ref[...], pot_ref[...]
    outer = [
        (0.5 * time_step) * (own + other) for own, other in zip(edges(mobility), halo(2))
    ]
    diagonal = add_edges(diagonal_ref[...], *outer)
    excess_mass = add_edges(
        mass_part_ref[...],
        *(f * (other - own) for f, own, other in zip(outer, edges(raw_pot), halo(1))),
    )
    excess_pot = add_edges(pot_part_ref[...], *(-interface * other for other in halo(0)))
    conc, pot = relax_pair(
        raw_conc, raw_pot, excess_mass, excess_pot, diagonal, scale_from(diagonal)
    )

    own_mass, own_pot = inner_excess(
        conc, pot, [faces_ref[i] for i in range(5)], diagonal, mass_ref[...], pots_ref[...]
    )
    give_mass, give_pot = (
        [field[x] + field[x + 1] for x in range(0, plan.x, 2)] for field in (own_mass, own_pot)
    )
    for x, side in ((0, 0), (last_x, 1)):
        give_mass.append(outer[side] * pot[x])
        give_pot.append(-interface * conc[x])

    def packed(mass, other):
        first = iota(mass.shape, 1) & 1 == 0
        return jnp.where(
            first, mass + pltpu.roll(mass, plan.p - 1, 1), other + pltpu.roll(other, 1, 1)
        )

    give = packed(jnp.concatenate(give_mass, axis=0), jnp.concatenate(give_pot, axis=0))
    h = lax.axis_index("gy")
    inside = (h > 0, None, h < plan.groups - 1)
    maps = [rows[plan.map_row : plan.map_row + plan.owners, : plan.columns] for rows in ends]
    maps.insert(1, owner_ref[...].astype(F32))
    owner = iota((plan.owners, 1), 0)
    is_mine = owner == lax.axis_index("gx")

    own = lax.dot_general(
        gather_ref[...].astype(BF16),
        three_terms(give, 1).astype(BF16),
        (((1,), (0,)), ((), ())),
        preferred_element_type=F32,
    )
    own = own[:, : plan.p] + own[:, plan.p : 2 * plan.p] + own[:, 2 * plan.p :]
    sums = [None, own * scale_ref[...], None]
    for place, y, at, side in ((0, 0, plan.half_y - 1, 2), (2, plan.y - 1, 0, 3)):
        edge_pot, edge_conc = (
            jnp.concatenate([field[x, y : y + 1] for x in range(plan.x)], axis=0)
            for field in (pot, conc)
        )
        both = packed(outer[side][:, 0] * edge_pot, -interface * edge_conc)
        part = jnp.zeros((plan.owners, plan.p), F32)
        for i in range(plan.half_x):
            column = owner_column(plan, maps[place], i, at)
            ident = jnp.sum(jnp.where(is_mine, column, 0.0), axis=0, keepdims=True)
            pair = both[2 * i : 2 * i + 1] + both[2 * i + 1 : 2 * i + 2]
            part = part + jnp.where((owner.astype(F32) == ident) & inside[place], pair, 0.0)
        sums[place] = part * scale_of(plan, maps[place])
    def store_fields():
        conc_out[...] = conc
        pot_out[...] = pot
        for at, field in enumerate((raw_conc, raw_pot)):
            for x in range(plan.x):
                raw_out[pl.ds(2 * at * plan.x + x, 1), :] = field[x, 0:1]
                raw_out[pl.ds((2 * at + 1) * plan.x + x, 1), :] = field[x, last_y : last_y + 1]
        put_x(plan, (conc[0], pot[0]), (conc[last_x], pot[last_x]), x_near_out, x_far_out)
        up = even("gx")
        base = 2 * plan.y
        for which in range(3):
            for end, rows in enumerate(ends):
                low = rows[which * plan.x : which * plan.x + 1]
                high = rows[(which + 1) * plan.x - 1 : (which + 1) * plan.x]
                x_near_out[pl.ds(base + 2 * which + end, 1), :] = jnp.where(up, high, low)
                x_far_out[pl.ds(base + 2 * which + end, 1), :] = jnp.where(up, low, high)
        for ref in (x_near_out, x_far_out):
            ref[pl.ds(base + 6, 2), :] = jnp.zeros((2, plan.p), F32)

    if not plan.slots:
        total_out[...] = jnp.concatenate(sums, axis=0)
        copies = [pltpu.make_async_copy(total_out, total_hbm, sems.at[0])]
        copies[0].start()
        store_fields()
        copies[0].wait()
        return

    def picked(place, i, at):
        column = owner_column(plan, maps[place], i, at)
        ident = jnp.broadcast_to(column, (plan.owners, plan.p))
        out = jnp.zeros((plan.owners, plan.p), F32)
        for o in range(plan.owners):
            out = jnp.where(ident == float(o), sums[place][o : o + 1], out)
        return out

    below = [[picked(k, i, plan.half_y - 1) for i in range(plan.half_x)] for k in range(3)]
    above = [[picked(k, i, 0) for i in range(plan.half_x)] for k in range(3)]

    def of_plane(plane, choices):
        out = jnp.zeros((plan.owners, plan.p), F32)
        for k in range(3):
            out = jnp.where(plane == h + (k - 1), choices[k], out)
        return out

    size = 4 * plan.slot_parts
    rows = []
    for plane in range(plan.groups):
        beside = []
        for i in range(plan.half_x):
            beside.append((plan.low_row + i, of_plane(plane - 1, [k[i] for k in below])))
            beside.append((plan.high_row + i, of_plane(plane + 1, [k[i] for k in above])))
        blank = jnp.zeros((plan.owners, plan.p), F32)
        beside += [(at, blank) for at in range(plan.high_row + plan.half_x, size)]
        rows.append((of_plane(plane, sums), beside))
    copies = []
    for plane, (main, beside) in enumerate(rows):
        for g in range(plan.owners):
            slot = plan.slot_of(g, plane)
            for part in range(plan.owners // 4):
                total_out[slot, part] = main[4 * part : 4 * part + 4]
            for row, values in beside:
                total_out[slot, row // 4, pl.ds(row % 4, 1), :] = values[g : g + 1]
        some = pl.ds(plan.slot_of(plan.owners - 2, plane), plan.owners)
        copies.append(
            pltpu.make_async_copy(total_out.at[some], total_hbm.at[some], sems.at[plane])
        )
        copies[-1].start()
    store_fields()
    for copy in copies:
        copy.wait()


def owner_column(plan, owners, i, at):
    b = i * plan.half_y + at
    return owners[:, b : b + 1]


def coarse_solve(packed, planes):
    lane = iota(packed.shape, 1)
    even = lane & 1 == 0
    mass_mean = jnp.where(even, packed, pltpu.roll(packed, 1, 1))
    pot_mean = jnp.where(even, pltpu.roll(packed, planes - 1, 1), packed)

    def neighbour_sum(values):
        return jnp.where(lane >= 2, pltpu.roll(values, 2, 1), 0.0) + jnp.where(
            lane < planes - 2, pltpu.roll(values, planes - 2, 1), 0.0
        )

    def step(mass_gap, pot_gap):
        scale = relax_coarse / coarse_det
        return (
            scale * (mass_gap - 2.0 * coarse_flux * pot_gap),
            scale * (pot_gap + (split_slope + 2.0 * coarse_bend) * mass_gap),
        )

    coarse_conc, coarse_pot = step(mass_mean, pot_mean)
    for _ in range(CSWEEP - 1):
        mass_gap = mass_mean - (
            coarse_conc + coarse_flux * (2.0 * coarse_pot - neighbour_sum(coarse_pot))
        )
        pot_gap = pot_mean - (
            coarse_pot
            - split_slope * coarse_conc
            + coarse_bend * (neighbour_sum(coarse_conc) - 2.0 * coarse_conc)
        )
        more_conc, more_pot = step(mass_gap, pot_gap)
        coarse_conc, coarse_pot = coarse_conc + more_conc, coarse_pot + more_pot
    return coarse_conc, coarse_pot


def beside_kernel(
    plan, x_far_ref, x_near_ref, conc_ref, pot_ref, mass_ref, pots_ref, mob_ref, raw_ref,
    x_near_msg, x_far_msg, y_near_msg, y_far_msg,
    faces_out, diagonal_out, scale_out, mass_out, pots_out,
):
    mobility = mob_ref[...]
    sides = received("gx", x_near_msg, x_far_msg)
    ends = received("gy", y_near_msg, y_far_msg)
    halo = tuple(side_rows(plan, rows, 2) for rows in sides) + tuple(
        side_columns(plan, rows, 2) for rows in ends
    )
    faces, diagonal = faces_of(mobility, neighbours(mobility, halo))
    block_terms = faces, diagonal, mass_ref[...], pots_ref[...]
    for i, face in enumerate(faces):
        faces_out[i] = face
    diagonal_out[...] = diagonal
    scale_out[...] = scale_from(diagonal)

    corners = received("gx", x_near_ref, x_far_ref)
    h = lax.axis_index("gy")
    inside = (h > 0, h < plan.groups - 1)
    own_mob = [
        jnp.concatenate([mobility[x, y : y + 1] for x in range(plan.x)], axis=0)
        for y in (0, plan.y - 1)
    ]
    halos = [[side_rows(plan, rows, which) for rows in corners] for which in range(2)]
    for end, rows in enumerate(ends):

        def row(which):
            return rows[which * plan.x : (which + 1) * plan.x]

        def beside(which, own):
            here = row(which)
            at = 2 * plan.y + 2 * which + end
            wide = jnp.concatenate([corners[0][at : at + 1], here, corners[1][at : at + 1]], axis=0)
            return (
                wide[: plan.x], wide[2:], own, row(which + 3),
                *(part[0] for part in plane_pair(here[None])),
            )

        raw = [
            raw_ref[pl.ds((2 * which + end) * plan.x, plan.x), :] for which in range(2)
        ]
        faces, diagonal = faces_of(row(2), beside(2, own_mob[end]))
        excess = excess_of(
            row(0), row(1), beside(0, raw[0]), beside(1, raw[1]), faces, diagonal, row(6), row(7)
        )
        new = relax_pair(row(0), row(1), *excess, diagonal, scale_from(diagonal))
        for which, values in enumerate(new):
            halos[which].append(jnp.where(inside[end], values, 0.0)[:, None])
    conc, pot = conc_ref[...], pot_ref[...]
    mass_out[...], pots_out[...] = excess_of(
        conc, pot, neighbours(conc, halos[0]), neighbours(pot, halos[1]), *block_terms
    )


def last_kernel(
    plan, conc_ref, pot_ref, mass_ref, pots_ref, faces_ref, diagonal_ref, scale_ref,
    spread_ref, total_ref,
    conc_hbm, pot_hbm, conc_out, pot_out, sems,
):
    parts = []
    for part in range(plan.slot_parts):
        terms = [total_ref[slot, part] for slot in range(total_ref.shape[0])]
        while len(terms) > 1:
            pairs = [a + b for a, b in zip(terms[::2], terms[1::2])]
            terms = pairs + terms[len(pairs) * 2 :]
        parts.append(terms[0])
    solved = jnp.concatenate(
        coarse_solve(jnp.concatenate(parts, axis=0), plan.p), axis=1
    )
    own = lax.dot_general(
        spread_ref[...].astype(BF16),
        three_terms(solved[: plan.owners]).astype(BF16),
        (((1,), (0,)), ((), ())),
        preferred_element_type=F32,
    )

    def shifted(which):
        lanes = slice(which * plan.p, (which + 1) * plan.p)
        rows = [own[i * plan.y : (i + 1) * plan.y, lanes][None] for i in range(plan.half_x + 2)]
        beside = []
        for i in range(plan.half_x):
            ends = [
                solved[begin + i : begin + i + 1, lanes][None]
                for begin in (plan.low_row, plan.high_row)
            ]
            beside.append((*y_pair(rows[i], *ends), *plane_pair(rows[i])))
        return [rows[plan.half_x], *rows[: plan.half_x], rows[plan.half_x + 1]], beside

    conc_rows, conc_beside = shifted(0)
    pot_rows, pot_beside = shifted(1)
    conc_sums = [a + b + c + d for a, b, c, d in conc_beside]
    copies = []
    for x in range(plan.x):
        one = pl.ds(x, 1)
        i = x >> 1
        low, high = (i, i + 1) if x % 2 == 0 else (i + 1, i + 2)
        diagonal = diagonal_ref[one]
        conc, pot = conc_rows[i + 1], pot_rows[i + 1]
        excess_mass = mass_ref[one] - conc - diagonal * pot
        beside = (pot_rows[low], pot_rows[high], *pot_beside[i])
        for k, other in enumerate(beside):
            excess_mass = excess_mass + faces_ref[k, one] * other
        excess_pot = (pots_ref[one] - pot) + (split_slope + 6.0 * interface) * conc
        excess_pot = excess_pot - interface * (conc_rows[low] + conc_rows[high] + conc_sums[i])
        conc_out[one], pot_out[one] = relax_pair(
            conc_ref[one] + conc, pot_ref[one] + pot, excess_mass, excess_pot, diagonal, scale_ref[one]
        )
        for source, target in ((conc_out, conc_hbm), (pot_out, pot_hbm)):
            copies.append(
                pltpu.make_async_copy(source.at[one], target.at[one], sems.at[len(copies)])
            )
            copies[-1].start()
    for copy in copies:
        copy.wait()


def call(kernel, plan, outs, args, far=(), smem=(), scratch=(), out_far=()):
    def space(i):
        return pl.ANY if i in far else pltpu.SMEM if i in smem else pltpu.VMEM

    return pl.pallas_call(
        functools.partial(kernel, plan),
        out_shape=[jax.ShapeDtypeStruct(shape, F32) for shape in outs],
        in_specs=[pl.BlockSpec(memory_space=space(i)) for i in range(len(args))],
        out_specs=[
            pl.BlockSpec(memory_space=pl.ANY if i in out_far else pltpu.VMEM)
            for i in range(len(outs))
        ],
        scratch_shapes=list(scratch),
        compiler_params=pltpu.CompilerParams(vmem_limit_bytes=VMEM_LIMIT),
    )(*[
        pltpu.with_memory_space_constraint(arg, pltpu.HBM) if i in far else arg
        for i, arg in enumerate(args)
    ])


def swap_near(axis, rows, begin=0):
    pairs = [(i, i + 1) for i in range(begin, lax.axis_size(axis) - 1, 2)]
    return lax.ppermute(rows, axis, pairs + [(j, i) for i, j in pairs])


def swap_far(axis, rows):
    return swap_near(axis, rows, 1)


def gather_totals(plan, total, y_near, y_far):
    if plan.slots:
        order = [0] * plan.slots
        for g in range(plan.owners):
            for h in range(plan.groups):
                order[plan.slot_of(g, h)] = g * plan.groups + h
        return lax.all_to_all(
            total, ("gx", "gy"), split_axis=0, concat_axis=0, axis_index_groups=[order], tiled=True
        )
    shape = (plan.groups, 3, plan.owners, plan.p)
    parts = lax.all_gather(lax.psum(total, "gx"), "gy").reshape(shape)
    blank = jnp.zeros((1, plan.owners, plan.p), F32)
    to_below, own, to_above = (parts[:, k] for k in range(3))
    own = own + jnp.concatenate([blank, to_above[:-1]]) + jnp.concatenate([to_below[1:], blank])
    own = jnp.concatenate([blank, own, blank])
    g, h = lax.axis_index("gx"), lax.axis_index("gy")
    rows = [lax.dynamic_index_in_dim(own, h + 1, 0, False)]
    up = lax.rem(h, 2) == 0
    far = y_far[: y_near.shape[0]]
    for place, at, msg in (
        (h, plan.half_y - 1, jnp.where(up, far, y_near)),
        (h + 2, 0, jnp.where(up, y_near, far)),
    ):
        ident = lax.dynamic_index_in_dim(msg, plan.map_row + g, 0, False).astype(jnp.int32)
        ident = jnp.stack([ident[i * plan.half_y + at] for i in range(plan.half_x)])
        rows.append(lax.dynamic_index_in_dim(own, place, 0, False)[ident])
    rows = jnp.concatenate(rows)
    rows = jnp.pad(rows, ((0, 4 * plan.slot_parts - rows.shape[0]), (0, 0)))
    return rows.reshape(1, plan.slot_parts, 4, plan.p)


def on_device(conc, pot, mass_source, pot_source, mask, kind, table, owner_map):
    plan = Plan(conc.shape, lax.axis_size("gx"), lax.axis_size("gy"))
    block = conc.shape
    fields = [conc, pot, mask, kind, mass_source, pot_source]
    messages = call(
        prepare_kernel,
        plan,
        [*[(3 * plan.y, plan.p)] * 2, (plan.y_rows, plan.p), (plan.y_far_rows, plan.p)],
        [*fields, owner_map, table],
        far=range(8),
        scratch=(
            *[pltpu.VMEM((2, plan.y, plan.p), field.dtype) for field in fields[:4]],
            *[pltpu.VMEM((2, plan.x, 8, plan.p), field.dtype) for field in fields],
            pltpu.VMEM(owner_map.shape, owner_map.dtype),
            pltpu.SMEM(table.shape, table.dtype),
            pltpu.SemaphoreType.DMA((22,)),
        ),
    )
    x_near, x_far = swap_near("gx", messages[0]), swap_far("gx", messages[1])
    y_near, y_far = swap_near("gy", messages[2]), swap_far("gy", messages[3])
    y_far, mask, kind = lax.optimization_barrier((y_far, mask, kind))
    mob, gather, spread, scale, *parts = call(
        local_kernel,
        plan,
        [
            block, (plan.owners, plan.rows), (plan.rows, 3 * plan.owners), (plan.owners, plan.p),
            (5, *block), block, block, block,
        ],
        [conc, pot, mask, kind, mass_source, pot_source, table, owner_map],
        smem=(6,),
    )
    slots = (plan.slots, plan.slot_parts, 4, plan.p) if plan.slots else (3 * plan.owners, plan.p)
    conc, pot, total, raw, near, far = call(
        first_kernel,
        plan,
        [
            block,
            block,
            slots,
            (4 * plan.x, plan.p),
            *[(2 * plan.y + 8, plan.p)] * 2,
        ],
        [
            x_far, x_near, y_far, y_near,
            conc, pot, mob, mass_source, pot_source, gather, scale, owner_map, *parts,
        ],
        out_far=(2,),
        scratch=(pltpu.VMEM(slots, F32), pltpu.SemaphoreType.DMA((plan.groups,))),
    )
    total = gather_totals(plan, total, y_near, y_far)
    far = swap_far("gx", far)
    near = swap_near("gx", near)
    faces, diagonal, scale, mass_part, pot_part = call(
        beside_kernel,
        plan,
        [(6, *block), block, block, block, block],
        [
            far, near, conc, pot, mass_source, pot_source, mob, raw,
            x_near, x_far, y_near, y_far,
        ],
    )
    return tuple(
        call(
            last_kernel,
            plan,
            [block, block],
            [conc, pot, mass_part, pot_part, faces, diagonal, scale, spread, total],
            out_far=(0, 1),
            scratch=(
                pltpu.VMEM(block, F32),
                pltpu.VMEM(block, F32),
                pltpu.SemaphoreType.DMA((2 * plan.x,)),
            ),
        )
    )


def solution(mesh):
    grid = P("gx", "gy", None)
    return jax.shard_map(
        on_device,
        mesh=mesh,
        in_specs=(grid,) * 6 + (P(), P(None, "gy")),
        out_specs=(grid, grid),
        check_vma=False,
    )
```
